32 devices in a mesh: seq: 8 (over z, x), tensor: 4 (over y, core).
Axes of the slice: x: 2, y: 2, z: 4, core: 2. Of those that a mesh axis runs over, the one named last changes fastest.
Arguments:
- hidden_in: bfloat16 [1024, 4096], P(('seq', 'tensor')), may hold values from -30 to 30
- prev_amax: float32 [], replicated, may hold values from 5 to 9
- w_x: bfloat16 [4096, 8192], P('seq', 'tensor'), may hold values from -0.09375 to 0.09375
- w_bc: bfloat16 [4096, 8, 2, 128], P('seq', 'tensor'), may hold values from -0.046875 to 0.046875
- w_dt: bfloat16 [4096, 128], P('seq', 'tensor'), may hold values from -0.09375 to 0.09375
- conv_x: float32 [4, 8192], P(None, 'tensor'), may hold values from -4 to 4
- conv_bc: float32 [4, 8, 2, 128], P(None, 'tensor'), may hold values from -4 to 4
- conv_state_x: bfloat16 [3, 8192], P(None, 'tensor'), may hold values from -6 to 6
- conv_state_bc: bfloat16 [3, 8, 2, 128], P(None, 'tensor'), may hold values from -3 to 3
- dt_bias: float32 [128], P('tensor'), may hold values from -2 to 1
- decay_rate: float32 [128], P('tensor'), may hold values from 9.765625e-05 to 0.12
- skip: float32 [128], P('tensor'), may hold values from 0.5 to 4
- init_state: float32 [128, 64, 128], P('tensor'), may hold values from -48 to 48
- norm_gain: float32 [8192], P('tensor'), may hold values from 0.1 to 1.9
- w_out: bfloat16 [8192, 4096], P('tensor', 'seq'), may hold values from -0.0625 to 0.0625
Outputs:
- layer_out: bfloat16 [1024, 4096], P(('seq', 'tensor'))
- abs_max: float32 [], replicated
The draws below stay inside these ranges and needn't reach their ends.
All inputs are finite; a program needn't handle non-finite values.
Results may differ from the reference program's by a relative error of at most 0.019.
Values may be sent and summed in bfloat16 or wider, within the bound.
No kernel may reach another device: no remote copies, remote signals or barrier semaphores. Data moves between devices by JAX's collectives and lax.ppermute only.
A program may use at most 64 MiB of HBM per device.

```python
import math
import jax
import jax.numpy as jnp
from jax import lax

D = 4096
HEADS = 128
HEAD_DIM = 64
STATE = 128
GROUPS = 8
KERNEL = 4
SPAN = 128
TOKENS = 1024
N_TENSOR = 4


def draw_hidden_in(key, part):
    noise_key, scale_key = jax.random.split(key)
    position = jnp.arange(TOKENS, dtype=jnp.float32) / TOKENS
    rising = jnp.exp(jnp.log(3.0) * position)
    roughness = jnp.exp(jax.random.uniform(scale_key, (TOKENS, 1), minval=0.0, maxval=jnp.log(10.0)))
    values = jax.random.truncated_normal(noise_key, -4.0, 4.0, (TOKENS, D))
    return (values * rising[:, None] * roughness * 0.25).astype(jnp.bfloat16)


def draw_decay_rate(key, part):
    pick_key, slow_key, fast_key = jax.random.split(key, 3)
    share = 0.5
    slow_side = jax.random.uniform(pick_key, (HEADS,)) < share
    slow_rate = jnp.exp(jax.random.uniform(slow_key, (HEADS,), minval=jnp.log(0.1 / TOKENS), maxval=jnp.log(1.0 / TOKENS)))
    fast_rate = jnp.exp(jax.random.uniform(fast_key, (HEADS,), minval=jnp.log(0.03), maxval=jnp.log(0.12)))
    return jnp.where(slow_side, slow_rate, fast_rate).astype(jnp.float32)


def level_of(own_key, extent, cuts, smallest, high):
    loudness, own = 1.0, jax.random.fold_in(own_key, 6)
    for dim, shards_of in cuts:
        steps = jnp.exp(jax.random.uniform(jax.random.fold_in(own, dim), (shards_of,), jnp.float32, smallest / len(cuts), high / len(cuts)))
        loudness = loudness * jnp.repeat(steps, extent[dim] // shards_of).reshape([-1 if axis == dim else 1 for axis in range(len(extent))])
    return loudness


def scatter_about(key, shape, deviation, bound, cuts=(), held_as=jnp.bfloat16):
    result = jax.random.normal(key, shape, jnp.float32) * deviation
    if len(cuts) > 0:
        result = level_of(key, shape, cuts, -0.22, 0.18) * result
    return jnp.clip(result, min=-bound, max=bound).astype(held_as)


def setup_inputs(seed: int = 0) -> dict:
    keys = jax.random.split(jax.random.key(seed), 16)
    hidden_in = draw_hidden_in(jax.random.fold_in(keys[15], 71), 0)
    prev_amax = jnp.clip(jax.random.uniform(keys[1], (), jnp.float32, 5.0, 9.0), 5.0, 9.0)
    w_x = scatter_about(keys[2], (D, HEADS * HEAD_DIM), D ** -0.5, 0.09375, ((0, 8), (1, 4)))
    w_bc = scatter_about(keys[3], (D, GROUPS, 2, STATE), (4 * D) ** -0.5, 0.046875, ((0, 8), (1, 4)))
    w_dt = scatter_about(keys[4], (D, HEADS), D ** -0.5, 0.09375, ((0, 8), (1, 4)))
    conv_x = scatter_about(keys[5], (KERNEL, HEADS * HEAD_DIM), 2 ** -0.5, 4.0, ((1, 4),), jnp.float32)
    conv_bc = scatter_about(keys[6], (KERNEL, GROUPS, 2, STATE), 2 ** -0.5, 4.0, ((1, 4),), jnp.float32)
    conv_state_x = scatter_about(keys[7], (KERNEL - 1, HEADS * HEAD_DIM), 1.0, 6.0, ((1, 4),))
    conv_state_bc = scatter_about(keys[8], (KERNEL - 1, GROUPS, 2, STATE), 0.5, 3.0, ((1, 4),))
    dt_bias = jnp.clip(-2.0 + 3.0 * jax.random.uniform(keys[9], (HEADS,), jnp.float32) ** level_of(keys[9], (HEADS,), ((0, 4),), -0.2, 0.2), -2.0, 1.0)
    decay_rate = draw_decay_rate(jax.random.fold_in(keys[15], 71), 0)
    skip = jnp.clip(jnp.exp(math.log(4.0) - 2.0794415 * jax.random.uniform(keys[11], (HEADS,), jnp.float32) ** level_of(keys[11], (HEADS,), ((0, 4),), -0.2, 0.2)), 0.5, 4.0)
    init_state = scatter_about(keys[12], (HEADS, HEAD_DIM, STATE), 8.0, 48.0, ((0, 4),), jnp.float32)
    norm_gain = jnp.clip(1.0 + 0.18 * jax.random.normal(keys[13], (HEADS * HEAD_DIM,), jnp.float32), 0.1, 1.9)
    w_out = scatter_about(keys[14], (HEADS * HEAD_DIM, D), (HEADS * HEAD_DIM) ** -0.5, 0.0625, ((0, 4), (1, 8)))
    return {"hidden_in": hidden_in, "prev_amax": prev_amax, "w_x": w_x, "w_bc": w_bc, "w_dt": w_dt, "conv_x": conv_x, "conv_bc": conv_bc, "conv_state_x": conv_state_x, "conv_state_bc": conv_state_bc, "dt_bias": dt_bias, "decay_rate": decay_rate, "skip": skip, "init_state": init_state, "norm_gain": norm_gain, "w_out": w_out}


epsilon = 1e-05
quant_range = 448.0

def depthwise(before, projected, conv_taps, length):
    extended = jnp.concatenate([before, projected], axis=0)
    summed = conv_taps[0] * extended[0:length]
    for offset in range(1, KERNEL):
        summed = summed + conv_taps[offset] * extended[offset:offset + length]
    return jax.nn.silu(summed).astype(jnp.bfloat16)

def reference(hidden_in, prev_amax, w_x, w_bc, w_dt, conv_x, conv_bc, conv_state_x, conv_state_bc, dt_bias, decay_rate, skip, init_state, norm_gain, w_out):
    abs_max = jnp.max(jnp.abs(hidden_in.astype(jnp.float32)))
    in_scale = prev_amax / quant_range
    scaled = hidden_in.astype(jnp.float32) * (quant_range / prev_amax)
    quant = jnp.clip(scaled, -quant_range, quant_range).astype(jnp.bfloat16)
    bc_width = GROUPS * 2 * STATE
    x_pre = (jnp.dot(quant, w_x, preferred_element_type=jnp.float32) * in_scale).astype(jnp.bfloat16)
    bc_pre = (jnp.dot(quant, w_bc.reshape(D, bc_width), preferred_element_type=jnp.float32) * in_scale).astype(jnp.bfloat16)
    dt_raw = jnp.dot(quant, w_dt, preferred_element_type=jnp.float32) * in_scale
    x_act = depthwise(conv_state_x, x_pre, conv_x, TOKENS)
    bc_act = depthwise(conv_state_bc.reshape(KERNEL - 1, bc_width), bc_pre, conv_bc.reshape(KERNEL, bc_width), TOKENS)
    step_size = jax.nn.softplus(dt_raw + dt_bias)
    blocks = TOKENS // SPAN
    per_group = HEADS // GROUPS
    x_blocks = x_act.reshape(blocks, SPAN, HEADS, HEAD_DIM)
    bc_blocks = bc_act.reshape(blocks, SPAN, GROUPS, 2, STATE)
    step_blocks = step_size.reshape(blocks, SPAN, HEADS)
    cum_blocks = jnp.cumsum(-step_blocks * decay_rate, axis=1)
    index_row = jnp.arange(SPAN, dtype=jnp.int32)
    lower_mask = index_row[:, None] >= index_row[None, :]

    def advance(carried, element):
        x_block, in_map, out_map, step_block, cum_block = element
        in_heads = jnp.repeat(in_map, per_group, axis=1).astype(jnp.float32)
        out_heads = jnp.repeat(out_map, per_group, axis=1).astype(jnp.float32)
        intersection = jnp.einsum('tgn,ugn->gtu', out_map.astype(jnp.float32), in_map.astype(jnp.float32))
        intersection = jnp.repeat(intersection, per_group, axis=0)
        cum_heads = cum_block.T
        log_gap = cum_heads[:, :, None] - cum_heads[:, None, :]
        decay = jnp.exp(jnp.where(lower_mask[None], log_gap, -1e+30))
        weights = (intersection * decay * step_block.T[:, None, :]).astype(jnp.bfloat16)
        x_float = x_block.astype(jnp.float32)
        local_part = jnp.einsum('htu,uhp->thp', weights.astype(jnp.float32), x_float)
        carried_part = jnp.einsum('thn,hpn->thp', out_heads, carried, precision=lax.Precision.HIGHEST) * jnp.exp(cum_block)[:, :, None]
        ssm_out = local_part + carried_part + skip[None, :, None] * x_float
        x_weighted = (x_float * (step_block * jnp.exp(cum_block[-1] - cum_block))[:, :, None]).astype(jnp.bfloat16)
        added = jnp.einsum('uhp,uhn->hpn', x_weighted.astype(jnp.float32), in_heads)
        carried = jnp.exp(cum_block[-1])[:, None, None] * carried + added
        return (carried, ssm_out)
    inputs = (x_blocks, bc_blocks[:, :, :, 0], bc_blocks[:, :, :, 1], step_blocks, cum_blocks)
    unused, outputs = lax.scan(advance, init_state.astype(jnp.float32), inputs)
    ssm_out = outputs.reshape(TOKENS, HEADS * HEAD_DIM)
    mean_sq = lax.optimization_barrier(jnp.mean(ssm_out * ssm_out, axis=1))
    normed = (ssm_out * lax.rsqrt(mean_sq + epsilon)[:, None] * norm_gain).astype(jnp.bfloat16)
    run_width = HEADS * HEAD_DIM // N_TENSOR
    summed = jnp.zeros((TOKENS, D), jnp.float32)
    for run_index in range(N_TENSOR):
        partial_out = jnp.dot(normed[:, run_index * run_width:(run_index + 1) * run_width], w_out[run_index * run_width:(run_index + 1) * run_width], preferred_element_type=jnp.float32)
        summed = summed + partial_out.astype(jnp.bfloat16).astype(jnp.float32)
    return (summed.astype(jnp.bfloat16), abs_max)
```

```python
import jax
import jax.numpy as jnp
from jax import lax
from jax.sharding import PartitionSpec as P

HEADS = 128
HEAD_DIM = 64
STATE = 128
GROUPS = 8
KERNEL = 4
SPAN = 128


epsilon = 1e-05
quant_range = 448.0


def from_behind(value, axis, steps):
    count = lax.axis_size(axis)
    first, last = (max(0, -steps), min(count, count - steps))
    return lax.ppermute(value, axis, [(source, source + steps) for source in range(first, last)])


def carried_in(shard, axis, combine, identity):
    count, here = (lax.axis_size(axis), lax.axis_index(axis))
    everything = jax.tree.map(
        lambda part, kind: lax.all_gather(part.astype(kind), axis),
        shard,
        (jnp.bfloat16, jnp.bfloat16),
    )
    start = jax.tree.map(
        lambda part, zero: jnp.broadcast_to(jnp.asarray(zero, part.dtype), part.shape),
        shard,
        identity,
    )

    def turn(k, before):
        reached = k < here
        new = combine(
            before, jax.tree.map(lambda part, own: part[k].astype(own.dtype), everything, shard)
        )
        return jax.tree.map(lambda a, b: jnp.where(reached, a, b), new, before)

    return lax.fori_loop(0, count, turn, start)


def depthwise(before, projected, conv_taps, length):
    extended = jnp.concatenate([before, projected], axis=0)
    summed = conv_taps[0] * extended[0:length]
    for offset in range(1, KERNEL):
        summed = summed + conv_taps[offset] * extended[offset : offset + length]
    return jax.nn.silu(summed).astype(jnp.bfloat16)


def combine(earlier, later):
    return (earlier[0] * later[0], later[0][:, None, None] * earlier[1] + later[1])


def by_tokens(
    hidden_in,
    prev_amax,
    w_x,
    w_bc,
    w_dt,
    conv_x,
    conv_bc,
    conv_state_x,
    conv_state_bc,
    dt_bias,
    decay_rate,
    skip,
    init_state,
    norm_gain,
    w_out,
):
    margin = KERNEL - 1
    gathered = lax.all_gather(hidden_in, "tensor", axis=0, tiled=True)
    abs_max = lax.pmax(jnp.max(jnp.abs(gathered.astype(jnp.float32))), "seq")
    in_scale = prev_amax / quant_range
    leading = lax.axis_index("seq") == 0
    row_count = gathered.shape[0]
    bc_width = w_bc.shape[1] * w_bc.shape[2] * w_bc.shape[3]
    bc_rows = jnp.reshape(w_bc, (w_bc.shape[0], bc_width))
    scaled = gathered.astype(jnp.float32) * (quant_range / prev_amax)
    quant = jnp.clip(scaled, -quant_range, quant_range).astype(jnp.bfloat16)
    pieces = (
        lax.all_gather(w_x, "seq", axis=0, tiled=True),
        lax.all_gather(bc_rows, "seq", axis=0, tiled=True),
        lax.all_gather(w_dt, "seq", axis=0, tiled=True),
    )
    x_proj, bc_proj, dt_proj = tuple(
        (
            jnp.dot(quant, weight_piece, preferred_element_type=jnp.float32)
            for weight_piece in pieces
        )
    )
    x_whole = (x_proj * in_scale).astype(jnp.bfloat16)
    bc_whole = (bc_proj * in_scale).astype(jnp.bfloat16)
    dt_raw = dt_proj * in_scale
    state_bc = jnp.reshape(conv_state_bc, (margin, bc_width))
    received = from_behind(
        (x_whole[row_count - margin :], bc_whole[row_count - margin :]), "seq", 1
    )
    x_edge = jnp.where(leading, conv_state_x, received[0])
    bc_edge = jnp.where(leading, state_bc, received[1])
    x_act = depthwise(x_edge, x_whole, conv_x, row_count)
    bc_act = depthwise(bc_edge, bc_whole, jnp.reshape(conv_bc, (KERNEL, bc_width)), row_count)
    step_size = jax.nn.softplus(dt_raw + dt_bias)
    heads_here = step_size.shape[1]
    groups_here = w_bc.shape[1]
    per_group = HEADS // GROUPS
    blocks = row_count // SPAN
    x_blocks = x_act.reshape(blocks, SPAN, heads_here, HEAD_DIM)
    bc_blocks = bc_act.reshape(blocks, SPAN, groups_here, 2, STATE)
    in_map = bc_blocks[:, :, :, 0]
    out_map = bc_blocks[:, :, :, 1]
    step_blocks = step_size.reshape(blocks, SPAN, heads_here)
    cum_blocks = jnp.cumsum(-step_blocks * decay_rate, axis=1)
    index_row = jnp.arange(SPAN, dtype=jnp.int32)
    lower_mask = index_row[:, None] >= index_row[None, :]
    intersection = jnp.einsum(
        "ctgn,cugn->cgtu", out_map, in_map, preferred_element_type=jnp.float32
    )
    intersection = jnp.repeat(intersection, per_group, axis=1)
    cum_heads = jnp.transpose(cum_blocks, (0, 2, 1))
    log_gap = cum_heads[:, :, :, None] - cum_heads[:, :, None, :]
    decay = jnp.exp(jnp.where(lower_mask[None, None], log_gap, -1e30))
    step_heads = jnp.transpose(step_blocks, (0, 2, 1))
    weights = (intersection * decay * step_heads[:, :, None, :]).astype(jnp.bfloat16)
    local_part = jnp.einsum(
        "chtu,cuhp->cthp", weights, x_blocks, preferred_element_type=jnp.float32
    )
    last_cum = cum_blocks[:, SPAN - 1, :]
    x_weighted = (
        x_blocks.astype(jnp.float32)
        * (step_blocks * jnp.exp(last_cum[:, None, :] - cum_blocks))[:, :, :, None]
    ).astype(jnp.bfloat16)
    in_heads = jnp.repeat(in_map, per_group, axis=2)
    added = jnp.einsum("cuhp,cuhn->chpn", x_weighted, in_heads, preferred_element_type=jnp.float32)

    def carry_on(carried, element):
        block_decay, block_added = element
        return (block_decay[:, None, None] * carried + block_added, carried)

    empty_state = jnp.zeros((heads_here, HEAD_DIM, STATE), jnp.float32)
    device_state, entering = lax.scan(carry_on, empty_state, (jnp.exp(last_cum), added))
    device_decay = jnp.exp(jnp.sum(last_cum, axis=0))
    seeded = device_state + jnp.where(leading, device_decay[:, None, None] * init_state, 0.0)
    identity = (jnp.ones_like(device_decay), jnp.zeros_like(device_state))
    scanned = carried_in((device_decay, seeded), "seq", combine, identity)
    incoming = jnp.where(leading, init_state, scanned[1])
    prefix = jnp.exp(jnp.cumsum(last_cum, axis=0) - last_cum)
    states_in = entering + prefix[:, :, None, None] * incoming[None]
    out_heads = jnp.repeat(out_map, per_group, axis=2).astype(jnp.float32)
    carried_part = (
        jnp.einsum("cthn,chpn->cthp", out_heads, states_in, precision=lax.Precision.HIGHEST)
        * jnp.exp(cum_blocks)[:, :, :, None]
    )
    ssm_out = local_part + carried_part + skip[None, None, :, None] * x_blocks.astype(jnp.float32)
    ssm_out = ssm_out.reshape(row_count, heads_here * HEAD_DIM)
    squares = lax.psum(jnp.sum(ssm_out * ssm_out, axis=1), "tensor")
    mean_sq = squares / (HEADS * HEAD_DIM)
    normed = (ssm_out * lax.rsqrt(mean_sq + epsilon)[:, None] * norm_gain).astype(jnp.bfloat16)
    partial_out = jnp.dot(
        normed, lax.all_gather(w_out, "seq", axis=1, tiled=True), preferred_element_type=jnp.float32
    )
    layer_out = lax.psum_scatter(
        partial_out.astype(jnp.bfloat16), "tensor", scatter_dimension=0, tiled=True
    )
    return (layer_out, abs_max)


def project(weight, quant, in_scale):
    return jnp.dot(quant, weight, preferred_element_type=jnp.float32) * in_scale


def by_heads(
    hidden_in,
    prev_amax,
    w_x,
    w_bc,
    w_dt,
    conv_x,
    conv_bc,
    conv_state_x,
    conv_state_bc,
    dt_bias,
    decay_rate,
    skip,
    init_state,
    norm_gain,
    w_out,
):
    margin = KERNEL - 1
    count, here = (lax.axis_size("seq"), lax.axis_index("seq"))
    abs_max = lax.pmax(jnp.max(jnp.abs(hidden_in.astype(jnp.float32))), ("seq", "tensor"))
    in_scale = prev_amax / quant_range
    scaled = hidden_in.astype(jnp.float32) * (quant_range / prev_amax)
    quant_rows = jnp.clip(scaled, -quant_range, quant_range).astype(jnp.bfloat16)
    depth = w_x.shape[0]
    own = hidden_in.shape[0]
    ranks = lax.axis_size("tensor")
    pieces = quant_rows.reshape(own, count, depth).transpose(1, 0, 2)
    mine = lax.all_to_all(pieces, "seq", split_axis=0, concat_axis=0, tiled=True)
    rows = lax.all_gather(mine, "tensor", axis=1)
    tokens = count * ranks * own
    quant = rows.reshape(tokens, depth)
    bc_width = w_bc.shape[1] * w_bc.shape[2] * w_bc.shape[3]
    channels = w_x.shape[1] // count
    heads_all = w_dt.shape[1]
    heads_here = heads_all // count
    groups_here = w_bc.shape[1]
    sharing = count // groups_here
    x_part = jnp.stack(
        [
            project(w_x[:, k * channels : (k + 1) * channels], quant, in_scale)
            for k in range(count)
        ]
    ).astype(jnp.bfloat16)
    x_pre = lax.psum_scatter(x_part, "seq", scatter_dimension=0, tiled=True)[0]
    bc_part = project(w_bc.reshape(depth, bc_width), quant, in_scale).astype(jnp.bfloat16)
    bc_pre = lax.psum(bc_part, "seq")
    dt_part = project(w_dt, quant, in_scale)
    dt_raw = lax.psum(dt_part, "seq")
    group = here // sharing
    group_width = 2 * STATE
    bc_mine = lax.dynamic_slice_in_dim(bc_pre, group * group_width, group_width, axis=1)
    dt_mine = lax.dynamic_slice_in_dim(dt_raw, here * heads_here, heads_here, axis=1)
    channel_at = here * channels
    head_at = here * heads_here
    x_edge = lax.dynamic_slice_in_dim(conv_state_x, channel_at, channels, axis=1)
    x_taps = lax.dynamic_slice_in_dim(conv_x, channel_at, channels, axis=1)
    bc_edge = lax.dynamic_slice_in_dim(
        conv_state_bc.reshape(margin, bc_width), group * group_width, group_width, axis=1
    )
    bc_taps = lax.dynamic_slice_in_dim(
        conv_bc.reshape(KERNEL, bc_width), group * group_width, group_width, axis=1
    )
    x_act = depthwise(x_edge, x_pre, x_taps, tokens)
    bc_act = depthwise(bc_edge, bc_mine, bc_taps, tokens)
    bias = lax.dynamic_slice_in_dim(dt_bias, head_at, heads_here)
    rate = lax.dynamic_slice_in_dim(decay_rate, head_at, heads_here)
    skips = lax.dynamic_slice_in_dim(skip, head_at, heads_here)
    start = lax.dynamic_slice_in_dim(init_state, head_at, heads_here, axis=0)
    step_size = jax.nn.softplus(dt_mine + bias)
    blocks = tokens // SPAN
    x_blocks = x_act.reshape(blocks, SPAN, heads_here, HEAD_DIM)
    in_map = bc_act[:, :STATE].reshape(blocks, SPAN, STATE)
    out_map = bc_act[:, STATE:].reshape(blocks, SPAN, STATE)
    step_blocks = step_size.reshape(blocks, SPAN, heads_here)
    cum_blocks = jnp.cumsum(-step_blocks * rate, axis=1)
    index_row = jnp.arange(SPAN, dtype=jnp.int32)
    lower_mask = index_row[:, None] >= index_row[None, :]
    intersection = jnp.einsum("ctn,cun->ctu", out_map, in_map, preferred_element_type=jnp.float32)
    cum_heads = jnp.transpose(cum_blocks, (0, 2, 1))
    log_gap = cum_heads[:, :, :, None] - cum_heads[:, :, None, :]
    decay = jnp.exp(jnp.where(lower_mask[None, None], log_gap, -1e30))
    step_heads = jnp.transpose(step_blocks, (0, 2, 1))
    weights = (intersection[:, None] * decay * step_heads[:, :, None, :]).astype(jnp.bfloat16)
    local_part = jnp.einsum("chtu,cuhp->cthp", weights, x_blocks, preferred_element_type=jnp.float32)
    last_cum = cum_blocks[:, SPAN - 1, :]
    x_weighted = (
        x_blocks.astype(jnp.float32)
        * (step_blocks * jnp.exp(last_cum[:, None, :] - cum_blocks))[:, :, :, None]
    ).astype(jnp.bfloat16)
    added = jnp.einsum("cuhp,cun->chpn", x_weighted, in_map, preferred_element_type=jnp.float32)

    def carry_on(carried, element):
        block_decay, block_added = element
        return (block_decay[:, None, None] * carried + block_added, carried)

    unused, states_in = lax.scan(carry_on, start, (jnp.exp(last_cum), added))
    carried_part = (
        jnp.einsum(
            "ctn,chpn->cthp", out_map.astype(jnp.float32), states_in, precision=lax.Precision.HIGHEST
        )
        * jnp.exp(cum_blocks)[:, :, :, None]
    )
    ssm_out = local_part + carried_part + skips[None, None, :, None] * x_blocks.astype(jnp.float32)
    ssm_out = ssm_out.reshape(tokens, channels)
    squares = lax.psum(jnp.sum(ssm_out * ssm_out, axis=1), ("seq", "tensor"))
    gain = lax.dynamic_slice_in_dim(norm_gain, channel_at, channels)
    gained = (ssm_out * gain).astype(jnp.bfloat16)
    every = lax.all_gather(gained, "seq")
    partial_out = sum(
        jnp.dot(
            every[k], w_out[k * channels : (k + 1) * channels], preferred_element_type=jnp.float32
        )
        for k in range(count)
    )
    mean_sq = squares / (HEADS * HEAD_DIM)
    partial_out = (partial_out * lax.rsqrt(mean_sq + epsilon)[:, None]).astype(jnp.bfloat16)
    width = w_out.shape[1]
    by_owner = partial_out.reshape(count, ranks, own, width)
    reduced = lax.psum_scatter(by_owner, "tensor", scatter_dimension=1, tiled=True)[:, 0]
    final = lax.all_to_all(reduced, "seq", split_axis=0, concat_axis=0, tiled=True)
    layer_out = final.transpose(1, 0, 2).reshape(own, count * width)
    return (layer_out, abs_max)


def solution(mesh):
    blocks_of_tokens = mesh.shape["seq"]
    heads_here = HEADS // mesh.shape["tensor"]
    groups_here = GROUPS // mesh.shape["tensor"]
    splits = heads_here % blocks_of_tokens == 0 and blocks_of_tokens % groups_here == 0
    return jax.shard_map(
        by_heads if splits else by_tokens,
        mesh=mesh,
        in_specs=(
            P(("seq", "tensor"), None),
            P(),
            P("seq", "tensor"),
            P("seq", "tensor", None, None),
            P("seq", "tensor"),
            P(None, "tensor"),
            P(None, "tensor", None, None),
            P(None, "tensor"),
            P(None, "tensor", None, None),
            P("tensor"),
            P("tensor"),
            P("tensor"),
            P("tensor", None, None),
            P("tensor"),
            P("tensor", "seq"),
        ),
        out_specs=(P(("seq", "tensor"), None), P()),
        check_vma=False,
    )
```

```python
import jax
import jax.numpy as jnp
from jax import lax
from jax.experimental import pallas as pl
from jax.experimental.pallas import tpu as pltpu
from jax.sharding import PartitionSpec as P

HEADS = 128
HEAD_DIM = 64
STATE = 128
GROUPS = 8
KERNEL = 4
SPAN = 128


epsilon = 1e-05
quant_range = 448.0


def from_behind(value, axis, steps):
    count = lax.axis_size(axis)
    first, last = (max(0, -steps), min(count, count - steps))
    return lax.ppermute(value, axis, [(source, source + steps) for source in range(first, last)])


def carried_in(shard, axis, combine, identity):
    count, here = (lax.axis_size(axis), lax.axis_index(axis))
    everything = jax.tree.map(
        lambda part, kind: lax.all_gather(part.astype(kind), axis),
        shard,
        (jnp.bfloat16, jnp.bfloat16),
    )
    start = jax.tree.map(
        lambda part, zero: jnp.broadcast_to(jnp.asarray(zero, part.dtype), part.shape),
        shard,
        identity,
    )

    def turn(k, before):
        reached = k < here
        new = combine(
            before, jax.tree.map(lambda part, own: part[k].astype(own.dtype), everything, shard)
        )
        return jax.tree.map(lambda a, b: jnp.where(reached, a, b), new, before)

    return lax.fori_loop(0, count, turn, start)


def depthwise(before, projected, conv_taps, length):
    extended = jnp.concatenate([before, projected], axis=0)
    summed = conv_taps[0] * extended[0:length]
    for offset in range(1, KERNEL):
        summed = summed + conv_taps[offset] * extended[offset : offset + length]
    return jax.nn.silu(summed).astype(jnp.bfloat16)


def combine(earlier, later):
    return (earlier[0] * later[0], later[0][:, None, None] * earlier[1] + later[1])


def by_tokens(
    hidden_in,
    prev_amax,
    w_x,
    w_bc,
    w_dt,
    conv_x,
    conv_bc,
    conv_state_x,
    conv_state_bc,
    dt_bias,
    decay_rate,
    skip,
    init_state,
    norm_gain,
    w_out,
):
    margin = KERNEL - 1
    gathered = lax.all_gather(hidden_in, "tensor", axis=0, tiled=True)
    abs_max = lax.pmax(jnp.max(jnp.abs(gathered.astype(jnp.float32))), "seq")
    in_scale = prev_amax / quant_range
    leading = lax.axis_index("seq") == 0
    row_count = gathered.shape[0]
    bc_width = w_bc.shape[1] * w_bc.shape[2] * w_bc.shape[3]
    bc_rows = jnp.reshape(w_bc, (w_bc.shape[0], bc_width))
    scaled = gathered.astype(jnp.float32) * (quant_range / prev_amax)
    quant = jnp.clip(scaled, -quant_range, quant_range).astype(jnp.bfloat16)
    pieces = (
        lax.all_gather(w_x, "seq", axis=0, tiled=True),
        lax.all_gather(bc_rows, "seq", axis=0, tiled=True),
        lax.all_gather(w_dt, "seq", axis=0, tiled=True),
    )
    x_proj, bc_proj, dt_proj = tuple(
        (
            jnp.dot(quant, weight_piece, preferred_element_type=jnp.float32)
            for weight_piece in pieces
        )
    )
    x_whole = (x_proj * in_scale).astype(jnp.bfloat16)
    bc_whole = (bc_proj * in_scale).astype(jnp.bfloat16)
    dt_raw = dt_proj * in_scale
    state_bc = jnp.reshape(conv_state_bc, (margin, bc_width))
    received = from_behind(
        (x_whole[row_count - margin :], bc_whole[row_count - margin :]), "seq", 1
    )
    x_edge = jnp.where(leading, conv_state_x, received[0])
    bc_edge = jnp.where(leading, state_bc, received[1])
    x_act = depthwise(x_edge, x_whole, conv_x, row_count)
    bc_act = depthwise(bc_edge, bc_whole, jnp.reshape(conv_bc, (KERNEL, bc_width)), row_count)
    step_size = jax.nn.softplus(dt_raw + dt_bias)
    heads_here = step_size.shape[1]
    groups_here = w_bc.shape[1]
    per_group = HEADS // GROUPS
    blocks = row_count // SPAN
    x_blocks = x_act.reshape(blocks, SPAN, heads_here, HEAD_DIM)
    bc_blocks = bc_act.reshape(blocks, SPAN, groups_here, 2, STATE)
    in_map = bc_blocks[:, :, :, 0]
    out_map = bc_blocks[:, :, :, 1]
    step_blocks = step_size.reshape(blocks, SPAN, heads_here)
    cum_blocks = jnp.cumsum(-step_blocks * decay_rate, axis=1)
    index_row = jnp.arange(SPAN, dtype=jnp.int32)
    lower_mask = index_row[:, None] >= index_row[None, :]
    intersection = jnp.einsum(
        "ctgn,cugn->cgtu", out_map, in_map, preferred_element_type=jnp.float32
    )
    intersection = jnp.repeat(intersection, per_group, axis=1)
    cum_heads = jnp.transpose(cum_blocks, (0, 2, 1))
    log_gap = cum_heads[:, :, :, None] - cum_heads[:, :, None, :]
    decay = jnp.exp(jnp.where(lower_mask[None, None], log_gap, -1e30))
    step_heads = jnp.transpose(step_blocks, (0, 2, 1))
    weights = (intersection * decay * step_heads[:, :, None, :]).astype(jnp.bfloat16)
    local_part = jnp.einsum(
        "chtu,cuhp->cthp", weights, x_blocks, preferred_element_type=jnp.float32
    )
    last_cum = cum_blocks[:, SPAN - 1, :]
    x_weighted = (
        x_blocks.astype(jnp.float32)
        * (step_blocks * jnp.exp(last_cum[:, None, :] - cum_blocks))[:, :, :, None]
    ).astype(jnp.bfloat16)
    in_heads = jnp.repeat(in_map, per_group, axis=2)
    added = jnp.einsum("cuhp,cuhn->chpn", x_weighted, in_heads, preferred_element_type=jnp.float32)

    def carry_on(carried, element):
        block_decay, block_added = element
        return (block_decay[:, None, None] * carried + block_added, carried)

    empty_state = jnp.zeros((heads_here, HEAD_DIM, STATE), jnp.float32)
    device_state, entering = lax.scan(carry_on, empty_state, (jnp.exp(last_cum), added))
    device_decay = jnp.exp(jnp.sum(last_cum, axis=0))
    seeded = device_state + jnp.where(leading, device_decay[:, None, None] * init_state, 0.0)
    identity = (jnp.ones_like(device_decay), jnp.zeros_like(device_state))
    scanned = carried_in((device_decay, seeded), "seq", combine, identity)
    incoming = jnp.where(leading, init_state, scanned[1])
    prefix = jnp.exp(jnp.cumsum(last_cum, axis=0) - last_cum)
    states_in = entering + prefix[:, :, None, None] * incoming[None]
    out_heads = jnp.repeat(out_map, per_group, axis=2).astype(jnp.float32)
    carried_part = (
        jnp.einsum("cthn,chpn->cthp", out_heads, states_in, precision=lax.Precision.HIGHEST)
        * jnp.exp(cum_blocks)[:, :, :, None]
    )
    ssm_out = local_part + carried_part + skip[None, None, :, None] * x_blocks.astype(jnp.float32)
    ssm_out = ssm_out.reshape(row_count, heads_here * HEAD_DIM)
    squares = lax.psum(jnp.sum(ssm_out * ssm_out, axis=1), "tensor")
    mean_sq = squares / (HEADS * HEAD_DIM)
    normed = (ssm_out * lax.rsqrt(mean_sq + epsilon)[:, None] * norm_gain).astype(jnp.bfloat16)
    partial_out = jnp.dot(
        normed, lax.all_gather(w_out, "seq", axis=1, tiled=True), preferred_element_type=jnp.float32
    )
    layer_out = lax.psum_scatter(
        partial_out.astype(jnp.bfloat16), "tensor", scatter_dimension=0, tiled=True
    )
    return (layer_out, abs_max)


PAIR = 2
VMEM = pl.BlockSpec(memory_space=pltpu.VMEM)
SMEM = pl.BlockSpec(memory_space=pltpu.SMEM)
HIGHEST = lax.Precision.HIGHEST


def splits(mesh):
    count, ranks = (mesh.shape["seq"], mesh.shape["tensor"])
    heads_all, groups_here = (HEADS // ranks, GROUPS // ranks)
    if heads_all % count or count % (PAIR * groups_here) or ranks & (ranks - 1):
        return False
    return heads_all // count * HEAD_DIM == 2 * SPAN and count <= 8


def project_kernel(factor_ref, *refs):
    ranks = len(refs) - 11
    hidden = refs[:ranks]
    own_x, other_x, own_bc, other_bc, own_dt, other_dt = refs[ranks : ranks + 6]
    x_ref, bc_ref, dt_ref, largest_ref, quant_ref = refs[ranks + 6 :]
    factor = factor_ref[0]
    largest = None
    for j in range(ranks):
        values = hidden[j][...].astype(jnp.float32)
        quant_ref[:, j] = jnp.clip(values * factor, -quant_range, quant_range).astype(jnp.bfloat16)
        flat = jnp.abs(values).reshape(-1, 8, values.shape[-1])
        top = jnp.max(flat, axis=0)
        largest = top if largest is None else jnp.maximum(largest, top)
    depth = own_x.shape[0]
    width = largest_ref.shape[1]
    top = largest[:, :width]
    for at in range(width, largest.shape[1], width):
        top = jnp.maximum(top, largest[:, at : at + width])
    first = pl.program_id(0) == 0

    @pl.when(first)
    def _():
        largest_ref[...] = top

    @pl.when(jnp.logical_not(first))
    def _():
        largest_ref[...] = jnp.maximum(largest_ref[...], top)

    rows = x_ref.shape[1]
    quant = quant_ref[...].reshape(rows, PAIR * depth)
    near, far = (quant[:, :depth], quant[:, depth:])

    def both(own, other):
        return jnp.dot(near, own, preferred_element_type=jnp.float32) + jnp.dot(
            far, other, preferred_element_type=jnp.float32
        )

    for out_ref, own, other in ((x_ref, own_x, other_x), (bc_ref, own_bc, other_bc)):
        wide = out_ref.shape[2]
        for k in range(out_ref.shape[0]):
            cut = slice(k * wide, (k + 1) * wide)
            out_ref[k] = both(own[:, cut], other[:, cut]).astype(jnp.bfloat16)
    last = (((1,), (1,)), ((), ()))
    dt_ref[...] = lax.dot_general(
        own_dt[...], near, last, preferred_element_type=jnp.float32
    ) + lax.dot_general(other_dt[...], far, last, preferred_element_type=jnp.float32)


def project(factor, hidden, weights, blocks_z, groups_here):
    count, own, wide = hidden[0].shape
    ranks = len(hidden)
    tokens = count * ranks * own
    cuts = 2 if count % 2 == 0 else 1
    own_x, _, own_bc, _, own_dt, _ = weights
    x_wide = own_x.shape[1] // blocks_z
    bc_wide = own_bc.shape[1] // groups_here
    part = tokens // cuts
    return pl.pallas_call(
        project_kernel,
        grid=(cuts,),
        in_specs=[SMEM]
        + [pl.BlockSpec((count // cuts, own, wide), lambda i: (i, 0, 0))] * ranks
        + [pl.BlockSpec(w.shape, lambda i: (0, 0)) for w in weights],
        out_specs=[
            pl.BlockSpec((blocks_z, part, x_wide), lambda i: (0, i, 0)),
            pl.BlockSpec((groups_here, part, bc_wide), lambda i: (0, i, 0)),
            pl.BlockSpec((own_dt.shape[0], part), lambda i: (0, i)),
            pl.BlockSpec((8, 128), lambda i: (0, 0)),
        ],
        out_shape=[
            jax.ShapeDtypeStruct((blocks_z, tokens, x_wide), jnp.bfloat16),
            jax.ShapeDtypeStruct((groups_here, tokens, bc_wide), jnp.bfloat16),
            jax.ShapeDtypeStruct((own_dt.shape[0], tokens), jnp.float32),
            jax.ShapeDtypeStruct((8, 128), jnp.float32),
        ],
        scratch_shapes=[pltpu.VMEM((count // cuts, ranks, own, wide), jnp.bfloat16)],
        compiler_params=pltpu.CompilerParams(vmem_limit_bytes=40 * 2**20),
        cost_estimate=pl.CostEstimate(
            flops=2 * tokens * wide * (own_x.shape[1] + own_bc.shape[1]),
            bytes_accessed=2 * tokens * (wide + own_x.shape[1]),
            transcendentals=0,
        ),
        name="project",
    )(factor, *hidden, *weights)


def scan_kernel(
    place_ref,
    scale_ref,
    own_ref,
    right_ref,
    left_ref,
    bc_mine_ref,
    bc_other_ref,
    dt_ref,
    x_edge_ref,
    x_taps_ref,
    bc_edge_ref,
    bc_taps_ref,
    bias_ref,
    rate_ref,
    skip_ref,
    gain_ref,
    state_ref,
    largest_ref,
    out_ref,
    x_buf,
    bc_buf,
    state,
    squares,
):
    block = pl.program_id(0)
    ranks, own, channels = own_ref.shape[1:]
    heads = channels // HEAD_DIM
    rank, side = (place_ref[0], place_ref[1])
    edge = 8

    @pl.when(block == 0)
    def _():
        x_buf[:edge] = x_edge_ref[...]
        bc_buf[:edge] = bc_edge_ref[...]
        state[...] = state_ref[...].T
        squares[...] = jnp.zeros_like(squares)

    @pl.when(block > 0)
    def _():
        x_buf[:edge] = x_buf[SPAN : SPAN + edge]
        bc_buf[:edge] = bc_buf[SPAN : SPAN + edge]

    in_scale = scale_ref[0]
    for true_rank in range(ranks):
        j = true_rank ^ rank
        at = slice(edge + true_rank * own, edge + (true_rank + 1) * own)
        total = own_ref[0, j].astype(jnp.float32) + right_ref[0, j].astype(jnp.float32)
        total = (total + left_ref[0, j].astype(jnp.float32)) * in_scale
        x_buf[at] = total.astype(jnp.bfloat16).astype(jnp.float32)
        mine = bc_mine_ref[0, j].astype(jnp.float32)
        other = bc_other_ref[0, j].astype(jnp.float32)
        bc_buf[at, :STATE] = jnp.where(side == 0, mine, other)
        bc_buf[at, STATE:] = jnp.where(side == 0, other, mine)

    def activate(buf, taps_ref):
        start = edge - (KERNEL - 1)
        summed = taps_ref[0:1] * buf[start : start + SPAN]
        for k in range(1, KERNEL):
            summed = summed + taps_ref[k : k + 1] * buf[start + k : start + k + SPAN]
        return (summed / (1.0 + jnp.exp(-summed))).astype(jnp.bfloat16)

    x_act = activate(x_buf, x_taps_ref)
    bc_act = activate(bc_buf, bc_taps_ref)
    in_map, out_map = (bc_act[:, :STATE], bc_act[:, STATE:])
    raw = dt_ref[...] + bias_ref[...]
    step = jnp.maximum(raw, 0.0) + jnp.log1p(jnp.exp(-jnp.abs(raw)))
    up = lax.broadcasted_iota(jnp.int32, (SPAN, SPAN), 0)
    across = lax.broadcasted_iota(jnp.int32, (SPAN, SPAN), 1)
    upper = (up <= across).astype(jnp.float32)
    cum = jnp.dot(
        -step * rate_ref[...], upper, precision=HIGHEST, preferred_element_type=jnp.float32
    )
    last = cum[:, SPAN - 1 : SPAN]
    rows = cum.shape[0]
    stacked = jnp.concatenate(
        [
            cum,
            step * jnp.exp(last - cum),
            jnp.exp(cum),
            jnp.zeros((SPAN - 3 * rows, SPAN), jnp.float32),
        ],
        axis=0,
    )
    turned = stacked.T
    lane = lax.broadcasted_iota(jnp.int32, (SPAN, channels), 1)

    def spread(first):
        result = jnp.broadcast_to(turned[:, first : first + 1], (SPAN, channels))
        for h in range(1, heads):
            column = turned[:, first + h : first + h + 1]
            result = jnp.where(lane >= h * HEAD_DIM, column, result)
        return result

    inner = lax.dot_general(
        out_map, in_map, (((1,), (1,)), ((), ())), preferred_element_type=jnp.float32
    )
    inner = jnp.where(up >= across, inner, 0.0)
    weights, spaced = ([], [])
    for h in range(heads):
        gap = jnp.where(up >= across, turned[:, h : h + 1] - cum[h : h + 1], 0.0)
        weights.append((inner * jnp.exp(gap) * step[h : h + 1]).astype(jnp.bfloat16))
        inside = (lane >= h * HEAD_DIM) & (lane < (h + 1) * HEAD_DIM)
        spaced.append(jnp.where(inside, x_act.astype(jnp.float32), 0.0).astype(jnp.bfloat16))
    local_part = jnp.dot(
        jnp.concatenate(weights, axis=1),
        jnp.concatenate(spaced, axis=0),
        preferred_element_type=jnp.float32,
    )
    before = state[...]
    high = before.astype(jnp.bfloat16)
    rest = before - high.astype(jnp.float32)
    middle = rest.astype(jnp.bfloat16)
    low = (rest - middle.astype(jnp.float32)).astype(jnp.bfloat16)
    carried = jnp.dot(out_map, high, preferred_element_type=jnp.float32)
    carried = carried + jnp.dot(out_map, middle, preferred_element_type=jnp.float32)
    carried = carried + jnp.dot(out_map, low, preferred_element_type=jnp.float32)
    x_wide = x_act.astype(jnp.float32)
    grown = spread(2 * rows)
    ssm_out = local_part + grown * carried + skip_ref[...] * x_wide
    x_weighted = (x_wide * spread(rows)).astype(jnp.bfloat16)
    added = lax.dot_general(
        in_map, x_weighted, (((0,), (0,)), ((), ())), preferred_element_type=jnp.float32
    )
    state[...] = grown[SPAN - 1 : SPAN] * before + added
    at = pl.multiple_of(block * SPAN, SPAN)
    out_ref[pl.ds(at, SPAN)] = (ssm_out * gain_ref[...]).astype(jnp.bfloat16)
    summed = lax.dot_general(
        jnp.ones((8, channels), jnp.float32),
        ssm_out * ssm_out,
        (((1,), (1,)), ((), ())),
        precision=HIGHEST,
        preferred_element_type=jnp.float32,
    )
    slot = lax.broadcasted_iota(jnp.int32, squares.shape, 0)
    squares[...] = jnp.where(slot == block, summed, squares[...])

    @pl.when(block == pl.num_programs(0) - 1)
    def _():
        whole = squares[...]
        top = whole.astype(jnp.bfloat16).astype(jnp.float32)
        below = whole - top
        largest = jnp.broadcast_to(jnp.max(largest_ref[...]), (8, channels))
        extra = jnp.concatenate([jnp.concatenate([top, below], axis=1), largest], axis=0)
        end = pl.num_programs(0) * SPAN
        out_ref[pl.ds(pl.multiple_of(end, SPAN), 16)] = extra.astype(jnp.bfloat16)


def scan(place, in_scale, parts, maps, dt_rows, small, start, largest):
    blocks, ranks, own, channels = parts[0].shape
    tokens = blocks * ranks * own
    step_block = pl.BlockSpec((1, ranks, own, channels), lambda i: (i, 0, 0, 0))
    map_block = pl.BlockSpec((1, ranks, own, maps[0].shape[3]), lambda i: (i, 0, 0, 0))

    def fixed(array):
        return pl.BlockSpec(array.shape, lambda i: (0, 0))

    return pl.pallas_call(
        scan_kernel,
        grid=(blocks,),
        in_specs=[SMEM, SMEM]
        + [step_block] * 3
        + [map_block] * 2
        + [pl.BlockSpec((dt_rows.shape[0], SPAN), lambda i: (0, i))]
        + [fixed(array) for array in (*small, start, largest)],
        out_specs=pl.BlockSpec((tokens + 16, channels), lambda i: (0, 0)),
        out_shape=jax.ShapeDtypeStruct((tokens + 16, channels), jnp.bfloat16),
        scratch_shapes=[
            pltpu.VMEM((SPAN + 8, channels), jnp.float32),
            pltpu.VMEM((SPAN + 8, 2 * STATE), jnp.float32),
            pltpu.VMEM((STATE, channels), jnp.float32),
            pltpu.VMEM((8, SPAN), jnp.float32),
        ],
        compiler_params=pltpu.CompilerParams(vmem_limit_bytes=40 * 2**20),
        cost_estimate=pl.CostEstimate(
            flops=8 * tokens * SPAN * channels,
            bytes_accessed=8 * tokens * channels,
            transcendentals=tokens * (channels + 8 * SPAN),
        ),
        name="scan",
    )(place, in_scale, *parts, *maps, dt_rows, *small, start, largest)


def by_heads(
    hidden_in,
    prev_amax,
    w_x,
    w_bc,
    w_dt,
    conv_x,
    conv_bc,
    conv_state_x,
    conv_state_bc,
    dt_bias,
    decay_rate,
    skip,
    init_state,
    norm_gain,
    w_out,
):
    margin = KERNEL - 1
    count, here = (lax.axis_size("seq"), lax.axis_index("seq"))
    ranks, rank = (lax.axis_size("tensor"), lax.axis_index("tensor"))
    line, z, side = (count // PAIR, here // PAIR, here % PAIR)
    f32, bf16 = (jnp.float32, jnp.bfloat16)
    in_scale = prev_amax / quant_range
    factor = quant_range / prev_amax
    own, width = hidden_in.shape
    depth = w_x.shape[0]
    tokens = count * ranks * own
    groups_here = w_bc.shape[1]
    channels = w_x.shape[1] // count
    heads_here = w_dt.shape[1] // count
    sharing = line // groups_here
    swap = [(s, s ^ 1) for s in range(count)]

    def pick(array, axis, index):
        return lax.dynamic_index_in_dim(array, index, axis, keepdims=False)

    def exchange(array, axis, flat):
        kept = pick(array, axis, side).reshape(flat)
        return kept, lax.ppermute(pick(array, axis, 1 - side).reshape(flat), "seq", swap)

    x_own, x_other = exchange(
        w_x.reshape(depth, line, PAIR, channels), 2, (depth, line * channels)
    )
    bc_own, bc_other = exchange(w_bc, 2, (depth, groups_here * STATE))
    dt_own, dt_other = exchange(
        w_dt.T.reshape(line, PAIR, heads_here, depth), 1, (line * heads_here, depth)
    )

    cut = hidden_in.reshape(own, line, PAIR, depth)
    pieces = jnp.stack([cut, cut[:, :, ::-1]], axis=2).reshape(own, count, PAIR * depth)
    pieces = pieces.transpose(1, 0, 2)
    rows = [lax.all_to_all(pieces, "seq", split_axis=0, concat_axis=0, tiled=True)]
    for j in range(1, ranks):
        bit = j & -j
        rows.append(lax.ppermute(rows[j - bit], "tensor", [(t, t ^ bit) for t in range(ranks)]))

    x_part, bc_part, dt_part, largest = project(
        factor.reshape(1),
        rows,
        (x_own, x_other, bc_own, bc_other, dt_own, dt_other),
        line,
        groups_here,
    )
    dt_part = dt_part.reshape(line, heads_here, tokens)

    right_x = left_x = right_bc = left_bc = right_dt = left_dt = None
    group = z // sharing
    bc_sum = pick(bc_part, 0, group).astype(f32)

    def onward(parts, index, received, step, keep=None):
        value = pick(parts, 0, jnp.clip(index, 0, parts.shape[0] - 1))
        if received is None:
            return value
        return (value.astype(f32) + received.astype(f32)).astype(value.dtype)

    def moves(step, towards, wanted):
        pairs = []
        for at in range(line):
            owner = at + towards * (line - step)
            if 0 <= owner < line and wanted(owner):
                for x in range(PAIR):
                    pairs.append((at * PAIR + x, (at + towards) * PAIR + x))
        return pairs

    def always(owner):
        return True

    def ends(owner):
        return (owner + 1) % sharing == 0

    def begins(owner):
        return owner % sharing == 0

    for k in range(1, line):
        to_right, to_left = (z + line - k, z - (line - k))
        send_right = onward(bc_part, to_right // sharing, right_bc, k)
        send_left = onward(bc_part, to_left // sharing, left_bc, k)
        right_bc = lax.ppermute(send_right, "seq", moves(k, 1, ends))
        left_bc = lax.ppermute(send_left, "seq", moves(k, -1, begins))
        mine_right = (to_right - 1) == (group + 1) * sharing - 1
        mine_left = (to_left + 1) == group * sharing
        bc_sum = bc_sum + jnp.where(mine_right, right_bc.astype(f32), 0.0)
        bc_sum = bc_sum + jnp.where(mine_left, left_bc.astype(f32), 0.0)
        send_right = onward(dt_part, to_right, right_dt, k)
        send_left = onward(dt_part, to_left, left_dt, k)
        right_dt = lax.ppermute(send_right, "seq", moves(k, 1, always))
        left_dt = lax.ppermute(send_left, "seq", moves(k, -1, always))
        send_right = onward(x_part, to_right, right_x, k)
        send_left = onward(x_part, to_left, left_x, k)
        right_x = lax.ppermute(send_right, "seq", moves(k, 1, always))
        left_x = lax.ppermute(send_left, "seq", moves(k, -1, always))
    bc_mine = (bc_sum * in_scale).astype(bf16)
    bc_far = lax.ppermute(bc_mine, "seq", swap)
    dt_sum = (pick(dt_part, 0, z) + right_dt + left_dt) * in_scale
    dt_rows = dt_sum.reshape(heads_here, count, ranks, own)
    for bit in (1 << b for b in range(ranks.bit_length() - 1)):
        turned = dt_rows.reshape(heads_here, count, ranks // (2 * bit), 2, bit, own)
        turned = turned[:, :, :, ::-1].reshape(dt_rows.shape)
        dt_rows = jnp.where((rank & bit) != 0, turned, dt_rows)
    padded = -heads_here % 8
    dt_rows = jnp.pad(dt_rows.reshape(heads_here, tokens), ((0, padded), (0, 0)))

    channel_at, head_at = (here * channels, here * heads_here)

    def by_channel(array):
        return lax.dynamic_slice_in_dim(array, channel_at, channels, axis=-1)

    def by_head(array):
        here_only = lax.dynamic_slice_in_dim(array, head_at, heads_here, axis=0)
        return jnp.broadcast_to(jnp.pad(here_only, (0, padded))[:, None], (8, SPAN))

    def edge_rows(array):
        return jnp.pad(array.astype(f32), ((8 - margin, 0), (0, 0)))

    small = (
        edge_rows(by_channel(conv_state_x)),
        by_channel(conv_x),
        edge_rows(pick(conv_state_bc, 1, group).reshape(margin, 2 * STATE)),
        pick(conv_bc, 1, group).reshape(KERNEL, 2 * STATE),
        by_head(dt_bias),
        by_head(decay_rate),
        jnp.repeat(lax.dynamic_slice_in_dim(skip, head_at, heads_here), HEAD_DIM)[None],
        by_channel(norm_gain)[None],
    )
    start = lax.dynamic_slice_in_dim(init_state, head_at, heads_here, axis=0)
    shape = (count, ranks, own, channels)
    gained = scan(
        jnp.stack([rank, side]).astype(jnp.int32),
        in_scale.reshape(1),
        [pick(x_part, 0, z).reshape(shape), right_x.reshape(shape), left_x.reshape(shape)],
        [bc_mine.reshape(count, ranks, own, STATE), bc_far.reshape(count, ranks, own, STATE)],
        dt_rows,
        small,
        start.reshape(channels, STATE),
        largest,
    )

    def meet(total, block, at):
        piece = lax.dynamic_slice_in_dim(
            w_out, jnp.clip(at, 0, count - 1) * channels, channels, axis=0
        )
        return total + jnp.dot(block, piece, preferred_element_type=f32)

    def square_rows(block):
        rows = block[tokens : tokens + 8].astype(f32)
        return rows[:, :SPAN] + rows[:, SPAN:]

    def line_moves(step, towards):
        return [
            (at * PAIR + x, (at + towards) * PAIR + x)
            for at in range(line)
            for x in range(PAIR)
            if 0 <= at + towards < line and 0 <= at - towards * (step - 1) < line
        ]

    def pair_moves(wanted):
        return [(s, s ^ 1) for s in range(count) if wanted(s // PAIR)]

    got = [(gained, 0, lambda at: True)]
    from_left = from_right = gained
    for k in range(1, line):
        from_left = lax.ppermute(from_left, "seq", line_moves(k, 1))
        from_right = lax.ppermute(from_right, "seq", line_moves(k, -1))
        if 2 * k >= line:
            one = jnp.where(z >= k, from_left, from_right)
            got.append(
                (one, jnp.where(z >= k, -k, k), lambda at, k=k: at >= k or at + k < line)
            )
        else:
            got.append((from_left, -k, lambda at, k=k: at >= k))
            got.append((from_right, k, lambda at, k=k: at + k < line))
    total = jnp.zeros((tokens + 16, w_out.shape[1]), f32)
    squares = jnp.zeros((8, SPAN), f32)
    abs_max = None
    for block, offset, wanted in got:
        far = lax.ppermute(block, "seq", pair_moves(wanted))
        total = meet(total, block, (z + offset) * PAIR + side)
        total = meet(total, far, (z + offset) * PAIR + 1 - side)
        squares = squares + square_rows(block) + square_rows(far)
        top = block[tokens + 8, 0].astype(f32)
        abs_max = top if abs_max is None else jnp.maximum(abs_max, top)

    wide = w_out.shape[1]
    kept = total[:tokens].reshape(count, ranks, own, wide)
    for bit in (1 << b for b in range(ranks.bit_length() - 1)):
        pairs = [(t, t ^ bit) for t in range(ranks)]
        squares = squares + lax.ppermute(squares, "tensor", pairs)
        mine = (rank // bit) % 2
        halves = kept.reshape(count, -1, 2, own, wide)
        received = lax.ppermute(pick(halves, 2, 1 - mine).astype(bf16), "tensor", pairs)
        kept = pick(halves, 2, mine) + received.astype(f32)
    kept = kept.reshape(count, own, wide)
    mean_sq = squares[:count].reshape(count, ranks, own) / (HEADS * HEAD_DIM)
    factors = lax.rsqrt(pick(mean_sq, 1, rank) + epsilon)
    final = (kept * factors[:, :, None]).astype(bf16)
    final = lax.all_to_all(final, "seq", split_axis=0, concat_axis=0, tiled=True)
    layer_out = final.transpose(1, 0, 2).reshape(own, count * wide)
    return (layer_out, abs_max)


def solution(mesh):
    return jax.shard_map(
        by_heads if splits(mesh) else by_tokens,
        mesh=mesh,
        in_specs=(
            P(("seq", "tensor"), None),
            P(),
            P("seq", "tensor"),
            P("seq", "tensor", None, None),
            P("seq", "tensor"),
            P(None, "tensor"),
            P(None, "tensor", None, None),
            P(None, "tensor"),
            P(None, "tensor", None, None),
            P("tensor"),
            P("tensor"),
            P("tensor"),
            P("tensor", None, None),
            P("tensor"),
            P("tensor", "seq"),
        ),
        out_specs=(P(("seq", "tensor"), None), P()),
        check_vma=False,
    )
```

```python
import functools

import jax
import jax.numpy as jnp
from jax import lax
from jax.experimental import pallas as pl
from jax.experimental.pallas import tpu as pltpu
from jax.sharding import PartitionSpec as P

HEADS = 128
HEAD_DIM = 64
STATE = 128
GROUPS = 8
KERNEL = 4
SPAN = 128


epsilon = 1e-05
quant_range = 448.0


def from_behind(value, axis, steps):
    count = lax.axis_size(axis)
    first, last = (max(0, -steps), min(count, count - steps))
    return lax.ppermute(value, axis, [(source, source + steps) for source in range(first, last)])


def carried_in(shard, axis, combine, identity):
    count, here = (lax.axis_size(axis), lax.axis_index(axis))
    everything = jax.tree.map(
        lambda part, kind: lax.all_gather(part.astype(kind), axis),
        shard,
        (jnp.bfloat16, jnp.bfloat16),
    )
    start = jax.tree.map(
        lambda part, zero: jnp.broadcast_to(jnp.asarray(zero, part.dtype), part.shape),
        shard,
        identity,
    )

    def turn(k, before):
        reached = k < here
        new = combine(
            before, jax.tree.map(lambda part, own: part[k].astype(own.dtype), everything, shard)
        )
        return jax.tree.map(lambda a, b: jnp.where(reached, a, b), new, before)

    return lax.fori_loop(0, count, turn, start)


def depthwise(before, projected, conv_taps, length):
    extended = jnp.concatenate([before, projected], axis=0)
    summed = conv_taps[0] * extended[0:length]
    for offset in range(1, KERNEL):
        summed = summed + conv_taps[offset] * extended[offset : offset + length]
    return jax.nn.silu(summed).astype(jnp.bfloat16)


def combine(earlier, later):
    return (earlier[0] * later[0], later[0][:, None, None] * earlier[1] + later[1])


def by_tokens(
    hidden_in,
    prev_amax,
    w_x,
    w_bc,
    w_dt,
    conv_x,
    conv_bc,
    conv_state_x,
    conv_state_bc,
    dt_bias,
    decay_rate,
    skip,
    init_state,
    norm_gain,
    w_out,
):
    margin = KERNEL - 1
    gathered = lax.all_gather(hidden_in, "tensor", axis=0, tiled=True)
    abs_max = lax.pmax(jnp.max(jnp.abs(gathered.astype(jnp.float32))), "seq")
    in_scale = prev_amax / quant_range
    leading = lax.axis_index("seq") == 0
    row_count = gathered.shape[0]
    bc_width = w_bc.shape[1] * w_bc.shape[2] * w_bc.shape[3]
    bc_rows = jnp.reshape(w_bc, (w_bc.shape[0], bc_width))
    scaled = gathered.astype(jnp.float32) * (quant_range / prev_amax)
    quant = jnp.clip(scaled, -quant_range, quant_range).astype(jnp.bfloat16)
    pieces = (
        lax.all_gather(w_x, "seq", axis=0, tiled=True),
        lax.all_gather(bc_rows, "seq", axis=0, tiled=True),
        lax.all_gather(w_dt, "seq", axis=0, tiled=True),
    )
    x_proj, bc_proj, dt_proj = tuple(
        (
            jnp.dot(quant, weight_piece, preferred_element_type=jnp.float32)
            for weight_piece in pieces
        )
    )
    x_whole = (x_proj * in_scale).astype(jnp.bfloat16)
    bc_whole = (bc_proj * in_scale).astype(jnp.bfloat16)
    dt_raw = dt_proj * in_scale
    state_bc = jnp.reshape(conv_state_bc, (margin, bc_width))
    received = from_behind(
        (x_whole[row_count - margin :], bc_whole[row_count - margin :]), "seq", 1
    )
    x_edge = jnp.where(leading, conv_state_x, received[0])
    bc_edge = jnp.where(leading, state_bc, received[1])
    x_act = depthwise(x_edge, x_whole, conv_x, row_count)
    bc_act = depthwise(bc_edge, bc_whole, jnp.reshape(conv_bc, (KERNEL, bc_width)), row_count)
    step_size = jax.nn.softplus(dt_raw + dt_bias)
    heads_here = step_size.shape[1]
    groups_here = w_bc.shape[1]
    per_group = HEADS // GROUPS
    blocks = row_count // SPAN
    x_blocks = x_act.reshape(blocks, SPAN, heads_here, HEAD_DIM)
    bc_blocks = bc_act.reshape(blocks, SPAN, groups_here, 2, STATE)
    in_map = bc_blocks[:, :, :, 0]
    out_map = bc_blocks[:, :, :, 1]
    step_blocks = step_size.reshape(blocks, SPAN, heads_here)
    cum_blocks = jnp.cumsum(-step_blocks * decay_rate, axis=1)
    index_row = jnp.arange(SPAN, dtype=jnp.int32)
    lower_mask = index_row[:, None] >= index_row[None, :]
    intersection = jnp.einsum(
        "ctgn,cugn->cgtu", out_map, in_map, preferred_element_type=jnp.float32
    )
    intersection = jnp.repeat(intersection, per_group, axis=1)
    cum_heads = jnp.transpose(cum_blocks, (0, 2, 1))
    log_gap = cum_heads[:, :, :, None] - cum_heads[:, :, None, :]
    decay = jnp.exp(jnp.where(lower_mask[None, None], log_gap, -1e30))
    step_heads = jnp.transpose(step_blocks, (0, 2, 1))
    weights = (intersection * decay * step_heads[:, :, None, :]).astype(jnp.bfloat16)
    local_part = jnp.einsum(
        "chtu,cuhp->cthp", weights, x_blocks, preferred_element_type=jnp.float32
    )
    last_cum = cum_blocks[:, SPAN - 1, :]
    x_weighted = (
        x_blocks.astype(jnp.float32)
        * (step_blocks * jnp.exp(last_cum[:, None, :] - cum_blocks))[:, :, :, None]
    ).astype(jnp.bfloat16)
    in_heads = jnp.repeat(in_map, per_group, axis=2)
    added = jnp.einsum("cuhp,cuhn->chpn", x_weighted, in_heads, preferred_element_type=jnp.float32)

    def carry_on(carried, element):
        block_decay, block_added = element
        return (block_decay[:, None, None] * carried + block_added, carried)

    empty_state = jnp.zeros((heads_here, HEAD_DIM, STATE), jnp.float32)
    device_state, entering = lax.scan(carry_on, empty_state, (jnp.exp(last_cum), added))
    device_decay = jnp.exp(jnp.sum(last_cum, axis=0))
    seeded = device_state + jnp.where(leading, device_decay[:, None, None] * init_state, 0.0)
    identity = (jnp.ones_like(device_decay), jnp.zeros_like(device_state))
    scanned = carried_in((device_decay, seeded), "seq", combine, identity)
    incoming = jnp.where(leading, init_state, scanned[1])
    prefix = jnp.exp(jnp.cumsum(last_cum, axis=0) - last_cum)
    states_in = entering + prefix[:, :, None, None] * incoming[None]
    out_heads = jnp.repeat(out_map, per_group, axis=2).astype(jnp.float32)
    carried_part = (
        jnp.einsum("cthn,chpn->cthp", out_heads, states_in, precision=lax.Precision.HIGHEST)
        * jnp.exp(cum_blocks)[:, :, :, None]
    )
    ssm_out = local_part + carried_part + skip[None, None, :, None] * x_blocks.astype(jnp.float32)
    ssm_out = ssm_out.reshape(row_count, heads_here * HEAD_DIM)
    squares = lax.psum(jnp.sum(ssm_out * ssm_out, axis=1), "tensor")
    mean_sq = squares / (HEADS * HEAD_DIM)
    normed = (ssm_out * lax.rsqrt(mean_sq + epsilon)[:, None] * norm_gain).astype(jnp.bfloat16)
    partial_out = jnp.dot(
        normed, lax.all_gather(w_out, "seq", axis=1, tiled=True), preferred_element_type=jnp.float32
    )
    layer_out = lax.psum_scatter(
        partial_out.astype(jnp.bfloat16), "tensor", scatter_dimension=0, tiled=True
    )
    return (layer_out, abs_max)


PAIR = 2
LINE = 4
PARTS = 1
ROWS = 8
SMEM = pl.BlockSpec(memory_space=pltpu.SMEM)
HIGHEST = lax.Precision.HIGHEST


def splits(mesh):
    count, ranks = (mesh.shape["seq"], mesh.shape["tensor"])
    heads_all, groups_here = (HEADS // ranks, GROUPS // ranks)
    if count != PAIR * LINE or groups_here != PAIR or ranks & (ranks - 1):
        return False
    heads_here = heads_all // count
    return 2 * heads_here == ROWS and heads_here * HEAD_DIM == 2 * SPAN


def nt_dot(a, b, **kw):
    return lax.dot_general(
        a, b, (((1,), (1,)), ((), ())), preferred_element_type=jnp.float32, **kw
    )


def project_kernel(place_ref, factor_ref, *refs):
    outs = LINE + 4
    ranks = len(refs) - 6 - outs
    hidden = refs[:ranks]
    own_x, other_x, own_bc, other_bc, own_dt, other_dt = refs[ranks : ranks + 6]
    x_refs = refs[ranks + 6 : ranks + 6 + LINE]
    bc_ref, largest_ref, quant_ref, dt_buf = refs[ranks + 6 + LINE :]
    side, z = (place_ref[1], place_ref[2])
    step = pl.program_id(0)
    factor = factor_ref[0]
    depth = own_x.shape[0]
    largest = None
    for j in range(ranks):
        for half in range(PAIR):
            values = hidden[j][:, :, half * depth : (half + 1) * depth].astype(jnp.float32)
            scaled = jnp.clip(values * factor, -quant_range, quant_range)
            quant_ref[half, :, j] = scaled.astype(jnp.bfloat16)
            top = jnp.max(jnp.abs(values).reshape(-1, ROWS, depth), axis=0)
            largest = top if largest is None else jnp.maximum(largest, top)
    width = largest_ref.shape[1]
    top = largest[:, :width]
    for at in range(width, depth, width):
        top = jnp.maximum(top, largest[:, at : at + width])

    @pl.when(step == 0)
    def _():
        largest_ref[...] = top

    @pl.when(step > 0)
    def _():
        largest_ref[...] = jnp.maximum(largest_ref[...], top)

    rows = quant_ref.shape[1] * quant_ref.shape[2] * quant_ref.shape[3]
    near = quant_ref[side].reshape(rows, depth)
    far = quant_ref[1 - side].reshape(rows, depth)

    def both(own, other):
        return jnp.dot(near, own, preferred_element_type=jnp.float32) + jnp.dot(
            far, other, preferred_element_type=jnp.float32
        )

    at_rows = pl.ds(pl.multiple_of(step * rows, rows), rows)
    dt_buf[...] = (nt_dot(own_dt[...], near) + nt_dot(other_dt[...], far)).reshape(dt_buf.shape)
    channels = x_refs[0].shape[1]
    tokens = pl.num_programs(0) * rows
    extra = rows // channels * ROWS
    upper = lax.broadcasted_iota(jnp.int32, (ROWS, channels), 0) < ROWS // 2
    for m in reversed(range(LINE)):
        owner = z ^ m
        cut = pl.ds(pl.multiple_of(owner * channels, channels), channels)
        x_refs[m][at_rows] = both(own_x[:, cut], other_x[:, cut]).astype(jnp.bfloat16)
        dt = dt_buf[owner]
        pieces = [
            split_parts(dt[:, at : at + channels], upper) for at in range(0, rows, channels)
        ]
        x_refs[m][pl.ds(pl.multiple_of(tokens + step * extra, 16), extra)] = jnp.concatenate(
            pieces, axis=0
        ).astype(jnp.bfloat16)
    bc_ref[at_rows] = both(own_bc[...], other_bc[...]).astype(jnp.bfloat16)


def split_parts(values, upper):
    top = values.astype(jnp.bfloat16).astype(jnp.float32)
    return jnp.where(upper, top, values - top)


def project(place, factor, hidden, weights, part):
    count, own, wide = hidden[0].shape
    ranks = len(hidden)
    w_x, other_x = weights[:2]
    depth, x_wide = other_x.shape
    channels = x_wide // LINE
    here = count // PARTS
    steps = max(1, 2 // PARTS)
    each = here // steps
    tokens = here * ranks * own
    extra = tokens // channels * ROWS

    def fixed(array):
        return pl.BlockSpec(array.shape, lambda i, p: (0,) * array.ndim)

    payload = jax.ShapeDtypeStruct((tokens + extra, channels), jnp.bfloat16)
    maps = jax.ShapeDtypeStruct((tokens, weights[2].shape[1]), jnp.bfloat16)
    largest = jax.ShapeDtypeStruct((ROWS, 128), jnp.float32)
    outs = [payload] * LINE + [maps, largest]
    first = part * steps
    return pl.pallas_call(
        project_kernel,
        grid_spec=pltpu.PrefetchScalarGridSpec(
            num_scalar_prefetch=1,
            grid=(steps,),
            in_specs=[SMEM]
            + [pl.BlockSpec((each, own, wide), lambda i, p: (first + i, 0, 0))] * ranks
            + [pl.BlockSpec((depth, x_wide), lambda i, p: (0, p[1]))]
            + [fixed(w) for w in weights[1:]],
            out_specs=[fixed(out) for out in outs],
            scratch_shapes=[
                pltpu.VMEM((PAIR, each, ranks, own, depth), jnp.bfloat16),
                pltpu.VMEM((LINE, ROWS, each * ranks * own), jnp.float32),
            ],
        ),
        out_shape=outs,
        compiler_params=pltpu.CompilerParams(vmem_limit_bytes=40 * 2**20),
        cost_estimate=pl.CostEstimate(
            flops=2 * tokens * wide * (x_wide + maps.shape[1]),
            bytes_accessed=2 * tokens * (wide + x_wide),
            transcendentals=0,
        ),
        name="project",
    )(place, factor, *hidden, *weights)


def onward_kernel(own_ref, received_ref, out_ref):
    rows, channels = own_ref.shape
    tokens = rows * channels // (channels + ROWS)
    total = own_ref[:tokens].astype(jnp.float32) + received_ref[:tokens].astype(jnp.float32)
    out_ref[:tokens] = total.astype(jnp.bfloat16)
    upper = lax.broadcasted_iota(jnp.int32, (ROWS, channels), 0) < ROWS // 2
    extra = own_ref[tokens:].astype(jnp.float32) + received_ref[tokens:].astype(jnp.float32)
    pieces = []
    for at in range(0, rows - tokens, ROWS):
        piece = extra[at : at + ROWS]
        pieces.append(split_parts(piece + pltpu.roll(piece, ROWS // 2, 0), upper))
    out_ref[tokens:] = jnp.concatenate(pieces, axis=0).astype(jnp.bfloat16)


def onward(own, received):
    whole = pl.BlockSpec(own.shape, lambda: (0, 0))
    return pl.pallas_call(
        onward_kernel,
        in_specs=[whole, whole],
        out_specs=whole,
        out_shape=jax.ShapeDtypeStruct(own.shape, own.dtype),
        compiler_params=pltpu.CompilerParams(vmem_limit_bytes=20 * 2**20),
        cost_estimate=pl.CostEstimate(
            flops=own.size, bytes_accessed=6 * own.size, transcendentals=0
        ),
        name="onward",
    )(own, received)


def scan_kernel(first, place_ref, scale_ref, *refs):
    x_refs, dt_refs = (refs[:4], refs[4:8])
    bc_refs = refs[8:11]
    small_ref, largest_ref, carry_ref, out_ref, carry_out_ref = refs[11:16]
    x_buf, bc_buf, state, squares, steps = refs[16:]
    block = pl.program_id(0)
    channels = out_ref.shape[1]
    heads = channels // HEAD_DIM
    rank, z = (place_ref[0], place_ref[2])
    ranks = place_ref.shape[0] - 3
    own = SPAN // ranks
    edge = ROWS
    in_scale = scale_ref[0]
    at_end = (z == 0) | (z == LINE - 1)
    half = ROWS // 2

    @pl.when(block == 0)
    def _():
        if first:
            x_buf[:edge] = small_ref[:edge]
            bc_buf[:edge] = small_ref[edge : 2 * edge]
            state[...] = carry_ref[...].T
        else:
            state[...] = carry_ref[:STATE]
            x_buf[:edge] = carry_ref[STATE : STATE + edge]
            bc_buf[:edge] = carry_ref[STATE + edge :]
        squares[...] = jnp.zeros_like(squares)
        total = sum(ref[...].astype(jnp.float32) for ref in dt_refs)
        for k in range(steps.shape[0]):
            piece = total[k * ROWS : (k + 1) * ROWS]
            steps[k] = (piece + pltpu.roll(piece, half, 0)) * in_scale

    @pl.when(block > 0)
    def _():
        x_buf[:edge] = x_buf[SPAN : SPAN + edge]
        bc_buf[:edge] = bc_buf[SPAN : SPAN + edge]

    for true_rank in range(ranks):
        source = pl.ds(pl.multiple_of((true_rank ^ rank) * own, own), own)
        at = slice(edge + true_rank * own, edge + (true_rank + 1) * own)
        total = sum(ref[source].astype(jnp.float32) for ref in x_refs) * in_scale
        x_buf[at] = total.astype(jnp.bfloat16).astype(jnp.float32)
        near, far, done = (ref[source].astype(jnp.float32) for ref in bc_refs)
        total = ((near + far) * in_scale).astype(jnp.bfloat16).astype(jnp.float32)
        bc_buf[at] = jnp.where(at_end, done, total)

    taps = 2 * edge

    def activate(buf, row):
        start = edge - (KERNEL - 1)
        summed = small_ref[row : row + 1] * buf[start : start + SPAN]
        for k in range(1, KERNEL):
            summed = summed + small_ref[row + k : row + k + 1] * buf[start + k : start + k + SPAN]
        return (summed / (1.0 + jnp.exp(-summed))).astype(jnp.bfloat16)

    x_act = activate(x_buf, taps)
    bc_act = activate(bc_buf, taps + KERNEL)
    in_map, out_map = (bc_act[:, :STATE], bc_act[:, STATE:])
    skip = small_ref[taps + 2 * KERNEL : taps + 2 * KERNEL + 1]
    gain = small_ref[taps + 2 * KERNEL + 1 : taps + 2 * KERNEL + 2]
    bias = small_ref[4 * edge :, :SPAN]
    rate = small_ref[4 * edge :, SPAN:]

    up = lax.broadcasted_iota(jnp.int32, (SPAN, SPAN), 0)
    across = lax.broadcasted_iota(jnp.int32, (SPAN, SPAN), 1)
    wide = channels // SPAN
    raw = steps[block // wide]
    cut = raw[:, :SPAN]
    for k in range(1, wide):
        cut = jnp.where(block % wide == k, raw[:, k * SPAN : (k + 1) * SPAN], cut)
    lanes = across[:ROWS]
    bit = 1
    while bit < ranks:
        shift = bit * own
        flipped = jnp.where(
            (lanes // shift) % 2 == 1, pltpu.roll(cut, shift, 1), pltpu.roll(cut, SPAN - shift, 1)
        )
        cut = jnp.where((rank & bit) != 0, flipped, cut)
        bit *= 2
    raw = cut + bias
    step = jnp.maximum(raw, 0.0) + jnp.log1p(jnp.exp(-jnp.abs(raw)))
    upper = (up <= across).astype(jnp.float32)
    cum = jnp.dot(-step * rate, upper, precision=HIGHEST, preferred_element_type=jnp.float32)
    last = cum[:, SPAN - 1 : SPAN]
    stacked = jnp.concatenate(
        [
            cum,
            step * jnp.exp(last - cum),
            jnp.exp(cum),
            jnp.zeros((SPAN - 3 * ROWS, SPAN), jnp.float32),
        ],
        axis=0,
    )
    turned = stacked.T
    lane = lax.broadcasted_iota(jnp.int32, (SPAN, channels), 1)

    def spread(row):
        result = jnp.broadcast_to(turned[:, row : row + 1], (SPAN, channels))
        for h in range(1, heads):
            result = jnp.where(lane >= h * HEAD_DIM, turned[:, row + h : row + h + 1], result)
        return result

    inner = jnp.where(up >= across, nt_dot(out_map, in_map), 0.0)
    x_wide = x_act.astype(jnp.float32)
    weights, spaced = ([], [])
    for h in range(heads):
        gap = jnp.where(up >= across, turned[:, h : h + 1] - cum[h : h + 1], 0.0)
        weights.append((inner * jnp.exp(gap) * step[h : h + 1]).astype(jnp.bfloat16))
        inside = (lane >= h * HEAD_DIM) & (lane < (h + 1) * HEAD_DIM)
        spaced.append(jnp.where(inside, x_wide, 0.0).astype(jnp.bfloat16))
    local_part = jnp.dot(
        jnp.concatenate(weights, axis=1),
        jnp.concatenate(spaced, axis=0),
        preferred_element_type=jnp.float32,
    )
    before = state[...]
    high = before.astype(jnp.bfloat16)
    rest = before - high.astype(jnp.float32)
    middle = rest.astype(jnp.bfloat16)
    low = (rest - middle.astype(jnp.float32)).astype(jnp.bfloat16)
    carried = jnp.dot(out_map, high, preferred_element_type=jnp.float32)
    carried = carried + jnp.dot(out_map, middle, preferred_element_type=jnp.float32)
    carried = carried + jnp.dot(out_map, low, preferred_element_type=jnp.float32)
    grown = spread(2 * ROWS)
    ssm_out = local_part + grown * carried + skip * x_wide
    x_weighted = (x_wide * spread(ROWS)).astype(jnp.bfloat16)
    added = lax.dot_general(
        in_map, x_weighted, (((0,), (0,)), ((), ())), preferred_element_type=jnp.float32
    )
    after = grown[SPAN - 1 : SPAN] * before + added
    state[...] = after
    out_ref[pl.ds(pl.multiple_of(block * SPAN, SPAN), SPAN)] = (ssm_out * gain).astype(jnp.bfloat16)
    summed = nt_dot(jnp.ones((ROWS, channels), jnp.float32), ssm_out * ssm_out, precision=HIGHEST)
    slot = lax.broadcasted_iota(jnp.int32, squares.shape, 0)
    squares[...] = jnp.where(slot == block, summed, squares[...])

    @pl.when(block == pl.num_programs(0) - 1)
    def _():
        whole = squares[...]
        top = whole.astype(jnp.bfloat16).astype(jnp.float32)
        largest = jnp.broadcast_to(jnp.max(largest_ref[...]), (ROWS, channels))
        extra = jnp.concatenate([jnp.concatenate([top, whole - top], axis=1), largest], axis=0)
        end = pl.num_programs(0) * SPAN
        out_ref[pl.ds(pl.multiple_of(end, SPAN), 2 * ROWS)] = extra.astype(jnp.bfloat16)
        carry_out_ref[:STATE] = after
        carry_out_ref[STATE : STATE + edge] = x_buf[SPAN : SPAN + edge]
        carry_out_ref[STATE + edge :] = bc_buf[SPAN : SPAN + edge]


def scan(place, in_scale, sums, maps, small, largest, carry, first):
    channels = sums[0].shape[1]
    tokens = maps[0].shape[0]
    extra = tokens // channels * ROWS
    blocks = tokens // SPAN
    step_block = pl.BlockSpec((SPAN, channels), lambda i, p: (i, 0))
    dt_block = pl.BlockSpec((extra, channels), lambda i, p: (tokens // extra, 0))

    def fixed(array):
        return pl.BlockSpec(array.shape, lambda i, p: (0, 0))

    held = pl.BlockSpec((channels, STATE), lambda i, p: (p[1] * LINE + p[2], 0))
    outs = [
        jax.ShapeDtypeStruct((tokens + 2 * ROWS, channels), jnp.bfloat16),
        jax.ShapeDtypeStruct((STATE + 2 * ROWS, channels), jnp.float32),
    ]
    return pl.pallas_call(
        functools.partial(scan_kernel, first),
        grid_spec=pltpu.PrefetchScalarGridSpec(
            num_scalar_prefetch=1,
            grid=(blocks,),
            in_specs=[SMEM]
            + [step_block] * len(sums)
            + [dt_block] * len(sums)
            + [step_block] * len(maps)
            + [fixed(small), fixed(largest), held if first else fixed(carry)],
            out_specs=[fixed(out) for out in outs],
            scratch_shapes=[
                pltpu.VMEM((SPAN + ROWS, channels), jnp.float32),
                pltpu.VMEM((SPAN + ROWS, 2 * STATE), jnp.float32),
                pltpu.VMEM((STATE, channels), jnp.float32),
                pltpu.VMEM((ROWS, SPAN), jnp.float32),
                pltpu.VMEM((extra // ROWS, ROWS, channels), jnp.float32),
            ],
        ),
        out_shape=outs,
        compiler_params=pltpu.CompilerParams(vmem_limit_bytes=40 * 2**20),
        cost_estimate=pl.CostEstimate(
            flops=8 * tokens * SPAN * channels,
            bytes_accessed=8 * tokens * channels,
            transcendentals=tokens * (channels + 8 * SPAN),
        ),
        name="scan",
    )(place, in_scale, *sums, *sums, *maps, small, largest, carry)


def by_heads(
    hidden_in,
    prev_amax,
    w_x,
    w_bc,
    w_dt,
    conv_x,
    conv_bc,
    conv_state_x,
    conv_state_bc,
    dt_bias,
    decay_rate,
    skip,
    init_state,
    norm_gain,
    w_out,
):
    margin = KERNEL - 1
    count, here = (lax.axis_size("seq"), lax.axis_index("seq"))
    ranks, rank = (lax.axis_size("tensor"), lax.axis_index("tensor"))
    z, side = (here // PAIR, here % PAIR)
    place_of = side * LINE + z
    f32, bf16 = (jnp.float32, jnp.bfloat16)
    own, width = hidden_in.shape
    depth = w_x.shape[0]
    channels = w_x.shape[1] // count
    heads_here = w_dt.shape[1] // count
    in_scale = (prev_amax / quant_range).reshape(1)
    factor = (quant_range / prev_amax).reshape(1)
    place = jnp.stack([rank, side, z] + [rank] * ranks).astype(jnp.int32)

    def pick(array, axis, index):
        return lax.dynamic_index_in_dim(array, index, axis, keepdims=False)

    def along(value, pairs):
        moves = [(a * PAIR + x, b * PAIR + x) for a, b in pairs for x in range(PAIR)]
        return lax.ppermute(value, "seq", moves)

    def across(value):
        return lax.ppermute(value, "seq", [(s, s ^ 1) for s in range(count)])

    half = w_x.shape[1] // PAIR
    x_send = lax.dynamic_slice_in_dim(w_x, (1 - side) * half, half, axis=1)
    x_other = across(x_send)
    bc_own = pick(w_bc, 1, side).reshape(depth, 2 * STATE)
    bc_other = across(pick(w_bc, 1, 1 - side).reshape(depth, 2 * STATE))
    dt_rows = w_dt.T.reshape(PAIR, LINE, 1, heads_here, depth)
    dt_rows = jnp.broadcast_to(dt_rows, (PAIR, LINE, ROWS // heads_here, heads_here, depth))
    dt_rows = dt_rows.reshape(PAIR, LINE * ROWS, depth)
    dt_own = pick(dt_rows, 0, side)
    dt_other = across(pick(dt_rows, 0, 1 - side))

    pieces = hidden_in.reshape(own, LINE, 1, PAIR * depth).transpose(1, 2, 0, 3)
    pieces = jnp.broadcast_to(pieces, (LINE, PAIR, own, PAIR * depth))
    pieces = pieces.reshape(count, own, PAIR * depth)
    rows = [lax.all_to_all(pieces, "seq", split_axis=0, concat_axis=0, tiled=True)]
    for j in range(1, ranks):
        bit = j & -j
        rows.append(lax.ppermute(rows[j - bit], "tensor", [(t, t ^ bit) for t in range(ranks)]))

    def of_heads(array):
        return jnp.repeat(array, HEAD_DIM)[None]

    by_channel = jnp.concatenate(
        [conv_state_x.astype(f32), conv_x, of_heads(skip), norm_gain[None]], axis=0
    )
    by_channel = lax.dynamic_slice_in_dim(by_channel, place_of * channels, channels, axis=1)
    by_map = jnp.concatenate([conv_state_bc.astype(f32), conv_bc], axis=0)
    by_map = pick(by_map, 1, side).reshape(margin + KERNEL, 2 * STATE)
    by_head = jnp.stack([dt_bias, decay_rate]).reshape(2, count, heads_here)
    by_head = jnp.tile(pick(by_head, 1, place_of).T, (ROWS // heads_here, 1))
    by_head = jnp.repeat(by_head, SPAN, axis=1)
    blank = jnp.zeros((ROWS - margin, channels), f32)
    small = jnp.concatenate(
        [
            blank,
            by_channel[:margin],
            blank,
            by_map[:margin],
            by_channel[margin : margin + KERNEL],
            by_map[margin:],
            by_channel[margin + KERNEL :],
            jnp.zeros((2 * ROWS - 2 * KERNEL - 2, channels), f32),
            by_head,
        ],
        axis=0,
    )

    start, end = (0, LINE - 1)
    next_start, next_end = (1, LINE - 2)
    weights = (w_x, x_other, bc_own, bc_other, dt_own, dt_other)
    carry = init_state.reshape(-1, STATE)
    totals, tops = ([], [])
    for part in range(PARTS):
        mine, near, over, far, maps, largest = project(place, factor, rows, weights, part)
        map_hop = along(maps, [(start, next_start), (end, next_end)])
        hop_far = along(far, [(start, next_start), (end, next_end)])
        hop_over = along(over, [(start, next_start), (end, next_end)])
        got_near = along(near, [(s, s ^ 1) for s in range(LINE)])
        map_sum = (maps.astype(f32) + map_hop.astype(f32)).astype(bf16)
        map_far = along(map_sum, [(next_start, next_end), (next_end, next_start)])
        map_done = ((map_sum.astype(f32) + map_far.astype(f32)) * in_scale).astype(bf16)
        map_done = along(map_done, [(next_start, start), (next_end, end)])
        got_end = along(onward(over, hop_far), [(next_start, end), (next_end, start)])
        got_next = along(onward(far, hop_over), [(next_start, next_end), (next_end, next_start)])
        gained, carry = scan(
            place,
            in_scale,
            [mine, got_near, got_end, got_next],
            [map_sum, map_far, map_done],
            small,
            largest,
            carry,
            part == 0,
        )
        tokens = gained.shape[0] - 2 * ROWS
        got = [gained]
        for m in range(1, LINE):
            got.append(along(gained, [(s, s ^ m) for s in range(LINE)]))
        total = squares = top = None
        for m, block in enumerate(got):
            for x, piece in enumerate((block, across(block))):
                at = ((side ^ x) * LINE + (z ^ m)) * channels
                w_rows = lax.dynamic_slice_in_dim(w_out, at, channels, axis=0)
                product = jnp.dot(piece, w_rows, preferred_element_type=f32)
                tail = piece[tokens:].astype(f32)
                low, high = (tail[:ROWS, :SPAN] + tail[:ROWS, SPAN:], tail[ROWS:, :SPAN])
                if total is None:
                    total, squares, top = (product, low, high)
                else:
                    total = total + product
                    squares = squares + low
                    top = jnp.maximum(top, high)
        tops.append(top)
        wide = w_out.shape[1]
        blocks = tokens // SPAN
        kept = total[:tokens].reshape(blocks, ranks, own, wide)
        for bit in (1 << b for b in range(ranks.bit_length() - 1)):
            pairs = [(t, t ^ bit) for t in range(ranks)]
            squares = squares + lax.ppermute(squares, "tensor", pairs)
            keeps = (rank // bit) % 2
            halves = kept.reshape(blocks, -1, 2, own, wide)
            received = lax.ppermute(pick(halves, 2, 1 - keeps).astype(bf16), "tensor", pairs)
            kept = pick(halves, 2, keeps) + received.astype(f32)
        kept = kept.reshape(blocks, own, wide)
        mean_sq = squares[:blocks].reshape(blocks, ranks, own) / (HEADS * HEAD_DIM)
        factors = lax.rsqrt(pick(mean_sq, 1, rank) + epsilon)
        totals.append((kept * factors[:, :, None]).astype(bf16))
    final = jnp.concatenate(totals, axis=0)
    final = lax.all_to_all(final, "seq", split_axis=0, concat_axis=0, tiled=True)
    layer_out = final.transpose(1, 0, 2).reshape(own, count * final.shape[2])
    abs_max = jnp.max(functools.reduce(jnp.maximum, tops))
    return (layer_out, abs_max)


def solution(mesh):
    return jax.shard_map(
        by_heads if splits(mesh) else by_tokens,
        mesh=mesh,
        in_specs=(
            P(("seq", "tensor"), None),
            P(),
            P("seq", "tensor"),
            P("seq", "tensor", None, None),
            P("seq", "tensor"),
            P(None, "tensor"),
            P(None, "tensor", None, None),
            P(None, "tensor"),
            P(None, "tensor", None, None),
            P("tensor"),
            P("tensor"),
            P("tensor"),
            P("tensor", None, None),
            P("tensor"),
            P("tensor", "seq"),
        ),
        out_specs=(P(("seq", "tensor"), None), P()),
        check_vma=False,
    )
```

```python
import functools

import jax
import jax.numpy as jnp
from jax import lax
from jax.experimental import pallas as pl
from jax.experimental.pallas import tpu as pltpu
from jax.sharding import PartitionSpec as P

HEADS = 128
HEAD_DIM = 64
STATE = 128
GROUPS = 8
KERNEL = 4
SPAN = 128


epsilon = 1e-05
quant_range = 448.0


def from_behind(value, axis, steps):
    count = lax.axis_size(axis)
    first, last = (max(0, -steps), min(count, count - steps))
    return lax.ppermute(value, axis, [(source, source + steps) for source in range(first, last)])


def carried_in(shard, axis, combine, identity):
    count, here = (lax.axis_size(axis), lax.axis_index(axis))
    everything = jax.tree.map(
        lambda part, kind: lax.all_gather(part.astype(kind), axis),
        shard,
        (jnp.bfloat16, jnp.bfloat16),
    )
    start = jax.tree.map(
        lambda part, zero: jnp.broadcast_to(jnp.asarray(zero, part.dtype), part.shape),
        shard,
        identity,
    )

    def turn(k, before):
        reached = k < here
        new = combine(
            before, jax.tree.map(lambda part, own: part[k].astype(own.dtype), everything, shard)
        )
        return jax.tree.map(lambda a, b: jnp.where(reached, a, b), new, before)

    return lax.fori_loop(0, count, turn, start)


def depthwise(before, projected, conv_taps, length):
    extended = jnp.concatenate([before, projected], axis=0)
    summed = conv_taps[0] * extended[0:length]
    for offset in range(1, KERNEL):
        summed = summed + conv_taps[offset] * extended[offset : offset + length]
    return jax.nn.silu(summed).astype(jnp.bfloat16)


def combine(earlier, later):
    return (earlier[0] * later[0], later[0][:, None, None] * earlier[1] + later[1])


def by_tokens(
    hidden_in,
    prev_amax,
    w_x,
    w_bc,
    w_dt,
    conv_x,
    conv_bc,
    conv_state_x,
    conv_state_bc,
    dt_bias,
    decay_rate,
    skip,
    init_state,
    norm_gain,
    w_out,
):
    margin = KERNEL - 1
    gathered = lax.all_gather(hidden_in, "tensor", axis=0, tiled=True)
    abs_max = lax.pmax(jnp.max(jnp.abs(gathered.astype(jnp.float32))), "seq")
    in_scale = prev_amax / quant_range
    leading = lax.axis_index("seq") == 0
    row_count = gathered.shape[0]
    bc_width = w_bc.shape[1] * w_bc.shape[2] * w_bc.shape[3]
    bc_rows = jnp.reshape(w_bc, (w_bc.shape[0], bc_width))
    scaled = gathered.astype(jnp.float32) * (quant_range / prev_amax)
    quant = jnp.clip(scaled, -quant_range, quant_range).astype(jnp.bfloat16)
    pieces = (
        lax.all_gather(w_x, "seq", axis=0, tiled=True),
        lax.all_gather(bc_rows, "seq", axis=0, tiled=True),
        lax.all_gather(w_dt, "seq", axis=0, tiled=True),
    )
    x_proj, bc_proj, dt_proj = tuple(
        (
            jnp.dot(quant, weight_piece, preferred_element_type=jnp.float32)
            for weight_piece in pieces
        )
    )
    x_whole = (x_proj * in_scale).astype(jnp.bfloat16)
    bc_whole = (bc_proj * in_scale).astype(jnp.bfloat16)
    dt_raw = dt_proj * in_scale
    state_bc = jnp.reshape(conv_state_bc, (margin, bc_width))
    received = from_behind(
        (x_whole[row_count - margin :], bc_whole[row_count - margin :]), "seq", 1
    )
    x_edge = jnp.where(leading, conv_state_x, received[0])
    bc_edge = jnp.where(leading, state_bc, received[1])
    x_act = depthwise(x_edge, x_whole, conv_x, row_count)
    bc_act = depthwise(bc_edge, bc_whole, jnp.reshape(conv_bc, (KERNEL, bc_width)), row_count)
    step_size = jax.nn.softplus(dt_raw + dt_bias)
    heads_here = step_size.shape[1]
    groups_here = w_bc.shape[1]
    per_group = HEADS // GROUPS
    blocks = row_count // SPAN
    x_blocks = x_act.reshape(blocks, SPAN, heads_here, HEAD_DIM)
    bc_blocks = bc_act.reshape(blocks, SPAN, groups_here, 2, STATE)
    in_map = bc_blocks[:, :, :, 0]
    out_map = bc_blocks[:, :, :, 1]
    step_blocks = step_size.reshape(blocks, SPAN, heads_here)
    cum_blocks = jnp.cumsum(-step_blocks * decay_rate, axis=1)
    index_row = jnp.arange(SPAN, dtype=jnp.int32)
    lower_mask = index_row[:, None] >= index_row[None, :]
    intersection = jnp.einsum(
        "ctgn,cugn->cgtu", out_map, in_map, preferred_element_type=jnp.float32
    )
    intersection = jnp.repeat(intersection, per_group, axis=1)
    cum_heads = jnp.transpose(cum_blocks, (0, 2, 1))
    log_gap = cum_heads[:, :, :, None] - cum_heads[:, :, None, :]
    decay = jnp.exp(jnp.where(lower_mask[None, None], log_gap, -1e30))
    step_heads = jnp.transpose(step_blocks, (0, 2, 1))
    weights = (intersection * decay * step_heads[:, :, None, :]).astype(jnp.bfloat16)
    local_part = jnp.einsum(
        "chtu,cuhp->cthp", weights, x_blocks, preferred_element_type=jnp.float32
    )
    last_cum = cum_blocks[:, SPAN - 1, :]
    x_weighted = (
        x_blocks.astype(jnp.float32)
        * (step_blocks * jnp.exp(last_cum[:, None, :] - cum_blocks))[:, :, :, None]
    ).astype(jnp.bfloat16)
    in_heads = jnp.repeat(in_map, per_group, axis=2)
    added = jnp.einsum("cuhp,cuhn->chpn", x_weighted, in_heads, preferred_element_type=jnp.float32)

    def carry_on(carried, element):
        block_decay, block_added = element
        return (block_decay[:, None, None] * carried + block_added, carried)

    empty_state = jnp.zeros((heads_here, HEAD_DIM, STATE), jnp.float32)
    device_state, entering = lax.scan(carry_on, empty_state, (jnp.exp(last_cum), added))
    device_decay = jnp.exp(jnp.sum(last_cum, axis=0))
    seeded = device_state + jnp.where(leading, device_decay[:, None, None] * init_state, 0.0)
    identity = (jnp.ones_like(device_decay), jnp.zeros_like(device_state))
    scanned = carried_in((device_decay, seeded), "seq", combine, identity)
    incoming = jnp.where(leading, init_state, scanned[1])
    prefix = jnp.exp(jnp.cumsum(last_cum, axis=0) - last_cum)
    states_in = entering + prefix[:, :, None, None] * incoming[None]
    out_heads = jnp.repeat(out_map, per_group, axis=2).astype(jnp.float32)
    carried_part = (
        jnp.einsum("cthn,chpn->cthp", out_heads, states_in, precision=lax.Precision.HIGHEST)
        * jnp.exp(cum_blocks)[:, :, :, None]
    )
    ssm_out = local_part + carried_part + skip[None, None, :, None] * x_blocks.astype(jnp.float32)
    ssm_out = ssm_out.reshape(row_count, heads_here * HEAD_DIM)
    squares = lax.psum(jnp.sum(ssm_out * ssm_out, axis=1), "tensor")
    mean_sq = squares / (HEADS * HEAD_DIM)
    normed = (ssm_out * lax.rsqrt(mean_sq + epsilon)[:, None] * norm_gain).astype(jnp.bfloat16)
    partial_out = jnp.dot(
        normed, lax.all_gather(w_out, "seq", axis=1, tiled=True), preferred_element_type=jnp.float32
    )
    layer_out = lax.psum_scatter(
        partial_out.astype(jnp.bfloat16), "tensor", scatter_dimension=0, tiled=True
    )
    return (layer_out, abs_max)


PAIR = 2
LINE = 4
PARTS = 2
ROWS = 8
SMEM = pl.BlockSpec(memory_space=pltpu.SMEM)
HIGHEST = lax.Precision.HIGHEST


def splits(mesh):
    count, ranks = (mesh.shape["seq"], mesh.shape["tensor"])
    heads_all, groups_here = (HEADS // ranks, GROUPS // ranks)
    if count != PAIR * LINE or groups_here != PAIR or ranks & (ranks - 1):
        return False
    heads_here = heads_all // count
    return 2 * heads_here == ROWS and heads_here * HEAD_DIM == 2 * SPAN


def nt_dot(a, b, **kw):
    return lax.dot_general(
        a, b, (((1,), (1,)), ((), ())), preferred_element_type=jnp.float32, **kw
    )


def project_kernel(place_ref, factor_ref, *refs):
    outs = LINE + 4
    ranks = len(refs) - 6 - outs
    hidden = refs[:ranks]
    own_x, other_x, own_bc, other_bc, own_dt, other_dt = refs[ranks : ranks + 6]
    x_refs = refs[ranks + 6 : ranks + 6 + LINE]
    bc_ref, largest_ref, quant_ref, dt_buf = refs[ranks + 6 + LINE :]
    side, z = (place_ref[1], place_ref[2])
    step = pl.program_id(0)
    factor = factor_ref[0]
    depth = own_x.shape[0]
    largest = None
    for j in range(ranks):
        for half in range(PAIR):
            values = hidden[j][:, :, half * depth : (half + 1) * depth].astype(jnp.float32)
            scaled = jnp.clip(values * factor, -quant_range, quant_range)
            quant_ref[half, :, j] = scaled.astype(jnp.bfloat16)
            top = jnp.max(jnp.abs(values).reshape(-1, ROWS, depth), axis=0)
            largest = top if largest is None else jnp.maximum(largest, top)
    width = largest_ref.shape[1]
    top = largest[:, :width]
    for at in range(width, depth, width):
        top = jnp.maximum(top, largest[:, at : at + width])

    @pl.when(step == 0)
    def _():
        largest_ref[...] = top

    @pl.when(step > 0)
    def _():
        largest_ref[...] = jnp.maximum(largest_ref[...], top)

    rows = quant_ref.shape[1] * quant_ref.shape[2] * quant_ref.shape[3]
    near = quant_ref[side].reshape(rows, depth)
    far = quant_ref[1 - side].reshape(rows, depth)

    def both(own, other):
        return jnp.dot(near, own, preferred_element_type=jnp.float32) + jnp.dot(
            far, other, preferred_element_type=jnp.float32
        )

    at_rows = pl.ds(pl.multiple_of(step * rows, rows), rows)
    dt_buf[...] = (nt_dot(own_dt[...], near) + nt_dot(other_dt[...], far)).reshape(dt_buf.shape)
    channels = x_refs[0].shape[1]
    tokens = pl.num_programs(0) * rows
    extra = rows // channels * ROWS
    upper = lax.broadcasted_iota(jnp.int32, (ROWS, channels), 0) < ROWS // 2
    for m in reversed(range(LINE)):
        owner = z ^ m
        cut = pl.ds(pl.multiple_of(owner * channels, channels), channels)
        x_refs[m][at_rows] = both(own_x[:, cut], other_x[:, cut]).astype(jnp.bfloat16)
        dt = dt_buf[owner]
        pieces = [
            split_parts(dt[:, at : at + channels], upper) for at in range(0, rows, channels)
        ]
        x_refs[m][pl.ds(pl.multiple_of(tokens + step * extra, 16), extra)] = jnp.concatenate(
            pieces, axis=0
        ).astype(jnp.bfloat16)
    bc_ref[at_rows] = both(own_bc[...], other_bc[...]).astype(jnp.bfloat16)


def split_parts(values, upper):
    top = values.astype(jnp.bfloat16).astype(jnp.float32)
    return jnp.where(upper, top, values - top)


def project(place, factor, hidden, weights, part):
    count, own, wide = hidden[0].shape
    ranks = len(hidden)
    w_x, other_x = weights[:2]
    depth, x_wide = other_x.shape
    channels = x_wide // LINE
    here = count // PARTS
    steps = max(1, 2 // PARTS)
    each = here // steps
    tokens = here * ranks * own
    extra = tokens // channels * ROWS

    def fixed(array):
        return pl.BlockSpec(array.shape, lambda i, p: (0,) * array.ndim)

    payload = jax.ShapeDtypeStruct((tokens + extra, channels), jnp.bfloat16)
    maps = jax.ShapeDtypeStruct((tokens, weights[2].shape[1]), jnp.bfloat16)
    largest = jax.ShapeDtypeStruct((ROWS, 128), jnp.float32)
    outs = [payload] * LINE + [maps, largest]
    first = part * steps
    return pl.pallas_call(
        project_kernel,
        grid_spec=pltpu.PrefetchScalarGridSpec(
            num_scalar_prefetch=1,
            grid=(steps,),
            in_specs=[SMEM]
            + [pl.BlockSpec((each, own, wide), lambda i, p: (first + i, 0, 0))] * ranks
            + [pl.BlockSpec((depth, x_wide), lambda i, p: (0, p[1]))]
            + [fixed(w) for w in weights[1:]],
            out_specs=[fixed(out) for out in outs],
            scratch_shapes=[
                pltpu.VMEM((PAIR, each, ranks, own, depth), jnp.bfloat16),
                pltpu.VMEM((LINE, ROWS, each * ranks * own), jnp.float32),
            ],
        ),
        out_shape=outs,
        compiler_params=pltpu.CompilerParams(vmem_limit_bytes=40 * 2**20),
        cost_estimate=pl.CostEstimate(
            flops=2 * tokens * wide * (x_wide + maps.shape[1]),
            bytes_accessed=2 * tokens * (wide + x_wide),
            transcendentals=0,
        ),
        name="project",
    )(place, factor, *hidden, *weights)


def onward_kernel(own_ref, received_ref, out_ref):
    rows, channels = own_ref.shape
    tokens = rows * channels // (channels + ROWS)
    total = own_ref[:tokens].astype(jnp.float32) + received_ref[:tokens].astype(jnp.float32)
    out_ref[:tokens] = total.astype(jnp.bfloat16)
    upper = lax.broadcasted_iota(jnp.int32, (ROWS, channels), 0) < ROWS // 2
    extra = own_ref[tokens:].astype(jnp.float32) + received_ref[tokens:].astype(jnp.float32)
    pieces = []
    for at in range(0, rows - tokens, ROWS):
        piece = extra[at : at + ROWS]
        pieces.append(split_parts(piece + pltpu.roll(piece, ROWS // 2, 0), upper))
    out_ref[tokens:] = jnp.concatenate(pieces, axis=0).astype(jnp.bfloat16)


def onward(own, received):
    whole = pl.BlockSpec(own.shape, lambda: (0, 0))
    return pl.pallas_call(
        onward_kernel,
        in_specs=[whole, whole],
        out_specs=whole,
        out_shape=jax.ShapeDtypeStruct(own.shape, own.dtype),
        compiler_params=pltpu.CompilerParams(vmem_limit_bytes=20 * 2**20),
        cost_estimate=pl.CostEstimate(
            flops=own.size, bytes_accessed=6 * own.size, transcendentals=0
        ),
        name="onward",
    )(own, received)


def scan_kernel(first, place_ref, scale_ref, *refs):
    x_refs, bc_refs = (refs[:4], refs[4:7])
    small_ref, largest_ref, carry_ref, out_ref, carry_out_ref, x_buf, bc_buf = refs[7:]
    tokens, channels = bc_refs[0].shape
    blocks = tokens // SPAN
    heads = channels // HEAD_DIM
    rank, z = (place_ref[0], place_ref[2])
    ranks = place_ref.shape[0] - 3
    own = SPAN // ranks
    edge = ROWS
    in_scale = scale_ref[0]
    at_end = (z == 0) | (z == LINE - 1)
    if first:
        x_buf[:edge] = small_ref[:edge]
        bc_buf[:edge] = small_ref[edge : 2 * edge]
        state = carry_ref[...].T
    else:
        x_buf[:edge] = carry_ref[STATE : STATE + edge]
        bc_buf[:edge] = carry_ref[STATE + edge :]
        state = carry_ref[:STATE]

    for block in range(blocks):
        for true_rank in range(ranks):
            source = block * SPAN + (true_rank ^ rank) * own
            source = pl.ds(pl.multiple_of(source, own), own)
            at = edge + block * SPAN + true_rank * own
            at = slice(at, at + own)
            total = sum(ref[source].astype(jnp.float32) for ref in x_refs) * in_scale
            x_buf[at] = total.astype(jnp.bfloat16).astype(jnp.float32)
            near, far, done = (ref[source].astype(jnp.float32) for ref in bc_refs)
            total = ((near + far) * in_scale).astype(jnp.bfloat16).astype(jnp.float32)
            bc_buf[at] = jnp.where(at_end, done, total)

    taps = 2 * edge

    def activate(buf, row, block):
        start = edge - (KERNEL - 1) + block * SPAN
        summed = small_ref[row : row + 1] * buf[start : start + SPAN]
        for k in range(1, KERNEL):
            summed = summed + small_ref[row + k : row + k + 1] * buf[start + k : start + k + SPAN]
        return (summed / (1.0 + jnp.exp(-summed))).astype(jnp.bfloat16)

    skip = small_ref[taps + 2 * KERNEL : taps + 2 * KERNEL + 1]
    gain = small_ref[taps + 2 * KERNEL + 1 : taps + 2 * KERNEL + 2]
    bias = small_ref[4 * edge :, :SPAN]
    rate = small_ref[4 * edge :, SPAN:]

    up = lax.broadcasted_iota(jnp.int32, (SPAN, SPAN), 0)
    across = lax.broadcasted_iota(jnp.int32, (SPAN, SPAN), 1)
    lane = lax.broadcasted_iota(jnp.int32, (SPAN, channels), 1)
    lower = up >= across
    upper = (up <= across).astype(jnp.float32)
    lanes = across[:ROWS]

    dt = sum(ref[tokens:].astype(jnp.float32) for ref in x_refs)
    steps = []
    wide = channels // SPAN
    for block in range(blocks):
        tile = dt[block // wide * ROWS : (block // wide + 1) * ROWS]
        cut = tile[:, block % wide * SPAN : (block % wide + 1) * SPAN]
        cut = (cut + pltpu.roll(cut, ROWS // 2, 0)) * in_scale
        bit = 1
        while bit < ranks:
            shift = bit * own
            flipped = jnp.where(
                (lanes // shift) % 2 == 1,
                pltpu.roll(cut, shift, 1),
                pltpu.roll(cut, SPAN - shift, 1),
            )
            cut = jnp.where((rank & bit) != 0, flipped, cut)
            bit *= 2
        raw = cut + bias
        steps.append(jnp.maximum(raw, 0.0) + jnp.log1p(jnp.exp(-jnp.abs(raw))))
    drops = jnp.concatenate([-step * rate for step in steps], axis=0)
    cums = jnp.dot(drops, upper, precision=HIGHEST, preferred_element_type=jnp.float32)

    sums = jnp.zeros((SPAN, SPAN), jnp.float32)
    for block in range(blocks):
        x_act = activate(x_buf, taps, block)
        bc_act = activate(bc_buf, taps + KERNEL, block)
        in_map, out_map = (bc_act[:, :STATE], bc_act[:, STATE:])
        step, cum = (steps[block], cums[block * ROWS : (block + 1) * ROWS])
        last = cum[:, SPAN - 1 : SPAN]
        turned = jnp.concatenate(
            [
                cum,
                step * jnp.exp(last - cum),
                jnp.exp(cum),
                jnp.zeros((SPAN - 3 * ROWS, SPAN), jnp.float32),
            ],
            axis=0,
        ).T

        def spread(row):
            result = jnp.broadcast_to(turned[:, row : row + 1], (SPAN, channels))
            for h in range(1, heads):
                result = jnp.where(lane >= h * HEAD_DIM, turned[:, row + h : row + h + 1], result)
            return result

        inner = jnp.where(lower, nt_dot(out_map, in_map), 0.0)
        x_wide = x_act.astype(jnp.float32)
        weights, spaced = ([], [])
        for h in range(heads):
            gap = jnp.where(lower, turned[:, h : h + 1] - cum[h : h + 1], 0.0)
            weights.append((inner * jnp.exp(gap) * step[h : h + 1]).astype(jnp.bfloat16))
            inside = (lane >= h * HEAD_DIM) & (lane < (h + 1) * HEAD_DIM)
            spaced.append(jnp.where(inside, x_wide, 0.0).astype(jnp.bfloat16))
        local_part = jnp.dot(
            jnp.concatenate(weights, axis=1),
            jnp.concatenate(spaced, axis=0),
            preferred_element_type=jnp.float32,
        )
        grown = spread(2 * ROWS)
        x_weighted = (x_wide * spread(ROWS)).astype(jnp.bfloat16)
        added = lax.dot_general(
            in_map, x_weighted, (((0,), (0,)), ((), ())), preferred_element_type=jnp.float32
        )
        high = state.astype(jnp.bfloat16)
        rest = state - high.astype(jnp.float32)
        middle = rest.astype(jnp.bfloat16)
        low = (rest - middle.astype(jnp.float32)).astype(jnp.bfloat16)
        carried = jnp.dot(out_map, high, preferred_element_type=jnp.float32)
        carried = carried + jnp.dot(out_map, middle, preferred_element_type=jnp.float32)
        carried = carried + jnp.dot(out_map, low, preferred_element_type=jnp.float32)
        ssm_out = local_part + grown * carried + skip * x_wide
        state = grown[SPAN - 1 : SPAN] * state + added
        out_ref[block * SPAN : (block + 1) * SPAN] = (ssm_out * gain).astype(jnp.bfloat16)
        summed = jnp.sum(ssm_out * ssm_out, axis=1, keepdims=True)
        sums = jnp.where(across == block, summed, sums)

    whole = sums.T[:ROWS]
    top = whole.astype(jnp.bfloat16).astype(jnp.float32)
    largest = jnp.broadcast_to(jnp.max(largest_ref[...]), (ROWS, channels))
    extra = jnp.concatenate([jnp.concatenate([top, whole - top], axis=1), largest], axis=0)
    out_ref[tokens:] = extra.astype(jnp.bfloat16)
    carry_out_ref[:STATE] = state
    carry_out_ref[STATE : STATE + edge] = x_buf[tokens : tokens + edge]
    carry_out_ref[STATE + edge :] = bc_buf[tokens : tokens + edge]


def scan(place, in_scale, sums, maps, small, largest, carry, first):
    channels = sums[0].shape[1]
    tokens = maps[0].shape[0]

    def fixed(array):
        return pl.BlockSpec(array.shape, lambda i, p: (0, 0))

    held = pl.BlockSpec((channels, STATE), lambda i, p: (p[1] * LINE + p[2], 0))
    outs = [
        jax.ShapeDtypeStruct((tokens + 2 * ROWS, channels), jnp.bfloat16),
        jax.ShapeDtypeStruct((STATE + 2 * ROWS, channels), jnp.float32),
    ]
    return pl.pallas_call(
        functools.partial(scan_kernel, first),
        grid_spec=pltpu.PrefetchScalarGridSpec(
            num_scalar_prefetch=1,
            grid=(1,),
            in_specs=[SMEM]
            + [fixed(array) for array in (*sums, *maps, small, largest)]
            + [held if first else fixed(carry)],
            out_specs=[fixed(out) for out in outs],
            scratch_shapes=[
                pltpu.VMEM((tokens + ROWS, channels), jnp.float32),
                pltpu.VMEM((tokens + ROWS, 2 * STATE), jnp.float32),
            ],
        ),
        out_shape=outs,
        compiler_params=pltpu.CompilerParams(vmem_limit_bytes=40 * 2**20),
        cost_estimate=pl.CostEstimate(
            flops=8 * tokens * SPAN * channels,
            bytes_accessed=8 * tokens * channels,
            transcendentals=tokens * (channels + 8 * SPAN),
        ),
        name="scan",
    )(place, in_scale, *sums, *maps, small, largest, carry)


def by_heads(
    hidden_in,
    prev_amax,
    w_x,
    w_bc,
    w_dt,
    conv_x,
    conv_bc,
    conv_state_x,
    conv_state_bc,
    dt_bias,
    decay_rate,
    skip,
    init_state,
    norm_gain,
    w_out,
):
    margin = KERNEL - 1
    count, here = (lax.axis_size("seq"), lax.axis_index("seq"))
    ranks, rank = (lax.axis_size("tensor"), lax.axis_index("tensor"))
    z, side = (here // PAIR, here % PAIR)
    place_of = side * LINE + z
    f32, bf16 = (jnp.float32, jnp.bfloat16)
    own, width = hidden_in.shape
    depth = w_x.shape[0]
    channels = w_x.shape[1] // count
    heads_here = w_dt.shape[1] // count
    in_scale = (prev_amax / quant_range).reshape(1)
    factor = (quant_range / prev_amax).reshape(1)
    place = jnp.stack([rank, side, z] + [rank] * ranks).astype(jnp.int32)

    def pick(array, axis, index):
        return lax.dynamic_index_in_dim(array, index, axis, keepdims=False)

    def along(value, pairs):
        moves = [(a * PAIR + x, b * PAIR + x) for a, b in pairs for x in range(PAIR)]
        return lax.ppermute(value, "seq", moves)

    def across(value):
        return lax.ppermute(value, "seq", [(s, s ^ 1) for s in range(count)])

    half = w_x.shape[1] // PAIR
    x_send = lax.dynamic_slice_in_dim(w_x, (1 - side) * half, half, axis=1)
    bc_own = pick(w_bc, 1, side).reshape(depth, 2 * STATE)
    bc_send = pick(w_bc, 1, 1 - side).reshape(depth, 2 * STATE)
    x_send, bc_send, hidden_in = lax.optimization_barrier((x_send, bc_send, hidden_in))
    x_other = across(x_send)
    bc_other = across(bc_send)
    dt_rows = w_dt.T.reshape(PAIR, LINE, 1, heads_here, depth)
    dt_rows = jnp.broadcast_to(dt_rows, (PAIR, LINE, ROWS // heads_here, heads_here, depth))
    dt_rows = dt_rows.reshape(PAIR, LINE * ROWS, depth)
    dt_own = pick(dt_rows, 0, side)
    dt_other = across(pick(dt_rows, 0, 1 - side))

    pieces = hidden_in.reshape(own, LINE, 1, PAIR * depth).transpose(1, 2, 0, 3)
    pieces = jnp.broadcast_to(pieces, (LINE, PAIR, own, PAIR * depth))
    pieces = pieces.reshape(count, own, PAIR * depth)
    rows = [lax.all_to_all(pieces, "seq", split_axis=0, concat_axis=0, tiled=True)]
    for j in range(1, ranks):
        bit = j & -j
        rows.append(lax.ppermute(rows[j - bit], "tensor", [(t, t ^ bit) for t in range(ranks)]))

    def of_heads(array):
        return jnp.repeat(array, HEAD_DIM)[None]

    by_channel = jnp.concatenate(
        [conv_state_x.astype(f32), conv_x, of_heads(skip), norm_gain[None]], axis=0
    )
    by_channel = lax.dynamic_slice_in_dim(by_channel, place_of * channels, channels, axis=1)
    by_map = jnp.concatenate([conv_state_bc.astype(f32), conv_bc], axis=0)
    by_map = pick(by_map, 1, side).reshape(margin + KERNEL, 2 * STATE)
    by_head = jnp.stack([dt_bias, decay_rate]).reshape(2, count, heads_here)
    by_head = jnp.tile(pick(by_head, 1, place_of).T, (ROWS // heads_here, 1))
    by_head = jnp.repeat(by_head, SPAN, axis=1)
    blank = jnp.zeros((ROWS - margin, channels), f32)
    small = jnp.concatenate(
        [
            blank,
            by_channel[:margin],
            blank,
            by_map[:margin],
            by_channel[margin : margin + KERNEL],
            by_map[margin:],
            by_channel[margin + KERNEL :],
            jnp.zeros((2 * ROWS - 2 * KERNEL - 2, channels), f32),
            by_head,
        ],
        axis=0,
    )

    start, end = (0, LINE - 1)
    at_end = (z == start) | (z == end)
    next_start, next_end = (1, LINE - 2)
    weights = (w_x, x_other, bc_own, bc_other, dt_own, dt_other)
    carry = init_state.reshape(-1, STATE)
    totals, tops = ([], [])
    for part in range(PARTS):
        mine, near, over, far, maps, largest = project(place, factor, rows, weights, part)
        map_hop = along(maps, [(start, next_start), (end, next_end)])
        hop_far = along(far, [(start, next_start), (end, next_end)])
        hop_over = along(over, [(start, next_start), (end, next_end)])
        got_near = along(near, [(s, s ^ 1) for s in range(LINE)])
        map_sum = (maps.astype(f32) + map_hop.astype(f32)).astype(bf16)
        map_far = along(map_sum, [(next_start, next_end), (next_end, next_start)])
        map_done = ((map_sum.astype(f32) + map_far.astype(f32)) * in_scale).astype(bf16)
        map_done, got_near = lax.optimization_barrier((map_done, got_near))
        map_done = along(map_done, [(next_start, start), (next_end, end)])
        sent_end = onward(over, hop_far)
        hop_over, sent_end = lax.optimization_barrier((hop_over, sent_end))
        got_end = along(sent_end, [(next_start, end), (next_end, start)])
        got_next = along(onward(far, hop_over), [(next_start, next_end), (next_end, next_start)])
        gained, carry = scan(
            place,
            in_scale,
            [mine, got_near, got_end, got_next],
            [map_sum, map_far, map_done],
            small,
            largest,
            carry,
            part == 0,
        )
        tokens = gained.shape[0] - 2 * ROWS
        beside = along(gained, [(s, s ^ 1) for s in range(LINE)])
        middle = [(next_start, next_end), (next_end, next_start)]
        outward = [(next_start, start), (next_end, end)]
        facing = along(gained, middle)
        beyond = along(beside, middle)
        second = jnp.where(at_end, along(facing, outward), facing)
        third = jnp.where(at_end, along(beyond, outward), beyond)
        two, three = (jnp.where(at_end, 2, 3), jnp.where(at_end, 3, 2))
        got = ((0, gained), (1, beside), (two, second), (three, third))
        total = squares = top = None
        for m, block in got:
            for x, piece in enumerate((block, across(block))):
                at = ((side ^ x) * LINE + (z ^ m)) * channels
                w_rows = lax.dynamic_slice_in_dim(w_out, at, channels, axis=0)
                product = jnp.dot(piece, w_rows, preferred_element_type=f32)
                tail = piece[tokens:].astype(f32)
                low, high = (tail[:ROWS, :SPAN] + tail[:ROWS, SPAN:], tail[ROWS:, :SPAN])
                if total is None:
                    total, squares, top = (product, low, high)
                else:
                    total = total + product
                    squares = squares + low
                    top = jnp.maximum(top, high)
        tops.append(top)
        wide = w_out.shape[1]
        blocks = tokens // SPAN
        kept = total[:tokens].reshape(blocks, ranks, own, wide)
        for bit in (1 << b for b in range(ranks.bit_length() - 1)):
            pairs = [(t, t ^ bit) for t in range(ranks)]
            squares = squares + lax.ppermute(squares, "tensor", pairs)
            keeps = (rank // bit) % 2
            halves = kept.reshape(blocks, -1, 2, own, wide)
            received = lax.ppermute(pick(halves, 2, 1 - keeps).astype(bf16), "tensor", pairs)
            kept = pick(halves, 2, keeps) + received.astype(f32)
        kept = kept.reshape(blocks, own, wide)
        mean_sq = squares[:blocks].reshape(blocks, ranks, own) / (HEADS * HEAD_DIM)
        factors = lax.rsqrt(pick(mean_sq, 1, rank) + epsilon)
        totals.append((kept * factors[:, :, None]).astype(bf16))
    final = jnp.concatenate(totals, axis=0)
    final = lax.all_to_all(final, "seq", split_axis=0, concat_axis=0, tiled=True)
    layer_out = final.transpose(1, 0, 2).reshape(own, count * final.shape[2])
    abs_max = jnp.max(functools.reduce(jnp.maximum, tops))
    return (layer_out, abs_max)


def solution(mesh):
    return jax.shard_map(
        by_heads if splits(mesh) else by_tokens,
        mesh=mesh,
        in_specs=(
            P(("seq", "tensor"), None),
            P(),
            P("seq", "tensor"),
            P("seq", "tensor", None, None),
            P("seq", "tensor"),
            P(None, "tensor"),
            P(None, "tensor", None, None),
            P(None, "tensor"),
            P(None, "tensor", None, None),
            P("tensor"),
            P("tensor"),
            P("tensor"),
            P("tensor", None, None),
            P("tensor"),
            P("tensor", "seq"),
        ),
        out_specs=(P(("seq", "tensor"), None), P()),
        check_vma=False,
    )
```

```python
import functools

import jax
import jax.numpy as jnp
from jax import lax
from jax.experimental import pallas as pl
from jax.experimental.pallas import tpu as pltpu
from jax.sharding import PartitionSpec as P

HEADS = 128
HEAD_DIM = 64
STATE = 128
GROUPS = 8
KERNEL = 4
SPAN = 128


epsilon = 1e-05
quant_range = 448.0


def from_behind(value, axis, steps):
    count = lax.axis_size(axis)
    first, last = (max(0, -steps), min(count, count - steps))
    return lax.ppermute(value, axis, [(source, source + steps) for source in range(first, last)])


def carried_in(shard, axis, combine, identity):
    count, here = (lax.axis_size(axis), lax.axis_index(axis))
    everything = jax.tree.map(
        lambda part, kind: lax.all_gather(part.astype(kind), axis),
        shard,
        (jnp.bfloat16, jnp.bfloat16),
    )
    start = jax.tree.map(
        lambda part, zero: jnp.broadcast_to(jnp.asarray(zero, part.dtype), part.shape),
        shard,
        identity,
    )

    def turn(k, before):
        reached = k < here
        new = combine(
            before, jax.tree.map(lambda part, own: part[k].astype(own.dtype), everything, shard)
        )
        return jax.tree.map(lambda a, b: jnp.where(reached, a, b), new, before)

    return lax.fori_loop(0, count, turn, start)


def depthwise(before, projected, conv_taps, length):
    extended = jnp.concatenate([before, projected], axis=0)
    summed = conv_taps[0] * extended[0:length]
    for offset in range(1, KERNEL):
        summed = summed + conv_taps[offset] * extended[offset : offset + length]
    return jax.nn.silu(summed).astype(jnp.bfloat16)


def combine(earlier, later):
    return (earlier[0] * later[0], later[0][:, None, None] * earlier[1] + later[1])


def by_tokens(
    hidden_in,
    prev_amax,
    w_x,
    w_bc,
    w_dt,
    conv_x,
    conv_bc,
    conv_state_x,
    conv_state_bc,
    dt_bias,
    decay_rate,
    skip,
    init_state,
    norm_gain,
    w_out,
):
    margin = KERNEL - 1
    gathered = lax.all_gather(hidden_in, "tensor", axis=0, tiled=True)
    abs_max = lax.pmax(jnp.max(jnp.abs(gathered.astype(jnp.float32))), "seq")
    in_scale = prev_amax / quant_range
    leading = lax.axis_index("seq") == 0
    row_count = gathered.shape[0]
    bc_width = w_bc.shape[1] * w_bc.shape[2] * w_bc.shape[3]
    bc_rows = jnp.reshape(w_bc, (w_bc.shape[0], bc_width))
    scaled = gathered.astype(jnp.float32) * (quant_range / prev_amax)
    quant = jnp.clip(scaled, -quant_range, quant_range).astype(jnp.bfloat16)
    pieces = (
        lax.all_gather(w_x, "seq", axis=0, tiled=True),
        lax.all_gather(bc_rows, "seq", axis=0, tiled=True),
        lax.all_gather(w_dt, "seq", axis=0, tiled=True),
    )
    x_proj, bc_proj, dt_proj = tuple(
        (
            jnp.dot(quant, weight_piece, preferred_element_type=jnp.float32)
            for weight_piece in pieces
        )
    )
    x_whole = (x_proj * in_scale).astype(jnp.bfloat16)
    bc_whole = (bc_proj * in_scale).astype(jnp.bfloat16)
    dt_raw = dt_proj * in_scale
    state_bc = jnp.reshape(conv_state_bc, (margin, bc_width))
    received = from_behind(
        (x_whole[row_count - margin :], bc_whole[row_count - margin :]), "seq", 1
    )
    x_edge = jnp.where(leading, conv_state_x, received[0])
    bc_edge = jnp.where(leading, state_bc, received[1])
    x_act = depthwise(x_edge, x_whole, conv_x, row_count)
    bc_act = depthwise(bc_edge, bc_whole, jnp.reshape(conv_bc, (KERNEL, bc_width)), row_count)
    step_size = jax.nn.softplus(dt_raw + dt_bias)
    heads_here = step_size.shape[1]
    groups_here = w_bc.shape[1]
    per_group = HEADS // GROUPS
    blocks = row_count // SPAN
    x_blocks = x_act.reshape(blocks, SPAN, heads_here, HEAD_DIM)
    bc_blocks = bc_act.reshape(blocks, SPAN, groups_here, 2, STATE)
    in_map = bc_blocks[:, :, :, 0]
    out_map = bc_blocks[:, :, :, 1]
    step_blocks = step_size.reshape(blocks, SPAN, heads_here)
    cum_blocks = jnp.cumsum(-step_blocks * decay_rate, axis=1)
    index_row = jnp.arange(SPAN, dtype=jnp.int32)
    lower_mask = index_row[:, None] >= index_row[None, :]
    intersection = jnp.einsum(
        "ctgn,cugn->cgtu", out_map, in_map, preferred_element_type=jnp.float32
    )
    intersection = jnp.repeat(intersection, per_group, axis=1)
    cum_heads = jnp.transpose(cum_blocks, (0, 2, 1))
    log_gap = cum_heads[:, :, :, None] - cum_heads[:, :, None, :]
    decay = jnp.exp(jnp.where(lower_mask[None, None], log_gap, -1e30))
    step_heads = jnp.transpose(step_blocks, (0, 2, 1))
    weights = (intersection * decay * step_heads[:, :, None, :]).astype(jnp.bfloat16)
    local_part = jnp.einsum(
        "chtu,cuhp->cthp", weights, x_blocks, preferred_element_type=jnp.float32
    )
    last_cum = cum_blocks[:, SPAN - 1, :]
    x_weighted = (
        x_blocks.astype(jnp.float32)
        * (step_blocks * jnp.exp(last_cum[:, None, :] - cum_blocks))[:, :, :, None]
    ).astype(jnp.bfloat16)
    in_heads = jnp.repeat(in_map, per_group, axis=2)
    added = jnp.einsum("cuhp,cuhn->chpn", x_weighted, in_heads, preferred_element_type=jnp.float32)

    def carry_on(carried, element):
        block_decay, block_added = element
        return (block_decay[:, None, None] * carried + block_added, carried)

    empty_state = jnp.zeros((heads_here, HEAD_DIM, STATE), jnp.float32)
    device_state, entering = lax.scan(carry_on, empty_state, (jnp.exp(last_cum), added))
    device_decay = jnp.exp(jnp.sum(last_cum, axis=0))
    seeded = device_state + jnp.where(leading, device_decay[:, None, None] * init_state, 0.0)
    identity = (jnp.ones_like(device_decay), jnp.zeros_like(device_state))
    scanned = carried_in((device_decay, seeded), "seq", combine, identity)
    incoming = jnp.where(leading, init_state, scanned[1])
    prefix = jnp.exp(jnp.cumsum(last_cum, axis=0) - last_cum)
    states_in = entering + prefix[:, :, None, None] * incoming[None]
    out_heads = jnp.repeat(out_map, per_group, axis=2).astype(jnp.float32)
    carried_part = (
        jnp.einsum("cthn,chpn->cthp", out_heads, states_in, precision=lax.Precision.HIGHEST)
        * jnp.exp(cum_blocks)[:, :, :, None]
    )
    ssm_out = local_part + carried_part + skip[None, None, :, None] * x_blocks.astype(jnp.float32)
    ssm_out = ssm_out.reshape(row_count, heads_here * HEAD_DIM)
    squares = lax.psum(jnp.sum(ssm_out * ssm_out, axis=1), "tensor")
    mean_sq = squares / (HEADS * HEAD_DIM)
    normed = (ssm_out * lax.rsqrt(mean_sq + epsilon)[:, None] * norm_gain).astype(jnp.bfloat16)
    partial_out = jnp.dot(
        normed, lax.all_gather(w_out, "seq", axis=1, tiled=True), preferred_element_type=jnp.float32
    )
    layer_out = lax.psum_scatter(
        partial_out.astype(jnp.bfloat16), "tensor", scatter_dimension=0, tiled=True
    )
    return (layer_out, abs_max)


PAIR = 2
LINE = 4
PARTS = 1
ROWS = 8
SMEM = pl.BlockSpec(memory_space=pltpu.SMEM)
HIGHEST = lax.Precision.HIGHEST


def splits(mesh):
    count, ranks = (mesh.shape["seq"], mesh.shape["tensor"])
    heads_all, groups_here = (HEADS // ranks, GROUPS // ranks)
    if count != PAIR * LINE or groups_here != PAIR or ranks & (ranks - 1):
        return False
    heads_here = heads_all // count
    return 2 * heads_here == ROWS and heads_here * HEAD_DIM == 2 * SPAN


def nt_dot(a, b, **kw):
    return lax.dot_general(
        a, b, (((1,), (1,)), ((), ())), preferred_element_type=jnp.float32, **kw
    )


def project_kernel(place_ref, factor_ref, *refs):
    outs = LINE + 4
    ranks = len(refs) - 6 - outs
    hidden = refs[:ranks]
    own_x, other_x, own_bc, other_bc, own_dt, other_dt = refs[ranks : ranks + 6]
    x_refs = refs[ranks + 6 : ranks + 6 + LINE]
    bc_ref, largest_ref, quant_ref, dt_buf = refs[ranks + 6 + LINE :]
    side, z = (place_ref[1], place_ref[2])
    step = pl.program_id(0)
    factor = factor_ref[0]
    depth = own_x.shape[0]
    largest = None
    each = hidden[0].shape[0]
    for j in range(ranks):
        for k in range(each):
            for half in range(PAIR):
                values = hidden[j][k, :, half * depth : (half + 1) * depth].astype(jnp.float32)
                scaled = jnp.clip(values * factor, -quant_range, quant_range)
                quant_ref[half, k ^ ((z * PAIR + side) % each), j] = scaled.astype(jnp.bfloat16)
                top = jnp.max(jnp.abs(values).reshape(-1, ROWS, depth), axis=0)
                largest = top if largest is None else jnp.maximum(largest, top)
    width = largest_ref.shape[1]
    top = largest[:, :width]
    for at in range(width, depth, width):
        top = jnp.maximum(top, largest[:, at : at + width])

    @pl.when(step == 0)
    def _():
        largest_ref[...] = top

    @pl.when(step > 0)
    def _():
        largest_ref[...] = jnp.maximum(largest_ref[...], top)

    rows = quant_ref.shape[1] * quant_ref.shape[2] * quant_ref.shape[3]
    near = quant_ref[side].reshape(rows, depth)
    far = quant_ref[1 - side].reshape(rows, depth)

    def both(own, other):
        return jnp.dot(near, own, preferred_element_type=jnp.float32) + jnp.dot(
            far, other, preferred_element_type=jnp.float32
        )

    at_rows = pl.ds(pl.multiple_of(step * rows, rows), rows)
    dt_buf[...] = (nt_dot(own_dt[...], near) + nt_dot(other_dt[...], far)).reshape(dt_buf.shape)
    channels = x_refs[0].shape[1]
    tokens = pl.num_programs(0) * rows
    extra = rows // channels * ROWS
    upper = lax.broadcasted_iota(jnp.int32, (ROWS, channels), 0) < ROWS // 2
    for m in reversed(range(LINE)):
        owner = z ^ m
        cut = pl.ds(pl.multiple_of(owner * channels, channels), channels)
        x_refs[m][at_rows] = both(own_x[:, cut], other_x[:, cut]).astype(jnp.bfloat16)
        dt = dt_buf[owner]
        pieces = [
            split_parts(dt[:, at : at + channels], upper) for at in range(0, rows, channels)
        ]
        x_refs[m][pl.ds(pl.multiple_of(tokens + step * extra, 16), extra)] = jnp.concatenate(
            pieces, axis=0
        ).astype(jnp.bfloat16)
    bc_ref[at_rows] = both(own_bc[...], other_bc[...]).astype(jnp.bfloat16)


def split_parts(values, upper):
    top = values.astype(jnp.bfloat16).astype(jnp.float32)
    return jnp.where(upper, top, values - top)


def project(place, factor, hidden, weights, part):
    count, own, wide = hidden[0].shape
    ranks = len(hidden)
    w_x, other_x = weights[:2]
    depth, x_wide = other_x.shape
    channels = x_wide // LINE
    here = count // PARTS
    steps = max(1, 2 // PARTS)
    each = here // steps
    tokens = here * ranks * own
    extra = tokens // channels * ROWS

    def fixed(array):
        return pl.BlockSpec(array.shape, lambda i, p: (0,) * array.ndim)

    payload = jax.ShapeDtypeStruct((tokens + extra, channels), jnp.bfloat16)
    maps = jax.ShapeDtypeStruct((tokens, weights[2].shape[1]), jnp.bfloat16)
    largest = jax.ShapeDtypeStruct((ROWS, 128), jnp.float32)
    outs = [payload] * LINE + [maps, largest]
    first = part * steps
    return pl.pallas_call(
        project_kernel,
        grid_spec=pltpu.PrefetchScalarGridSpec(
            num_scalar_prefetch=1,
            grid=(steps,),
            in_specs=[SMEM]
            + [pl.BlockSpec((each, own, wide), lambda i, p: ((first + i) ^ ((p[2] * PAIR + p[1]) // each), 0, 0))]
            * ranks
            + [pl.BlockSpec((depth, x_wide), lambda i, p: (0, p[1]))]
            + [fixed(w) for w in weights[1:]],
            out_specs=[fixed(out) for out in outs],
            scratch_shapes=[
                pltpu.VMEM((PAIR, each, ranks, own, depth), jnp.bfloat16),
                pltpu.VMEM((LINE, ROWS, each * ranks * own), jnp.float32),
            ],
        ),
        out_shape=outs,
        compiler_params=pltpu.CompilerParams(vmem_limit_bytes=40 * 2**20),
        cost_estimate=pl.CostEstimate(
            flops=2 * tokens * wide * (x_wide + maps.shape[1]),
            bytes_accessed=2 * tokens * (wide + x_wide),
            transcendentals=0,
        ),
        name="project",
    )(place, factor, *hidden, *weights)


def onward_kernel(own_ref, received_ref, out_ref):
    rows, channels = own_ref.shape
    tokens = rows * channels // (channels + ROWS)
    total = own_ref[:tokens].astype(jnp.float32) + received_ref[:tokens].astype(jnp.float32)
    out_ref[:tokens] = total.astype(jnp.bfloat16)
    upper = lax.broadcasted_iota(jnp.int32, (ROWS, channels), 0) < ROWS // 2
    extra = own_ref[tokens:].astype(jnp.float32) + received_ref[tokens:].astype(jnp.float32)
    pieces = []
    for at in range(0, rows - tokens, ROWS):
        piece = extra[at : at + ROWS]
        pieces.append(split_parts(piece + pltpu.roll(piece, ROWS // 2, 0), upper))
    out_ref[tokens:] = jnp.concatenate(pieces, axis=0).astype(jnp.bfloat16)


def onward(own, received):
    whole = pl.BlockSpec(own.shape, lambda: (0, 0))
    return pl.pallas_call(
        onward_kernel,
        in_specs=[whole, whole],
        out_specs=whole,
        out_shape=jax.ShapeDtypeStruct(own.shape, own.dtype),
        compiler_params=pltpu.CompilerParams(vmem_limit_bytes=20 * 2**20),
        cost_estimate=pl.CostEstimate(
            flops=own.size, bytes_accessed=6 * own.size, transcendentals=0
        ),
        name="onward",
    )(own, received)


def scan_kernel(first, place_ref, scale_ref, *refs):
    x_refs, bc_refs = (refs[:4], refs[4:7])
    small_ref, largest_ref, carry_ref, out_ref, carry_out_ref, x_buf, bc_buf = refs[7:]
    tokens, channels = bc_refs[0].shape
    blocks = tokens // SPAN
    heads = channels // HEAD_DIM
    rank, z = (place_ref[0], place_ref[2])
    ranks = place_ref.shape[0] - 3
    own = SPAN // ranks
    edge = ROWS
    in_scale = scale_ref[0]
    at_end = (z == 0) | (z == LINE - 1)
    if first:
        x_buf[:edge] = small_ref[:edge]
        bc_buf[:edge] = small_ref[edge : 2 * edge]
        state = carry_ref[...].T
    else:
        x_buf[:edge] = carry_ref[STATE : STATE + edge]
        bc_buf[:edge] = carry_ref[STATE + edge :]
        state = carry_ref[:STATE]

    for block in range(blocks):
        for true_rank in range(ranks):
            source = block * SPAN + (true_rank ^ rank) * own
            source = pl.ds(pl.multiple_of(source, own), own)
            at = edge + block * SPAN + true_rank * own
            at = slice(at, at + own)
            total = sum(ref[source].astype(jnp.float32) for ref in x_refs) * in_scale
            x_buf[at] = total.astype(jnp.bfloat16).astype(jnp.float32)
            near, far, done = (ref[source].astype(jnp.float32) for ref in bc_refs)
            total = ((near + far) * in_scale).astype(jnp.bfloat16).astype(jnp.float32)
            bc_buf[at] = jnp.where(at_end, done, total)

    taps = 2 * edge

    def activate(buf, row, block):
        start = edge - (KERNEL - 1) + block * SPAN
        summed = small_ref[row : row + 1] * buf[start : start + SPAN]
        for k in range(1, KERNEL):
            summed = summed + small_ref[row + k : row + k + 1] * buf[start + k : start + k + SPAN]
        return (summed / (1.0 + jnp.exp(-summed))).astype(jnp.bfloat16)

    skip = small_ref[taps + 2 * KERNEL : taps + 2 * KERNEL + 1]
    gain = small_ref[taps + 2 * KERNEL + 1 : taps + 2 * KERNEL + 2]
    bias = small_ref[4 * edge :, :SPAN]
    rate = small_ref[4 * edge :, SPAN:]

    up = lax.broadcasted_iota(jnp.int32, (SPAN, SPAN), 0)
    across = lax.broadcasted_iota(jnp.int32, (SPAN, SPAN), 1)
    lane = lax.broadcasted_iota(jnp.int32, (SPAN, channels), 1)
    lower = up >= across
    upper = (up <= across).astype(jnp.float32)
    lanes = across[:ROWS]

    dt = sum(ref[tokens:].astype(jnp.float32) for ref in x_refs)
    steps = []
    wide = channels // SPAN
    for block in range(blocks):
        tile = dt[block // wide * ROWS : (block // wide + 1) * ROWS]
        cut = tile[:, block % wide * SPAN : (block % wide + 1) * SPAN]
        cut = (cut + pltpu.roll(cut, ROWS // 2, 0)) * in_scale
        bit = 1
        while bit < ranks:
            shift = bit * own
            flipped = jnp.where(
                (lanes // shift) % 2 == 1,
                pltpu.roll(cut, shift, 1),
                pltpu.roll(cut, SPAN - shift, 1),
            )
            cut = jnp.where((rank & bit) != 0, flipped, cut)
            bit *= 2
        raw = cut + bias
        steps.append(jnp.maximum(raw, 0.0) + jnp.log1p(jnp.exp(-jnp.abs(raw))))
    drops = jnp.concatenate([-step * rate for step in steps], axis=0)
    cums = jnp.dot(drops, upper, precision=HIGHEST, preferred_element_type=jnp.float32)

    sums = jnp.zeros((SPAN, SPAN), jnp.float32)
    for block in range(blocks):
        x_act = activate(x_buf, taps, block)
        bc_act = activate(bc_buf, taps + KERNEL, block)
        in_map, out_map = (bc_act[:, :STATE], bc_act[:, STATE:])
        step, cum = (steps[block], cums[block * ROWS : (block + 1) * ROWS])
        last = cum[:, SPAN - 1 : SPAN]
        turned = jnp.concatenate(
            [
                cum,
                step * jnp.exp(last - cum),
                jnp.exp(cum),
                jnp.zeros((SPAN - 3 * ROWS, SPAN), jnp.float32),
            ],
            axis=0,
        ).T

        def spread(row):
            result = jnp.broadcast_to(turned[:, row : row + 1], (SPAN, channels))
            for h in range(1, heads):
                result = jnp.where(lane >= h * HEAD_DIM, turned[:, row + h : row + h + 1], result)
            return result

        inner = jnp.where(lower, nt_dot(out_map, in_map), 0.0)
        x_wide = x_act.astype(jnp.float32)
        weights, spaced = ([], [])
        for h in range(heads):
            gap = jnp.where(lower, turned[:, h : h + 1] - cum[h : h + 1], 0.0)
            weights.append((inner * jnp.exp(gap) * step[h : h + 1]).astype(jnp.bfloat16))
            inside = (lane >= h * HEAD_DIM) & (lane < (h + 1) * HEAD_DIM)
            spaced.append(jnp.where(inside, x_wide, 0.0).astype(jnp.bfloat16))
        local_part = jnp.dot(
            jnp.concatenate(weights, axis=1),
            jnp.concatenate(spaced, axis=0),
            preferred_element_type=jnp.float32,
        )
        grown = spread(2 * ROWS)
        x_weighted = (x_wide * spread(ROWS)).astype(jnp.bfloat16)
        added = lax.dot_general(
            in_map, x_weighted, (((0,), (0,)), ((), ())), preferred_element_type=jnp.float32
        )
        high = state.astype(jnp.bfloat16)
        rest = state - high.astype(jnp.float32)
        middle = rest.astype(jnp.bfloat16)
        low = (rest - middle.astype(jnp.float32)).astype(jnp.bfloat16)
        carried = jnp.dot(out_map, high, preferred_element_type=jnp.float32)
        carried = carried + jnp.dot(out_map, middle, preferred_element_type=jnp.float32)
        carried = carried + jnp.dot(out_map, low, preferred_element_type=jnp.float32)
        ssm_out = local_part + grown * carried + skip * x_wide
        state = grown[SPAN - 1 : SPAN] * state + added
        out_ref[block * SPAN : (block + 1) * SPAN] = (ssm_out * gain).astype(jnp.bfloat16)
        summed = jnp.sum(ssm_out * ssm_out, axis=1, keepdims=True)
        sums = jnp.where(across == block, summed, sums)

    whole = sums.T[:ROWS]
    top = whole.astype(jnp.bfloat16).astype(jnp.float32)
    largest = jnp.broadcast_to(jnp.max(largest_ref[...]), (ROWS, channels))
    extra = jnp.concatenate([jnp.concatenate([top, whole - top], axis=1), largest], axis=0)
    out_ref[tokens:] = extra.astype(jnp.bfloat16)
    carry_out_ref[:STATE] = state
    carry_out_ref[STATE : STATE + edge] = x_buf[tokens : tokens + edge]
    carry_out_ref[STATE + edge :] = bc_buf[tokens : tokens + edge]


def scan(place, in_scale, sums, maps, small, largest, carry, first):
    channels = sums[0].shape[1]
    tokens = maps[0].shape[0]

    def fixed(array):
        return pl.BlockSpec(array.shape, lambda i, p: (0, 0))

    held = pl.BlockSpec((channels, STATE), lambda i, p: (p[1] * LINE + p[2], 0))
    outs = [
        jax.ShapeDtypeStruct((tokens + 2 * ROWS, channels), jnp.bfloat16),
        jax.ShapeDtypeStruct((STATE + 2 * ROWS, channels), jnp.float32),
    ]
    return pl.pallas_call(
        functools.partial(scan_kernel, first),
        grid_spec=pltpu.PrefetchScalarGridSpec(
            num_scalar_prefetch=1,
            grid=(1,),
            in_specs=[SMEM]
            + [fixed(array) for array in (*sums, *maps, small, largest)]
            + [held if first else fixed(carry)],
            out_specs=[fixed(out) for out in outs],
            scratch_shapes=[
                pltpu.VMEM((tokens + ROWS, channels), jnp.float32),
                pltpu.VMEM((tokens + ROWS, 2 * STATE), jnp.float32),
            ],
        ),
        out_shape=outs,
        compiler_params=pltpu.CompilerParams(vmem_limit_bytes=40 * 2**20),
        cost_estimate=pl.CostEstimate(
            flops=8 * tokens * SPAN * channels,
            bytes_accessed=8 * tokens * channels,
            transcendentals=tokens * (channels + 8 * SPAN),
        ),
        name="scan",
    )(place, in_scale, *sums, *maps, small, largest, carry)


def by_heads(
    hidden_in,
    prev_amax,
    w_x,
    w_bc,
    w_dt,
    conv_x,
    conv_bc,
    conv_state_x,
    conv_state_bc,
    dt_bias,
    decay_rate,
    skip,
    init_state,
    norm_gain,
    w_out,
):
    margin = KERNEL - 1
    count, here = (lax.axis_size("seq"), lax.axis_index("seq"))
    ranks, rank = (lax.axis_size("tensor"), lax.axis_index("tensor"))
    z, side = (here // PAIR, here % PAIR)
    place_of = side * LINE + z
    f32, bf16 = (jnp.float32, jnp.bfloat16)
    own, width = hidden_in.shape
    depth = w_x.shape[0]
    channels = w_x.shape[1] // count
    heads_here = w_dt.shape[1] // count
    in_scale = (prev_amax / quant_range).reshape(1)
    factor = (quant_range / prev_amax).reshape(1)
    place = jnp.stack([rank, side, z] + [rank] * ranks).astype(jnp.int32)

    def pick(array, axis, index):
        return lax.dynamic_index_in_dim(array, index, axis, keepdims=False)

    def along(value, pairs):
        moves = [(a * PAIR + x, b * PAIR + x) for a, b in pairs for x in range(PAIR)]
        return lax.ppermute(value, "seq", moves)

    def across(value):
        return lax.ppermute(value, "seq", [(s, s ^ 1) for s in range(count)])

    half = w_x.shape[1] // PAIR
    x_send = lax.dynamic_slice_in_dim(w_x, (1 - side) * half, half, axis=1)
    bc_own = pick(w_bc, 1, side).reshape(depth, 2 * STATE)
    bc_send = pick(w_bc, 1, 1 - side).reshape(depth, 2 * STATE)
    x_send, bc_send, hidden_in = lax.optimization_barrier((x_send, bc_send, hidden_in))
    x_other = across(x_send)
    bc_other = across(bc_send)
    dt_rows = w_dt.T.reshape(PAIR, LINE, 1, heads_here, depth)
    dt_rows = jnp.broadcast_to(dt_rows, (PAIR, LINE, ROWS // heads_here, heads_here, depth))
    dt_rows = dt_rows.reshape(PAIR, LINE * ROWS, depth)
    dt_own = pick(dt_rows, 0, side)
    dt_other = across(pick(dt_rows, 0, 1 - side))

    cut = hidden_in.reshape(own, LINE, PAIR * depth)
    pieces = [pick(cut, 1, z ^ m) for m in range(LINE)]
    arrived = [pieces[0]]
    for r in range(1, count):
        arrived.append(lax.ppermute(pieces[r // PAIR], "seq", [(s, s ^ r) for s in range(count)]))
    rows = [jnp.stack(arrived)]
    for j in range(1, ranks):
        bit = j & -j
        rows.append(lax.ppermute(rows[j - bit], "tensor", [(t, t ^ bit) for t in range(ranks)]))

    def of_heads(array):
        return jnp.repeat(array, HEAD_DIM)[None]

    by_channel = jnp.concatenate(
        [conv_state_x.astype(f32), conv_x, of_heads(skip), norm_gain[None]], axis=0
    )
    by_channel = lax.dynamic_slice_in_dim(by_channel, place_of * channels, channels, axis=1)
    by_map = jnp.concatenate([conv_state_bc.astype(f32), conv_bc], axis=0)
    by_map = pick(by_map, 1, side).reshape(margin + KERNEL, 2 * STATE)
    by_head = jnp.stack([dt_bias, decay_rate]).reshape(2, count, heads_here)
    by_head = jnp.tile(pick(by_head, 1, place_of).T, (ROWS // heads_here, 1))
    by_head = jnp.repeat(by_head, SPAN, axis=1)
    blank = jnp.zeros((ROWS - margin, channels), f32)
    small = jnp.concatenate(
        [
            blank,
            by_channel[:margin],
            blank,
            by_map[:margin],
            by_channel[margin : margin + KERNEL],
            by_map[margin:],
            by_channel[margin + KERNEL :],
            jnp.zeros((2 * ROWS - 2 * KERNEL - 2, channels), f32),
            by_head,
        ],
        axis=0,
    )

    start, end = (0, LINE - 1)
    at_end = (z == start) | (z == end)
    next_start, next_end = (1, LINE - 2)
    weights = (w_x, x_other, bc_own, bc_other, dt_own, dt_other)
    carry = init_state.reshape(-1, STATE)
    totals, tops = ([], [])
    for part in range(PARTS):
        mine, near, over, far, maps, largest = project(place, factor, rows, weights, part)
        map_hop = along(maps, [(start, next_start), (end, next_end)])
        hop_far = along(far, [(start, next_start), (end, next_end)])
        hop_over = along(over, [(start, next_start), (end, next_end)])
        got_near = along(near, [(s, s ^ 1) for s in range(LINE)])
        map_sum = (maps.astype(f32) + map_hop.astype(f32)).astype(bf16)
        map_far = along(map_sum, [(next_start, next_end), (next_end, next_start)])
        map_done = ((map_sum.astype(f32) + map_far.astype(f32)) * in_scale).astype(bf16)
        map_done, got_near = lax.optimization_barrier((map_done, got_near))
        map_done = along(map_done, [(next_start, start), (next_end, end)])
        sent_end = onward(over, hop_far)
        hop_over, sent_end = lax.optimization_barrier((hop_over, sent_end))
        got_end = along(sent_end, [(next_start, end), (next_end, start)])
        got_next = along(onward(far, hop_over), [(next_start, next_end), (next_end, next_start)])
        gained, carry = scan(
            place,
            in_scale,
            [mine, got_near, got_end, got_next],
            [map_sum, map_far, map_done],
            small,
            largest,
            carry,
            part == 0,
        )
        tokens = gained.shape[0] - 2 * ROWS
        beside = along(gained, [(s, s ^ 1) for s in range(LINE)])
        middle = [(next_start, next_end), (next_end, next_start)]
        outward = [(next_start, start), (next_end, end)]
        facing = along(gained, middle)
        beyond = along(beside, middle)
        second = jnp.where(at_end, along(facing, outward), facing)
        third = jnp.where(at_end, along(beyond, outward), beyond)
        two, three = (jnp.where(at_end, 2, 3), jnp.where(at_end, 3, 2))
        far_own = across(gained)
        far_beside = across(beside)
        second, far_own = lax.optimization_barrier((second, far_own))
        far_second = across(second)
        third, far_beside = lax.optimization_barrier((third, far_beside))
        far_third = across(third)
        got = (
            (0, (gained, far_own)),
            (1, (beside, far_beside)),
            (two, (second, far_second)),
            (three, (third, far_third)),
        )
        total = squares = top = None
        for m, pair in got:
            for x, piece in enumerate(pair):
                at = ((side ^ x) * LINE + (z ^ m)) * channels
                w_rows = lax.dynamic_slice_in_dim(w_out, at, channels, axis=0)
                product = jnp.dot(piece, w_rows, preferred_element_type=f32)
                tail = piece[tokens:].astype(f32)
                low, high = (tail[:ROWS, :SPAN] + tail[:ROWS, SPAN:], tail[ROWS:, :SPAN])
                if total is None:
                    total, squares, top = (product, low, high)
                else:
                    total = total + product
                    squares = squares + low
                    top = jnp.maximum(top, high)
        tops.append(top)
        wide = w_out.shape[1]
        blocks = tokens // SPAN
        kept = total[:tokens].reshape(blocks, ranks, own, wide)
        for bit in (1 << b for b in range(ranks.bit_length() - 1)):
            pairs = [(t, t ^ bit) for t in range(ranks)]
            squares = squares + lax.ppermute(squares, "tensor", pairs)
            keeps = (rank // bit) % 2
            halves = kept.reshape(blocks, -1, 2, own, wide)
            received = lax.ppermute(pick(halves, 2, 1 - keeps).astype(bf16), "tensor", pairs)
            kept = pick(halves, 2, keeps) + received.astype(f32)
        kept = kept.reshape(blocks, own, wide)
        mean_sq = squares[:blocks].reshape(blocks, ranks, own) / (HEADS * HEAD_DIM)
        factors = lax.rsqrt(pick(mean_sq, 1, rank) + epsilon)
        totals.append((kept * factors[:, :, None]).astype(bf16))
    final = jnp.concatenate(totals, axis=0)
    final = lax.all_to_all(final, "seq", split_axis=0, concat_axis=0, tiled=True)
    layer_out = final.transpose(1, 0, 2).reshape(own, count * final.shape[2])
    abs_max = jnp.max(functools.reduce(jnp.maximum, tops))
    return (layer_out, abs_max)


def solution(mesh):
    return jax.shard_map(
        by_heads if splits(mesh) else by_tokens,
        mesh=mesh,
        in_specs=(
            P(("seq", "tensor"), None),
            P(),
            P("seq", "tensor"),
            P("seq", "tensor", None, None),
            P("seq", "tensor"),
            P(None, "tensor"),
            P(None, "tensor", None, None),
            P(None, "tensor"),
            P(None, "tensor", None, None),
            P("tensor"),
            P("tensor"),
            P("tensor"),
            P("tensor", None, None),
            P("tensor"),
            P("tensor", "seq"),
        ),
        out_specs=(P(("seq", "tensor"), None), P()),
        check_vma=False,
    )
```

```python
import functools

import jax
import jax.numpy as jnp
from jax import lax
from jax.experimental import pallas as pl
from jax.experimental.pallas import tpu as pltpu
from jax.sharding import PartitionSpec as P

HEADS = 128
HEAD_DIM = 64
STATE = 128
GROUPS = 8
KERNEL = 4
SPAN = 128


epsilon = 1e-05
quant_range = 448.0


def from_behind(value, axis, steps):
    count = lax.axis_size(axis)
    first, last = (max(0, -steps), min(count, count - steps))
    return lax.ppermute(value, axis, [(source, source + steps) for source in range(first, last)])


def carried_in(shard, axis, combine, identity):
    count, here = (lax.axis_size(axis), lax.axis_index(axis))
    everything = jax.tree.map(
        lambda part, kind: lax.all_gather(part.astype(kind), axis),
        shard,
        (jnp.bfloat16, jnp.bfloat16),
    )
    start = jax.tree.map(
        lambda part, zero: jnp.broadcast_to(jnp.asarray(zero, part.dtype), part.shape),
        shard,
        identity,
    )

    def turn(k, before):
        reached = k < here
        new = combine(
            before, jax.tree.map(lambda part, own: part[k].astype(own.dtype), everything, shard)
        )
        return jax.tree.map(lambda a, b: jnp.where(reached, a, b), new, before)

    return lax.fori_loop(0, count, turn, start)


def depthwise(before, projected, conv_taps, length):
    extended = jnp.concatenate([before, projected], axis=0)
    summed = conv_taps[0] * extended[0:length]
    for offset in range(1, KERNEL):
        summed = summed + conv_taps[offset] * extended[offset : offset + length]
    return jax.nn.silu(summed).astype(jnp.bfloat16)


def combine(earlier, later):
    return (earlier[0] * later[0], later[0][:, None, None] * earlier[1] + later[1])


def by_tokens(
    hidden_in,
    prev_amax,
    w_x,
    w_bc,
    w_dt,
    conv_x,
    conv_bc,
    conv_state_x,
    conv_state_bc,
    dt_bias,
    decay_rate,
    skip,
    init_state,
    norm_gain,
    w_out,
):
    margin = KERNEL - 1
    gathered = lax.all_gather(hidden_in, "tensor", axis=0, tiled=True)
    abs_max = lax.pmax(jnp.max(jnp.abs(gathered.astype(jnp.float32))), "seq")
    in_scale = prev_amax / quant_range
    leading = lax.axis_index("seq") == 0
    row_count = gathered.shape[0]
    bc_width = w_bc.shape[1] * w_bc.shape[2] * w_bc.shape[3]
    bc_rows = jnp.reshape(w_bc, (w_bc.shape[0], bc_width))
    scaled = gathered.astype(jnp.float32) * (quant_range / prev_amax)
    quant = jnp.clip(scaled, -quant_range, quant_range).astype(jnp.bfloat16)
    pieces = (
        lax.all_gather(w_x, "seq", axis=0, tiled=True),
        lax.all_gather(bc_rows, "seq", axis=0, tiled=True),
        lax.all_gather(w_dt, "seq", axis=0, tiled=True),
    )
    x_proj, bc_proj, dt_proj = tuple(
        (
            jnp.dot(quant, weight_piece, preferred_element_type=jnp.float32)
            for weight_piece in pieces
        )
    )
    x_whole = (x_proj * in_scale).astype(jnp.bfloat16)
    bc_whole = (bc_proj * in_scale).astype(jnp.bfloat16)
    dt_raw = dt_proj * in_scale
    state_bc = jnp.reshape(conv_state_bc, (margin, bc_width))
    received = from_behind(
        (x_whole[row_count - margin :], bc_whole[row_count - margin :]), "seq", 1
    )
    x_edge = jnp.where(leading, conv_state_x, received[0])
    bc_edge = jnp.where(leading, state_bc, received[1])
    x_act = depthwise(x_edge, x_whole, conv_x, row_count)
    bc_act = depthwise(bc_edge, bc_whole, jnp.reshape(conv_bc, (KERNEL, bc_width)), row_count)
    step_size = jax.nn.softplus(dt_raw + dt_bias)
    heads_here = step_size.shape[1]
    groups_here = w_bc.shape[1]
    per_group = HEADS // GROUPS
    blocks = row_count // SPAN
    x_blocks = x_act.reshape(blocks, SPAN, heads_here, HEAD_DIM)
    bc_blocks = bc_act.reshape(blocks, SPAN, groups_here, 2, STATE)
    in_map = bc_blocks[:, :, :, 0]
    out_map = bc_blocks[:, :, :, 1]
    step_blocks = step_size.reshape(blocks, SPAN, heads_here)
    cum_blocks = jnp.cumsum(-step_blocks * decay_rate, axis=1)
    index_row = jnp.arange(SPAN, dtype=jnp.int32)
    lower_mask = index_row[:, None] >= index_row[None, :]
    intersection = jnp.einsum(
        "ctgn,cugn->cgtu", out_map, in_map, preferred_element_type=jnp.float32
    )
    intersection = jnp.repeat(intersection, per_group, axis=1)
    cum_heads = jnp.transpose(cum_blocks, (0, 2, 1))
    log_gap = cum_heads[:, :, :, None] - cum_heads[:, :, None, :]
    decay = jnp.exp(jnp.where(lower_mask[None, None], log_gap, -1e30))
    step_heads = jnp.transpose(step_blocks, (0, 2, 1))
    weights = (intersection * decay * step_heads[:, :, None, :]).astype(jnp.bfloat16)
    local_part = jnp.einsum(
        "chtu,cuhp->cthp", weights, x_blocks, preferred_element_type=jnp.float32
    )
    last_cum = cum_blocks[:, SPAN - 1, :]
    x_weighted = (
        x_blocks.astype(jnp.float32)
        * (step_blocks * jnp.exp(last_cum[:, None, :] - cum_blocks))[:, :, :, None]
    ).astype(jnp.bfloat16)
    in_heads = jnp.repeat(in_map, per_group, axis=2)
    added = jnp.einsum("cuhp,cuhn->chpn", x_weighted, in_heads, preferred_element_type=jnp.float32)

    def carry_on(carried, element):
        block_decay, block_added = element
        return (block_decay[:, None, None] * carried + block_added, carried)

    empty_state = jnp.zeros((heads_here, HEAD_DIM, STATE), jnp.float32)
    device_state, entering = lax.scan(carry_on, empty_state, (jnp.exp(last_cum), added))
    device_decay = jnp.exp(jnp.sum(last_cum, axis=0))
    seeded = device_state + jnp.where(leading, device_decay[:, None, None] * init_state, 0.0)
    identity = (jnp.ones_like(device_decay), jnp.zeros_like(device_state))
    scanned = carried_in((device_decay, seeded), "seq", combine, identity)
    incoming = jnp.where(leading, init_state, scanned[1])
    prefix = jnp.exp(jnp.cumsum(last_cum, axis=0) - last_cum)
    states_in = entering + prefix[:, :, None, None] * incoming[None]
    out_heads = jnp.repeat(out_map, per_group, axis=2).astype(jnp.float32)
    carried_part = (
        jnp.einsum("cthn,chpn->cthp", out_heads, states_in, precision=lax.Precision.HIGHEST)
        * jnp.exp(cum_blocks)[:, :, :, None]
    )
    ssm_out = local_part + carried_part + skip[None, None, :, None] * x_blocks.astype(jnp.float32)
    ssm_out = ssm_out.reshape(row_count, heads_here * HEAD_DIM)
    squares = lax.psum(jnp.sum(ssm_out * ssm_out, axis=1), "tensor")
    mean_sq = squares / (HEADS * HEAD_DIM)
    normed = (ssm_out * lax.rsqrt(mean_sq + epsilon)[:, None] * norm_gain).astype(jnp.bfloat16)
    partial_out = jnp.dot(
        normed, lax.all_gather(w_out, "seq", axis=1, tiled=True), preferred_element_type=jnp.float32
    )
    layer_out = lax.psum_scatter(
        partial_out.astype(jnp.bfloat16), "tensor", scatter_dimension=0, tiled=True
    )
    return (layer_out, abs_max)


PAIR = 2
LINE = 4
ROWS = 8
SMEM = pl.BlockSpec(memory_space=pltpu.SMEM)
HIGHEST = lax.Precision.HIGHEST


def splits(mesh):
    count, ranks = (mesh.shape["seq"], mesh.shape["tensor"])
    heads_all, groups_here = (HEADS // ranks, GROUPS // ranks)
    if count != PAIR * LINE or groups_here != PAIR or ranks & (ranks - 1):
        return False
    heads_here = heads_all // count
    return 2 * heads_here == ROWS and heads_here * HEAD_DIM == 2 * SPAN


def nt_dot(a, b, **kw):
    return lax.dot_general(
        a, b, (((1,), (1,)), ((), ())), preferred_element_type=jnp.float32, **kw
    )


def project_kernel(steps_to, with_maps, place_ref, factor_ref, *refs):
    owners = len(steps_to)
    outs = owners + (2 if with_maps else 0) + 2
    taken = 6 if with_maps else 4
    ranks = len(refs) - taken - outs
    hidden = refs[:ranks]
    own_x, other_x, own_dt, other_dt = refs[ranks : ranks + 4]
    x_refs = refs[ranks + taken : ranks + taken + owners]
    quant_ref, dt_buf = refs[-2:]
    side, z = (place_ref[1], place_ref[2])
    step = pl.program_id(0)
    factor = factor_ref[0]
    depth = own_x.shape[0]
    each = hidden[0].shape[0]
    largest = None
    for j in range(ranks):
        for k in range(each):
            for half in range(PAIR):
                values = hidden[j][k, :, half * depth : (half + 1) * depth].astype(jnp.float32)
                scaled = jnp.clip(values * factor, -quant_range, quant_range)
                quant_ref[half, k ^ ((z * PAIR + side) % each), j] = scaled.astype(jnp.bfloat16)
                if with_maps:
                    top = jnp.max(jnp.abs(values).reshape(-1, ROWS, depth), axis=0)
                    largest = top if largest is None else jnp.maximum(largest, top)

    rows = quant_ref.shape[1] * quant_ref.shape[2] * quant_ref.shape[3]
    near = quant_ref[side].reshape(rows, depth)
    far = quant_ref[1 - side].reshape(rows, depth)

    def both(own, other):
        return jnp.dot(near, own, preferred_element_type=jnp.float32) + jnp.dot(
            far, other, preferred_element_type=jnp.float32
        )

    at_rows = pl.ds(pl.multiple_of(step * rows, rows), rows)
    if with_maps:
        own_bc, other_bc = refs[ranks + 4 : ranks + 6]
        bc_ref, largest_ref = refs[ranks + taken + owners : ranks + taken + owners + 2]
        bc_ref[at_rows] = both(own_bc[...], other_bc[...]).astype(jnp.bfloat16)
        width = largest_ref.shape[1]
        top = largest[:, :width]
        for at in range(width, depth, width):
            top = jnp.maximum(top, largest[:, at : at + width])

        @pl.when(step == 0)
        def _():
            largest_ref[...] = top

        @pl.when(step > 0)
        def _():
            largest_ref[...] = jnp.maximum(largest_ref[...], top)

    dt_buf[...] = (nt_dot(own_dt[...], near) + nt_dot(other_dt[...], far)).reshape(dt_buf.shape)
    channels = x_refs[0].shape[1]
    tokens = pl.num_programs(0) * rows
    extra = rows // channels * ROWS
    upper = lax.broadcasted_iota(jnp.int32, (ROWS, channels), 0) < ROWS // 2
    for m, x_ref in zip(steps_to, x_refs):
        owner = z ^ m
        cut = pl.ds(pl.multiple_of(owner % (LINE // 2) * channels, channels), channels)
        x_ref[at_rows] = both(own_x[:, cut], other_x[:, cut]).astype(jnp.bfloat16)
        dt = dt_buf[owner]
        pieces = [
            split_parts(dt[:, at : at + channels], upper) for at in range(0, rows, channels)
        ]
        x_ref[pl.ds(pl.multiple_of(tokens + step * extra, 16), extra)] = jnp.concatenate(
            pieces, axis=0
        ).astype(jnp.bfloat16)


def split_parts(values, upper):
    top = values.astype(jnp.bfloat16).astype(jnp.float32)
    return jnp.where(upper, top, values - top)


def project(place, factor, hidden, weights, steps_to):
    count, own, wide = hidden[0].shape
    ranks = len(hidden)
    with_maps = len(weights) > 4
    far_half = steps_to[0] // (LINE // 2)
    depth, x_wide = weights[1].shape
    channels = x_wide // (LINE // 2)
    steps = 2
    each = count // steps
    tokens = count * ranks * own
    extra = tokens // channels * ROWS

    def fixed(array):
        return pl.BlockSpec(array.shape, lambda i, p: (0,) * array.ndim)

    def own_columns(i, p):
        return (0, p[1] * 2 + ((p[2] // (LINE // 2)) ^ far_half))

    outs = [jax.ShapeDtypeStruct((tokens + extra, channels), jnp.bfloat16)] * len(steps_to)
    if with_maps:
        outs.append(jax.ShapeDtypeStruct((tokens, weights[4].shape[1]), jnp.bfloat16))
        outs.append(jax.ShapeDtypeStruct((ROWS, 128), jnp.float32))
    return pl.pallas_call(
        functools.partial(project_kernel, steps_to, with_maps),
        grid_spec=pltpu.PrefetchScalarGridSpec(
            num_scalar_prefetch=1,
            grid=(steps,),
            in_specs=[SMEM]
            + [pl.BlockSpec((each, own, wide), lambda i, p: (i ^ ((p[2] * PAIR + p[1]) // each), 0, 0))]
            * ranks
            + [pl.BlockSpec((depth, x_wide), own_columns)]
            + [fixed(w) for w in weights[1:]],
            out_specs=[fixed(out) for out in outs],
            scratch_shapes=[
                pltpu.VMEM((PAIR, each, ranks, own, depth), jnp.bfloat16),
                pltpu.VMEM((LINE, ROWS, each * ranks * own), jnp.float32),
            ],
        ),
        out_shape=outs,
        compiler_params=pltpu.CompilerParams(vmem_limit_bytes=40 * 2**20),
        cost_estimate=pl.CostEstimate(
            flops=2 * tokens * wide * (x_wide + 256 * with_maps),
            bytes_accessed=2 * tokens * (wide + x_wide),
            transcendentals=0,
        ),
        name="project",
    )(place, factor, *hidden, *weights)


def onward_kernel(own_ref, received_ref, out_ref):
    rows, channels = own_ref.shape
    tokens = rows * channels // (channels + ROWS)
    total = own_ref[:tokens].astype(jnp.float32) + received_ref[:tokens].astype(jnp.float32)
    out_ref[:tokens] = total.astype(jnp.bfloat16)
    upper = lax.broadcasted_iota(jnp.int32, (ROWS, channels), 0) < ROWS // 2
    extra = own_ref[tokens:].astype(jnp.float32) + received_ref[tokens:].astype(jnp.float32)
    pieces = []
    for at in range(0, rows - tokens, ROWS):
        piece = extra[at : at + ROWS]
        pieces.append(split_parts(piece + pltpu.roll(piece, ROWS // 2, 0), upper))
    out_ref[tokens:] = jnp.concatenate(pieces, axis=0).astype(jnp.bfloat16)


def onward(own, received):
    whole = pl.BlockSpec(own.shape, lambda: (0, 0))
    return pl.pallas_call(
        onward_kernel,
        in_specs=[whole, whole],
        out_specs=whole,
        out_shape=jax.ShapeDtypeStruct(own.shape, own.dtype),
        compiler_params=pltpu.CompilerParams(vmem_limit_bytes=20 * 2**20),
        cost_estimate=pl.CostEstimate(
            flops=own.size, bytes_accessed=6 * own.size, transcendentals=0
        ),
        name="onward",
    )(own, received)


def scan_kernel(first, place_ref, scale_ref, *refs):
    x_refs, bc_refs = (refs[:4], refs[4:7])
    small_ref, largest_ref, carry_ref, out_ref, carry_out_ref, x_buf, bc_buf = refs[7:]
    tokens, channels = bc_refs[0].shape
    blocks = tokens // SPAN
    heads = channels // HEAD_DIM
    rank, z = (place_ref[0], place_ref[2])
    ranks = place_ref.shape[0] - 3
    own = SPAN // ranks
    edge = ROWS
    in_scale = scale_ref[0]
    at_end = (z == 0) | (z == LINE - 1)
    if first:
        x_buf[:edge] = small_ref[:edge]
        bc_buf[:edge] = small_ref[edge : 2 * edge]
        state = carry_ref[...].T
    else:
        x_buf[:edge] = carry_ref[STATE : STATE + edge]
        bc_buf[:edge] = carry_ref[STATE + edge :]
        state = carry_ref[:STATE]

    for block in range(blocks):
        for true_rank in range(ranks):
            source = block * SPAN + (true_rank ^ rank) * own
            source = pl.ds(pl.multiple_of(source, own), own)
            at = edge + block * SPAN + true_rank * own
            at = slice(at, at + own)
            total = sum(ref[source].astype(jnp.float32) for ref in x_refs) * in_scale
            x_buf[at] = total.astype(jnp.bfloat16).astype(jnp.float32)
            near, far, done = (ref[source].astype(jnp.float32) for ref in bc_refs)
            total = ((near + far) * in_scale).astype(jnp.bfloat16).astype(jnp.float32)
            bc_buf[at] = jnp.where(at_end, done, total)

    taps = 2 * edge

    def activate(buf, row, block):
        start = edge - (KERNEL - 1) + block * SPAN
        summed = small_ref[row : row + 1] * buf[start : start + SPAN]
        for k in range(1, KERNEL):
            summed = summed + small_ref[row + k : row + k + 1] * buf[start + k : start + k + SPAN]
        return (summed / (1.0 + jnp.exp(-summed))).astype(jnp.bfloat16)

    skip = small_ref[taps + 2 * KERNEL : taps + 2 * KERNEL + 1]
    gain = small_ref[taps + 2 * KERNEL + 1 : taps + 2 * KERNEL + 2]
    bias = small_ref[4 * edge :, :SPAN]
    rate = small_ref[4 * edge :, SPAN:]

    up = lax.broadcasted_iota(jnp.int32, (SPAN, SPAN), 0)
    across = lax.broadcasted_iota(jnp.int32, (SPAN, SPAN), 1)
    lane = lax.broadcasted_iota(jnp.int32, (SPAN, channels), 1)
    lower = up >= across
    upper = (up <= across).astype(jnp.float32)
    lanes = across[:ROWS]

    dt = sum(ref[tokens:].astype(jnp.float32) for ref in x_refs)
    steps = []
    wide = channels // SPAN
    for block in range(blocks):
        tile = dt[block // wide * ROWS : (block // wide + 1) * ROWS]
        cut = tile[:, block % wide * SPAN : (block % wide + 1) * SPAN]
        cut = (cut + pltpu.roll(cut, ROWS // 2, 0)) * in_scale
        bit = 1
        while bit < ranks:
            shift = bit * own
            flipped = jnp.where(
                (lanes // shift) % 2 == 1,
                pltpu.roll(cut, shift, 1),
                pltpu.roll(cut, SPAN - shift, 1),
            )
            cut = jnp.where((rank & bit) != 0, flipped, cut)
            bit *= 2
        raw = cut + bias
        steps.append(jnp.maximum(raw, 0.0) + jnp.log1p(jnp.exp(-jnp.abs(raw))))
    drops = jnp.concatenate([-step * rate for step in steps], axis=0)
    cums = jnp.dot(drops, upper, precision=HIGHEST, preferred_element_type=jnp.float32)

    sums = jnp.zeros((SPAN, SPAN), jnp.float32)
    for block in range(blocks):
        x_act = activate(x_buf, taps, block)
        bc_act = activate(bc_buf, taps + KERNEL, block)
        in_map, out_map = (bc_act[:, :STATE], bc_act[:, STATE:])
        step, cum = (steps[block], cums[block * ROWS : (block + 1) * ROWS])
        last = cum[:, SPAN - 1 : SPAN]
        turned = jnp.concatenate(
            [
                cum,
                step * jnp.exp(last - cum),
                jnp.exp(cum),
                jnp.zeros((SPAN - 3 * ROWS, SPAN), jnp.float32),
            ],
            axis=0,
        ).T

        def spread(row):
            result = jnp.broadcast_to(turned[:, row : row + 1], (SPAN, channels))
            for h in range(1, heads):
                result = jnp.where(lane >= h * HEAD_DIM, turned[:, row + h : row + h + 1], result)
            return result

        inner = jnp.where(lower, nt_dot(out_map, in_map), 0.0)
        x_wide = x_act.astype(jnp.float32)
        weights, spaced = ([], [])
        for h in range(heads):
            gap = jnp.where(lower, turned[:, h : h + 1] - cum[h : h + 1], 0.0)
            weights.append((inner * jnp.exp(gap) * step[h : h + 1]).astype(jnp.bfloat16))
            inside = (lane >= h * HEAD_DIM) & (lane < (h + 1) * HEAD_DIM)
            spaced.append(jnp.where(inside, x_wide, 0.0).astype(jnp.bfloat16))
        local_part = jnp.dot(
            jnp.concatenate(weights, axis=1),
            jnp.concatenate(spaced, axis=0),
            preferred_element_type=jnp.float32,
        )
        grown = spread(2 * ROWS)
        x_weighted = (x_wide * spread(ROWS)).astype(jnp.bfloat16)
        added = lax.dot_general(
            in_map, x_weighted, (((0,), (0,)), ((), ())), preferred_element_type=jnp.float32
        )
        high = state.astype(jnp.bfloat16)
        rest = state - high.astype(jnp.float32)
        middle = rest.astype(jnp.bfloat16)
        low = (rest - middle.astype(jnp.float32)).astype(jnp.bfloat16)
        carried = jnp.dot(out_map, high, preferred_element_type=jnp.float32)
        carried = carried + jnp.dot(out_map, middle, preferred_element_type=jnp.float32)
        carried = carried + jnp.dot(out_map, low, preferred_element_type=jnp.float32)
        ssm_out = local_part + grown * carried + skip * x_wide
        state = grown[SPAN - 1 : SPAN] * state + added
        out_ref[block * SPAN : (block + 1) * SPAN] = (ssm_out * gain).astype(jnp.bfloat16)
        summed = jnp.sum(ssm_out * ssm_out, axis=1, keepdims=True)
        sums = jnp.where(across == block, summed, sums)

    whole = sums.T[:ROWS]
    top = whole.astype(jnp.bfloat16).astype(jnp.float32)
    largest = jnp.broadcast_to(jnp.max(largest_ref[...]), (ROWS, channels))
    extra = jnp.concatenate([jnp.concatenate([top, whole - top], axis=1), largest], axis=0)
    out_ref[tokens:] = extra.astype(jnp.bfloat16)
    carry_out_ref[:STATE] = state
    carry_out_ref[STATE : STATE + edge] = x_buf[tokens : tokens + edge]
    carry_out_ref[STATE + edge :] = bc_buf[tokens : tokens + edge]


def scan(place, in_scale, sums, maps, small, largest, carry, first):
    channels = sums[0].shape[1]
    tokens = maps[0].shape[0]

    def fixed(array):
        return pl.BlockSpec(array.shape, lambda i, p: (0, 0))

    held = pl.BlockSpec((channels, STATE), lambda i, p: (p[1] * LINE + p[2], 0))
    outs = [
        jax.ShapeDtypeStruct((tokens + 2 * ROWS, channels), jnp.bfloat16),
        jax.ShapeDtypeStruct((STATE + 2 * ROWS, channels), jnp.float32),
    ]
    return pl.pallas_call(
        functools.partial(scan_kernel, first),
        grid_spec=pltpu.PrefetchScalarGridSpec(
            num_scalar_prefetch=1,
            grid=(1,),
            in_specs=[SMEM]
            + [fixed(array) for array in (*sums, *maps, small, largest)]
            + [held if first else fixed(carry)],
            out_specs=[fixed(out) for out in outs],
            scratch_shapes=[
                pltpu.VMEM((tokens + ROWS, channels), jnp.float32),
                pltpu.VMEM((tokens + ROWS, 2 * STATE), jnp.float32),
            ],
        ),
        out_shape=outs,
        compiler_params=pltpu.CompilerParams(vmem_limit_bytes=40 * 2**20),
        cost_estimate=pl.CostEstimate(
            flops=8 * tokens * SPAN * channels,
            bytes_accessed=8 * tokens * channels,
            transcendentals=tokens * (channels + 8 * SPAN),
        ),
        name="scan",
    )(place, in_scale, *sums, *maps, small, largest, carry)


def square_parts(squares, wide):
    top = squares.astype(jnp.bfloat16).astype(jnp.float32)
    blank = jnp.zeros((ROWS, wide - 2 * SPAN), jnp.float32)
    rows = jnp.concatenate([top, squares - top, blank], axis=1)
    return jnp.concatenate([rows, jnp.zeros_like(rows)], axis=0).astype(jnp.bfloat16)


def square_sum(tail):
    tail = tail.astype(jnp.float32)[:ROWS]
    return tail[:, :SPAN] + tail[:, SPAN : 2 * SPAN]


def share(sums_at, mine, send_ref, keep_ref, groups, own):
    for g in range(groups):
        out = slice(g * own, (g + 1) * own)
        keep_ref[out] = sums_at((2 * g + mine) * own)
        send_ref[out] = sums_at((2 * g + 1 - mine) * own).astype(jnp.bfloat16)


def meet_kernel(place_ref, total_ref, last_ref, w_ref, *refs):
    send_ref, keep_ref, squares_ref, top_ref, sums = refs[-5:]
    tails = refs[:-5]
    tokens = sums.shape[0]
    own = SPAN // (place_ref.shape[0] - 3)
    sums[...] = total_ref[:tokens] + jnp.dot(
        last_ref[:tokens], w_ref[...], preferred_element_type=jnp.float32
    )
    rows = [tail[...] for tail in tails] + [last_ref[tokens:]]
    squares = sum(square_sum(row) for row in rows)
    tops = [row.astype(jnp.float32)[ROWS:, :SPAN] for row in rows]
    top_ref[...] = functools.reduce(jnp.maximum, tops)
    squares_ref[...] = squares
    share(
        lambda at: sums[pl.ds(pl.multiple_of(at, own), own)],
        place_ref[0] & 1,
        send_ref,
        keep_ref,
        tokens // (2 * own),
        own,
    )
    send_ref[tokens // 2 :] = square_parts(squares, sums.shape[1])


def meet(place, total, last, w_out, tails):
    wide = total.shape[1]
    tokens, channels = (last.shape[0] - 2 * ROWS, last.shape[1])

    def fixed(array):
        return pl.BlockSpec(array.shape, lambda i, p: (0, 0))

    def rows_of(i, p):
        z, side = (p[2], p[1])
        at_end = (z == 0) | (z == LINE - 1)
        return ((side ^ 1) * LINE + (z ^ jnp.where(at_end, 3, 2)), 0)

    outs = [
        jax.ShapeDtypeStruct((tokens // 2 + 2 * ROWS, wide), jnp.bfloat16),
        jax.ShapeDtypeStruct((tokens // 2, wide), jnp.float32),
        jax.ShapeDtypeStruct((ROWS, SPAN), jnp.float32),
        jax.ShapeDtypeStruct((ROWS, SPAN), jnp.float32),
    ]
    return pl.pallas_call(
        meet_kernel,
        grid_spec=pltpu.PrefetchScalarGridSpec(
            num_scalar_prefetch=1,
            grid=(1,),
            in_specs=[fixed(total), fixed(last), pl.BlockSpec((channels, wide), rows_of)]
            + [
                pl.BlockSpec((2 * ROWS, channels), lambda i, p: (tokens // (2 * ROWS), 0))
                for tail in tails
            ],
            out_specs=[fixed(out) for out in outs],
            scratch_shapes=[pltpu.VMEM((tokens, wide), jnp.float32)],
        ),
        out_shape=outs,
        compiler_params=pltpu.CompilerParams(vmem_limit_bytes=40 * 2**20),
        cost_estimate=pl.CostEstimate(
            flops=2 * tokens * wide * channels, bytes_accessed=8 * tokens * wide, transcendentals=0
        ),
        name="meet",
    )(place, total, last, w_out, *tails)


def halve_kernel(bit, place_ref, keep_ref, got_ref, squares_ref, send_ref, kept_ref, sum_ref):
    rows, wide = keep_ref.shape
    own = SPAN // (place_ref.shape[0] - 3)
    squares = squares_ref[...] + square_sum(got_ref[rows:])
    sum_ref[...] = squares

    def sums_at(at):
        at = pl.ds(pl.multiple_of(at, own), own)
        return keep_ref[at] + got_ref[at].astype(jnp.float32)

    mine = (place_ref[0] // bit) % 2
    share(sums_at, mine, send_ref, kept_ref, rows // (2 * own), own)
    send_ref[rows // 2 :] = square_parts(squares, wide)


def halve(bit, place, keep, got, squares):
    rows, wide = keep.shape

    def fixed(array):
        return pl.BlockSpec(array.shape, lambda i, p: (0, 0))

    outs = [
        jax.ShapeDtypeStruct((rows // 2 + 2 * ROWS, wide), jnp.bfloat16),
        jax.ShapeDtypeStruct((rows // 2, wide), jnp.float32),
        jax.ShapeDtypeStruct((ROWS, SPAN), jnp.float32),
    ]
    return pl.pallas_call(
        functools.partial(halve_kernel, bit),
        grid_spec=pltpu.PrefetchScalarGridSpec(
            num_scalar_prefetch=1,
            grid=(1,),
            in_specs=[fixed(keep), fixed(got), fixed(squares)],
            out_specs=[fixed(out) for out in outs],
        ),
        out_shape=outs,
        cost_estimate=pl.CostEstimate(
            flops=rows * wide, bytes_accessed=10 * rows * wide, transcendentals=0
        ),
        name="halve",
    )(place, keep, got, squares)


def finish_kernel(place_ref, keep_ref, got_ref, squares_ref, out_ref, turned):
    rows, wide = keep_ref.shape
    own = SPAN // (place_ref.shape[0] - 3)
    squares = squares_ref[...] + square_sum(got_ref[rows:])
    scale = lax.rsqrt(squares / (HEADS * HEAD_DIM) + epsilon)
    padded = jnp.concatenate([scale, jnp.zeros((SPAN - ROWS, SPAN), jnp.float32)], axis=0)
    turned[...] = padded.T
    mine = turned[pl.ds(pl.multiple_of(place_ref[0] * own, own), own)]
    for block in range(rows // own):
        at = slice(block * own, (block + 1) * own)
        total = keep_ref[at] + got_ref[at].astype(jnp.float32)
        out_ref[at] = (total * mine[:, block : block + 1]).astype(jnp.bfloat16)


def finish(place, keep, got, squares):
    rows, wide = keep.shape

    def fixed(array):
        return pl.BlockSpec(array.shape, lambda i, p: (0, 0))

    out = jax.ShapeDtypeStruct((rows, wide), jnp.bfloat16)
    return pl.pallas_call(
        finish_kernel,
        grid_spec=pltpu.PrefetchScalarGridSpec(
            num_scalar_prefetch=1,
            grid=(1,),
            in_specs=[fixed(keep), fixed(got), fixed(squares)],
            out_specs=fixed(out),
            scratch_shapes=[pltpu.VMEM((SPAN, SPAN), jnp.float32)],
        ),
        out_shape=out,
        cost_estimate=pl.CostEstimate(
            flops=2 * rows * wide, bytes_accessed=8 * rows * wide, transcendentals=0
        ),
        name="finish",
    )(place, keep, got, squares)


def by_heads(
    hidden_in,
    prev_amax,
    w_x,
    w_bc,
    w_dt,
    conv_x,
    conv_bc,
    conv_state_x,
    conv_state_bc,
    dt_bias,
    decay_rate,
    skip,
    init_state,
    norm_gain,
    w_out,
):
    margin = KERNEL - 1
    count, here = (lax.axis_size("seq"), lax.axis_index("seq"))
    ranks, rank = (lax.axis_size("tensor"), lax.axis_index("tensor"))
    z, side = (here // PAIR, here % PAIR)
    place_of = side * LINE + z
    f32, bf16 = (jnp.float32, jnp.bfloat16)
    own, width = hidden_in.shape
    depth = w_x.shape[0]
    channels = w_x.shape[1] // count
    heads_here = w_dt.shape[1] // count
    in_scale = (prev_amax / quant_range).reshape(1)
    factor = (quant_range / prev_amax).reshape(1)
    place = jnp.stack([rank, side, z] + [rank] * ranks).astype(jnp.int32)

    def pick(array, axis, index):
        return lax.dynamic_index_in_dim(array, index, axis, keepdims=False)

    def along(value, pairs):
        moves = [(a * PAIR + x, b * PAIR + x) for a, b in pairs for x in range(PAIR)]
        return lax.ppermute(value, "seq", moves)

    def across(value):
        return lax.ppermute(value, "seq", [(s, s ^ 1) for s in range(count)])

    quarter = w_x.shape[1] // (2 * PAIR)
    pair_of = z // (LINE // 2)

    def columns(half):
        at = (1 - side) * 2 + (pair_of ^ half)
        return lax.dynamic_slice_in_dim(w_x, at * quarter, quarter, axis=1)

    far_send = columns(1)
    far_send, hidden_in = lax.optimization_barrier((far_send, hidden_in))
    x_far = across(far_send)
    x_near = across(columns(0))
    bc_own = pick(w_bc, 1, side).reshape(depth, 2 * STATE)
    bc_other = across(pick(w_bc, 1, 1 - side).reshape(depth, 2 * STATE))
    dt_rows = w_dt.T.reshape(PAIR, LINE, 1, heads_here, depth)
    dt_rows = jnp.broadcast_to(dt_rows, (PAIR, LINE, ROWS // heads_here, heads_here, depth))
    dt_rows = dt_rows.reshape(PAIR, LINE * ROWS, depth)
    dt_own = pick(dt_rows, 0, side)
    dt_other = across(pick(dt_rows, 0, 1 - side))

    cut = hidden_in.reshape(own, LINE, PAIR * depth)
    pieces = [pick(cut, 1, z ^ m) for m in range(LINE)]
    arrived = [pieces[0]]
    for r in range(1, count):
        arrived.append(lax.ppermute(pieces[r // PAIR], "seq", [(s, s ^ r) for s in range(count)]))
    whole, x_far = lax.optimization_barrier((jnp.stack(arrived), x_far))
    rows = [whole]
    for j in range(1, ranks):
        bit = j & -j
        rows.append(lax.ppermute(rows[j - bit], "tensor", [(t, t ^ bit) for t in range(ranks)]))

    def of_heads(array):
        return jnp.repeat(array, HEAD_DIM)[None]

    by_channel = jnp.concatenate(
        [conv_state_x.astype(f32), conv_x, of_heads(skip), norm_gain[None]], axis=0
    )
    by_channel = lax.dynamic_slice_in_dim(by_channel, place_of * channels, channels, axis=1)
    by_map = jnp.concatenate([conv_state_bc.astype(f32), conv_bc], axis=0)
    by_map = pick(by_map, 1, side).reshape(margin + KERNEL, 2 * STATE)
    by_head = jnp.stack([dt_bias, decay_rate]).reshape(2, count, heads_here)
    by_head = jnp.tile(pick(by_head, 1, place_of).T, (ROWS // heads_here, 1))
    by_head = jnp.repeat(by_head, SPAN, axis=1)
    blank = jnp.zeros((ROWS - margin, channels), f32)
    small = jnp.concatenate(
        [
            blank,
            by_channel[:margin],
            blank,
            by_map[:margin],
            by_channel[margin : margin + KERNEL],
            by_map[margin:],
            by_channel[margin + KERNEL :],
            jnp.zeros((2 * ROWS - 2 * KERNEL - 2, channels), f32),
            by_head,
        ],
        axis=0,
    )

    start, end = (0, LINE - 1)
    at_end = (z == start) | (z == end)
    next_start, next_end = (1, LINE - 2)
    carry = init_state.reshape(-1, STATE)
    far, over, maps, largest = project(
        place, factor, rows, (w_x, x_far, dt_own, dt_other, bc_own, bc_other), (3, 2)
    )
    near, mine = project(place, factor, rows, (w_x, x_near, dt_own, dt_other), (1, 0))
    map_hop = along(maps, [(start, next_start), (end, next_end)])
    hop_far = along(far, [(start, next_start), (end, next_end)])
    hop_over = along(over, [(start, next_start), (end, next_end)])
    got_near = along(near, [(s, s ^ 1) for s in range(LINE)])
    map_sum = (maps.astype(f32) + map_hop.astype(f32)).astype(bf16)
    map_far = along(map_sum, [(next_start, next_end), (next_end, next_start)])
    map_done = ((map_sum.astype(f32) + map_far.astype(f32)) * in_scale).astype(bf16)
    sent_end = onward(over, hop_far)
    hop_over, sent_end = lax.optimization_barrier((hop_over, sent_end))
    got_end = along(sent_end, [(next_start, end), (next_end, start)])
    map_done, got_near, got_end = lax.optimization_barrier((map_done, got_near, got_end))
    map_done = along(map_done, [(next_start, start), (next_end, end)])
    got_next = along(onward(far, hop_over), [(next_start, next_end), (next_end, next_start)])
    gained, carry = scan(
        place,
        in_scale,
        [mine, got_near, got_end, got_next],
        [map_sum, map_far, map_done],
        small,
        largest,
        carry,
        True,
    )
    tokens = gained.shape[0] - 2 * ROWS
    beside = along(gained, [(s, s ^ 1) for s in range(LINE)])
    middle = [(next_start, next_end), (next_end, next_start)]
    outward = [(next_start, start), (next_end, end)]
    facing = along(gained, middle)
    beyond = along(beside, middle)
    second = jnp.where(at_end, along(facing, outward), facing)
    third = jnp.where(at_end, along(beyond, outward), beyond)
    two, three = (jnp.where(at_end, 2, 3), jnp.where(at_end, 3, 2))
    far_own = across(gained)
    far_beside = across(beside)
    second, far_own = lax.optimization_barrier((second, far_own))
    far_second = across(second)
    third, far_beside = lax.optimization_barrier((third, far_beside))
    far_third = across(third)
    got = (
        (0, (gained, far_own)),
        (1, (beside, far_beside)),
        (two, (second, far_second)),
        (three, (third,)),
    )
    total = None
    for m, pair in got:
        for x, piece in enumerate(pair):
            at = ((side ^ x) * LINE + (z ^ m)) * channels
            w_rows = lax.dynamic_slice_in_dim(w_out, at, channels, axis=0)
            product = jnp.dot(piece, w_rows, preferred_element_type=f32)
            total = product if total is None else total + product
    tails = [piece for m, pair in got for piece in pair]

    send, kept, squares, top = meet(place, total, far_third, w_out, tails)
    bit = 1
    while True:
        received = lax.ppermute(send, "tensor", [(t, t ^ bit) for t in range(ranks)])
        bit *= 2
        if bit == ranks:
            break
        send, kept, squares = halve(bit, place, kept, received, squares)
    final = finish(place, kept, received, squares).reshape(count, own, -1)
    final = lax.all_to_all(final, "seq", split_axis=0, concat_axis=0, tiled=True)
    layer_out = final.transpose(1, 0, 2).reshape(own, count * final.shape[2])
    abs_max = jnp.max(top)
    return (layer_out, abs_max)


def solution(mesh):
    return jax.shard_map(
        by_heads if splits(mesh) else by_tokens,
        mesh=mesh,
        in_specs=(
            P(("seq", "tensor"), None),
            P(),
            P("seq", "tensor"),
            P("seq", "tensor", None, None),
            P("seq", "tensor"),
            P(None, "tensor"),
            P(None, "tensor", None, None),
            P(None, "tensor"),
            P(None, "tensor", None, None),
            P("tensor"),
            P("tensor"),
            P("tensor"),
            P("tensor", None, None),
            P("tensor"),
            P("tensor", "seq"),
        ),
        out_specs=(P(("seq", "tensor"), None), P()),
        check_vma=False,
    )
```

```python
import functools

import jax
import jax.numpy as jnp
from jax import lax
from jax.experimental import pallas as pl
from jax.experimental.pallas import tpu as pltpu
from jax.sharding import PartitionSpec as P

HEADS = 128
HEAD_DIM = 64
STATE = 128
GROUPS = 8
KERNEL = 4
SPAN = 128


epsilon = 1e-05
quant_range = 448.0


def from_behind(value, axis, steps):
    count = lax.axis_size(axis)
    first, last = (max(0, -steps), min(count, count - steps))
    return lax.ppermute(value, axis, [(source, source + steps) for source in range(first, last)])


def carried_in(shard, axis, combine, identity):
    count, here = (lax.axis_size(axis), lax.axis_index(axis))
    everything = jax.tree.map(
        lambda part, kind: lax.all_gather(part.astype(kind), axis),
        shard,
        (jnp.bfloat16, jnp.bfloat16),
    )
    start = jax.tree.map(
        lambda part, zero: jnp.broadcast_to(jnp.asarray(zero, part.dtype), part.shape),
        shard,
        identity,
    )

    def turn(k, before):
        reached = k < here
        new = combine(
            before, jax.tree.map(lambda part, own: part[k].astype(own.dtype), everything, shard)
        )
        return jax.tree.map(lambda a, b: jnp.where(reached, a, b), new, before)

    return lax.fori_loop(0, count, turn, start)


def depthwise(before, projected, conv_taps, length):
    extended = jnp.concatenate([before, projected], axis=0)
    summed = conv_taps[0] * extended[0:length]
    for offset in range(1, KERNEL):
        summed = summed + conv_taps[offset] * extended[offset : offset + length]
    return jax.nn.silu(summed).astype(jnp.bfloat16)


def combine(earlier, later):
    return (earlier[0] * later[0], later[0][:, None, None] * earlier[1] + later[1])


def by_tokens(
    hidden_in,
    prev_amax,
    w_x,
    w_bc,
    w_dt,
    conv_x,
    conv_bc,
    conv_state_x,
    conv_state_bc,
    dt_bias,
    decay_rate,
    skip,
    init_state,
    norm_gain,
    w_out,
):
    margin = KERNEL - 1
    gathered = lax.all_gather(hidden_in, "tensor", axis=0, tiled=True)
    abs_max = lax.pmax(jnp.max(jnp.abs(gathered.astype(jnp.float32))), "seq")
    in_scale = prev_amax / quant_range
    leading = lax.axis_index("seq") == 0
    row_count = gathered.shape[0]
    bc_width = w_bc.shape[1] * w_bc.shape[2] * w_bc.shape[3]
    bc_rows = jnp.reshape(w_bc, (w_bc.shape[0], bc_width))
    scaled = gathered.astype(jnp.float32) * (quant_range / prev_amax)
    quant = jnp.clip(scaled, -quant_range, quant_range).astype(jnp.bfloat16)
    pieces = (
        lax.all_gather(w_x, "seq", axis=0, tiled=True),
        lax.all_gather(bc_rows, "seq", axis=0, tiled=True),
        lax.all_gather(w_dt, "seq", axis=0, tiled=True),
    )
    x_proj, bc_proj, dt_proj = tuple(
        (
            jnp.dot(quant, weight_piece, preferred_element_type=jnp.float32)
            for weight_piece in pieces
        )
    )
    x_whole = (x_proj * in_scale).astype(jnp.bfloat16)
    bc_whole = (bc_proj * in_scale).astype(jnp.bfloat16)
    dt_raw = dt_proj * in_scale
    state_bc = jnp.reshape(conv_state_bc, (margin, bc_width))
    received = from_behind(
        (x_whole[row_count - margin :], bc_whole[row_count - margin :]), "seq", 1
    )
    x_edge = jnp.where(leading, conv_state_x, received[0])
    bc_edge = jnp.where(leading, state_bc, received[1])
    x_act = depthwise(x_edge, x_whole, conv_x, row_count)
    bc_act = depthwise(bc_edge, bc_whole, jnp.reshape(conv_bc, (KERNEL, bc_width)), row_count)
    step_size = jax.nn.softplus(dt_raw + dt_bias)
    heads_here = step_size.shape[1]
    groups_here = w_bc.shape[1]
    per_group = HEADS // GROUPS
    blocks = row_count // SPAN
    x_blocks = x_act.reshape(blocks, SPAN, heads_here, HEAD_DIM)
    bc_blocks = bc_act.reshape(blocks, SPAN, groups_here, 2, STATE)
    in_map = bc_blocks[:, :, :, 0]
    out_map = bc_blocks[:, :, :, 1]
    step_blocks = step_size.reshape(blocks, SPAN, heads_here)
    cum_blocks = jnp.cumsum(-step_blocks * decay_rate, axis=1)
    index_row = jnp.arange(SPAN, dtype=jnp.int32)
    lower_mask = index_row[:, None] >= index_row[None, :]
    intersection = jnp.einsum(
        "ctgn,cugn->cgtu", out_map, in_map, preferred_element_type=jnp.float32
    )
    intersection = jnp.repeat(intersection, per_group, axis=1)
    cum_heads = jnp.transpose(cum_blocks, (0, 2, 1))
    log_gap = cum_heads[:, :, :, None] - cum_heads[:, :, None, :]
    decay = jnp.exp(jnp.where(lower_mask[None, None], log_gap, -1e30))
    step_heads = jnp.transpose(step_blocks, (0, 2, 1))
    weights = (intersection * decay * step_heads[:, :, None, :]).astype(jnp.bfloat16)
    local_part = jnp.einsum(
        "chtu,cuhp->cthp", weights, x_blocks, preferred_element_type=jnp.float32
    )
    last_cum = cum_blocks[:, SPAN - 1, :]
    x_weighted = (
        x_blocks.astype(jnp.float32)
        * (step_blocks * jnp.exp(last_cum[:, None, :] - cum_blocks))[:, :, :, None]
    ).astype(jnp.bfloat16)
    in_heads = jnp.repeat(in_map, per_group, axis=2)
    added = jnp.einsum("cuhp,cuhn->chpn", x_weighted, in_heads, preferred_element_type=jnp.float32)

    def carry_on(carried, element):
        block_decay, block_added = element
        return (block_decay[:, None, None] * carried + block_added, carried)

    empty_state = jnp.zeros((heads_here, HEAD_DIM, STATE), jnp.float32)
    device_state, entering = lax.scan(carry_on, empty_state, (jnp.exp(last_cum), added))
    device_decay = jnp.exp(jnp.sum(last_cum, axis=0))
    seeded = device_state + jnp.where(leading, device_decay[:, None, None] * init_state, 0.0)
    identity = (jnp.ones_like(device_decay), jnp.zeros_like(device_state))
    scanned = carried_in((device_decay, seeded), "seq", combine, identity)
    incoming = jnp.where(leading, init_state, scanned[1])
    prefix = jnp.exp(jnp.cumsum(last_cum, axis=0) - last_cum)
    states_in = entering + prefix[:, :, None, None] * incoming[None]
    out_heads = jnp.repeat(out_map, per_group, axis=2).astype(jnp.float32)
    carried_part = (
        jnp.einsum("cthn,chpn->cthp", out_heads, states_in, precision=lax.Precision.HIGHEST)
        * jnp.exp(cum_blocks)[:, :, :, None]
    )
    ssm_out = local_part + carried_part + skip[None, None, :, None] * x_blocks.astype(jnp.float32)
    ssm_out = ssm_out.reshape(row_count, heads_here * HEAD_DIM)
    squares = lax.psum(jnp.sum(ssm_out * ssm_out, axis=1), "tensor")
    mean_sq = squares / (HEADS * HEAD_DIM)
    normed = (ssm_out * lax.rsqrt(mean_sq + epsilon)[:, None] * norm_gain).astype(jnp.bfloat16)
    partial_out = jnp.dot(
        normed, lax.all_gather(w_out, "seq", axis=1, tiled=True), preferred_element_type=jnp.float32
    )
    layer_out = lax.psum_scatter(
        partial_out.astype(jnp.bfloat16), "tensor", scatter_dimension=0, tiled=True
    )
    return (layer_out, abs_max)


PAIR = 2
LINE = 4
ROWS = 8
SMEM = pl.BlockSpec(memory_space=pltpu.SMEM)
HIGHEST = lax.Precision.HIGHEST


def splits(mesh):
    count, ranks = (mesh.shape["seq"], mesh.shape["tensor"])
    heads_all, groups_here = (HEADS // ranks, GROUPS // ranks)
    if count != PAIR * LINE or groups_here != PAIR or ranks & (ranks - 1):
        return False
    heads_here = heads_all // count
    return 2 * heads_here == ROWS and heads_here * HEAD_DIM == 2 * SPAN


def nt_dot(a, b, **kw):
    return lax.dot_general(
        a, b, (((1,), (1,)), ((), ())), preferred_element_type=jnp.float32, **kw
    )


def project_kernel(ranks, place_ref, factor_ref, *refs):
    hidden = [refs[x * ranks : (x + 1) * ranks] for x in range(PAIR)]
    refs = refs[PAIR * ranks :]
    own_x, other_x = (refs[0], refs[1 : 1 + LINE])
    own_bc, other_bc, own_dt, other_dt = refs[1 + LINE : 5 + LINE]
    x_refs = refs[5 + LINE : 5 + 2 * LINE]
    bc_ref, largest_ref, quant_ref, dt_buf = refs[5 + 2 * LINE :]
    side, z = (place_ref[1], place_ref[2])
    step = pl.program_id(0)
    factor = factor_ref[0]
    depth = own_x.shape[0]
    largest = None
    each = hidden[0][0].shape[0]
    for x in range(PAIR):
        for k in range(each):
            block = (k ^ (z % each)) * PAIR + (side ^ x)
            for j in range(ranks):
                for half in range(PAIR):
                    cut = slice(half * depth, (half + 1) * depth)
                    values = hidden[x][j][k, :, cut].astype(jnp.float32)
                    scaled = jnp.clip(values * factor, -quant_range, quant_range)
                    quant_ref[half, block, j] = scaled.astype(jnp.bfloat16)
                    top = jnp.max(jnp.abs(values).reshape(-1, ROWS, depth), axis=0)
                    largest = top if largest is None else jnp.maximum(largest, top)
    width = largest_ref.shape[1]
    top = largest[:, :width]
    for at in range(width, depth, width):
        top = jnp.maximum(top, largest[:, at : at + width])

    @pl.when(step == 0)
    def _():
        largest_ref[...] = top

    @pl.when(step > 0)
    def _():
        largest_ref[...] = jnp.maximum(largest_ref[...], top)

    rows = quant_ref.shape[1] * quant_ref.shape[2] * quant_ref.shape[3]
    near = quant_ref[side].reshape(rows, depth)
    far = quant_ref[1 - side].reshape(rows, depth)

    def both(own, other):
        return jnp.dot(near, own, preferred_element_type=jnp.float32) + jnp.dot(
            far, other, preferred_element_type=jnp.float32
        )

    at_rows = pl.ds(pl.multiple_of(step * rows, rows), rows)
    dt_buf[...] = both(own_dt[...], other_dt[...]).T[: LINE * ROWS].reshape(dt_buf.shape)
    channels = x_refs[0].shape[1]
    tokens = pl.num_programs(0) * rows
    extra = rows // channels * ROWS
    upper = lax.broadcasted_iota(jnp.int32, (ROWS, channels), 0) < ROWS // 2
    for m in reversed(range(LINE)):
        owner = z ^ m
        cut = pl.ds(pl.multiple_of(owner * channels, channels), channels)
        x_refs[m][at_rows] = both(own_x[:, cut], other_x[m][...]).astype(jnp.bfloat16)
        dt = dt_buf[owner]
        pieces = [
            split_parts(dt[:, at : at + channels], upper) for at in range(0, rows, channels)
        ]
        x_refs[m][pl.ds(pl.multiple_of(tokens + step * extra, 16), extra)] = jnp.concatenate(
            pieces, axis=0
        ).astype(jnp.bfloat16)
    bc_ref[at_rows] = both(own_bc[...], other_bc[...]).astype(jnp.bfloat16)


def split_parts(values, upper):
    top = values.astype(jnp.bfloat16).astype(jnp.float32)
    return jnp.where(upper, top, values - top)


def project(place, factor, hidden, w_x, weights):
    line, own, wide = hidden[0].shape
    ranks = len(hidden) // PAIR
    depth, channels = weights[0].shape
    maps_wide = weights[LINE].shape[1]
    x_wide = channels * LINE
    steps = 2
    each = line // steps
    tokens = line * PAIR * ranks * own
    extra = tokens // channels * ROWS

    def fixed(array):
        return pl.BlockSpec(array.shape, lambda i, p: (0,) * array.ndim)

    payload = jax.ShapeDtypeStruct((tokens + extra, channels), jnp.bfloat16)
    maps = jax.ShapeDtypeStruct((tokens, maps_wide), jnp.bfloat16)
    largest = jax.ShapeDtypeStruct((ROWS, 128), jnp.float32)
    outs = [payload] * LINE + [maps, largest]
    rows_of = pl.BlockSpec((each, own, wide), lambda i, p: (i ^ (p[2] // each), 0, 0))
    return pl.pallas_call(
        functools.partial(project_kernel, ranks),
        grid_spec=pltpu.PrefetchScalarGridSpec(
            num_scalar_prefetch=1,
            grid=(steps,),
            in_specs=[SMEM]
            + [rows_of] * (PAIR * ranks)
            + [pl.BlockSpec((depth, x_wide), lambda i, p: (0, p[1]))]
            + [fixed(w) for w in weights],
            out_specs=[fixed(out) for out in outs],
            scratch_shapes=[
                pltpu.VMEM((PAIR, each * PAIR, ranks, own, depth), jnp.bfloat16),
                pltpu.VMEM((LINE, ROWS, tokens // steps), jnp.float32),
            ],
        ),
        out_shape=outs,
        compiler_params=pltpu.CompilerParams(vmem_limit_bytes=26 * 2**20),
        cost_estimate=pl.CostEstimate(
            flops=2 * tokens * wide * (x_wide + maps_wide),
            bytes_accessed=2 * tokens * (wide + x_wide),
            transcendentals=0,
        ),
        name="project",
    )(place, factor, *hidden, w_x, *weights)


def onward_kernel(own_ref, received_ref, out_ref):
    rows, channels = own_ref.shape
    tokens = rows * channels // (channels + ROWS)
    total = own_ref[:tokens].astype(jnp.float32) + received_ref[:tokens].astype(jnp.float32)
    out_ref[:tokens] = total.astype(jnp.bfloat16)
    upper = lax.broadcasted_iota(jnp.int32, (ROWS, channels), 0) < ROWS // 2
    extra = own_ref[tokens:].astype(jnp.float32) + received_ref[tokens:].astype(jnp.float32)
    pieces = []
    for at in range(0, rows - tokens, ROWS):
        piece = extra[at : at + ROWS]
        pieces.append(split_parts(piece + pltpu.roll(piece, ROWS // 2, 0), upper))
    out_ref[tokens:] = jnp.concatenate(pieces, axis=0).astype(jnp.bfloat16)


def onward(own, received):
    whole = pl.BlockSpec(own.shape, lambda: (0, 0))
    return pl.pallas_call(
        onward_kernel,
        in_specs=[whole, whole],
        out_specs=whole,
        out_shape=jax.ShapeDtypeStruct(own.shape, own.dtype),
        compiler_params=pltpu.CompilerParams(vmem_limit_bytes=8 * 2**20),
        cost_estimate=pl.CostEstimate(
            flops=own.size, bytes_accessed=6 * own.size, transcendentals=0
        ),
        name="onward",
    )(own, received)


def scan_kernel(first, place_ref, scale_ref, *refs):
    x_refs, bc_refs = (refs[:4], refs[4:7])
    small_ref, largest_ref, carry_ref, out_ref, carry_out_ref, x_buf, bc_buf = refs[7:]
    tokens, channels = bc_refs[0].shape
    blocks = tokens // SPAN
    heads = channels // HEAD_DIM
    rank, z = (place_ref[0], place_ref[2])
    ranks = place_ref.shape[0] - 3
    own = SPAN // ranks
    edge = ROWS
    in_scale = scale_ref[0]
    at_end = (z == 0) | (z == LINE - 1)
    if first:
        x_buf[:edge] = small_ref[:edge]
        bc_buf[:edge] = small_ref[edge : 2 * edge]
        state = carry_ref[...].T
    else:
        x_buf[:edge] = carry_ref[STATE : STATE + edge]
        bc_buf[:edge] = carry_ref[STATE + edge :]
        state = carry_ref[:STATE]

    for block in range(blocks):
        for true_rank in range(ranks):
            source = block * SPAN + (true_rank ^ rank) * own
            source = pl.ds(pl.multiple_of(source, own), own)
            at = edge + block * SPAN + true_rank * own
            at = slice(at, at + own)
            total = sum(ref[source].astype(jnp.float32) for ref in x_refs) * in_scale
            x_buf[at] = total.astype(jnp.bfloat16).astype(jnp.float32)
            near, far, done = (ref[source].astype(jnp.float32) for ref in bc_refs)
            total = ((near + far) * in_scale).astype(jnp.bfloat16).astype(jnp.float32)
            bc_buf[at] = jnp.where(at_end, done, total)

    taps = 2 * edge

    def activate(buf, row, block):
        start = edge - (KERNEL - 1) + block * SPAN
        summed = small_ref[row : row + 1] * buf[start : start + SPAN]
        for k in range(1, KERNEL):
            summed = summed + small_ref[row + k : row + k + 1] * buf[start + k : start + k + SPAN]
        return (summed / (1.0 + jnp.exp(-summed))).astype(jnp.bfloat16)

    skip = small_ref[taps + 2 * KERNEL : taps + 2 * KERNEL + 1]
    gain = small_ref[taps + 2 * KERNEL + 1 : taps + 2 * KERNEL + 2]
    bias = small_ref[4 * edge :, :SPAN]
    rate = small_ref[4 * edge :, SPAN:]

    up = lax.broadcasted_iota(jnp.int32, (SPAN, SPAN), 0)
    across = lax.broadcasted_iota(jnp.int32, (SPAN, SPAN), 1)
    lane = lax.broadcasted_iota(jnp.int32, (SPAN, channels), 1)
    lower = up >= across
    upper = (up <= across).astype(jnp.float32)
    lanes = across[:ROWS]

    dt = sum(ref[tokens:].astype(jnp.float32) for ref in x_refs)
    steps = []
    wide = channels // SPAN
    for block in range(blocks):
        tile = dt[block // wide * ROWS : (block // wide + 1) * ROWS]
        cut = tile[:, block % wide * SPAN : (block % wide + 1) * SPAN]
        cut = (cut + pltpu.roll(cut, ROWS // 2, 0)) * in_scale
        bit = 1
        while bit < ranks:
            shift = bit * own
            flipped = jnp.where(
                (lanes // shift) % 2 == 1,
                pltpu.roll(cut, shift, 1),
                pltpu.roll(cut, SPAN - shift, 1),
            )
            cut = jnp.where((rank & bit) != 0, flipped, cut)
            bit *= 2
        raw = cut + bias
        steps.append(jnp.maximum(raw, 0.0) + jnp.log1p(jnp.exp(-jnp.abs(raw))))
    drops = jnp.concatenate([-step * rate for step in steps], axis=0)
    cums = jnp.dot(drops, upper, precision=HIGHEST, preferred_element_type=jnp.float32)

    sums = jnp.zeros((SPAN, SPAN), jnp.float32)
    for block in range(blocks):
        x_act = activate(x_buf, taps, block)
        bc_act = activate(bc_buf, taps + KERNEL, block)
        in_map, out_map = (bc_act[:, :STATE], bc_act[:, STATE:])
        step, cum = (steps[block], cums[block * ROWS : (block + 1) * ROWS])
        last = cum[:, SPAN - 1 : SPAN]
        turned = jnp.concatenate(
            [
                cum,
                step * jnp.exp(last - cum),
                jnp.exp(cum),
                jnp.zeros((SPAN - 3 * ROWS, SPAN), jnp.float32),
            ],
            axis=0,
        ).T

        def spread(row):
            result = jnp.broadcast_to(turned[:, row : row + 1], (SPAN, channels))
            for h in range(1, heads):
                result = jnp.where(lane >= h * HEAD_DIM, turned[:, row + h : row + h + 1], result)
            return result

        inner = jnp.where(lower, nt_dot(out_map, in_map), 0.0)
        x_wide = x_act.astype(jnp.float32)
        weights, spaced = ([], [])
        for h in range(heads):
            gap = jnp.where(lower, turned[:, h : h + 1] - cum[h : h + 1], 0.0)
            weights.append((inner * jnp.exp(gap) * step[h : h + 1]).astype(jnp.bfloat16))
            inside = (lane >= h * HEAD_DIM) & (lane < (h + 1) * HEAD_DIM)
            spaced.append(jnp.where(inside, x_wide, 0.0).astype(jnp.bfloat16))
        local_part = jnp.dot(
            jnp.concatenate(weights, axis=1),
            jnp.concatenate(spaced, axis=0),
            preferred_element_type=jnp.float32,
        )
        grown = spread(2 * ROWS)
        x_weighted = (x_wide * spread(ROWS)).astype(jnp.bfloat16)
        added = lax.dot_general(
            in_map, x_weighted, (((0,), (0,)), ((), ())), preferred_element_type=jnp.float32
        )
        high = state.astype(jnp.bfloat16)
        rest = state - high.astype(jnp.float32)
        middle = rest.astype(jnp.bfloat16)
        low = (rest - middle.astype(jnp.float32)).astype(jnp.bfloat16)
        carried = jnp.dot(out_map, high, preferred_element_type=jnp.float32)
        carried = carried + jnp.dot(out_map, middle, preferred_element_type=jnp.float32)
        carried = carried + jnp.dot(out_map, low, preferred_element_type=jnp.float32)
        ssm_out = local_part + grown * carried + skip * x_wide
        state = grown[SPAN - 1 : SPAN] * state + added
        out_ref[block * SPAN : (block + 1) * SPAN] = (ssm_out * gain).astype(jnp.bfloat16)
        summed = jnp.sum(ssm_out * ssm_out, axis=1, keepdims=True)
        sums = jnp.where(across == block, summed, sums)

    whole = sums.T[:ROWS]
    top = whole.astype(jnp.bfloat16).astype(jnp.float32)
    largest = jnp.broadcast_to(jnp.max(largest_ref[...]), (ROWS, channels))
    extra = jnp.concatenate([jnp.concatenate([top, whole - top], axis=1), largest], axis=0)
    out_ref[tokens:] = extra.astype(jnp.bfloat16)
    carry_out_ref[:STATE] = state
    carry_out_ref[STATE : STATE + edge] = x_buf[tokens : tokens + edge]
    carry_out_ref[STATE + edge :] = bc_buf[tokens : tokens + edge]


def scan(place, in_scale, sums, maps, small, largest, carry, first):
    channels = sums[0].shape[1]
    tokens = maps[0].shape[0]

    def fixed(array):
        return pl.BlockSpec(array.shape, lambda i, p: (0, 0))

    held = pl.BlockSpec((channels, STATE), lambda i, p: (p[1] * LINE + p[2], 0))
    outs = [
        jax.ShapeDtypeStruct((tokens + 2 * ROWS, channels), jnp.bfloat16),
        jax.ShapeDtypeStruct((STATE + 2 * ROWS, channels), jnp.float32),
    ]
    return pl.pallas_call(
        functools.partial(scan_kernel, first),
        grid_spec=pltpu.PrefetchScalarGridSpec(
            num_scalar_prefetch=1,
            grid=(1,),
            in_specs=[SMEM]
            + [fixed(array) for array in (*sums, *maps, small, largest)]
            + [held if first else fixed(carry)],
            out_specs=[fixed(out) for out in outs],
            scratch_shapes=[
                pltpu.VMEM((tokens + ROWS, channels), jnp.float32),
                pltpu.VMEM((tokens + ROWS, 2 * STATE), jnp.float32),
            ],
        ),
        out_shape=outs,
        compiler_params=pltpu.CompilerParams(vmem_limit_bytes=20 * 2**20),
        cost_estimate=pl.CostEstimate(
            flops=8 * tokens * SPAN * channels,
            bytes_accessed=8 * tokens * channels,
            transcendentals=tokens * (channels + 8 * SPAN),
        ),
        name="scan",
    )(place, in_scale, *sums, *maps, small, largest, carry)


def by_heads(
    hidden_in,
    prev_amax,
    w_x,
    w_bc,
    w_dt,
    conv_x,
    conv_bc,
    conv_state_x,
    conv_state_bc,
    dt_bias,
    decay_rate,
    skip,
    init_state,
    norm_gain,
    w_out,
):
    margin = KERNEL - 1
    count, here = (lax.axis_size("seq"), lax.axis_index("seq"))
    ranks, rank = (lax.axis_size("tensor"), lax.axis_index("tensor"))
    z, side = (here // PAIR, here % PAIR)
    place_of = side * LINE + z
    f32, bf16 = (jnp.float32, jnp.bfloat16)
    own, width = hidden_in.shape
    depth = w_x.shape[0]
    channels = w_x.shape[1] // count
    heads_here = w_dt.shape[1] // count
    in_scale = (prev_amax / quant_range).reshape(1)
    factor = (quant_range / prev_amax).reshape(1)
    place = jnp.stack([rank, side, z] + [rank] * ranks).astype(jnp.int32)

    def pick(array, axis, index):
        return lax.dynamic_index_in_dim(array, index, axis, keepdims=False)

    def along(value, pairs):
        moves = [(a * PAIR + x, b * PAIR + x) for a, b in pairs for x in range(PAIR)]
        return lax.ppermute(value, "seq", moves)

    def across(value):
        return lax.ppermute(value, "seq", [(s, s ^ 1) for s in range(count)])

    other_side = (1 - side) * LINE
    sent = [
        lax.dynamic_slice_in_dim(w_x, (other_side + (z ^ m)) * channels, channels, axis=1)
        for m in reversed(range(LINE))
    ]
    sent[0], hidden_in = lax.optimization_barrier((sent[0], hidden_in))
    maps_sent = pick(w_bc, 1, 1 - side).reshape(depth, 2 * STATE)
    sent.insert(LINE // 2, maps_sent)
    swapped = []
    for value in sent:
        if swapped:
            swapped[-1], value = lax.optimization_barrier((swapped[-1], value))
        swapped.append(across(value))
    bc_other = swapped.pop(LINE // 2)
    swapped.reverse()
    bc_own = pick(w_bc, 1, side).reshape(depth, 2 * STATE)
    dt_columns = w_dt.reshape(depth, PAIR, LINE, 1, heads_here)
    dt_columns = jnp.broadcast_to(
        dt_columns, (depth, PAIR, LINE, ROWS // heads_here, heads_here)
    ).reshape(depth, PAIR, LINE * ROWS)
    dt_columns = jnp.pad(dt_columns, ((0, 0), (0, 0), (0, SPAN - LINE * ROWS)))
    dt_own = pick(dt_columns, 1, side)
    dt_other = across(pick(dt_columns, 1, 1 - side))

    cut = hidden_in.reshape(own, LINE, PAIR * depth)
    pieces = [pick(cut, 1, z ^ m) for m in range(LINE)]
    arrived = [pieces[0]]
    for m in range(1, LINE):
        arrived.append(along(pieces[m], [(s, s ^ m) for s in range(LINE)]))
    stacked = jnp.stack(arrived)
    rows = []
    for mine in (stacked, across(stacked)):
        ours = [mine]
        for j in range(1, ranks):
            bit = j & -j
            pairs = [(t, t ^ bit) for t in range(ranks)]
            ours.append(lax.ppermute(ours[j - bit], "tensor", pairs))
        rows.extend(ours)

    def of_heads(array):
        return jnp.repeat(array, HEAD_DIM)[None]

    by_channel = jnp.concatenate(
        [conv_state_x.astype(f32), conv_x, of_heads(skip), norm_gain[None]], axis=0
    )
    by_channel = lax.dynamic_slice_in_dim(by_channel, place_of * channels, channels, axis=1)
    by_map = jnp.concatenate([conv_state_bc.astype(f32), conv_bc], axis=0)
    by_map = pick(by_map, 1, side).reshape(margin + KERNEL, 2 * STATE)
    by_head = jnp.stack([dt_bias, decay_rate]).reshape(2, count, heads_here)
    by_head = jnp.tile(pick(by_head, 1, place_of).T, (ROWS // heads_here, 1))
    by_head = jnp.repeat(by_head, SPAN, axis=1)
    blank = jnp.zeros((ROWS - margin, channels), f32)
    small = jnp.concatenate(
        [
            blank,
            by_channel[:margin],
            blank,
            by_map[:margin],
            by_channel[margin : margin + KERNEL],
            by_map[margin:],
            by_channel[margin + KERNEL :],
            jnp.zeros((2 * ROWS - 2 * KERNEL - 2, channels), f32),
            by_head,
        ],
        axis=0,
    )

    start, end = (0, LINE - 1)
    at_end = (z == start) | (z == end)
    next_start, next_end = (1, LINE - 2)
    weights = (*swapped, bc_own, bc_other, dt_own, dt_other)
    carry = init_state.reshape(-1, STATE)
    mine, near, over, far, maps, largest = project(place, factor, rows, w_x, weights)
    map_hop = along(maps, [(start, next_start), (end, next_end)])
    hop_far = along(far, [(start, next_start), (end, next_end)])
    hop_over = along(over, [(start, next_start), (end, next_end)])
    got_near = along(near, [(s, s ^ 1) for s in range(LINE)])
    map_sum = (maps.astype(f32) + map_hop.astype(f32)).astype(bf16)
    map_far = along(map_sum, [(next_start, next_end), (next_end, next_start)])
    map_done = ((map_sum.astype(f32) + map_far.astype(f32)) * in_scale).astype(bf16)
    sent_end = onward(over, hop_far)
    hop_over, unused = lax.optimization_barrier((hop_over, sent_end))
    got_end = along(sent_end, [(next_start, end), (next_end, start)])
    map_done, got_near, got_end = lax.optimization_barrier((map_done, got_near, got_end))
    map_done = along(map_done, [(next_start, start), (next_end, end)])
    got_next = along(onward(far, hop_over), [(next_start, next_end), (next_end, next_start)])
    gained, carry = scan(
        place,
        in_scale,
        [mine, got_near, got_end, got_next],
        [map_sum, map_far, map_done],
        small,
        largest,
        carry,
        True,
    )
    tokens = gained.shape[0] - 2 * ROWS
    beside = along(gained, [(s, s ^ 1) for s in range(LINE)])
    middle = [(next_start, next_end), (next_end, next_start)]
    outward = [(next_start, start), (next_end, end)]
    facing = along(gained, middle)
    beyond = along(beside, middle)
    second = jnp.where(at_end, along(facing, outward), facing)
    third = jnp.where(at_end, along(beyond, outward), beyond)
    two, three = (jnp.where(at_end, 2, 3), jnp.where(at_end, 3, 2))
    far_own = across(gained)
    far_beside = across(beside)
    second, far_own = lax.optimization_barrier((second, far_own))
    far_second = across(second)
    third, far_beside = lax.optimization_barrier((third, far_beside))
    far_third = across(third)
    got = (
        (0, (gained, far_own)),
        (1, (beside, far_beside)),
        (two, (second, far_second)),
        (three, (third, far_third)),
    )
    total = squares = top = None
    for m, pair in got:
        for x, piece in enumerate(pair):
            at = ((side ^ x) * LINE + (z ^ m)) * channels
            w_rows = lax.dynamic_slice_in_dim(w_out, at, channels, axis=0)
            product = jnp.dot(piece, w_rows, preferred_element_type=f32)
            tail = piece[tokens:].astype(f32)
            low, high = (tail[:ROWS, :SPAN] + tail[:ROWS, SPAN:], tail[ROWS:, :SPAN])
            if total is None:
                total, squares, top = (product, low, high)
            else:
                total = total + product
                squares = squares + low
                top = jnp.maximum(top, high)
    wide = w_out.shape[1]
    squares = squares + lax.ppermute(squares, "tensor", [(t, t ^ 1) for t in range(ranks)])
    pairs = ranks // 2
    kept = total[:tokens].reshape(count, pairs, 2, own, wide)
    nearest = rank % 2
    received = lax.ppermute(
        pick(kept, 2, 1 - nearest).astype(bf16), "tensor", [(t, t ^ 1) for t in range(ranks)]
    )
    kept = (pick(kept, 2, nearest) + received.astype(f32)).astype(bf16)
    groups = [
        [s * ranks + t for s in range(count) for t in range(c, ranks, 2)] for c in range(2)
    ]
    final = lax.all_to_all(
        kept.reshape(count * pairs, own, wide),
        ("seq", "tensor"),
        split_axis=0,
        concat_axis=0,
        axis_index_groups=groups,
        tiled=True,
    )
    bit = 2
    while bit < ranks:
        swap = [(t, t ^ bit) for t in range(ranks)]
        squares = squares + lax.ppermute(squares, "tensor", swap)
        bit *= 2
    mean_sq = squares.reshape(count, ranks, own) / (HEADS * HEAD_DIM)
    factors = lax.rsqrt(lax.dynamic_slice_in_dim(mean_sq, here, 1)[0] + epsilon)
    factors = pick(factors, 0, rank)[:, None, None]
    final = jnp.sum(final.reshape(count, pairs, own, wide).astype(f32), axis=1)
    final = final.transpose(1, 0, 2) * factors
    layer_out = final.astype(bf16).reshape(own, count * wide)
    abs_max = jnp.max(top)
    return (layer_out, abs_max)


def solution(mesh):
    return jax.shard_map(
        by_heads if splits(mesh) else by_tokens,
        mesh=mesh,
        in_specs=(
            P(("seq", "tensor"), None),
            P(),
            P("seq", "tensor"),
            P("seq", "tensor", None, None),
            P("seq", "tensor"),
            P(None, "tensor"),
            P(None, "tensor", None, None),
            P(None, "tensor"),
            P(None, "tensor", None, None),
            P("tensor"),
            P("tensor"),
            P("tensor"),
            P("tensor", None, None),
            P("tensor"),
            P("tensor", "seq"),
        ),
        out_specs=(P(("seq", "tensor"), None), P()),
        check_vma=False,
    )
```

```python
import functools

import jax
import jax.numpy as jnp
from jax import lax
from jax.experimental import pallas as pl
from jax.experimental.pallas import tpu as pltpu
from jax.sharding import PartitionSpec as P

HEADS = 128
HEAD_DIM = 64
STATE = 128
GROUPS = 8
KERNEL = 4
SPAN = 128


epsilon = 1e-05
quant_range = 448.0


def from_behind(value, axis, steps):
    count = lax.axis_size(axis)
    first, last = (max(0, -steps), min(count, count - steps))
    return lax.ppermute(value, axis, [(source, source + steps) for source in range(first, last)])


def carried_in(shard, axis, combine, identity):
    count, here = (lax.axis_size(axis), lax.axis_index(axis))
    everything = jax.tree.map(
        lambda part, kind: lax.all_gather(part.astype(kind), axis),
        shard,
        (jnp.bfloat16, jnp.bfloat16),
    )
    start = jax.tree.map(
        lambda part, zero: jnp.broadcast_to(jnp.asarray(zero, part.dtype), part.shape),
        shard,
        identity,
    )

    def turn(k, before):
        reached = k < here
        new = combine(
            before, jax.tree.map(lambda part, own: part[k].astype(own.dtype), everything, shard)
        )
        return jax.tree.map(lambda a, b: jnp.where(reached, a, b), new, before)

    return lax.fori_loop(0, count, turn, start)


def depthwise(before, projected, conv_taps, length):
    extended = jnp.concatenate([before, projected], axis=0)
    summed = conv_taps[0] * extended[0:length]
    for offset in range(1, KERNEL):
        summed = summed + conv_taps[offset] * extended[offset : offset + length]
    return jax.nn.silu(summed).astype(jnp.bfloat16)


def combine(earlier, later):
    return (earlier[0] * later[0], later[0][:, None, None] * earlier[1] + later[1])


def by_tokens(
    hidden_in,
    prev_amax,
    w_x,
    w_bc,
    w_dt,
    conv_x,
    conv_bc,
    conv_state_x,
    conv_state_bc,
    dt_bias,
    decay_rate,
    skip,
    init_state,
    norm_gain,
    w_out,
):
    margin = KERNEL - 1
    gathered = lax.all_gather(hidden_in, "tensor", axis=0, tiled=True)
    abs_max = lax.pmax(jnp.max(jnp.abs(gathered.astype(jnp.float32))), "seq")
    in_scale = prev_amax / quant_range
    leading = lax.axis_index("seq") == 0
    row_count = gathered.shape[0]
    bc_width = w_bc.shape[1] * w_bc.shape[2] * w_bc.shape[3]
    bc_rows = jnp.reshape(w_bc, (w_bc.shape[0], bc_width))
    scaled = gathered.astype(jnp.float32) * (quant_range / prev_amax)
    quant = jnp.clip(scaled, -quant_range, quant_range).astype(jnp.bfloat16)
    pieces = (
        lax.all_gather(w_x, "seq", axis=0, tiled=True),
        lax.all_gather(bc_rows, "seq", axis=0, tiled=True),
        lax.all_gather(w_dt, "seq", axis=0, tiled=True),
    )
    x_proj, bc_proj, dt_proj = tuple(
        (
            jnp.dot(quant, weight_piece, preferred_element_type=jnp.float32)
            for weight_piece in pieces
        )
    )
    x_whole = (x_proj * in_scale).astype(jnp.bfloat16)
    bc_whole = (bc_proj * in_scale).astype(jnp.bfloat16)
    dt_raw = dt_proj * in_scale
    state_bc = jnp.reshape(conv_state_bc, (margin, bc_width))
    received = from_behind(
        (x_whole[row_count - margin :], bc_whole[row_count - margin :]), "seq", 1
    )
    x_edge = jnp.where(leading, conv_state_x, received[0])
    bc_edge = jnp.where(leading, state_bc, received[1])
    x_act = depthwise(x_edge, x_whole, conv_x, row_count)
    bc_act = depthwise(bc_edge, bc_whole, jnp.reshape(conv_bc, (KERNEL, bc_width)), row_count)
    step_size = jax.nn.softplus(dt_raw + dt_bias)
    heads_here = step_size.shape[1]
    groups_here = w_bc.shape[1]
    per_group = HEADS // GROUPS
    blocks = row_count // SPAN
    x_blocks = x_act.reshape(blocks, SPAN, heads_here, HEAD_DIM)
    bc_blocks = bc_act.reshape(blocks, SPAN, groups_here, 2, STATE)
    in_map = bc_blocks[:, :, :, 0]
    out_map = bc_blocks[:, :, :, 1]
    step_blocks = step_size.reshape(blocks, SPAN, heads_here)
    cum_blocks = jnp.cumsum(-step_blocks * decay_rate, axis=1)
    index_row = jnp.arange(SPAN, dtype=jnp.int32)
    lower_mask = index_row[:, None] >= index_row[None, :]
    intersection = jnp.einsum(
        "ctgn,cugn->cgtu", out_map, in_map, preferred_element_type=jnp.float32
    )
    intersection = jnp.repeat(intersection, per_group, axis=1)
    cum_heads = jnp.transpose(cum_blocks, (0, 2, 1))
    log_gap = cum_heads[:, :, :, None] - cum_heads[:, :, None, :]
    decay = jnp.exp(jnp.where(lower_mask[None, None], log_gap, -1e30))
    step_heads = jnp.transpose(step_blocks, (0, 2, 1))
    weights = (intersection * decay * step_heads[:, :, None, :]).astype(jnp.bfloat16)
    local_part = jnp.einsum(
        "chtu,cuhp->cthp", weights, x_blocks, preferred_element_type=jnp.float32
    )
    last_cum = cum_blocks[:, SPAN - 1, :]
    x_weighted = (
        x_blocks.astype(jnp.float32)
        * (step_blocks * jnp.exp(last_cum[:, None, :] - cum_blocks))[:, :, :, None]
    ).astype(jnp.bfloat16)
    in_heads = jnp.repeat(in_map, per_group, axis=2)
    added = jnp.einsum("cuhp,cuhn->chpn", x_weighted, in_heads, preferred_element_type=jnp.float32)

    def carry_on(carried, element):
        block_decay, block_added = element
        return (block_decay[:, None, None] * carried + block_added, carried)

    empty_state = jnp.zeros((heads_here, HEAD_DIM, STATE), jnp.float32)
    device_state, entering = lax.scan(carry_on, empty_state, (jnp.exp(last_cum), added))
    device_decay = jnp.exp(jnp.sum(last_cum, axis=0))
    seeded = device_state + jnp.where(leading, device_decay[:, None, None] * init_state, 0.0)
    identity = (jnp.ones_like(device_decay), jnp.zeros_like(device_state))
    scanned = carried_in((device_decay, seeded), "seq", combine, identity)
    incoming = jnp.where(leading, init_state, scanned[1])
    prefix = jnp.exp(jnp.cumsum(last_cum, axis=0) - last_cum)
    states_in = entering + prefix[:, :, None, None] * incoming[None]
    out_heads = jnp.repeat(out_map, per_group, axis=2).astype(jnp.float32)
    carried_part = (
        jnp.einsum("cthn,chpn->cthp", out_heads, states_in, precision=lax.Precision.HIGHEST)
        * jnp.exp(cum_blocks)[:, :, :, None]
    )
    ssm_out = local_part + carried_part + skip[None, None, :, None] * x_blocks.astype(jnp.float32)
    ssm_out = ssm_out.reshape(row_count, heads_here * HEAD_DIM)
    squares = lax.psum(jnp.sum(ssm_out * ssm_out, axis=1), "tensor")
    mean_sq = squares / (HEADS * HEAD_DIM)
    normed = (ssm_out * lax.rsqrt(mean_sq + epsilon)[:, None] * norm_gain).astype(jnp.bfloat16)
    partial_out = jnp.dot(
        normed, lax.all_gather(w_out, "seq", axis=1, tiled=True), preferred_element_type=jnp.float32
    )
    layer_out = lax.psum_scatter(
        partial_out.astype(jnp.bfloat16), "tensor", scatter_dimension=0, tiled=True
    )
    return (layer_out, abs_max)


PAIR = 2
LINE = 4
PARTS = 2
ROWS = 8
SMEM = pl.BlockSpec(memory_space=pltpu.SMEM)
HIGHEST = lax.Precision.HIGHEST


def splits(mesh):
    count, ranks = (mesh.shape["seq"], mesh.shape["tensor"])
    heads_all, groups_here = (HEADS // ranks, GROUPS // ranks)
    if count != PAIR * LINE or groups_here != PAIR or ranks & (ranks - 1):
        return False
    heads_here = heads_all // count
    return 2 * heads_here == ROWS and heads_here * HEAD_DIM == 2 * SPAN


def nt_dot(a, b, **kw):
    return lax.dot_general(
        a, b, (((1,), (1,)), ((), ())), preferred_element_type=jnp.float32, **kw
    )


def project_kernel(ranks, place_ref, factor_ref, *refs):
    hidden = [refs[x * ranks : (x + 1) * ranks] for x in range(PAIR)]
    refs = refs[PAIR * ranks :]
    own_x, other_x = (refs[0], refs[1 : 1 + LINE])
    own_bc, other_bc, own_dt, other_dt = refs[1 + LINE : 5 + LINE]
    x_refs = refs[5 + LINE : 5 + 2 * LINE]
    bc_ref, largest_ref, quant_ref, dt_buf = refs[5 + 2 * LINE :]
    side, z = (place_ref[1], place_ref[2])
    step = pl.program_id(0)
    factor = factor_ref[0]
    depth = own_x.shape[0]
    largest = None
    each = hidden[0][0].shape[0]
    for x in range(PAIR):
        for k in range(each):
            block = (k ^ (z % each)) * PAIR + (side ^ x)
            for j in range(ranks):
                for half in range(PAIR):
                    cut = slice(half * depth, (half + 1) * depth)
                    values = hidden[x][j][k, :, cut].astype(jnp.float32)
                    scaled = jnp.clip(values * factor, -quant_range, quant_range)
                    quant_ref[half, block, j] = scaled.astype(jnp.bfloat16)
                    top = jnp.max(jnp.abs(values).reshape(-1, ROWS, depth), axis=0)
                    largest = top if largest is None else jnp.maximum(largest, top)
    width = largest_ref.shape[1]
    top = largest[:, :width]
    for at in range(width, depth, width):
        top = jnp.maximum(top, largest[:, at : at + width])

    @pl.when(step == 0)
    def _():
        largest_ref[...] = top

    @pl.when(step > 0)
    def _():
        largest_ref[...] = jnp.maximum(largest_ref[...], top)

    rows = quant_ref.shape[1] * quant_ref.shape[2] * quant_ref.shape[3]
    near = quant_ref[side].reshape(rows, depth)
    far = quant_ref[1 - side].reshape(rows, depth)

    def both(own, other):
        return jnp.dot(near, own, preferred_element_type=jnp.float32) + jnp.dot(
            far, other, preferred_element_type=jnp.float32
        )

    at_rows = pl.ds(pl.multiple_of(step * rows, rows), rows)
    dt_buf[...] = both(own_dt[...], other_dt[...]).T[: LINE * ROWS].reshape(dt_buf.shape)
    channels = x_refs[0].shape[1]
    tokens = pl.num_programs(0) * rows
    extra = rows // channels * ROWS
    upper = lax.broadcasted_iota(jnp.int32, (ROWS, channels), 0) < ROWS // 2
    for m in reversed(range(LINE)):
        owner = z ^ m
        cut = pl.ds(pl.multiple_of(owner * channels, channels), channels)
        x_refs[m][at_rows] = both(own_x[:, cut], other_x[m][...]).astype(jnp.bfloat16)
        dt = dt_buf[owner]
        pieces = [
            split_parts(dt[:, at : at + channels], upper) for at in range(0, rows, channels)
        ]
        x_refs[m][pl.ds(pl.multiple_of(tokens + step * extra, 16), extra)] = jnp.concatenate(
            pieces, axis=0
        ).astype(jnp.bfloat16)
    bc_ref[at_rows] = both(own_bc[...], other_bc[...]).astype(jnp.bfloat16)


def split_parts(values, upper):
    top = values.astype(jnp.bfloat16).astype(jnp.float32)
    return jnp.where(upper, top, values - top)


def project(place, factor, hidden, w_x, weights, part):
    line, own, wide = hidden[0].shape
    ranks = len(hidden) // PAIR
    depth, channels = weights[0].shape
    maps_wide = weights[LINE].shape[1]
    x_wide = channels * LINE
    steps = 1
    each = line // PARTS
    tokens = each * PAIR * ranks * own
    extra = tokens // channels * ROWS

    def fixed(array):
        return pl.BlockSpec(array.shape, lambda i, p: (0,) * array.ndim)

    payload = jax.ShapeDtypeStruct((tokens + extra, channels), jnp.bfloat16)
    maps = jax.ShapeDtypeStruct((tokens, maps_wide), jnp.bfloat16)
    largest = jax.ShapeDtypeStruct((ROWS, 128), jnp.float32)
    outs = [payload] * LINE + [maps, largest]
    rows_of = pl.BlockSpec((each, own, wide), lambda i, p: (part ^ (p[2] // each), 0, 0))
    return pl.pallas_call(
        functools.partial(project_kernel, ranks),
        grid_spec=pltpu.PrefetchScalarGridSpec(
            num_scalar_prefetch=1,
            grid=(steps,),
            in_specs=[SMEM]
            + [rows_of] * (PAIR * ranks)
            + [pl.BlockSpec((depth, x_wide), lambda i, p: (0, p[1]))]
            + [fixed(w) for w in weights],
            out_specs=[fixed(out) for out in outs],
            scratch_shapes=[
                pltpu.VMEM((PAIR, each * PAIR, ranks, own, depth), jnp.bfloat16),
                pltpu.VMEM((LINE, ROWS, tokens // steps), jnp.float32),
            ],
        ),
        out_shape=outs,
        compiler_params=pltpu.CompilerParams(vmem_limit_bytes=26 * 2**20),
        cost_estimate=pl.CostEstimate(
            flops=2 * tokens * wide * (x_wide + maps_wide),
            bytes_accessed=2 * tokens * (wide + x_wide),
            transcendentals=0,
        ),
        name="project",
    )(place, factor, *hidden, w_x, *weights)


def onward_kernel(own_ref, received_ref, out_ref):
    rows, channels = own_ref.shape
    tokens = rows * channels // (channels + ROWS)
    total = own_ref[:tokens].astype(jnp.float32) + received_ref[:tokens].astype(jnp.float32)
    out_ref[:tokens] = total.astype(jnp.bfloat16)
    upper = lax.broadcasted_iota(jnp.int32, (ROWS, channels), 0) < ROWS // 2
    extra = own_ref[tokens:].astype(jnp.float32) + received_ref[tokens:].astype(jnp.float32)
    pieces = []
    for at in range(0, rows - tokens, ROWS):
        piece = extra[at : at + ROWS]
        pieces.append(split_parts(piece + pltpu.roll(piece, ROWS // 2, 0), upper))
    out_ref[tokens:] = jnp.concatenate(pieces, axis=0).astype(jnp.bfloat16)


def onward(own, received):
    whole = pl.BlockSpec(own.shape, lambda: (0, 0))
    return pl.pallas_call(
        onward_kernel,
        in_specs=[whole, whole],
        out_specs=whole,
        out_shape=jax.ShapeDtypeStruct(own.shape, own.dtype),
        compiler_params=pltpu.CompilerParams(vmem_limit_bytes=8 * 2**20),
        cost_estimate=pl.CostEstimate(
            flops=own.size, bytes_accessed=6 * own.size, transcendentals=0
        ),
        name="onward",
    )(own, received)


def scan_kernel(first, place_ref, scale_ref, *refs):
    x_refs, bc_refs = (refs[:4], refs[4:7])
    small_ref, largest_ref, carry_ref, out_ref, carry_out_ref, x_buf, bc_buf = refs[7:]
    tokens, channels = bc_refs[0].shape
    blocks = tokens // SPAN
    heads = channels // HEAD_DIM
    rank, z = (place_ref[0], place_ref[2])
    ranks = place_ref.shape[0] - 3
    own = SPAN // ranks
    edge = ROWS
    in_scale = scale_ref[0]
    at_end = (z == 0) | (z == LINE - 1)
    if first:
        x_buf[:edge] = small_ref[:edge]
        bc_buf[:edge] = small_ref[edge : 2 * edge]
        state = carry_ref[...].T
    else:
        x_buf[:edge] = carry_ref[STATE : STATE + edge]
        bc_buf[:edge] = carry_ref[STATE + edge :]
        state = carry_ref[:STATE]

    for block in range(blocks):
        for true_rank in range(ranks):
            source = block * SPAN + (true_rank ^ rank) * own
            source = pl.ds(pl.multiple_of(source, own), own)
            at = edge + block * SPAN + true_rank * own
            at = slice(at, at + own)
            total = sum(ref[source].astype(jnp.float32) for ref in x_refs) * in_scale
            x_buf[at] = total.astype(jnp.bfloat16).astype(jnp.float32)
            near, far, done = (ref[source].astype(jnp.float32) for ref in bc_refs)
            total = ((near + far) * in_scale).astype(jnp.bfloat16).astype(jnp.float32)
            bc_buf[at] = jnp.where(at_end, done, total)

    taps = 2 * edge

    def activate(buf, row, block):
        start = edge - (KERNEL - 1) + block * SPAN
        summed = small_ref[row : row + 1] * buf[start : start + SPAN]
        for k in range(1, KERNEL):
            summed = summed + small_ref[row + k : row + k + 1] * buf[start + k : start + k + SPAN]
        return (summed / (1.0 + jnp.exp(-summed))).astype(jnp.bfloat16)

    skip = small_ref[taps + 2 * KERNEL : taps + 2 * KERNEL + 1]
    gain = small_ref[taps + 2 * KERNEL + 1 : taps + 2 * KERNEL + 2]
    bias = small_ref[4 * edge :, :SPAN]
    rate = small_ref[4 * edge :, SPAN:]

    up = lax.broadcasted_iota(jnp.int32, (SPAN, SPAN), 0)
    across = lax.broadcasted_iota(jnp.int32, (SPAN, SPAN), 1)
    lane = lax.broadcasted_iota(jnp.int32, (SPAN, channels), 1)
    lower = up >= across
    upper = (up <= across).astype(jnp.float32)
    lanes = across[:ROWS]

    dt = sum(ref[tokens:].astype(jnp.float32) for ref in x_refs)
    steps = []
    wide = channels // SPAN
    for block in range(blocks):
        tile = dt[block // wide * ROWS : (block // wide + 1) * ROWS]
        cut = tile[:, block % wide * SPAN : (block % wide + 1) * SPAN]
        cut = (cut + pltpu.roll(cut, ROWS // 2, 0)) * in_scale
        bit = 1
        while bit < ranks:
            shift = bit * own
            flipped = jnp.where(
                (lanes // shift) % 2 == 1,
                pltpu.roll(cut, shift, 1),
                pltpu.roll(cut, SPAN - shift, 1),
            )
            cut = jnp.where((rank & bit) != 0, flipped, cut)
            bit *= 2
        raw = cut + bias
        steps.append(jnp.maximum(raw, 0.0) + jnp.log1p(jnp.exp(-jnp.abs(raw))))
    drops = jnp.concatenate([-step * rate for step in steps], axis=0)
    cums = jnp.dot(drops, upper, precision=HIGHEST, preferred_element_type=jnp.float32)

    sums = jnp.zeros((SPAN, SPAN), jnp.float32)
    for block in range(blocks):
        x_act = activate(x_buf, taps, block)
        bc_act = activate(bc_buf, taps + KERNEL, block)
        in_map, out_map = (bc_act[:, :STATE], bc_act[:, STATE:])
        step, cum = (steps[block], cums[block * ROWS : (block + 1) * ROWS])
        last = cum[:, SPAN - 1 : SPAN]
        turned = jnp.concatenate(
            [
                cum,
                step * jnp.exp(last - cum),
                jnp.exp(cum),
                jnp.zeros((SPAN - 3 * ROWS, SPAN), jnp.float32),
            ],
            axis=0,
        ).T

        def spread(row):
            result = jnp.broadcast_to(turned[:, row : row + 1], (SPAN, channels))
            for h in range(1, heads):
                result = jnp.where(lane >= h * HEAD_DIM, turned[:, row + h : row + h + 1], result)
            return result

        inner = jnp.where(lower, nt_dot(out_map, in_map), 0.0)
        x_wide = x_act.astype(jnp.float32)
        weights, spaced = ([], [])
        for h in range(heads):
            gap = jnp.where(lower, turned[:, h : h + 1] - cum[h : h + 1], 0.0)
            weights.append((inner * jnp.exp(gap) * step[h : h + 1]).astype(jnp.bfloat16))
            inside = (lane >= h * HEAD_DIM) & (lane < (h + 1) * HEAD_DIM)
            spaced.append(jnp.where(inside, x_wide, 0.0).astype(jnp.bfloat16))
        local_part = jnp.dot(
            jnp.concatenate(weights, axis=1),
            jnp.concatenate(spaced, axis=0),
            preferred_element_type=jnp.float32,
        )
        grown = spread(2 * ROWS)
        x_weighted = (x_wide * spread(ROWS)).astype(jnp.bfloat16)
        added = lax.dot_general(
            in_map, x_weighted, (((0,), (0,)), ((), ())), preferred_element_type=jnp.float32
        )
        high = state.astype(jnp.bfloat16)
        rest = state - high.astype(jnp.float32)
        middle = rest.astype(jnp.bfloat16)
        low = (rest - middle.astype(jnp.float32)).astype(jnp.bfloat16)
        carried = jnp.dot(out_map, high, preferred_element_type=jnp.float32)
        carried = carried + jnp.dot(out_map, middle, preferred_element_type=jnp.float32)
        carried = carried + jnp.dot(out_map, low, preferred_element_type=jnp.float32)
        ssm_out = local_part + grown * carried + skip * x_wide
        state = grown[SPAN - 1 : SPAN] * state + added
        out_ref[block * SPAN : (block + 1) * SPAN] = (ssm_out * gain).astype(jnp.bfloat16)
        summed = jnp.sum(ssm_out * ssm_out, axis=1, keepdims=True)
        sums = jnp.where(across == block, summed, sums)

    whole = sums.T[:ROWS]
    top = whole.astype(jnp.bfloat16).astype(jnp.float32)
    largest = jnp.broadcast_to(jnp.max(largest_ref[...]), (ROWS, channels))
    extra = jnp.concatenate([jnp.concatenate([top, whole - top], axis=1), largest], axis=0)
    out_ref[tokens:] = extra.astype(jnp.bfloat16)
    carry_out_ref[:STATE] = state
    carry_out_ref[STATE : STATE + edge] = x_buf[tokens : tokens + edge]
    carry_out_ref[STATE + edge :] = bc_buf[tokens : tokens + edge]


def scan(place, in_scale, sums, maps, small, largest, carry, first):
    channels = sums[0].shape[1]
    tokens = maps[0].shape[0]

    def fixed(array):
        return pl.BlockSpec(array.shape, lambda i, p: (0, 0))

    held = pl.BlockSpec((channels, STATE), lambda i, p: (p[1] * LINE + p[2], 0))
    outs = [
        jax.ShapeDtypeStruct((tokens + 2 * ROWS, channels), jnp.bfloat16),
        jax.ShapeDtypeStruct((STATE + 2 * ROWS, channels), jnp.float32),
    ]
    return pl.pallas_call(
        functools.partial(scan_kernel, first),
        grid_spec=pltpu.PrefetchScalarGridSpec(
            num_scalar_prefetch=1,
            grid=(1,),
            in_specs=[SMEM]
            + [fixed(array) for array in (*sums, *maps, small, largest)]
            + [held if first else fixed(carry)],
            out_specs=[fixed(out) for out in outs],
            scratch_shapes=[
                pltpu.VMEM((tokens + ROWS, channels), jnp.float32),
                pltpu.VMEM((tokens + ROWS, 2 * STATE), jnp.float32),
            ],
        ),
        out_shape=outs,
        compiler_params=pltpu.CompilerParams(vmem_limit_bytes=20 * 2**20),
        cost_estimate=pl.CostEstimate(
            flops=8 * tokens * SPAN * channels,
            bytes_accessed=8 * tokens * channels,
            transcendentals=tokens * (channels + 8 * SPAN),
        ),
        name="scan",
    )(place, in_scale, *sums, *maps, small, largest, carry)


def by_heads(
    hidden_in,
    prev_amax,
    w_x,
    w_bc,
    w_dt,
    conv_x,
    conv_bc,
    conv_state_x,
    conv_state_bc,
    dt_bias,
    decay_rate,
    skip,
    init_state,
    norm_gain,
    w_out,
):
    margin = KERNEL - 1
    count, here = (lax.axis_size("seq"), lax.axis_index("seq"))
    ranks, rank = (lax.axis_size("tensor"), lax.axis_index("tensor"))
    z, side = (here // PAIR, here % PAIR)
    place_of = side * LINE + z
    f32, bf16 = (jnp.float32, jnp.bfloat16)
    own, width = hidden_in.shape
    depth = w_x.shape[0]
    channels = w_x.shape[1] // count
    heads_here = w_dt.shape[1] // count
    in_scale = (prev_amax / quant_range).reshape(1)
    factor = (quant_range / prev_amax).reshape(1)
    place = jnp.stack([rank, side, z] + [rank] * ranks).astype(jnp.int32)

    def pick(array, axis, index):
        return lax.dynamic_index_in_dim(array, index, axis, keepdims=False)

    def along(value, pairs):
        moves = [(a * PAIR + x, b * PAIR + x) for a, b in pairs for x in range(PAIR)]
        return lax.ppermute(value, "seq", moves)

    def across(value):
        return lax.ppermute(value, "seq", [(s, s ^ 1) for s in range(count)])

    other_side = (1 - side) * LINE
    sent = [
        lax.dynamic_slice_in_dim(w_x, (other_side + (z ^ m)) * channels, channels, axis=1)
        for m in reversed(range(LINE))
    ]
    sent[0], hidden_in = lax.optimization_barrier((sent[0], hidden_in))
    maps_sent = pick(w_bc, 1, 1 - side).reshape(depth, 2 * STATE)
    sent.insert(LINE // 2, maps_sent)
    swapped = []
    for value in sent:
        if swapped:
            swapped[-1], value = lax.optimization_barrier((swapped[-1], value))
        swapped.append(across(value))
    bc_other = swapped.pop(LINE // 2)
    swapped.reverse()
    bc_own = pick(w_bc, 1, side).reshape(depth, 2 * STATE)
    dt_columns = w_dt.reshape(depth, PAIR, LINE, 1, heads_here)
    dt_columns = jnp.broadcast_to(
        dt_columns, (depth, PAIR, LINE, ROWS // heads_here, heads_here)
    ).reshape(depth, PAIR, LINE * ROWS)
    dt_columns = jnp.pad(dt_columns, ((0, 0), (0, 0), (0, SPAN - LINE * ROWS)))
    dt_own = pick(dt_columns, 1, side)
    dt_other = across(pick(dt_columns, 1, 1 - side))

    cut = hidden_in.reshape(own, LINE, PAIR * depth)
    pieces = [pick(cut, 1, z ^ m) for m in range(LINE)]
    arrived = [pieces[0]]
    for m in range(1, LINE):
        arrived.append(along(pieces[m], [(s, s ^ m) for s in range(LINE)]))
    stacked = jnp.stack(arrived)
    rows = []
    for mine in (stacked, across(stacked)):
        ours = [mine]
        for j in range(1, ranks):
            bit = j & -j
            pairs = [(t, t ^ bit) for t in range(ranks)]
            ours.append(lax.ppermute(ours[j - bit], "tensor", pairs))
        rows.extend(ours)

    def of_heads(array):
        return jnp.repeat(array, HEAD_DIM)[None]

    by_channel = jnp.concatenate(
        [conv_state_x.astype(f32), conv_x, of_heads(skip), norm_gain[None]], axis=0
    )
    by_channel = lax.dynamic_slice_in_dim(by_channel, place_of * channels, channels, axis=1)
    by_map = jnp.concatenate([conv_state_bc.astype(f32), conv_bc], axis=0)
    by_map = pick(by_map, 1, side).reshape(margin + KERNEL, 2 * STATE)
    by_head = jnp.stack([dt_bias, decay_rate]).reshape(2, count, heads_here)
    by_head = jnp.tile(pick(by_head, 1, place_of).T, (ROWS // heads_here, 1))
    by_head = jnp.repeat(by_head, SPAN, axis=1)
    blank = jnp.zeros((ROWS - margin, channels), f32)
    small = jnp.concatenate(
        [
            blank,
            by_channel[:margin],
            blank,
            by_map[:margin],
            by_channel[margin : margin + KERNEL],
            by_map[margin:],
            by_channel[margin + KERNEL :],
            jnp.zeros((2 * ROWS - 2 * KERNEL - 2, channels), f32),
            by_head,
        ],
        axis=0,
    )

    start, end = (0, LINE - 1)
    at_end = (z == start) | (z == end)
    next_start, next_end = (1, LINE - 2)
    inward = [(start, next_start), (end, next_end)]
    outward = [(next_start, start), (next_end, end)]
    middle = [(next_start, next_end), (next_end, next_start)]
    over_middle = [(next_start, end), (next_end, start)]
    beside_pairs = [(s, s ^ 1) for s in range(LINE)]
    tie = lax.optimization_barrier
    weights = (*swapped, bc_own, bc_other, dt_own, dt_other)
    parts = [project(place, factor, rows, w_x, weights, part) for part in range(PARTS)]
    sends = []
    for mine, near, over, far, maps, largest in parts:
        sends.append(
            (
                along(maps, inward),
                along(far, inward),
                along(over, inward),
                along(near, beside_pairs),
            )
        )
    carry = init_state.reshape(-1, STATE)
    scanned = []
    for part, (mine, near, over, far, maps, largest) in enumerate(parts):
        map_hop, hop_far, hop_over, got_near = sends[part]
        if part:
            map_hop, unused = tie((map_hop, scanned[-1]))
        map_sum = (maps.astype(f32) + map_hop.astype(f32)).astype(bf16)
        map_far = along(map_sum, middle)
        map_done = ((map_sum.astype(f32) + map_far.astype(f32)) * in_scale).astype(bf16)
        sent_end = onward(over, hop_far)
        got_end = along(sent_end, over_middle)
        hop_over, unused = tie((hop_over, sent_end))
        got_next = along(onward(far, hop_over), middle)
        map_done, got_near, got_end = tie((map_done, got_near, got_end))
        map_done = along(map_done, outward)
        if part + 1 < PARTS:
            map_done, ahead = tie((map_done, sends[part + 1][0]))
            sends[part + 1] = (ahead, *sends[part + 1][1:])
        gained, carry = scan(
            place,
            in_scale,
            [mine, got_near, got_end, got_next],
            [map_sum, map_far, map_done],
            small,
            largest,
            carry,
            part == 0,
        )
        scanned.append(gained)
    two, three = (jnp.where(at_end, 2, 3), jnp.where(at_end, 3, 2))
    wide = w_out.shape[1]
    totals, top = ([], None)
    for gained in scanned:
        tokens = gained.shape[0] - 2 * ROWS
        blocks = tokens // SPAN
        beside = along(gained, beside_pairs)
        facing = along(gained, middle)
        beyond = along(beside, middle)
        second = jnp.where(at_end, along(facing, outward), facing)
        third = jnp.where(at_end, along(beyond, outward), beyond)
        far_own = across(gained)
        far_beside = across(beside)
        second, far_own = tie((second, far_own))
        far_second = across(second)
        third, far_beside = tie((third, far_beside))
        far_third = across(third)
        got = (
            (0, (gained, far_own)),
            (1, (beside, far_beside)),
            (two, (second, far_second)),
            (three, (third, far_third)),
        )
        total = squares = None
        for m, pair in got:
            for x, piece in enumerate(pair):
                at = ((side ^ x) * LINE + (z ^ m)) * channels
                w_rows = lax.dynamic_slice_in_dim(w_out, at, channels, axis=0)
                product = jnp.dot(piece, w_rows, preferred_element_type=f32)
                tail = piece[tokens:].astype(f32)
                low, high = (tail[:ROWS, :SPAN] + tail[:ROWS, SPAN:], tail[ROWS:, :SPAN])
                total = product if total is None else total + product
                squares = low if squares is None else squares + low
                top = high if top is None else jnp.maximum(top, high)
        kept = total[:tokens].reshape(blocks, ranks, own, wide)
        bit = 1
        while bit < ranks:
            pairs = [(t, t ^ bit) for t in range(ranks)]
            squares = squares + lax.ppermute(squares, "tensor", pairs)
            keeps = (rank // bit) % 2
            halves = kept.reshape(blocks, -1, 2, own, wide)
            received = lax.ppermute(pick(halves, 2, 1 - keeps).astype(bf16), "tensor", pairs)
            kept = pick(halves, 2, keeps) + received.astype(f32)
            bit *= 2
        mean_sq = squares[:blocks].reshape(blocks, ranks, own) / (HEADS * HEAD_DIM)
        factors = lax.rsqrt(pick(mean_sq, 1, rank) + epsilon)
        totals.append((kept.reshape(blocks, own, wide) * factors[:, :, None]).astype(bf16))
    final = jnp.concatenate(totals, axis=0)
    final = lax.all_to_all(final, "seq", split_axis=0, concat_axis=0, tiled=True)
    layer_out = final.transpose(1, 0, 2).reshape(own, count * wide)
    return (layer_out, jnp.max(top))


def solution(mesh):
    return jax.shard_map(
        by_heads if splits(mesh) else by_tokens,
        mesh=mesh,
        in_specs=(
            P(("seq", "tensor"), None),
            P(),
            P("seq", "tensor"),
            P("seq", "tensor", None, None),
            P("seq", "tensor"),
            P(None, "tensor"),
            P(None, "tensor", None, None),
            P(None, "tensor"),
            P(None, "tensor", None, None),
            P("tensor"),
            P("tensor"),
            P("tensor"),
            P("tensor", None, None),
            P("tensor"),
            P("tensor", "seq"),
        ),
        out_specs=(P(("seq", "tensor"), None), P()),
        check_vma=False,
    )
```

```python
import functools

import jax
import jax.numpy as jnp
from jax import lax
from jax.experimental import pallas as pl
from jax.experimental.pallas import tpu as pltpu
from jax.sharding import PartitionSpec as P

HEADS = 128
HEAD_DIM = 64
STATE = 128
GROUPS = 8
KERNEL = 4
SPAN = 128


epsilon = 1e-05
quant_range = 448.0


def from_behind(value, axis, steps):
    count = lax.axis_size(axis)
    first, last = (max(0, -steps), min(count, count - steps))
    return lax.ppermute(value, axis, [(source, source + steps) for source in range(first, last)])


def carried_in(shard, axis, combine, identity):
    count, here = (lax.axis_size(axis), lax.axis_index(axis))
    everything = jax.tree.map(
        lambda part, kind: lax.all_gather(part.astype(kind), axis),
        shard,
        (jnp.bfloat16, jnp.bfloat16),
    )
    start = jax.tree.map(
        lambda part, zero: jnp.broadcast_to(jnp.asarray(zero, part.dtype), part.shape),
        shard,
        identity,
    )

    def turn(k, before):
        reached = k < here
        new = combine(
            before, jax.tree.map(lambda part, own: part[k].astype(own.dtype), everything, shard)
        )
        return jax.tree.map(lambda a, b: jnp.where(reached, a, b), new, before)

    return lax.fori_loop(0, count, turn, start)


def depthwise(before, projected, conv_taps, length):
    extended = jnp.concatenate([before, projected], axis=0)
    summed = conv_taps[0] * extended[0:length]
    for offset in range(1, KERNEL):
        summed = summed + conv_taps[offset] * extended[offset : offset + length]
    return jax.nn.silu(summed).astype(jnp.bfloat16)


def combine(earlier, later):
    return (earlier[0] * later[0], later[0][:, None, None] * earlier[1] + later[1])


def by_tokens(
    hidden_in,
    prev_amax,
    w_x,
    w_bc,
    w_dt,
    conv_x,
    conv_bc,
    conv_state_x,
    conv_state_bc,
    dt_bias,
    decay_rate,
    skip,
    init_state,
    norm_gain,
    w_out,
):
    margin = KERNEL - 1
    gathered = lax.all_gather(hidden_in, "tensor", axis=0, tiled=True)
    abs_max = lax.pmax(jnp.max(jnp.abs(gathered.astype(jnp.float32))), "seq")
    in_scale = prev_amax / quant_range
    leading = lax.axis_index("seq") == 0
    row_count = gathered.shape[0]
    bc_width = w_bc.shape[1] * w_bc.shape[2] * w_bc.shape[3]
    bc_rows = jnp.reshape(w_bc, (w_bc.shape[0], bc_width))
    scaled = gathered.astype(jnp.float32) * (quant_range / prev_amax)
    quant = jnp.clip(scaled, -quant_range, quant_range).astype(jnp.bfloat16)
    pieces = (
        lax.all_gather(w_x, "seq", axis=0, tiled=True),
        lax.all_gather(bc_rows, "seq", axis=0, tiled=True),
        lax.all_gather(w_dt, "seq", axis=0, tiled=True),
    )
    x_proj, bc_proj, dt_proj = tuple(
        (
            jnp.dot(quant, weight_piece, preferred_element_type=jnp.float32)
            for weight_piece in pieces
        )
    )
    x_whole = (x_proj * in_scale).astype(jnp.bfloat16)
    bc_whole = (bc_proj * in_scale).astype(jnp.bfloat16)
    dt_raw = dt_proj * in_scale
    state_bc = jnp.reshape(conv_state_bc, (margin, bc_width))
    received = from_behind(
        (x_whole[row_count - margin :], bc_whole[row_count - margin :]), "seq", 1
    )
    x_edge = jnp.where(leading, conv_state_x, received[0])
    bc_edge = jnp.where(leading, state_bc, received[1])
    x_act = depthwise(x_edge, x_whole, conv_x, row_count)
    bc_act = depthwise(bc_edge, bc_whole, jnp.reshape(conv_bc, (KERNEL, bc_width)), row_count)
    step_size = jax.nn.softplus(dt_raw + dt_bias)
    heads_here = step_size.shape[1]
    groups_here = w_bc.shape[1]
    per_group = HEADS // GROUPS
    blocks = row_count // SPAN
    x_blocks = x_act.reshape(blocks, SPAN, heads_here, HEAD_DIM)
    bc_blocks = bc_act.reshape(blocks, SPAN, groups_here, 2, STATE)
    in_map = bc_blocks[:, :, :, 0]
    out_map = bc_blocks[:, :, :, 1]
    step_blocks = step_size.reshape(blocks, SPAN, heads_here)
    cum_blocks = jnp.cumsum(-step_blocks * decay_rate, axis=1)
    index_row = jnp.arange(SPAN, dtype=jnp.int32)
    lower_mask = index_row[:, None] >= index_row[None, :]
    intersection = jnp.einsum(
        "ctgn,cugn->cgtu", out_map, in_map, preferred_element_type=jnp.float32
    )
    intersection = jnp.repeat(intersection, per_group, axis=1)
    cum_heads = jnp.transpose(cum_blocks, (0, 2, 1))
    log_gap = cum_heads[:, :, :, None] - cum_heads[:, :, None, :]
    decay = jnp.exp(jnp.where(lower_mask[None, None], log_gap, -1e30))
    step_heads = jnp.transpose(step_blocks, (0, 2, 1))
    weights = (intersection * decay * step_heads[:, :, None, :]).astype(jnp.bfloat16)
    local_part = jnp.einsum(
        "chtu,cuhp->cthp", weights, x_blocks, preferred_element_type=jnp.float32
    )
    last_cum = cum_blocks[:, SPAN - 1, :]
    x_weighted = (
        x_blocks.astype(jnp.float32)
        * (step_blocks * jnp.exp(last_cum[:, None, :] - cum_blocks))[:, :, :, None]
    ).astype(jnp.bfloat16)
    in_heads = jnp.repeat(in_map, per_group, axis=2)
    added = jnp.einsum("cuhp,cuhn->chpn", x_weighted, in_heads, preferred_element_type=jnp.float32)

    def carry_on(carried, element):
        block_decay, block_added = element
        return (block_decay[:, None, None] * carried + block_added, carried)

    empty_state = jnp.zeros((heads_here, HEAD_DIM, STATE), jnp.float32)
    device_state, entering = lax.scan(carry_on, empty_state, (jnp.exp(last_cum), added))
    device_decay = jnp.exp(jnp.sum(last_cum, axis=0))
    seeded = device_state + jnp.where(leading, device_decay[:, None, None] * init_state, 0.0)
    identity = (jnp.ones_like(device_decay), jnp.zeros_like(device_state))
    scanned = carried_in((device_decay, seeded), "seq", combine, identity)
    incoming = jnp.where(leading, init_state, scanned[1])
    prefix = jnp.exp(jnp.cumsum(last_cum, axis=0) - last_cum)
    states_in = entering + prefix[:, :, None, None] * incoming[None]
    out_heads = jnp.repeat(out_map, per_group, axis=2).astype(jnp.float32)
    carried_part = (
        jnp.einsum("cthn,chpn->cthp", out_heads, states_in, precision=lax.Precision.HIGHEST)
        * jnp.exp(cum_blocks)[:, :, :, None]
    )
    ssm_out = local_part + carried_part + skip[None, None, :, None] * x_blocks.astype(jnp.float32)
    ssm_out = ssm_out.reshape(row_count, heads_here * HEAD_DIM)
    squares = lax.psum(jnp.sum(ssm_out * ssm_out, axis=1), "tensor")
    mean_sq = squares / (HEADS * HEAD_DIM)
    normed = (ssm_out * lax.rsqrt(mean_sq + epsilon)[:, None] * norm_gain).astype(jnp.bfloat16)
    partial_out = jnp.dot(
        normed, lax.all_gather(w_out, "seq", axis=1, tiled=True), preferred_element_type=jnp.float32
    )
    layer_out = lax.psum_scatter(
        partial_out.astype(jnp.bfloat16), "tensor", scatter_dimension=0, tiled=True
    )
    return (layer_out, abs_max)


PAIR = 2
LINE = 4
ROWS = 8
SMEM = pl.BlockSpec(memory_space=pltpu.SMEM)
HIGHEST = lax.Precision.HIGHEST


def splits(mesh):
    count, ranks = (mesh.shape["seq"], mesh.shape["tensor"])
    heads_all, groups_here = (HEADS // ranks, GROUPS // ranks)
    if count != PAIR * LINE or groups_here != PAIR or ranks & (ranks - 1):
        return False
    heads_here = heads_all // count
    return 2 * heads_here == ROWS and heads_here * HEAD_DIM == 2 * SPAN


def nt_dot(a, b, **kw):
    return lax.dot_general(
        a, b, (((1,), (1,)), ((), ())), preferred_element_type=jnp.float32, **kw
    )


def project_kernel(ranks, place_ref, factor_ref, *refs):
    hidden = [refs[x * ranks : (x + 1) * ranks] for x in range(PAIR)]
    refs = refs[PAIR * ranks :]
    own_x, x_near, x_far, own_bc, other_bc, own_dt, other_dt = refs[:7]
    x_refs = refs[7 : 7 + LINE]
    bc_ref, largest_ref, quant_ref, dt_buf = refs[7 + LINE :]
    side, z = (place_ref[1], place_ref[2])
    step = pl.program_id(0)
    factor = factor_ref[0]
    depth = own_x.shape[0]
    largest = None
    each = hidden[0][0].shape[0]
    for x in range(PAIR):
        for k in range(each):
            block = (k ^ (z % each)) * PAIR + (side ^ x)
            for j in range(ranks):
                for half in range(PAIR):
                    cut = slice(half * depth, (half + 1) * depth)
                    values = hidden[x][j][k, :, cut].astype(jnp.float32)
                    scaled = jnp.clip(values * factor, -quant_range, quant_range)
                    quant_ref[half, block, j] = scaled.astype(jnp.bfloat16)
                    top = jnp.max(jnp.abs(values).reshape(-1, ROWS, depth), axis=0)
                    largest = top if largest is None else jnp.maximum(largest, top)
    width = largest_ref.shape[1]
    top = largest[:, :width]
    for at in range(width, depth, width):
        top = jnp.maximum(top, largest[:, at : at + width])

    @pl.when(step == 0)
    def _():
        largest_ref[...] = top

    @pl.when(step > 0)
    def _():
        largest_ref[...] = jnp.maximum(largest_ref[...], top)

    rows = quant_ref.shape[1] * quant_ref.shape[2] * quant_ref.shape[3]
    near = quant_ref[side].reshape(rows, depth)
    far = quant_ref[1 - side].reshape(rows, depth)

    def both(own, other):
        return jnp.dot(near, own, preferred_element_type=jnp.float32) + jnp.dot(
            far, other, preferred_element_type=jnp.float32
        )

    at_rows = pl.ds(pl.multiple_of(step * rows, rows), rows)
    dt_rows = both(own_dt[...], other_dt[...])
    blank = jnp.zeros((rows, 128 - dt_rows.shape[1]), jnp.float32)
    dt_rows = jnp.concatenate([dt_rows, blank], axis=1).T
    dt_buf[...] = dt_rows[: dt_buf.shape[0] * ROWS].reshape(dt_buf.shape)
    channels = x_refs[0].shape[1]
    tokens = pl.num_programs(0) * rows
    extra = rows // channels * ROWS
    upper = lax.broadcasted_iota(jnp.int32, (ROWS, channels), 0) < ROWS // 2
    for m in reversed(range(LINE)):
        owner = z ^ m
        cut = pl.ds(pl.multiple_of(owner * channels, channels), channels)
        other = x_near if m < LINE // 2 else x_far
        inner = owner % (LINE // 2) * channels
        inner = pl.ds(pl.multiple_of(inner, channels), channels)
        x_refs[m][at_rows] = both(own_x[:, cut], other[:, inner]).astype(jnp.bfloat16)
        run = side * LINE + owner
        dt = dt_buf[run // 2]
        pieces = []
        for at in range(0, rows, channels):
            piece = dt[:, at : at + channels]
            turned = pltpu.roll(piece, ROWS // 2, 0)
            lower_run = jnp.where(upper, piece, turned)
            upper_run = jnp.where(upper, turned, piece)
            pieces.append(split_parts(jnp.where(run % 2 == 0, lower_run, upper_run), upper))
        x_refs[m][pl.ds(pl.multiple_of(tokens + step * extra, 16), extra)] = jnp.concatenate(
            pieces, axis=0
        ).astype(jnp.bfloat16)
    bc_ref[at_rows] = both(own_bc[...], other_bc[...]).astype(jnp.bfloat16)


def split_parts(values, upper):
    top = values.astype(jnp.bfloat16).astype(jnp.float32)
    return jnp.where(upper, top, values - top)


def project(place, factor, hidden, w_x, weights):
    line, own, wide = hidden[0].shape
    ranks = len(hidden) // PAIR
    depth, x_wide = (weights[0].shape[0], 2 * weights[0].shape[1])
    channels, maps_wide = (x_wide // LINE, weights[2].shape[1])
    steps = 2
    each = line // steps
    tokens = line * PAIR * ranks * own
    extra = tokens // channels * ROWS

    def fixed(array):
        return pl.BlockSpec(array.shape, lambda i, p: (0,) * array.ndim)

    payload = jax.ShapeDtypeStruct((tokens + extra, channels), jnp.bfloat16)
    maps = jax.ShapeDtypeStruct((tokens, maps_wide), jnp.bfloat16)
    largest = jax.ShapeDtypeStruct((ROWS, 128), jnp.float32)
    outs = [payload] * LINE + [maps, largest]
    rows_of = pl.BlockSpec((each, own, wide), lambda i, p: (i ^ (p[2] // each), 0, 0))
    return pl.pallas_call(
        functools.partial(project_kernel, ranks),
        grid_spec=pltpu.PrefetchScalarGridSpec(
            num_scalar_prefetch=1,
            grid=(steps,),
            in_specs=[SMEM]
            + [rows_of] * (PAIR * ranks)
            + [pl.BlockSpec((depth, x_wide), lambda i, p: (0, p[1]))]
            + [fixed(w) for w in weights],
            out_specs=[fixed(out) for out in outs],
            scratch_shapes=[
                pltpu.VMEM((PAIR, each * PAIR, ranks, own, depth), jnp.bfloat16),
                pltpu.VMEM((weights[-1].shape[1] // ROWS, ROWS, tokens // steps), jnp.float32),
            ],
        ),
        out_shape=outs,
        compiler_params=pltpu.CompilerParams(vmem_limit_bytes=26 * 2**20),
        cost_estimate=pl.CostEstimate(
            flops=2 * tokens * wide * (x_wide + maps_wide),
            bytes_accessed=2 * tokens * (wide + x_wide),
            transcendentals=0,
        ),
        name="project",
    )(place, factor, *hidden, w_x, *weights)


def onward_kernel(own_ref, received_ref, out_ref):
    rows, channels = own_ref.shape
    tokens = rows * channels // (channels + ROWS)
    total = own_ref[:tokens].astype(jnp.float32) + received_ref[:tokens].astype(jnp.float32)
    out_ref[:tokens] = total.astype(jnp.bfloat16)
    upper = lax.broadcasted_iota(jnp.int32, (ROWS, channels), 0) < ROWS // 2
    extra = own_ref[tokens:].astype(jnp.float32) + received_ref[tokens:].astype(jnp.float32)
    pieces = []
    for at in range(0, rows - tokens, ROWS):
        piece = extra[at : at + ROWS]
        pieces.append(split_parts(piece + pltpu.roll(piece, ROWS // 2, 0), upper))
    out_ref[tokens:] = jnp.concatenate(pieces, axis=0).astype(jnp.bfloat16)


def onward(own, received):
    whole = pl.BlockSpec(own.shape, lambda: (0, 0))
    return pl.pallas_call(
        onward_kernel,
        in_specs=[whole, whole],
        out_specs=whole,
        out_shape=jax.ShapeDtypeStruct(own.shape, own.dtype),
        compiler_params=pltpu.CompilerParams(vmem_limit_bytes=8 * 2**20),
        cost_estimate=pl.CostEstimate(
            flops=own.size, bytes_accessed=6 * own.size, transcendentals=0
        ),
        name="onward",
    )(own, received)


def scan_kernel(place_ref, scale_ref, *refs):
    x_refs, bc_refs = (refs[:4], refs[4:7])
    small_ref, largest_ref, state_ref, out_ref, x_buf, bc_buf = refs[7:]
    tokens, channels = bc_refs[0].shape
    blocks = tokens // SPAN
    heads = channels // HEAD_DIM
    rank, z = (place_ref[0], place_ref[2])
    ranks = place_ref.shape[0] - 3
    own = SPAN // ranks
    edge = ROWS
    in_scale = scale_ref[0]
    at_end = (z == 0) | (z == LINE - 1)
    x_buf[:edge] = small_ref[:edge]
    bc_buf[:edge] = small_ref[edge : 2 * edge]
    state = state_ref[...].T

    for block in range(blocks):
        for true_rank in range(ranks):
            source = block * SPAN + (true_rank ^ rank) * own
            source = pl.ds(pl.multiple_of(source, own), own)
            at = edge + block * SPAN + true_rank * own
            at = slice(at, at + own)
            total = sum(ref[source].astype(jnp.float32) for ref in x_refs) * in_scale
            x_buf[at] = total.astype(jnp.bfloat16).astype(jnp.float32)
            near, far, done = (ref[source].astype(jnp.float32) for ref in bc_refs)
            total = ((near + far) * in_scale).astype(jnp.bfloat16).astype(jnp.float32)
            bc_buf[at] = jnp.where(at_end, done, total)

    taps = 2 * edge

    def activate(buf, row, block):
        start = edge - (KERNEL - 1) + block * SPAN
        summed = small_ref[row : row + 1] * buf[start : start + SPAN]
        for k in range(1, KERNEL):
            summed = summed + small_ref[row + k : row + k + 1] * buf[start + k : start + k + SPAN]
        return (summed / (1.0 + jnp.exp(-summed))).astype(jnp.bfloat16)

    skip = small_ref[taps + 2 * KERNEL : taps + 2 * KERNEL + 1]
    gain = small_ref[taps + 2 * KERNEL + 1 : taps + 2 * KERNEL + 2]
    bias = small_ref[4 * edge :, :SPAN]
    rate = small_ref[4 * edge :, SPAN:]

    up = lax.broadcasted_iota(jnp.int32, (SPAN, SPAN), 0)
    across = lax.broadcasted_iota(jnp.int32, (SPAN, SPAN), 1)
    lane = lax.broadcasted_iota(jnp.int32, (SPAN, channels), 1)
    lower = up >= across
    upper = (up <= across).astype(jnp.float32)
    lanes = across[:ROWS]

    dt = sum(ref[tokens:].astype(jnp.float32) for ref in x_refs)
    steps = []
    wide = channels // SPAN
    for block in range(blocks):
        tile = dt[block // wide * ROWS : (block // wide + 1) * ROWS]
        cut = tile[:, block % wide * SPAN : (block % wide + 1) * SPAN]
        cut = (cut + pltpu.roll(cut, ROWS // 2, 0)) * in_scale
        bit = 1
        while bit < ranks:
            shift = bit * own
            flipped = jnp.where(
                (lanes // shift) % 2 == 1,
                pltpu.roll(cut, shift, 1),
                pltpu.roll(cut, SPAN - shift, 1),
            )
            cut = jnp.where((rank & bit) != 0, flipped, cut)
            bit *= 2
        raw = cut + bias
        steps.append(jnp.maximum(raw, 0.0) + jnp.log1p(jnp.exp(-jnp.abs(raw))))
    drops = jnp.concatenate([-step * rate for step in steps], axis=0)
    cums = jnp.dot(drops, upper, precision=HIGHEST, preferred_element_type=jnp.float32)

    sums = jnp.zeros((SPAN, SPAN), jnp.float32)
    for block in range(blocks):
        x_act = activate(x_buf, taps, block)
        bc_act = activate(bc_buf, taps + KERNEL, block)
        in_map, out_map = (bc_act[:, :STATE], bc_act[:, STATE:])
        step, cum = (steps[block], cums[block * ROWS : (block + 1) * ROWS])
        last = cum[:, SPAN - 1 : SPAN]
        turned = jnp.concatenate(
            [
                cum,
                step * jnp.exp(last - cum),
                jnp.exp(cum),
                jnp.zeros((SPAN - 3 * ROWS, SPAN), jnp.float32),
            ],
            axis=0,
        ).T

        def spread(row):
            result = jnp.broadcast_to(turned[:, row : row + 1], (SPAN, channels))
            for h in range(1, heads):
                result = jnp.where(lane >= h * HEAD_DIM, turned[:, row + h : row + h + 1], result)
            return result

        inner = jnp.where(lower, nt_dot(out_map, in_map), 0.0)
        x_wide = x_act.astype(jnp.float32)
        weights, spaced = ([], [])
        for h in range(heads):
            gap = jnp.where(lower, turned[:, h : h + 1] - cum[h : h + 1], 0.0)
            weights.append((inner * jnp.exp(gap) * step[h : h + 1]).astype(jnp.bfloat16))
            inside = (lane >= h * HEAD_DIM) & (lane < (h + 1) * HEAD_DIM)
            spaced.append(jnp.where(inside, x_wide, 0.0).astype(jnp.bfloat16))
        local_part = jnp.dot(
            jnp.concatenate(weights, axis=1),
            jnp.concatenate(spaced, axis=0),
            preferred_element_type=jnp.float32,
        )
        grown = spread(2 * ROWS)
        x_weighted = (x_wide * spread(ROWS)).astype(jnp.bfloat16)
        added = lax.dot_general(
            in_map, x_weighted, (((0,), (0,)), ((), ())), preferred_element_type=jnp.float32
        )
        high = state.astype(jnp.bfloat16)
        rest = (state - high.astype(jnp.float32)).astype(jnp.bfloat16)
        carried = jnp.dot(
            jnp.concatenate([out_map, out_map], axis=1),
            jnp.concatenate([high, rest], axis=0),
            preferred_element_type=jnp.float32,
        )
        ssm_out = local_part + grown * carried + skip * x_wide
        state = grown[SPAN - 1 : SPAN] * state + added
        out_ref[block * SPAN : (block + 1) * SPAN] = (ssm_out * gain).astype(jnp.bfloat16)
        summed = jnp.sum(ssm_out * ssm_out, axis=1, keepdims=True)
        sums = jnp.where(across == block, summed, sums)

    whole = sums.T[:ROWS]
    top = whole.astype(jnp.bfloat16).astype(jnp.float32)
    largest = jnp.broadcast_to(jnp.max(largest_ref[...]), (ROWS, channels))
    extra = jnp.concatenate([jnp.concatenate([top, whole - top], axis=1), largest], axis=0)
    out_ref[tokens:] = extra.astype(jnp.bfloat16)


def scan(place, in_scale, sums, maps, small, largest, state):
    channels = sums[0].shape[1]
    tokens = maps[0].shape[0]

    def fixed(array):
        return pl.BlockSpec(array.shape, lambda i, p: (0, 0))

    out = jax.ShapeDtypeStruct((tokens + 2 * ROWS, channels), jnp.bfloat16)
    return pl.pallas_call(
        scan_kernel,
        grid_spec=pltpu.PrefetchScalarGridSpec(
            num_scalar_prefetch=1,
            grid=(1,),
            in_specs=[SMEM]
            + [fixed(array) for array in (*sums, *maps, small, largest, state)],
            out_specs=fixed(out),
            scratch_shapes=[
                pltpu.VMEM((tokens + ROWS, channels), jnp.float32),
                pltpu.VMEM((tokens + ROWS, 2 * STATE), jnp.float32),
            ],
        ),
        out_shape=out,
        compiler_params=pltpu.CompilerParams(vmem_limit_bytes=20 * 2**20),
        cost_estimate=pl.CostEstimate(
            flops=8 * tokens * SPAN * channels,
            bytes_accessed=8 * tokens * channels,
            transcendentals=tokens * (channels + 8 * SPAN),
        ),
        name="scan",
    )(place, in_scale, *sums, *maps, small, largest, state)


def by_heads(
    hidden_in,
    prev_amax,
    w_x,
    w_bc,
    w_dt,
    conv_x,
    conv_bc,
    conv_state_x,
    conv_state_bc,
    dt_bias,
    decay_rate,
    skip,
    init_state,
    norm_gain,
    w_out,
):
    margin = KERNEL - 1
    count, here = (lax.axis_size("seq"), lax.axis_index("seq"))
    ranks, rank = (lax.axis_size("tensor"), lax.axis_index("tensor"))
    z, side = (here // PAIR, here % PAIR)
    place_of = side * LINE + z
    f32, bf16 = (jnp.float32, jnp.bfloat16)
    own, width = hidden_in.shape
    depth = w_x.shape[0]
    channels = w_x.shape[1] // count
    heads_here = w_dt.shape[1] // count
    in_scale = (prev_amax / quant_range).reshape(1)
    factor = (quant_range / prev_amax).reshape(1)
    place = jnp.stack([rank, side, z] + [rank] * ranks).astype(jnp.int32)

    def pick(array, axis, index):
        return lax.dynamic_index_in_dim(array, index, axis, keepdims=False)

    def along(value, pairs):
        moves = [(a * PAIR + x, b * PAIR + x) for a, b in pairs for x in range(PAIR)]
        return lax.ppermute(value, "seq", moves)

    def across(value):
        return lax.ppermute(value, "seq", [(s, s ^ 1) for s in range(count)])

    def of_heads(array):
        return jnp.repeat(array, HEAD_DIM)[None]

    by_channel = jnp.concatenate(
        [conv_state_x.astype(f32), conv_x, of_heads(skip), norm_gain[None]], axis=0
    )
    by_channel = lax.dynamic_slice_in_dim(by_channel, place_of * channels, channels, axis=1)
    by_map = jnp.concatenate([conv_state_bc.astype(f32), conv_bc], axis=0)
    by_map = pick(by_map, 1, side).reshape(margin + KERNEL, 2 * STATE)
    by_head = jnp.stack([dt_bias, decay_rate]).reshape(2, count, heads_here)
    by_head = jnp.tile(pick(by_head, 1, place_of).T, (ROWS // heads_here, 1))
    by_head = jnp.repeat(by_head, SPAN, axis=1)
    blank = jnp.zeros((ROWS - margin, channels), f32)
    small = jnp.concatenate(
        [
            blank,
            by_channel[:margin],
            blank,
            by_map[:margin],
            by_channel[margin : margin + KERNEL],
            by_map[margin:],
            by_channel[margin + KERNEL :],
            jnp.zeros((2 * ROWS - 2 * KERNEL - 2, channels), f32),
            by_head,
        ],
        axis=0,
    )

    start_state = lax.dynamic_slice_in_dim(
        init_state, place_of * heads_here, heads_here, axis=0
    ).reshape(channels, STATE)

    tie = lax.optimization_barrier
    half_run = LINE // 2 * channels
    opposite = (z // (LINE // 2)) ^ 1

    def columns(half):
        at = (1 - side) * 2 + half
        return lax.dynamic_slice_in_dim(w_x, at * half_run, half_run, axis=1)

    x_sent, hidden_in = tie((columns(opposite), hidden_in))
    x_far = across(x_sent)
    x_far, x_sent = tie((x_far, columns(1 - opposite)))
    x_near = across(x_sent)
    x_near, maps_sent, dt_sent = tie(
        (x_near, pick(w_bc, 1, 1 - side).reshape(depth, 2 * STATE), w_dt)
    )
    bc_other, dt_other = (across(maps_sent), across(dt_sent))
    bc_own = pick(w_bc, 1, side).reshape(depth, 2 * STATE)

    def line_columns(m):
        return lax.dynamic_slice_in_dim(hidden_in, (z ^ m) * PAIR * depth, PAIR * depth, axis=1)

    arrived = [line_columns(0)]
    for m in range(1, LINE):
        arrived.append(along(line_columns(m), [(s, s ^ m) for s in range(LINE)]))
    stacked = jnp.stack(arrived)
    beyond_pair = across(stacked)
    beyond_pair, small, start_state, bc_own = tie((beyond_pair, small, start_state, bc_own))
    rows = []
    for mine in (stacked, beyond_pair):
        ours = [mine]
        for j in range(1, ranks):
            bit = j & -j
            pairs = [(t, t ^ bit) for t in range(ranks)]
            ours.append(lax.ppermute(ours[j - bit], "tensor", pairs))
        rows.extend(ours)

    start, end = (0, LINE - 1)
    at_end = (z == start) | (z == end)
    next_start, next_end = (1, LINE - 2)
    inward = [(start, next_start), (end, next_end)]
    outward = [(next_start, start), (next_end, end)]
    middle = [(next_start, next_end), (next_end, next_start)]
    over_middle = [(next_start, end), (next_end, start)]
    beside_pairs = [(s, s ^ 1) for s in range(LINE)]
    weights = (x_near, x_far, bc_own, bc_other, w_dt, dt_other)
    mine, near, over, far, maps, largest = project(place, factor, rows, w_x, weights)

    map_hop = along(maps, inward)
    hop_far = along(far, inward)
    hop_over = along(over, inward)
    got_near = along(near, beside_pairs)
    map_sum = (maps.astype(f32) + map_hop.astype(f32)).astype(bf16)
    map_far = along(map_sum, middle)
    map_done = ((map_sum.astype(f32) + map_far.astype(f32)) * in_scale).astype(bf16)
    sent_end = onward(over, hop_far)
    got_end = along(sent_end, over_middle)
    hop_over, unused = tie((hop_over, sent_end))
    got_next = along(onward(far, hop_over), middle)
    map_done, got_near, got_end = tie((map_done, got_near, got_end))
    map_done = along(map_done, outward)
    gained = scan(
        place,
        in_scale,
        [mine, got_near, got_end, got_next],
        [map_sum, map_far, map_done],
        small,
        largest,
        start_state,
    )

    tokens = gained.shape[0] - 2 * ROWS
    run = tokens // 2
    beside = along(gained, beside_pairs)
    facing = along(gained, middle)
    second = jnp.where(at_end, along(facing, outward), facing)
    far_own = across(gained)
    far_beside = across(beside)
    second, far_own = tie((second, far_own))
    far_second = across(second)
    two, three = (jnp.where(at_end, 2, 3), jnp.where(at_end, 3, 2))
    got = (
        (0, 0, gained),
        (1, 0, far_own),
        (0, 1, beside),
        (1, 1, far_beside),
        (0, two, second),
        (1, two, far_second),
    )

    def rows_for(x, m):
        at = ((side ^ x) * LINE + (z ^ m)) * channels
        return lax.dynamic_slice_in_dim(w_out, at, channels, axis=0)

    total = None
    tails = []
    for x, m, piece in got:
        product = jnp.dot(piece, rows_for(x, m), preferred_element_type=f32)
        total = product if total is None else total + product
        tails.append(piece[tokens:])

    wide = w_out.shape[1]
    cuts = (slice(0, run), slice(run, tokens + 2 * ROWS))
    totals = []
    for cut in cuts:
        beyond = along(beside[cut], middle)
        third = jnp.where(at_end, along(beyond, outward), beyond)
        if cut is cuts[0]:
            third, far_beside = tie((third, far_beside))
        far_third = across(third)
        if cut is not cuts[0]:
            tails.extend([third[run:], far_third[run:]])
        partial = total[cut] + jnp.dot(third, rows_for(0, three), preferred_element_type=f32)
        partial, far_third = tie((partial, far_third))
        partial = partial + jnp.dot(far_third, rows_for(1, three), preferred_element_type=f32)
        kept = partial[:run].reshape(run // SPAN, ranks, own, wide)
        bit = 1
        while bit < ranks:
            pairs = [(t, t ^ bit) for t in range(ranks)]
            keeps = (rank // bit) % 2
            halves = kept.reshape(run // SPAN, -1, 2, own, wide)
            received = lax.ppermute(pick(halves, 2, 1 - keeps).astype(bf16), "tensor", pairs)
            kept = pick(halves, 2, keeps) + received.astype(f32)
            bit *= 2
        totals.append(kept.reshape(run // SPAN, own, wide))
    tails = [tail.astype(f32) for tail in tails]
    squares = sum(tail[:ROWS, :SPAN] + tail[:ROWS, SPAN:] for tail in tails)
    top = functools.reduce(jnp.maximum, [tail[ROWS:, :SPAN] for tail in tails])
    bit = 1
    while bit < ranks:
        squares = squares + lax.ppermute(squares, "tensor", [(t, t ^ bit) for t in range(ranks)])
        bit *= 2
    mean_sq = squares.reshape(count, ranks, own) / (HEADS * HEAD_DIM)
    factors = lax.rsqrt(pick(mean_sq, 1, rank) + epsilon)
    final = jnp.concatenate(totals, axis=0) * factors[:, :, None]
    final = lax.all_to_all(final.astype(bf16), "seq", split_axis=0, concat_axis=0, tiled=True)
    layer_out = final.transpose(1, 0, 2).reshape(own, count * wide)
    return (layer_out, jnp.max(top))


def solution(mesh):
    return jax.shard_map(
        by_heads if splits(mesh) else by_tokens,
        mesh=mesh,
        in_specs=(
            P(("seq", "tensor"), None),
            P(),
            P("seq", "tensor"),
            P("seq", "tensor", None, None),
            P("seq", "tensor"),
            P(None, "tensor"),
            P(None, "tensor", None, None),
            P(None, "tensor"),
            P(None, "tensor", None, None),
            P("tensor"),
            P("tensor"),
            P("tensor"),
            P("tensor", None, None),
            P("tensor"),
            P("tensor", "seq"),
        ),
        out_specs=(P(("seq", "tensor"), None), P()),
        check_vma=False,
    )
```

```python
import functools

import jax
import jax.numpy as jnp
from jax import lax
from jax.experimental import pallas as pl
from jax.experimental.pallas import tpu as pltpu
from jax.sharding import PartitionSpec as P

HEADS = 128
HEAD_DIM = 64
STATE = 128
GROUPS = 8
KERNEL = 4
SPAN = 128


epsilon = 1e-05
quant_range = 448.0


def from_behind(value, axis, steps):
    count = lax.axis_size(axis)
    first, last = (max(0, -steps), min(count, count - steps))
    return lax.ppermute(value, axis, [(source, source + steps) for source in range(first, last)])


def carried_in(shard, axis, combine, identity):
    count, here = (lax.axis_size(axis), lax.axis_index(axis))
    everything = jax.tree.map(
        lambda part, kind: lax.all_gather(part.astype(kind), axis),
        shard,
        (jnp.bfloat16, jnp.bfloat16),
    )
    start = jax.tree.map(
        lambda part, zero: jnp.broadcast_to(jnp.asarray(zero, part.dtype), part.shape),
        shard,
        identity,
    )

    def turn(k, before):
        reached = k < here
        new = combine(
            before, jax.tree.map(lambda part, own: part[k].astype(own.dtype), everything, shard)
        )
        return jax.tree.map(lambda a, b: jnp.where(reached, a, b), new, before)

    return lax.fori_loop(0, count, turn, start)


def depthwise(before, projected, conv_taps, length):
    extended = jnp.concatenate([before, projected], axis=0)
    summed = conv_taps[0] * extended[0:length]
    for offset in range(1, KERNEL):
        summed = summed + conv_taps[offset] * extended[offset : offset + length]
    return jax.nn.silu(summed).astype(jnp.bfloat16)


def combine(earlier, later):
    return (earlier[0] * later[0], later[0][:, None, None] * earlier[1] + later[1])


def by_tokens(
    hidden_in,
    prev_amax,
    w_x,
    w_bc,
    w_dt,
    conv_x,
    conv_bc,
    conv_state_x,
    conv_state_bc,
    dt_bias,
    decay_rate,
    skip,
    init_state,
    norm_gain,
    w_out,
):
    margin = KERNEL - 1
    gathered = lax.all_gather(hidden_in, "tensor", axis=0, tiled=True)
    abs_max = lax.pmax(jnp.max(jnp.abs(gathered.astype(jnp.float32))), "seq")
    in_scale = prev_amax / quant_range
    leading = lax.axis_index("seq") == 0
    row_count = gathered.shape[0]
    bc_width = w_bc.shape[1] * w_bc.shape[2] * w_bc.shape[3]
    bc_rows = jnp.reshape(w_bc, (w_bc.shape[0], bc_width))
    scaled = gathered.astype(jnp.float32) * (quant_range / prev_amax)
    quant = jnp.clip(scaled, -quant_range, quant_range).astype(jnp.bfloat16)
    pieces = (
        lax.all_gather(w_x, "seq", axis=0, tiled=True),
        lax.all_gather(bc_rows, "seq", axis=0, tiled=True),
        lax.all_gather(w_dt, "seq", axis=0, tiled=True),
    )
    x_proj, bc_proj, dt_proj = tuple(
        (
            jnp.dot(quant, weight_piece, preferred_element_type=jnp.float32)
            for weight_piece in pieces
        )
    )
    x_whole = (x_proj * in_scale).astype(jnp.bfloat16)
    bc_whole = (bc_proj * in_scale).astype(jnp.bfloat16)
    dt_raw = dt_proj * in_scale
    state_bc = jnp.reshape(conv_state_bc, (margin, bc_width))
    received = from_behind(
        (x_whole[row_count - margin :], bc_whole[row_count - margin :]), "seq", 1
    )
    x_edge = jnp.where(leading, conv_state_x, received[0])
    bc_edge = jnp.where(leading, state_bc, received[1])
    x_act = depthwise(x_edge, x_whole, conv_x, row_count)
    bc_act = depthwise(bc_edge, bc_whole, jnp.reshape(conv_bc, (KERNEL, bc_width)), row_count)
    step_size = jax.nn.softplus(dt_raw + dt_bias)
    heads_here = step_size.shape[1]
    groups_here = w_bc.shape[1]
    per_group = HEADS // GROUPS
    blocks = row_count // SPAN
    x_blocks = x_act.reshape(blocks, SPAN, heads_here, HEAD_DIM)
    bc_blocks = bc_act.reshape(blocks, SPAN, groups_here, 2, STATE)
    in_map = bc_blocks[:, :, :, 0]
    out_map = bc_blocks[:, :, :, 1]
    step_blocks = step_size.reshape(blocks, SPAN, heads_here)
    cum_blocks = jnp.cumsum(-step_blocks * decay_rate, axis=1)
    index_row = jnp.arange(SPAN, dtype=jnp.int32)
    lower_mask = index_row[:, None] >= index_row[None, :]
    intersection = jnp.einsum(
        "ctgn,cugn->cgtu", out_map, in_map, preferred_element_type=jnp.float32
    )
    intersection = jnp.repeat(intersection, per_group, axis=1)
    cum_heads = jnp.transpose(cum_blocks, (0, 2, 1))
    log_gap = cum_heads[:, :, :, None] - cum_heads[:, :, None, :]
    decay = jnp.exp(jnp.where(lower_mask[None, None], log_gap, -1e30))
    step_heads = jnp.transpose(step_blocks, (0, 2, 1))
    weights = (intersection * decay * step_heads[:, :, None, :]).astype(jnp.bfloat16)
    local_part = jnp.einsum(
        "chtu,cuhp->cthp", weights, x_blocks, preferred_element_type=jnp.float32
    )
    last_cum = cum_blocks[:, SPAN - 1, :]
    x_weighted = (
        x_blocks.astype(jnp.float32)
        * (step_blocks * jnp.exp(last_cum[:, None, :] - cum_blocks))[:, :, :, None]
    ).astype(jnp.bfloat16)
    in_heads = jnp.repeat(in_map, per_group, axis=2)
    added = jnp.einsum("cuhp,cuhn->chpn", x_weighted, in_heads, preferred_element_type=jnp.float32)

    def carry_on(carried, element):
        block_decay, block_added = element
        return (block_decay[:, None, None] * carried + block_added, carried)

    empty_state = jnp.zeros((heads_here, HEAD_DIM, STATE), jnp.float32)
    device_state, entering = lax.scan(carry_on, empty_state, (jnp.exp(last_cum), added))
    device_decay = jnp.exp(jnp.sum(last_cum, axis=0))
    seeded = device_state + jnp.where(leading, device_decay[:, None, None] * init_state, 0.0)
    identity = (jnp.ones_like(device_decay), jnp.zeros_like(device_state))
    scanned = carried_in((device_decay, seeded), "seq", combine, identity)
    incoming = jnp.where(leading, init_state, scanned[1])
    prefix = jnp.exp(jnp.cumsum(last_cum, axis=0) - last_cum)
    states_in = entering + prefix[:, :, None, None] * incoming[None]
    out_heads = jnp.repeat(out_map, per_group, axis=2).astype(jnp.float32)
    carried_part = (
        jnp.einsum("cthn,chpn->cthp", out_heads, states_in, precision=lax.Precision.HIGHEST)
        * jnp.exp(cum_blocks)[:, :, :, None]
    )
    ssm_out = local_part + carried_part + skip[None, None, :, None] * x_blocks.astype(jnp.float32)
    ssm_out = ssm_out.reshape(row_count, heads_here * HEAD_DIM)
    squares = lax.psum(jnp.sum(ssm_out * ssm_out, axis=1), "tensor")
    mean_sq = squares / (HEADS * HEAD_DIM)
    normed = (ssm_out * lax.rsqrt(mean_sq + epsilon)[:, None] * norm_gain).astype(jnp.bfloat16)
    partial_out = jnp.dot(
        normed, lax.all_gather(w_out, "seq", axis=1, tiled=True), preferred_element_type=jnp.float32
    )
    layer_out = lax.psum_scatter(
        partial_out.astype(jnp.bfloat16), "tensor", scatter_dimension=0, tiled=True
    )
    return (layer_out, abs_max)


PAIR = 2
LINE = 4
ROWS = 8
SMEM = pl.BlockSpec(memory_space=pltpu.SMEM)
HIGHEST = lax.Precision.HIGHEST


def splits(mesh):
    count, ranks = (mesh.shape["seq"], mesh.shape["tensor"])
    heads_all, groups_here = (HEADS // ranks, GROUPS // ranks)
    if count != PAIR * LINE or groups_here != PAIR or ranks & (ranks - 1):
        return False
    heads_here = heads_all // count
    return 2 * heads_here == ROWS and heads_here * HEAD_DIM == 2 * SPAN


def nt_dot(a, b, **kw):
    return lax.dot_general(
        a, b, (((1,), (1,)), ((), ())), preferred_element_type=jnp.float32, **kw
    )


def project_kernel(ranks, place_ref, factor_ref, *refs):
    hidden = [refs[x * ranks : (x + 1) * ranks] for x in range(PAIR)]
    refs = refs[PAIR * ranks :]
    own_x, x_far, own_bc, other_bc, own_dt, other_dt = refs[:6]
    far_refs = refs[6 : 6 + LINE // 2]
    near_refs = refs[6 + LINE // 2 : 6 + LINE]
    sent_refs = refs[6 + LINE : 6 + LINE + LINE // 2]
    bc_ref, largest_ref, quant_ref, near_dt, all_dt = refs[6 + LINE + LINE // 2 :]
    side, z = (place_ref[1], place_ref[2])
    step = pl.program_id(0)
    factor = factor_ref[0]
    depth = own_x.shape[0]
    largest = None
    each = hidden[0][0].shape[0]
    for x in range(PAIR):
        for k in range(each):
            block = (k ^ (z % each)) * PAIR + (side ^ x)
            for j in range(ranks):
                for half in range(PAIR):
                    cut = slice(half * depth, (half + 1) * depth)
                    values = hidden[x][j][k, :, cut].astype(jnp.float32)
                    scaled = jnp.clip(values * factor, -quant_range, quant_range)
                    quant_ref[half, block, j] = scaled.astype(jnp.bfloat16)
                    top = jnp.max(jnp.abs(values).reshape(-1, ROWS, depth), axis=0)
                    largest = top if largest is None else jnp.maximum(largest, top)
    width = largest_ref.shape[1]
    top = largest[:, :width]
    for at in range(width, depth, width):
        top = jnp.maximum(top, largest[:, at : at + width])

    @pl.when(step == 0)
    def _():
        largest_ref[...] = top

    @pl.when(step > 0)
    def _():
        largest_ref[...] = jnp.maximum(largest_ref[...], top)

    rows = quant_ref.shape[1] * quant_ref.shape[2] * quant_ref.shape[3]
    near = quant_ref[side].reshape(rows, depth)
    far = quant_ref[1 - side].reshape(rows, depth)

    def both(own, other):
        return jnp.dot(near, own, preferred_element_type=jnp.float32) + jnp.dot(
            far, other, preferred_element_type=jnp.float32
        )

    at_rows = pl.ds(pl.multiple_of(step * rows, rows), rows)
    ours = nt_dot(own_dt[...], near)
    near_dt[...] = ours.reshape(near_dt.shape)
    all_dt[...] = (ours + nt_dot(other_dt[...], far)).reshape(all_dt.shape)
    channels = near_refs[0].shape[1]
    tokens = pl.num_programs(0) * rows
    extra = rows // channels * ROWS
    upper = lax.broadcasted_iota(jnp.int32, (ROWS, channels), 0) < ROWS // 2

    def steps_of(dt_ref, run):
        dt = dt_ref[run // 2]
        pieces = []
        for at in range(0, rows, channels):
            piece = dt[:, at : at + channels]
            turned = pltpu.roll(piece, ROWS // 2, 0)
            lower_run = jnp.where(upper, piece, turned)
            upper_run = jnp.where(upper, turned, piece)
            pieces.append(split_parts(jnp.where(run % 2 == 0, lower_run, upper_run), upper))
        return jnp.concatenate(pieces, axis=0).astype(jnp.bfloat16)

    extra_rows = pl.ds(pl.multiple_of(tokens + step * extra, 16), extra)

    def columns(run):
        return pl.ds(pl.multiple_of(run * channels, channels), channels)

    bc_ref[at_rows] = both(own_bc[...], other_bc[...]).astype(jnp.bfloat16)
    for m in range(LINE // 2):
        owner = z ^ (m + LINE // 2)
        run = side * LINE + owner
        other = x_far[:, columns(owner % (LINE // 2))]
        far_refs[m][at_rows] = both(own_x[:, columns(run)], other).astype(jnp.bfloat16)
        far_refs[m][extra_rows] = steps_of(all_dt, run)
        for out_refs, way in ((near_refs, side), (sent_refs, 1 - side)):
            run = way * LINE + (z ^ m)
            product = jnp.dot(near, own_x[:, columns(run)], preferred_element_type=jnp.float32)
            out_refs[m][at_rows] = product.astype(jnp.bfloat16)
            out_refs[m][extra_rows] = steps_of(near_dt, run)


def split_parts(values, upper):
    top = values.astype(jnp.bfloat16).astype(jnp.float32)
    return jnp.where(upper, top, values - top)


def project(place, factor, hidden, w_x, weights):
    line, own, wide = hidden[0].shape
    ranks = len(hidden) // PAIR
    depth, x_wide = (weights[0].shape[0], 2 * weights[0].shape[1])
    channels, maps_wide = (x_wide // LINE, weights[1].shape[1])
    steps = 2
    each = line // steps
    tokens = line * PAIR * ranks * own
    extra = tokens // channels * ROWS

    def fixed(array):
        return pl.BlockSpec(array.shape, lambda i, p: (0,) * array.ndim)

    dt_shape = (weights[-1].shape[0] // ROWS, ROWS, tokens // steps)
    payload = jax.ShapeDtypeStruct((tokens + extra, channels), jnp.bfloat16)
    maps = jax.ShapeDtypeStruct((tokens, maps_wide), jnp.bfloat16)
    largest = jax.ShapeDtypeStruct((ROWS, 128), jnp.float32)
    outs = [payload] * (LINE + LINE // 2) + [maps, largest]
    rows_of = pl.BlockSpec((each, own, wide), lambda i, p: (i ^ (p[2] // each), 0, 0))
    return pl.pallas_call(
        functools.partial(project_kernel, ranks),
        grid_spec=pltpu.PrefetchScalarGridSpec(
            num_scalar_prefetch=1,
            grid=(steps,),
            in_specs=[SMEM]
            + [rows_of] * (PAIR * ranks)
            + [fixed(w) for w in (w_x, *weights)],
            out_specs=[fixed(out) for out in outs],
            scratch_shapes=[
                pltpu.VMEM((PAIR, each * PAIR, ranks, own, depth), jnp.bfloat16),
                pltpu.VMEM(dt_shape, jnp.float32),
                pltpu.VMEM(dt_shape, jnp.float32),
            ],
        ),
        out_shape=outs,
        compiler_params=pltpu.CompilerParams(vmem_limit_bytes=26 * 2**20),
        cost_estimate=pl.CostEstimate(
            flops=2 * tokens * wide * (x_wide + maps_wide),
            bytes_accessed=2 * tokens * (wide + x_wide),
            transcendentals=0,
        ),
        name="project",
    )(place, factor, *hidden, w_x, *weights)


def onward_kernel(own_ref, received_ref, out_ref):
    rows, channels = own_ref.shape
    tokens = rows * channels // (channels + ROWS)
    total = own_ref[:tokens].astype(jnp.float32) + received_ref[:tokens].astype(jnp.float32)
    out_ref[:tokens] = total.astype(jnp.bfloat16)
    upper = lax.broadcasted_iota(jnp.int32, (ROWS, channels), 0) < ROWS // 2
    extra = own_ref[tokens:].astype(jnp.float32) + received_ref[tokens:].astype(jnp.float32)
    pieces = []
    for at in range(0, rows - tokens, ROWS):
        piece = extra[at : at + ROWS]
        pieces.append(split_parts(piece + pltpu.roll(piece, ROWS // 2, 0), upper))
    out_ref[tokens:] = jnp.concatenate(pieces, axis=0).astype(jnp.bfloat16)


def onward(own, received):
    whole = pl.BlockSpec(own.shape, lambda: (0, 0))
    return pl.pallas_call(
        onward_kernel,
        in_specs=[whole, whole],
        out_specs=whole,
        out_shape=jax.ShapeDtypeStruct(own.shape, own.dtype),
        compiler_params=pltpu.CompilerParams(vmem_limit_bytes=8 * 2**20),
        cost_estimate=pl.CostEstimate(
            flops=own.size, bytes_accessed=6 * own.size, transcendentals=0
        ),
        name="onward",
    )(own, received)


def turned_rank(rank, ranks):
    turned = 0
    while ranks > 1:
        turned, rank, ranks = (2 * turned + rank % 2, rank // 2, ranks // 2)
    return turned


def scan_kernel(place_ref, scale_ref, *refs):
    x_refs, bc_refs = (refs[:-9], refs[-9:-6])
    small_ref, largest_ref, state_ref, out_ref, x_buf, bc_buf = refs[-6:]
    tokens, channels = bc_refs[0].shape
    blocks = tokens // SPAN
    heads = channels // HEAD_DIM
    rank, z = (place_ref[0], place_ref[2])
    ranks = place_ref.shape[0] - 3
    own = SPAN // ranks
    edge = ROWS
    in_scale = scale_ref[0]
    at_end = (z == 0) | (z == LINE - 1)
    x_buf[:edge] = small_ref[:edge]
    bc_buf[:edge] = small_ref[edge : 2 * edge]
    state = state_ref[...].T

    for block in range(blocks):
        for true_rank in range(ranks):
            source = block * SPAN + (true_rank ^ rank) * own
            source = pl.ds(pl.multiple_of(source, own), own)
            at = edge + block * SPAN + true_rank * own
            at = slice(at, at + own)
            total = sum(ref[source].astype(jnp.float32) for ref in x_refs) * in_scale
            x_buf[at] = total.astype(jnp.bfloat16).astype(jnp.float32)
            near, far, done = (ref[source].astype(jnp.float32) for ref in bc_refs)
            total = ((near + far) * in_scale).astype(jnp.bfloat16).astype(jnp.float32)
            bc_buf[at] = jnp.where(at_end, done, total)

    taps = 2 * edge

    def activate(buf, row, block):
        start = edge - (KERNEL - 1) + block * SPAN
        summed = small_ref[row : row + 1] * buf[start : start + SPAN]
        for k in range(1, KERNEL):
            summed = summed + small_ref[row + k : row + k + 1] * buf[start + k : start + k + SPAN]
        return (summed / (1.0 + jnp.exp(-summed))).astype(jnp.bfloat16)

    skip = small_ref[taps + 2 * KERNEL : taps + 2 * KERNEL + 1]
    gain = small_ref[taps + 2 * KERNEL + 1 : taps + 2 * KERNEL + 2]
    bias = small_ref[4 * edge :, :SPAN]
    rate = small_ref[4 * edge :, SPAN:]

    up = lax.broadcasted_iota(jnp.int32, (SPAN, SPAN), 0)
    across = lax.broadcasted_iota(jnp.int32, (SPAN, SPAN), 1)
    lane = lax.broadcasted_iota(jnp.int32, (SPAN, channels), 1)
    lower = up >= across
    upper = (up <= across).astype(jnp.float32)
    lanes = across[:ROWS]

    dt = sum(ref[tokens:].astype(jnp.float32) for ref in x_refs)
    steps = []
    wide = channels // SPAN
    for block in range(blocks):
        tile = dt[block // wide * ROWS : (block // wide + 1) * ROWS]
        cut = tile[:, block % wide * SPAN : (block % wide + 1) * SPAN]
        cut = (cut + pltpu.roll(cut, ROWS // 2, 0)) * in_scale
        bit = 1
        while bit < ranks:
            shift = bit * own
            flipped = jnp.where(
                (lanes // shift) % 2 == 1,
                pltpu.roll(cut, shift, 1),
                pltpu.roll(cut, SPAN - shift, 1),
            )
            cut = jnp.where((rank & bit) != 0, flipped, cut)
            bit *= 2
        raw = cut + bias
        steps.append(jnp.maximum(raw, 0.0) + jnp.log1p(jnp.exp(-jnp.abs(raw))))
    drops = jnp.concatenate([-step * rate for step in steps], axis=0)
    cums = jnp.dot(drops, upper, precision=HIGHEST, preferred_element_type=jnp.float32)

    sums = jnp.zeros((SPAN, SPAN), jnp.float32)
    for block in range(blocks):
        x_act = activate(x_buf, taps, block)
        bc_act = activate(bc_buf, taps + KERNEL, block)
        in_map, out_map = (bc_act[:, :STATE], bc_act[:, STATE:])
        step, cum = (steps[block], cums[block * ROWS : (block + 1) * ROWS])
        last = cum[:, SPAN - 1 : SPAN]
        turned = jnp.concatenate(
            [
                cum,
                step * jnp.exp(last - cum),
                jnp.exp(cum),
                jnp.zeros((SPAN - 3 * ROWS, SPAN), jnp.float32),
            ],
            axis=0,
        ).T

        def spread(row):
            result = jnp.broadcast_to(turned[:, row : row + 1], (SPAN, channels))
            for h in range(1, heads):
                result = jnp.where(lane >= h * HEAD_DIM, turned[:, row + h : row + h + 1], result)
            return result

        inner = jnp.where(lower, nt_dot(out_map, in_map), 0.0)
        x_wide = x_act.astype(jnp.float32)
        weights, spaced = ([], [])
        for h in range(heads):
            gap = jnp.where(lower, turned[:, h : h + 1] - cum[h : h + 1], 0.0)
            weights.append((inner * jnp.exp(gap) * step[h : h + 1]).astype(jnp.bfloat16))
            inside = (lane >= h * HEAD_DIM) & (lane < (h + 1) * HEAD_DIM)
            spaced.append(jnp.where(inside, x_wide, 0.0).astype(jnp.bfloat16))
        local_part = jnp.dot(
            jnp.concatenate(weights, axis=1),
            jnp.concatenate(spaced, axis=0),
            preferred_element_type=jnp.float32,
        )
        grown = spread(2 * ROWS)
        x_weighted = (x_wide * spread(ROWS)).astype(jnp.bfloat16)
        added = lax.dot_general(
            in_map, x_weighted, (((0,), (0,)), ((), ())), preferred_element_type=jnp.float32
        )
        high = state.astype(jnp.bfloat16)
        rest = (state - high.astype(jnp.float32)).astype(jnp.bfloat16)
        carried = jnp.dot(
            jnp.concatenate([out_map, out_map], axis=1),
            jnp.concatenate([high, rest], axis=0),
            preferred_element_type=jnp.float32,
        )
        ssm_out = local_part + grown * carried + skip * x_wide
        state = grown[SPAN - 1 : SPAN] * state + added
        gained = (ssm_out * gain).astype(jnp.bfloat16)
        for true_rank in range(ranks):
            at = (turned_rank(true_rank, ranks) * blocks + block) * own
            out_ref[at : at + own] = gained[true_rank * own : (true_rank + 1) * own]
        summed = jnp.sum(ssm_out * ssm_out, axis=1, keepdims=True)
        sums = jnp.where(across == block, summed, sums)

    whole = sums.T[:ROWS]
    top = whole.astype(jnp.bfloat16).astype(jnp.float32)
    largest = jnp.broadcast_to(jnp.max(largest_ref[...]), (ROWS, channels))
    extra = jnp.concatenate([jnp.concatenate([top, whole - top], axis=1), largest], axis=0)
    out_ref[tokens:] = extra.astype(jnp.bfloat16)


def scan(place, in_scale, sums, maps, small, largest, state):
    channels = sums[0].shape[1]
    tokens = maps[0].shape[0]

    def fixed(array):
        return pl.BlockSpec(array.shape, lambda i, p: (0, 0))

    out = jax.ShapeDtypeStruct((tokens + 2 * ROWS, channels), jnp.bfloat16)
    return pl.pallas_call(
        scan_kernel,
        grid_spec=pltpu.PrefetchScalarGridSpec(
            num_scalar_prefetch=1,
            grid=(1,),
            in_specs=[SMEM]
            + [fixed(array) for array in (*sums, *maps, small, largest, state)],
            out_specs=fixed(out),
            scratch_shapes=[
                pltpu.VMEM((tokens + ROWS, channels), jnp.float32),
                pltpu.VMEM((tokens + ROWS, 2 * STATE), jnp.float32),
            ],
        ),
        out_shape=out,
        compiler_params=pltpu.CompilerParams(vmem_limit_bytes=20 * 2**20),
        cost_estimate=pl.CostEstimate(
            flops=8 * tokens * SPAN * channels,
            bytes_accessed=8 * tokens * channels,
            transcendentals=tokens * (channels + 8 * SPAN),
        ),
        name="scan",
    )(place, in_scale, *sums, *maps, small, largest, state)


def by_heads(
    hidden_in,
    prev_amax,
    w_x,
    w_bc,
    w_dt,
    conv_x,
    conv_bc,
    conv_state_x,
    conv_state_bc,
    dt_bias,
    decay_rate,
    skip,
    init_state,
    norm_gain,
    w_out,
):
    margin = KERNEL - 1
    count, here = (lax.axis_size("seq"), lax.axis_index("seq"))
    ranks, rank = (lax.axis_size("tensor"), lax.axis_index("tensor"))
    z, side = (here // PAIR, here % PAIR)
    place_of = side * LINE + z
    f32, bf16 = (jnp.float32, jnp.bfloat16)
    own, width = hidden_in.shape
    depth = w_x.shape[0]
    channels = w_x.shape[1] // count
    heads_here = w_dt.shape[1] // count
    in_scale = (prev_amax / quant_range).reshape(1)
    factor = (quant_range / prev_amax).reshape(1)
    place = jnp.stack([rank, side, z] + [rank] * ranks).astype(jnp.int32)

    def pick(array, axis, index):
        return lax.dynamic_index_in_dim(array, index, axis, keepdims=False)

    def along(value, pairs):
        moves = [(a * PAIR + x, b * PAIR + x) for a, b in pairs for x in range(PAIR)]
        return lax.ppermute(value, "seq", moves)

    def across(value):
        return lax.ppermute(value, "seq", [(s, s ^ 1) for s in range(count)])

    def of_heads(array):
        return jnp.repeat(array, HEAD_DIM)[None]

    by_channel = jnp.concatenate(
        [conv_state_x.astype(f32), conv_x, of_heads(skip), norm_gain[None]], axis=0
    )
    by_channel = lax.dynamic_slice_in_dim(by_channel, place_of * channels, channels, axis=1)
    by_map = jnp.concatenate([conv_state_bc.astype(f32), conv_bc], axis=0)
    by_map = pick(by_map, 1, side).reshape(margin + KERNEL, 2 * STATE)
    by_head = jnp.stack([dt_bias, decay_rate]).reshape(2, count, heads_here)
    by_head = jnp.tile(pick(by_head, 1, place_of).T, (ROWS // heads_here, 1))
    by_head = jnp.repeat(by_head, SPAN, axis=1)
    blank = jnp.zeros((ROWS - margin, channels), f32)
    small = jnp.concatenate(
        [
            blank,
            by_channel[:margin],
            blank,
            by_map[:margin],
            by_channel[margin : margin + KERNEL],
            by_map[margin:],
            by_channel[margin + KERNEL :],
            jnp.zeros((2 * ROWS - 2 * KERNEL - 2, channels), f32),
            by_head,
        ],
        axis=0,
    )

    start_state = lax.dynamic_slice_in_dim(
        init_state, place_of * heads_here, heads_here, axis=0
    ).reshape(channels, STATE)

    tie = lax.optimization_barrier
    half_run = LINE // 2 * channels
    opposite = (z // (LINE // 2)) ^ 1
    at = ((1 - side) * 2 + opposite) * half_run
    x_sent = lax.dynamic_slice_in_dim(w_x, at, half_run, axis=1)
    x_sent, hidden_in = tie((x_sent, hidden_in))
    x_far = across(x_sent)
    x_far, maps_sent, dt_sent = tie(
        (x_far, pick(w_bc, 1, 1 - side).reshape(depth, 2 * STATE), w_dt.T)
    )
    bc_other, dt_other = (across(maps_sent), across(dt_sent))
    bc_own = pick(w_bc, 1, side).reshape(depth, 2 * STATE)

    def line_columns(m):
        return lax.dynamic_slice_in_dim(hidden_in, (z ^ m) * PAIR * depth, PAIR * depth, axis=1)

    arrived = [line_columns(0)]
    for m in range(1, LINE):
        arrived.append(along(line_columns(m), [(s, s ^ m) for s in range(LINE)]))
    stacked = jnp.stack(arrived)
    beyond_pair = across(stacked)
    beyond_pair, small, start_state, bc_own, dt_sent = tie(
        (beyond_pair, small, start_state, bc_own, dt_sent)
    )
    rows = []
    for mine in (stacked, beyond_pair):
        ours = [mine]
        for j in range(1, ranks):
            bit = j & -j
            pairs = [(t, t ^ bit) for t in range(ranks)]
            ours.append(lax.ppermute(ours[j - bit], "tensor", pairs))
        rows.extend(ours)

    start, end = (0, LINE - 1)
    at_end = (z == start) | (z == end)
    next_start, next_end = (1, LINE - 2)
    inward = [(start, next_start), (end, next_end)]
    outward = [(next_start, start), (next_end, end)]
    middle = [(next_start, next_end), (next_end, next_start)]
    over_middle = [(next_start, end), (next_end, start)]
    beside_pairs = [(s, s ^ 1) for s in range(LINE)]
    weights = (x_far, bc_own, bc_other, dt_sent, dt_other)
    over, far, mine, near, mine_sent, near_sent, maps, largest = project(
        place, factor, rows, w_x, weights
    )

    map_hop = along(maps, inward)
    hop_far = along(far, inward)
    hop_over = along(over, inward)
    near = onward(near, across(near_sent))
    got_mine = across(mine_sent)
    near_out = along(near, outward)
    near_in = along(near, inward)
    map_sum = (maps.astype(f32) + map_hop.astype(f32)).astype(bf16)
    map_far = along(map_sum, middle)
    map_done = ((map_sum.astype(f32) + map_far.astype(f32)) * in_scale).astype(bf16)
    hop_far, near_out = tie((hop_far, near_out))
    sent_end = onward(over, hop_far)
    got_end = along(sent_end, over_middle)
    hop_over, unused = tie((hop_over, sent_end))
    got_next = along(onward(far, hop_over), middle)
    map_done, got_end, got_mine = tie((map_done, got_end, got_mine))
    map_done = along(map_done, outward)
    gained = scan(
        place,
        in_scale,
        [mine, got_mine, near_out, near_in, got_end, got_next],
        [map_sum, map_far, map_done],
        small,
        largest,
        start_state,
    )

    tokens = gained.shape[0] - 2 * ROWS
    beside = along(gained, beside_pairs)
    facing = along(gained, middle)
    second = jnp.where(at_end, along(facing, outward), facing)
    beyond = along(beside, middle)
    third = jnp.where(at_end, along(beyond, outward), beyond)
    far_own = across(gained)
    far_beside = across(beside)
    second, far_own = tie((second, far_own))
    far_second = across(second)
    third, far_beside = tie((third, far_beside))
    far_third = across(third)
    two, three = (jnp.where(at_end, 2, 3), jnp.where(at_end, 3, 2))

    def rows_for(x, m):
        at = ((side ^ x) * LINE + (z ^ m)) * channels
        return lax.dynamic_slice_in_dim(w_out, at, channels, axis=0)

    total = None
    tails = [far_third[tokens:]]
    for x, m, piece in (
        (0, 0, gained),
        (1, 0, far_own),
        (0, 1, beside),
        (1, 1, far_beside),
        (0, two, second),
        (1, two, far_second),
        (0, three, third),
    ):
        product = jnp.dot(piece, rows_for(x, m), preferred_element_type=f32)
        total = product if total is None else total + product
        tails.append(piece[tokens:])
    total, far_third = tie((total, far_third))
    last_rows = rows_for(1, three)
    tails = [tail.astype(f32) for tail in tails]
    squares = sum(tail[:ROWS, :SPAN] + tail[:ROWS, SPAN:] for tail in tails)
    top = functools.reduce(jnp.maximum, [tail[ROWS:, :SPAN] for tail in tails])

    def run_of(array, index, run):
        return lax.dynamic_slice_in_dim(array, index * run, run, axis=0)

    def first_sum(index):
        block, so_far = (run_of(far_third, index, run), run_of(total, index, run))
        return so_far + jnp.dot(block, last_rows, preferred_element_type=f32)

    run = tokens // 2
    keeps = rank % 2
    pairs = [(t, t ^ 1) for t in range(ranks)]
    received = lax.ppermute(first_sum(1 - keeps).astype(bf16), "tensor", pairs)
    kept = first_sum(keeps)
    squares = squares + lax.ppermute(squares, "tensor", pairs)
    bit = 2
    while bit < ranks:
        run //= 2
        keeps = (rank // bit) % 2
        pairs = [(t, t ^ bit) for t in range(ranks)]
        sent = run_of(kept, 1 - keeps, run) + run_of(received, 1 - keeps, run).astype(f32)
        kept = run_of(kept, keeps, run) + run_of(received, keeps, run).astype(f32)
        received = lax.ppermute(sent.astype(bf16), "tensor", pairs)
        squares = squares + lax.ppermute(squares, "tensor", pairs)
        bit *= 2
    mean_sq = squares.reshape(count, ranks, own) / (HEADS * HEAD_DIM)
    factors = lax.rsqrt(pick(mean_sq, 1, rank) + epsilon)
    final = (kept + received.astype(f32)).reshape(count, own, -1) * factors[:, :, None]
    final = lax.all_to_all(final.astype(bf16), "seq", split_axis=0, concat_axis=0, tiled=True)
    layer_out = final.transpose(1, 0, 2).reshape(own, count * final.shape[2])
    return (layer_out, jnp.max(top))


def solution(mesh):
    return jax.shard_map(
        by_heads if splits(mesh) else by_tokens,
        mesh=mesh,
        in_specs=(
            P(("seq", "tensor"), None),
            P(),
            P("seq", "tensor"),
            P("seq", "tensor", None, None),
            P("seq", "tensor"),
            P(None, "tensor"),
            P(None, "tensor", None, None),
            P(None, "tensor"),
            P(None, "tensor", None, None),
            P("tensor"),
            P("tensor"),
            P("tensor"),
            P("tensor", None, None),
            P("tensor"),
            P("tensor", "seq"),
        ),
        out_specs=(P(("seq", "tensor"), None), P()),
        check_vma=False,
    )
```

```python
import functools

import jax
import jax.numpy as jnp
from jax import lax
from jax.experimental import pallas as pl
from jax.experimental.pallas import tpu as pltpu
from jax.sharding import PartitionSpec as P

HEADS = 128
HEAD_DIM = 64
STATE = 128
GROUPS = 8
KERNEL = 4
SPAN = 128


epsilon = 1e-05
quant_range = 448.0


def from_behind(value, axis, steps):
    count = lax.axis_size(axis)
    first, last = (max(0, -steps), min(count, count - steps))
    return lax.ppermute(value, axis, [(source, source + steps) for source in range(first, last)])


def carried_in(shard, axis, combine, identity):
    count, here = (lax.axis_size(axis), lax.axis_index(axis))
    everything = jax.tree.map(
        lambda part, kind: lax.all_gather(part.astype(kind), axis),
        shard,
        (jnp.bfloat16, jnp.bfloat16),
    )
    start = jax.tree.map(
        lambda part, zero: jnp.broadcast_to(jnp.asarray(zero, part.dtype), part.shape),
        shard,
        identity,
    )

    def turn(k, before):
        reached = k < here
        new = combine(
            before, jax.tree.map(lambda part, own: part[k].astype(own.dtype), everything, shard)
        )
        return jax.tree.map(lambda a, b: jnp.where(reached, a, b), new, before)

    return lax.fori_loop(0, count, turn, start)


def depthwise(before, projected, conv_taps, length):
    extended = jnp.concatenate([before, projected], axis=0)
    summed = conv_taps[0] * extended[0:length]
    for offset in range(1, KERNEL):
        summed = summed + conv_taps[offset] * extended[offset : offset + length]
    return jax.nn.silu(summed).astype(jnp.bfloat16)


def combine(earlier, later):
    return (earlier[0] * later[0], later[0][:, None, None] * earlier[1] + later[1])


def by_tokens(
    hidden_in,
    prev_amax,
    w_x,
    w_bc,
    w_dt,
    conv_x,
    conv_bc,
    conv_state_x,
    conv_state_bc,
    dt_bias,
    decay_rate,
    skip,
    init_state,
    norm_gain,
    w_out,
):
    margin = KERNEL - 1
    gathered = lax.all_gather(hidden_in, "tensor", axis=0, tiled=True)
    abs_max = lax.pmax(jnp.max(jnp.abs(gathered.astype(jnp.float32))), "seq")
    in_scale = prev_amax / quant_range
    leading = lax.axis_index("seq") == 0
    row_count = gathered.shape[0]
    bc_width = w_bc.shape[1] * w_bc.shape[2] * w_bc.shape[3]
    bc_rows = jnp.reshape(w_bc, (w_bc.shape[0], bc_width))
    scaled = gathered.astype(jnp.float32) * (quant_range / prev_amax)
    quant = jnp.clip(scaled, -quant_range, quant_range).astype(jnp.bfloat16)
    pieces = (
        lax.all_gather(w_x, "seq", axis=0, tiled=True),
        lax.all_gather(bc_rows, "seq", axis=0, tiled=True),
        lax.all_gather(w_dt, "seq", axis=0, tiled=True),
    )
    x_proj, bc_proj, dt_proj = tuple(
        (
            jnp.dot(quant, weight_piece, preferred_element_type=jnp.float32)
            for weight_piece in pieces
        )
    )
    x_whole = (x_proj * in_scale).astype(jnp.bfloat16)
    bc_whole = (bc_proj * in_scale).astype(jnp.bfloat16)
    dt_raw = dt_proj * in_scale
    state_bc = jnp.reshape(conv_state_bc, (margin, bc_width))
    received = from_behind(
        (x_whole[row_count - margin :], bc_whole[row_count - margin :]), "seq", 1
    )
    x_edge = jnp.where(leading, conv_state_x, received[0])
    bc_edge = jnp.where(leading, state_bc, received[1])
    x_act = depthwise(x_edge, x_whole, conv_x, row_count)
    bc_act = depthwise(bc_edge, bc_whole, jnp.reshape(conv_bc, (KERNEL, bc_width)), row_count)
    step_size = jax.nn.softplus(dt_raw + dt_bias)
    heads_here = step_size.shape[1]
    groups_here = w_bc.shape[1]
    per_group = HEADS // GROUPS
    blocks = row_count // SPAN
    x_blocks = x_act.reshape(blocks, SPAN, heads_here, HEAD_DIM)
    bc_blocks = bc_act.reshape(blocks, SPAN, groups_here, 2, STATE)
    in_map = bc_blocks[:, :, :, 0]
    out_map = bc_blocks[:, :, :, 1]
    step_blocks = step_size.reshape(blocks, SPAN, heads_here)
    cum_blocks = jnp.cumsum(-step_blocks * decay_rate, axis=1)
    index_row = jnp.arange(SPAN, dtype=jnp.int32)
    lower_mask = index_row[:, None] >= index_row[None, :]
    intersection = jnp.einsum(
        "ctgn,cugn->cgtu", out_map, in_map, preferred_element_type=jnp.float32
    )
    intersection = jnp.repeat(intersection, per_group, axis=1)
    cum_heads = jnp.transpose(cum_blocks, (0, 2, 1))
    log_gap = cum_heads[:, :, :, None] - cum_heads[:, :, None, :]
    decay = jnp.exp(jnp.where(lower_mask[None, None], log_gap, -1e30))
    step_heads = jnp.transpose(step_blocks, (0, 2, 1))
    weights = (intersection * decay * step_heads[:, :, None, :]).astype(jnp.bfloat16)
    local_part = jnp.einsum(
        "chtu,cuhp->cthp", weights, x_blocks, preferred_element_type=jnp.float32
    )
    last_cum = cum_blocks[:, SPAN - 1, :]
    x_weighted = (
        x_blocks.astype(jnp.float32)
        * (step_blocks * jnp.exp(last_cum[:, None, :] - cum_blocks))[:, :, :, None]
    ).astype(jnp.bfloat16)
    in_heads = jnp.repeat(in_map, per_group, axis=2)
    added = jnp.einsum("cuhp,cuhn->chpn", x_weighted, in_heads, preferred_element_type=jnp.float32)

    def carry_on(carried, element):
        block_decay, block_added = element
        return (block_decay[:, None, None] * carried + block_added, carried)

    empty_state = jnp.zeros((heads_here, HEAD_DIM, STATE), jnp.float32)
    device_state, entering = lax.scan(carry_on, empty_state, (jnp.exp(last_cum), added))
    device_decay = jnp.exp(jnp.sum(last_cum, axis=0))
    seeded = device_state + jnp.where(leading, device_decay[:, None, None] * init_state, 0.0)
    identity = (jnp.ones_like(device_decay), jnp.zeros_like(device_state))
    scanned = carried_in((device_decay, seeded), "seq", combine, identity)
    incoming = jnp.where(leading, init_state, scanned[1])
    prefix = jnp.exp(jnp.cumsum(last_cum, axis=0) - last_cum)
    states_in = entering + prefix[:, :, None, None] * incoming[None]
    out_heads = jnp.repeat(out_map, per_group, axis=2).astype(jnp.float32)
    carried_part = (
        jnp.einsum("cthn,chpn->cthp", out_heads, states_in, precision=lax.Precision.HIGHEST)
        * jnp.exp(cum_blocks)[:, :, :, None]
    )
    ssm_out = local_part + carried_part + skip[None, None, :, None] * x_blocks.astype(jnp.float32)
    ssm_out = ssm_out.reshape(row_count, heads_here * HEAD_DIM)
    squares = lax.psum(jnp.sum(ssm_out * ssm_out, axis=1), "tensor")
    mean_sq = squares / (HEADS * HEAD_DIM)
    normed = (ssm_out * lax.rsqrt(mean_sq + epsilon)[:, None] * norm_gain).astype(jnp.bfloat16)
    partial_out = jnp.dot(
        normed, lax.all_gather(w_out, "seq", axis=1, tiled=True), preferred_element_type=jnp.float32
    )
    layer_out = lax.psum_scatter(
        partial_out.astype(jnp.bfloat16), "tensor", scatter_dimension=0, tiled=True
    )
    return (layer_out, abs_max)


PAIR = 2
LINE = 4
ROWS = 8
CUTS = 2
SMEM = pl.BlockSpec(memory_space=pltpu.SMEM)
VMEM = pl.BlockSpec(memory_space=pltpu.VMEM)
HIGHEST = lax.Precision.HIGHEST


def splits(mesh):
    count, ranks = (mesh.shape["seq"], mesh.shape["tensor"])
    heads_all, groups_here = (HEADS // ranks, GROUPS // ranks)
    if count != PAIR * LINE or groups_here != PAIR or ranks & (ranks - 1):
        return False
    heads_here = heads_all // count
    return 2 * heads_here == ROWS and heads_here * HEAD_DIM == 2 * SPAN


def nt_dot(a, b, **kw):
    return lax.dot_general(
        a, b, (((1,), (1,)), ((), ())), preferred_element_type=jnp.float32, **kw
    )


def project_kernel(ranks, place_ref, factor_ref, *refs):
    hidden = [refs[x * ranks : (x + 1) * ranks] for x in range(PAIR)]
    refs = refs[PAIR * ranks :]
    own_x, x_far, own_bc, other_bc, own_dt, other_dt = refs[:6]
    far_refs = refs[6 : 6 + LINE // 2]
    near_refs = refs[6 + LINE // 2 : 6 + LINE]
    sent_refs = refs[6 + LINE : 6 + LINE + LINE // 2]
    bc_ref, largest_ref, quant_ref, near_dt, all_dt = refs[6 + LINE + LINE // 2 :]
    side, z = (place_ref[1], place_ref[2])
    factor = factor_ref[0]
    depth = own_x.shape[0]
    largest = None
    for x in range(PAIR):
        for k in range(LINE):
            block = (k ^ z) * PAIR + (side ^ x)
            for j in range(ranks):
                for half in range(PAIR):
                    cut = slice(half * depth, (half + 1) * depth)
                    values = hidden[x][j][k, :, cut].astype(jnp.float32)
                    scaled = jnp.clip(values * factor, -quant_range, quant_range)
                    quant_ref[half, block, j] = scaled.astype(jnp.bfloat16)
                    top = jnp.max(jnp.abs(values).reshape(-1, ROWS, depth), axis=0)
                    largest = top if largest is None else jnp.maximum(largest, top)
    width = largest_ref.shape[1]
    top = largest[:, :width]
    for at in range(width, depth, width):
        top = jnp.maximum(top, largest[:, at : at + width])
    largest_ref[...] = top

    channels = near_refs[0].shape[1]
    tokens = bc_ref.shape[0]
    rows = tokens // CUTS
    blocks = quant_ref.shape[1] // CUTS
    extra = rows // channels * ROWS
    upper = lax.broadcasted_iota(jnp.int32, (ROWS, channels), 0) < ROWS // 2

    def steps_of(dt_ref, run):
        dt = dt_ref[run // 2]
        pieces = []
        for at in range(0, rows, channels):
            piece = dt[:, at : at + channels]
            turned = pltpu.roll(piece, ROWS // 2, 0)
            lower_run = jnp.where(upper, piece, turned)
            upper_run = jnp.where(upper, turned, piece)
            pieces.append(split_parts(jnp.where(run % 2 == 0, lower_run, upper_run), upper))
        return jnp.concatenate(pieces, axis=0).astype(jnp.bfloat16)

    def columns(run):
        return pl.ds(pl.multiple_of(run * channels, channels), channels)

    for cut in range(CUTS):
        part = slice(cut * blocks, (cut + 1) * blocks)
        near = quant_ref[side, part].reshape(rows, depth)
        far = quant_ref[1 - side, part].reshape(rows, depth)

        def both(own, other):
            return jnp.dot(near, own, preferred_element_type=jnp.float32) + jnp.dot(
                far, other, preferred_element_type=jnp.float32
            )

        at_rows = slice(cut * rows, (cut + 1) * rows)
        extra_rows = slice(tokens + cut * extra, tokens + (cut + 1) * extra)
        ours = nt_dot(own_dt[...], near)
        near_dt[...] = ours.reshape(near_dt.shape)
        all_dt[...] = (ours + nt_dot(other_dt[...], far)).reshape(all_dt.shape)
        bc_ref[at_rows] = both(own_bc[...], other_bc[...]).astype(jnp.bfloat16)
        for m in range(LINE // 2):
            owner = z ^ (m + LINE // 2)
            run = side * LINE + owner
            other = x_far[:, columns(owner % (LINE // 2))]
            far_refs[m][at_rows] = both(own_x[:, columns(run)], other).astype(jnp.bfloat16)
            far_refs[m][extra_rows] = steps_of(all_dt, run)
            for out_refs, way in ((near_refs, side), (sent_refs, 1 - side)):
                run = way * LINE + (z ^ m)
                product = jnp.dot(near, own_x[:, columns(run)], preferred_element_type=jnp.float32)
                out_refs[m][at_rows] = product.astype(jnp.bfloat16)
                out_refs[m][extra_rows] = steps_of(near_dt, run)


def split_parts(values, upper):
    top = values.astype(jnp.bfloat16).astype(jnp.float32)
    return jnp.where(upper, top, values - top)


def project(place, factor, hidden, w_x, weights):
    line, own, wide = hidden[0].shape
    ranks = len(hidden) // PAIR
    depth, x_wide = (weights[0].shape[0], 2 * weights[0].shape[1])
    channels, maps_wide = (x_wide // LINE, weights[1].shape[1])
    tokens = line * PAIR * ranks * own
    extra = tokens // channels * ROWS
    dt_shape = (weights[-1].shape[0] // ROWS, ROWS, tokens // CUTS)
    payload = jax.ShapeDtypeStruct((tokens + extra, channels), jnp.bfloat16)
    maps = jax.ShapeDtypeStruct((tokens, maps_wide), jnp.bfloat16)
    largest = jax.ShapeDtypeStruct((ROWS, 128), jnp.float32)
    outs = [payload] * (LINE + LINE // 2) + [maps, largest]
    return pl.pallas_call(
        functools.partial(project_kernel, ranks),
        in_specs=[SMEM, SMEM] + [VMEM] * (len(hidden) + 1 + len(weights)),
        out_specs=[VMEM] * len(outs),
        scratch_shapes=[
            pltpu.VMEM((PAIR, line * PAIR, ranks, own, depth), jnp.bfloat16),
            pltpu.VMEM(dt_shape, jnp.float32),
            pltpu.VMEM(dt_shape, jnp.float32),
        ],
        out_shape=outs,
        compiler_params=pltpu.CompilerParams(vmem_limit_bytes=32 * 2**20),
        cost_estimate=pl.CostEstimate(
            flops=2 * tokens * wide * (x_wide + maps_wide),
            bytes_accessed=2 * tokens * (wide + x_wide),
            transcendentals=0,
        ),
        name="project",
    )(place, factor, *hidden, w_x, *weights)


def onward_kernel(own_ref, received_ref, out_ref):
    rows, channels = own_ref.shape
    tokens = rows * channels // (channels + ROWS)
    total = own_ref[:tokens].astype(jnp.float32) + received_ref[:tokens].astype(jnp.float32)
    out_ref[:tokens] = total.astype(jnp.bfloat16)
    upper = lax.broadcasted_iota(jnp.int32, (ROWS, channels), 0) < ROWS // 2
    extra = own_ref[tokens:].astype(jnp.float32) + received_ref[tokens:].astype(jnp.float32)
    pieces = []
    for at in range(0, rows - tokens, ROWS):
        piece = extra[at : at + ROWS]
        pieces.append(split_parts(piece + pltpu.roll(piece, ROWS // 2, 0), upper))
    out_ref[tokens:] = jnp.concatenate(pieces, axis=0).astype(jnp.bfloat16)


def onward(own, received):
    return pl.pallas_call(
        onward_kernel,
        in_specs=[VMEM, VMEM],
        out_specs=VMEM,
        out_shape=jax.ShapeDtypeStruct(own.shape, own.dtype),
        compiler_params=pltpu.CompilerParams(vmem_limit_bytes=8 * 2**20),
        cost_estimate=pl.CostEstimate(
            flops=own.size, bytes_accessed=6 * own.size, transcendentals=0
        ),
        name="onward",
    )(own, received)


def turned_rank(rank, ranks):
    turned = 0
    while ranks > 1:
        turned, rank, ranks = (2 * turned + rank % 2, rank // 2, ranks // 2)
    return turned


def scan_kernel(place_ref, scale_ref, *refs):
    x_refs, bc_refs = (refs[:-9], refs[-9:-6])
    small_ref, largest_ref, state_ref, out_ref, x_buf, bc_buf = refs[-6:]
    tokens, channels = bc_refs[0].shape
    blocks = tokens // SPAN
    heads = channels // HEAD_DIM
    rank, z = (place_ref[0], place_ref[2])
    ranks = place_ref.shape[0] - 3
    own = SPAN // ranks
    edge = ROWS
    in_scale = scale_ref[0]
    at_end = (z == 0) | (z == LINE - 1)
    x_buf[:edge] = small_ref[:edge]
    bc_buf[:edge] = small_ref[edge : 2 * edge]
    state = state_ref[...].T

    for block in range(blocks):
        for true_rank in range(ranks):
            source = block * SPAN + (true_rank ^ rank) * own
            source = pl.ds(pl.multiple_of(source, own), own)
            at = edge + block * SPAN + true_rank * own
            at = slice(at, at + own)
            total = sum(ref[source].astype(jnp.float32) for ref in x_refs) * in_scale
            x_buf[at] = total.astype(jnp.bfloat16).astype(jnp.float32)
            near, far, done = (ref[source].astype(jnp.float32) for ref in bc_refs)
            total = ((near + far) * in_scale).astype(jnp.bfloat16).astype(jnp.float32)
            bc_buf[at] = jnp.where(at_end, done, total)

    taps = 2 * edge

    def activate(buf, row, block):
        start = edge - (KERNEL - 1) + block * SPAN
        summed = small_ref[row : row + 1] * buf[start : start + SPAN]
        for k in range(1, KERNEL):
            summed = summed + small_ref[row + k : row + k + 1] * buf[start + k : start + k + SPAN]
        return (summed / (1.0 + jnp.exp(-summed))).astype(jnp.bfloat16)

    skip = small_ref[taps + 2 * KERNEL : taps + 2 * KERNEL + 1]
    gain = small_ref[taps + 2 * KERNEL + 1 : taps + 2 * KERNEL + 2]
    bias = small_ref[4 * edge :, :SPAN]
    rate = small_ref[4 * edge :, SPAN:]

    up = lax.broadcasted_iota(jnp.int32, (SPAN, SPAN), 0)
    across = lax.broadcasted_iota(jnp.int32, (SPAN, SPAN), 1)
    lane = lax.broadcasted_iota(jnp.int32, (SPAN, channels), 1)
    lower = up >= across
    upper = (up <= across).astype(jnp.float32)
    lanes = across[:ROWS]

    dt = sum(ref[tokens:].astype(jnp.float32) for ref in x_refs)
    steps = []
    wide = channels // SPAN
    for block in range(blocks):
        tile = dt[block // wide * ROWS : (block // wide + 1) * ROWS]
        cut = tile[:, block % wide * SPAN : (block % wide + 1) * SPAN]
        cut = (cut + pltpu.roll(cut, ROWS // 2, 0)) * in_scale
        bit = 1
        while bit < ranks:
            shift = bit * own
            flipped = jnp.where(
                (lanes // shift) % 2 == 1,
                pltpu.roll(cut, shift, 1),
                pltpu.roll(cut, SPAN - shift, 1),
            )
            cut = jnp.where((rank & bit) != 0, flipped, cut)
            bit *= 2
        raw = cut + bias
        steps.append(jnp.maximum(raw, 0.0) + jnp.log1p(jnp.exp(-jnp.abs(raw))))
    drops = jnp.concatenate([-step * rate for step in steps], axis=0)
    cums = jnp.dot(drops, upper, precision=HIGHEST, preferred_element_type=jnp.float32)

    sums = jnp.zeros((SPAN, SPAN), jnp.float32)
    for block in range(blocks):
        x_act = activate(x_buf, taps, block)
        bc_act = activate(bc_buf, taps + KERNEL, block)
        in_map, out_map = (bc_act[:, :STATE], bc_act[:, STATE:])
        step, cum = (steps[block], cums[block * ROWS : (block + 1) * ROWS])
        last = cum[:, SPAN - 1 : SPAN]
        turned = jnp.concatenate(
            [
                cum,
                step * jnp.exp(last - cum),
                jnp.exp(cum),
                jnp.zeros((SPAN - 3 * ROWS, SPAN), jnp.float32),
            ],
            axis=0,
        ).T

        def spread(row):
            result = jnp.broadcast_to(turned[:, row : row + 1], (SPAN, channels))
            for h in range(1, heads):
                result = jnp.where(lane >= h * HEAD_DIM, turned[:, row + h : row + h + 1], result)
            return result

        inner = jnp.where(lower, nt_dot(out_map, in_map), 0.0)
        x_wide = x_act.astype(jnp.float32)
        weights, spaced = ([], [])
        for h in range(heads):
            gap = jnp.where(lower, turned[:, h : h + 1] - cum[h : h + 1], 0.0)
            weights.append((inner * jnp.exp(gap) * step[h : h + 1]).astype(jnp.bfloat16))
            inside = (lane >= h * HEAD_DIM) & (lane < (h + 1) * HEAD_DIM)
            spaced.append(jnp.where(inside, x_wide, 0.0).astype(jnp.bfloat16))
        local_part = jnp.dot(
            jnp.concatenate(weights, axis=1),
            jnp.concatenate(spaced, axis=0),
            preferred_element_type=jnp.float32,
        )
        grown = spread(2 * ROWS)
        x_weighted = (x_wide * spread(ROWS)).astype(jnp.bfloat16)
        added = lax.dot_general(
            in_map, x_weighted, (((0,), (0,)), ((), ())), preferred_element_type=jnp.float32
        )
        high = state.astype(jnp.bfloat16)
        rest = (state - high.astype(jnp.float32)).astype(jnp.bfloat16)
        carried = jnp.dot(
            jnp.concatenate([out_map, out_map], axis=1),
            jnp.concatenate([high, rest], axis=0),
            preferred_element_type=jnp.float32,
        )
        ssm_out = local_part + grown * carried + skip * x_wide
        state = grown[SPAN - 1 : SPAN] * state + added
        gained = (ssm_out * gain).astype(jnp.bfloat16)
        for true_rank in range(ranks):
            at = (turned_rank(true_rank, ranks) * blocks + block) * own
            out_ref[at : at + own] = gained[true_rank * own : (true_rank + 1) * own]
        summed = jnp.sum(ssm_out * ssm_out, axis=1, keepdims=True)
        sums = jnp.where(across == block, summed, sums)

    whole = sums.T[:ROWS]
    top = whole.astype(jnp.bfloat16).astype(jnp.float32)
    largest = jnp.broadcast_to(jnp.max(largest_ref[...]), (ROWS, channels))
    extra = jnp.concatenate([jnp.concatenate([top, whole - top], axis=1), largest], axis=0)
    out_ref[tokens:] = extra.astype(jnp.bfloat16)


def scan(place, in_scale, sums, maps, small, largest, state):
    channels = sums[0].shape[1]
    tokens = maps[0].shape[0]

    out = jax.ShapeDtypeStruct((tokens + 2 * ROWS, channels), jnp.bfloat16)
    return pl.pallas_call(
        scan_kernel,
        in_specs=[SMEM, SMEM] + [VMEM] * (len(sums) + len(maps) + 3),
        out_specs=VMEM,
        scratch_shapes=[
            pltpu.VMEM((tokens + ROWS, channels), jnp.float32),
            pltpu.VMEM((tokens + ROWS, 2 * STATE), jnp.float32),
        ],
        out_shape=out,
        compiler_params=pltpu.CompilerParams(vmem_limit_bytes=20 * 2**20),
        cost_estimate=pl.CostEstimate(
            flops=8 * tokens * SPAN * channels,
            bytes_accessed=8 * tokens * channels,
            transcendentals=tokens * (channels + 8 * SPAN),
        ),
        name="scan",
    )(place, in_scale, *sums, *maps, small, largest, state)


def by_heads(
    hidden_in,
    prev_amax,
    w_x,
    w_bc,
    w_dt,
    conv_x,
    conv_bc,
    conv_state_x,
    conv_state_bc,
    dt_bias,
    decay_rate,
    skip,
    init_state,
    norm_gain,
    w_out,
):
    margin = KERNEL - 1
    count, here = (lax.axis_size("seq"), lax.axis_index("seq"))
    ranks, rank = (lax.axis_size("tensor"), lax.axis_index("tensor"))
    z, side = (here // PAIR, here % PAIR)
    place_of = side * LINE + z
    f32, bf16 = (jnp.float32, jnp.bfloat16)
    own, width = hidden_in.shape
    depth = w_x.shape[0]
    channels = w_x.shape[1] // count
    heads_here = w_dt.shape[1] // count
    in_scale = (prev_amax / quant_range).reshape(1)
    factor = (quant_range / prev_amax).reshape(1)
    place = jnp.stack([rank, side, z] + [rank] * ranks).astype(jnp.int32)

    def pick(array, axis, index):
        return lax.dynamic_index_in_dim(array, index, axis, keepdims=False)

    def along(value, pairs):
        moves = [(a * PAIR + x, b * PAIR + x) for a, b in pairs for x in range(PAIR)]
        return lax.ppermute(value, "seq", moves)

    def across(value):
        return lax.ppermute(value, "seq", [(s, s ^ 1) for s in range(count)])

    def of_heads(array):
        return jnp.repeat(array, HEAD_DIM)[None]

    by_channel = jnp.concatenate(
        [conv_state_x.astype(f32), conv_x, of_heads(skip), norm_gain[None]], axis=0
    )
    by_channel = lax.dynamic_slice_in_dim(by_channel, place_of * channels, channels, axis=1)
    by_map = jnp.concatenate([conv_state_bc.astype(f32), conv_bc], axis=0)
    by_map = pick(by_map, 1, side).reshape(margin + KERNEL, 2 * STATE)
    by_head = jnp.stack([dt_bias, decay_rate]).reshape(2, count, heads_here)
    by_head = jnp.tile(pick(by_head, 1, place_of).T, (ROWS // heads_here, 1))
    by_head = jnp.repeat(by_head, SPAN, axis=1)
    blank = jnp.zeros((ROWS - margin, channels), f32)
    small = jnp.concatenate(
        [
            blank,
            by_channel[:margin],
            blank,
            by_map[:margin],
            by_channel[margin : margin + KERNEL],
            by_map[margin:],
            by_channel[margin + KERNEL :],
            jnp.zeros((2 * ROWS - 2 * KERNEL - 2, channels), f32),
            by_head,
        ],
        axis=0,
    )

    start_state = lax.dynamic_slice_in_dim(
        init_state, place_of * heads_here, heads_here, axis=0
    ).reshape(channels, STATE)

    tie = lax.optimization_barrier
    half_run = LINE // 2 * channels
    opposite = (z // (LINE // 2)) ^ 1
    at = ((1 - side) * 2 + opposite) * half_run
    x_sent = lax.dynamic_slice_in_dim(w_x, at, half_run, axis=1)
    x_sent, hidden_in = tie((x_sent, hidden_in))
    x_far = across(x_sent)
    x_far, maps_sent, dt_sent = tie(
        (x_far, pick(w_bc, 1, 1 - side).reshape(depth, 2 * STATE), w_dt.T)
    )
    bc_other, dt_other = (across(maps_sent), across(dt_sent))
    bc_own = pick(w_bc, 1, side).reshape(depth, 2 * STATE)

    def line_columns(m):
        return lax.dynamic_slice_in_dim(hidden_in, (z ^ m) * PAIR * depth, PAIR * depth, axis=1)

    arrived = [line_columns(0)]
    for m in range(1, LINE):
        arrived.append(along(line_columns(m), [(s, s ^ m) for s in range(LINE)]))
    stacked = jnp.stack(arrived)
    beyond_pair = across(stacked)
    beyond_pair, small, start_state, bc_own, dt_sent = tie(
        (beyond_pair, small, start_state, bc_own, dt_sent)
    )
    rows = []
    for mine in (stacked, beyond_pair):
        ours = [mine]
        for j in range(1, ranks):
            bit = j & -j
            pairs = [(t, t ^ bit) for t in range(ranks)]
            ours.append(lax.ppermute(ours[j - bit], "tensor", pairs))
        rows.extend(ours)

    start, end = (0, LINE - 1)
    at_end = (z == start) | (z == end)
    next_start, next_end = (1, LINE - 2)
    inward = [(start, next_start), (end, next_end)]
    outward = [(next_start, start), (next_end, end)]
    middle = [(next_start, next_end), (next_end, next_start)]
    over_middle = [(next_start, end), (next_end, start)]
    beside_pairs = [(s, s ^ 1) for s in range(LINE)]
    weights = (x_far, bc_own, bc_other, dt_sent, dt_other)
    over, far, mine, near, mine_sent, near_sent, maps, largest = project(
        place, factor, rows, w_x, weights
    )

    map_hop = along(maps, inward)
    hop_far = along(far, inward)
    hop_over = along(over, inward)
    near = onward(near, across(near_sent))
    got_mine = across(mine_sent)
    near_out = along(near, outward)
    near_in = along(near, inward)
    map_sum = (maps.astype(f32) + map_hop.astype(f32)).astype(bf16)
    map_far = along(map_sum, middle)
    map_done = ((map_sum.astype(f32) + map_far.astype(f32)) * in_scale).astype(bf16)
    sent_end = onward(over, hop_far)
    got_end = along(sent_end, over_middle)
    hop_over, near_out, unused = tie((hop_over, near_out, sent_end))
    got_next = along(onward(far, hop_over), middle)
    map_done, got_end, got_mine = tie((map_done, got_end, got_mine))
    map_done = along(map_done, outward)
    gained = scan(
        place,
        in_scale,
        [mine, got_mine, near_out, near_in, got_end, got_next],
        [map_sum, map_far, map_done],
        small,
        largest,
        start_state,
    )

    tokens = gained.shape[0] - 2 * ROWS
    beside = along(gained, beside_pairs)
    facing = along(gained, middle)
    second = jnp.where(at_end, along(facing, outward), facing)
    beyond = along(beside, middle)
    third = jnp.where(at_end, along(beyond, outward), beyond)
    far_own = across(gained)
    far_beside = across(beside)
    second, far_own = tie((second, far_own))
    far_second = across(second)
    third, far_beside = tie((third, far_beside))
    far_third = across(third)
    two, three = (jnp.where(at_end, 2, 3), jnp.where(at_end, 3, 2))

    def rows_for(x, m):
        at = ((side ^ x) * LINE + (z ^ m)) * channels
        return lax.dynamic_slice_in_dim(w_out, at, channels, axis=0)

    total = None
    tails = [far_third[tokens:]]
    for x, m, piece in (
        (0, 0, gained),
        (1, 0, far_own),
        (0, 1, beside),
        (1, 1, far_beside),
        (0, two, second),
        (1, two, far_second),
        (0, three, third),
    ):
        product = jnp.dot(piece, rows_for(x, m), preferred_element_type=f32)
        total = product if total is None else total + product
        tails.append(piece[tokens:])
    total, far_third = tie((total, far_third))
    last_rows = rows_for(1, three)
    tails = [tail.astype(f32) for tail in tails]
    squares = sum(tail[:ROWS, :SPAN] + tail[:ROWS, SPAN:] for tail in tails)
    top = functools.reduce(jnp.maximum, [tail[ROWS:, :SPAN] for tail in tails])

    def run_of(array, index, run):
        return lax.dynamic_slice_in_dim(array, index * run, run, axis=0)

    def first_sum(index):
        block, so_far = (run_of(far_third, index, run), run_of(total, index, run))
        return so_far + jnp.dot(block, last_rows, preferred_element_type=f32)

    run = tokens // 2
    keeps = rank % 2
    pairs = [(t, t ^ 1) for t in range(ranks)]
    received = lax.ppermute(first_sum(1 - keeps).astype(bf16), "tensor", pairs)
    kept = first_sum(keeps)
    squares = squares + lax.ppermute(squares, "tensor", pairs)
    bit = 2
    while bit < ranks:
        run //= 2
        keeps = (rank // bit) % 2
        pairs = [(t, t ^ bit) for t in range(ranks)]
        sent = run_of(kept, 1 - keeps, run) + run_of(received, 1 - keeps, run).astype(f32)
        kept = run_of(kept, keeps, run) + run_of(received, keeps, run).astype(f32)
        received = lax.ppermute(sent.astype(bf16), "tensor", pairs)
        squares = squares + lax.ppermute(squares, "tensor", pairs)
        bit *= 2
    mean_sq = squares.reshape(count, ranks, own) / (HEADS * HEAD_DIM)
    factors = lax.rsqrt(pick(mean_sq, 1, rank) + epsilon)
    final = (kept + received.astype(f32)).reshape(count, own, -1) * factors[:, :, None]
    final = lax.all_to_all(final.astype(bf16), "seq", split_axis=0, concat_axis=0, tiled=True)
    layer_out = final.transpose(1, 0, 2).reshape(own, count * final.shape[2])
    return (layer_out, jnp.max(top))


def solution(mesh):
    return jax.shard_map(
        by_heads if splits(mesh) else by_tokens,
        mesh=mesh,
        in_specs=(
            P(("seq", "tensor"), None),
            P(),
            P("seq", "tensor"),
            P("seq", "tensor", None, None),
            P("seq", "tensor"),
            P(None, "tensor"),
            P(None, "tensor", None, None),
            P(None, "tensor"),
            P(None, "tensor", None, None),
            P("tensor"),
            P("tensor"),
            P("tensor"),
            P("tensor", None, None),
            P("tensor"),
            P("tensor", "seq"),
        ),
        out_specs=(P(("seq", "tensor"), None), P()),
        check_vma=False,
    )
```

```python
import functools

import jax
import jax.numpy as jnp
from jax import lax
from jax.experimental import pallas as pl
from jax.experimental.pallas import tpu as pltpu
from jax.sharding import PartitionSpec as P

HEADS = 128
HEAD_DIM = 64
STATE = 128
GROUPS = 8
KERNEL = 4
SPAN = 128


epsilon = 1e-05
quant_range = 448.0


def from_behind(value, axis, steps):
    count = lax.axis_size(axis)
    first, last = (max(0, -steps), min(count, count - steps))
    return lax.ppermute(value, axis, [(source, source + steps) for source in range(first, last)])


def carried_in(shard, axis, combine, identity):
    count, here = (lax.axis_size(axis), lax.axis_index(axis))
    everything = jax.tree.map(
        lambda part, kind: lax.all_gather(part.astype(kind), axis),
        shard,
        (jnp.bfloat16, jnp.bfloat16),
    )
    start = jax.tree.map(
        lambda part, zero: jnp.broadcast_to(jnp.asarray(zero, part.dtype), part.shape),
        shard,
        identity,
    )

    def turn(k, before):
        reached = k < here
        new = combine(
            before, jax.tree.map(lambda part, own: part[k].astype(own.dtype), everything, shard)
        )
        return jax.tree.map(lambda a, b: jnp.where(reached, a, b), new, before)

    return lax.fori_loop(0, count, turn, start)


def depthwise(before, projected, conv_taps, length):
    extended = jnp.concatenate([before, projected], axis=0)
    summed = conv_taps[0] * extended[0:length]
    for offset in range(1, KERNEL):
        summed = summed + conv_taps[offset] * extended[offset : offset + length]
    return jax.nn.silu(summed).astype(jnp.bfloat16)


def combine(earlier, later):
    return (earlier[0] * later[0], later[0][:, None, None] * earlier[1] + later[1])


def by_tokens(
    hidden_in,
    prev_amax,
    w_x,
    w_bc,
    w_dt,
    conv_x,
    conv_bc,
    conv_state_x,
    conv_state_bc,
    dt_bias,
    decay_rate,
    skip,
    init_state,
    norm_gain,
    w_out,
):
    margin = KERNEL - 1
    gathered = lax.all_gather(hidden_in, "tensor", axis=0, tiled=True)
    abs_max = lax.pmax(jnp.max(jnp.abs(gathered.astype(jnp.float32))), "seq")
    in_scale = prev_amax / quant_range
    leading = lax.axis_index("seq") == 0
    row_count = gathered.shape[0]
    bc_width = w_bc.shape[1] * w_bc.shape[2] * w_bc.shape[3]
    bc_rows = jnp.reshape(w_bc, (w_bc.shape[0], bc_width))
    scaled = gathered.astype(jnp.float32) * (quant_range / prev_amax)
    quant = jnp.clip(scaled, -quant_range, quant_range).astype(jnp.bfloat16)
    pieces = (
        lax.all_gather(w_x, "seq", axis=0, tiled=True),
        lax.all_gather(bc_rows, "seq", axis=0, tiled=True),
        lax.all_gather(w_dt, "seq", axis=0, tiled=True),
    )
    x_proj, bc_proj, dt_proj = tuple(
        (
            jnp.dot(quant, weight_piece, preferred_element_type=jnp.float32)
            for weight_piece in pieces
        )
    )
    x_whole = (x_proj * in_scale).astype(jnp.bfloat16)
    bc_whole = (bc_proj * in_scale).astype(jnp.bfloat16)
    dt_raw = dt_proj * in_scale
    state_bc = jnp.reshape(conv_state_bc, (margin, bc_width))
    received = from_behind(
        (x_whole[row_count - margin :], bc_whole[row_count - margin :]), "seq", 1
    )
    x_edge = jnp.where(leading, conv_state_x, received[0])
    bc_edge = jnp.where(leading, state_bc, received[1])
    x_act = depthwise(x_edge, x_whole, conv_x, row_count)
    bc_act = depthwise(bc_edge, bc_whole, jnp.reshape(conv_bc, (KERNEL, bc_width)), row_count)
    step_size = jax.nn.softplus(dt_raw + dt_bias)
    heads_here = step_size.shape[1]
    groups_here = w_bc.shape[1]
    per_group = HEADS // GROUPS
    blocks = row_count // SPAN
    x_blocks = x_act.reshape(blocks, SPAN, heads_here, HEAD_DIM)
    bc_blocks = bc_act.reshape(blocks, SPAN, groups_here, 2, STATE)
    in_map = bc_blocks[:, :, :, 0]
    out_map = bc_blocks[:, :, :, 1]
    step_blocks = step_size.reshape(blocks, SPAN, heads_here)
    cum_blocks = jnp.cumsum(-step_blocks * decay_rate, axis=1)
    index_row = jnp.arange(SPAN, dtype=jnp.int32)
    lower_mask = index_row[:, None] >= index_row[None, :]
    intersection = jnp.einsum(
        "ctgn,cugn->cgtu", out_map, in_map, preferred_element_type=jnp.float32
    )
    intersection = jnp.repeat(intersection, per_group, axis=1)
    cum_heads = jnp.transpose(cum_blocks, (0, 2, 1))
    log_gap = cum_heads[:, :, :, None] - cum_heads[:, :, None, :]
    decay = jnp.exp(jnp.where(lower_mask[None, None], log_gap, -1e30))
    step_heads = jnp.transpose(step_blocks, (0, 2, 1))
    weights = (intersection * decay * step_heads[:, :, None, :]).astype(jnp.bfloat16)
    local_part = jnp.einsum(
        "chtu,cuhp->cthp", weights, x_blocks, preferred_element_type=jnp.float32
    )
    last_cum = cum_blocks[:, SPAN - 1, :]
    x_weighted = (
        x_blocks.astype(jnp.float32)
        * (step_blocks * jnp.exp(last_cum[:, None, :] - cum_blocks))[:, :, :, None]
    ).astype(jnp.bfloat16)
    in_heads = jnp.repeat(in_map, per_group, axis=2)
    added = jnp.einsum("cuhp,cuhn->chpn", x_weighted, in_heads, preferred_element_type=jnp.float32)

    def carry_on(carried, element):
        block_decay, block_added = element
        return (block_decay[:, None, None] * carried + block_added, carried)

    empty_state = jnp.zeros((heads_here, HEAD_DIM, STATE), jnp.float32)
    device_state, entering = lax.scan(carry_on, empty_state, (jnp.exp(last_cum), added))
    device_decay = jnp.exp(jnp.sum(last_cum, axis=0))
    seeded = device_state + jnp.where(leading, device_decay[:, None, None] * init_state, 0.0)
    identity = (jnp.ones_like(device_decay), jnp.zeros_like(device_state))
    scanned = carried_in((device_decay, seeded), "seq", combine, identity)
    incoming = jnp.where(leading, init_state, scanned[1])
    prefix = jnp.exp(jnp.cumsum(last_cum, axis=0) - last_cum)
    states_in = entering + prefix[:, :, None, None] * incoming[None]
    out_heads = jnp.repeat(out_map, per_group, axis=2).astype(jnp.float32)
    carried_part = (
        jnp.einsum("cthn,chpn->cthp", out_heads, states_in, precision=lax.Precision.HIGHEST)
        * jnp.exp(cum_blocks)[:, :, :, None]
    )
    ssm_out = local_part + carried_part + skip[None, None, :, None] * x_blocks.astype(jnp.float32)
    ssm_out = ssm_out.reshape(row_count, heads_here * HEAD_DIM)
    squares = lax.psum(jnp.sum(ssm_out * ssm_out, axis=1), "tensor")
    mean_sq = squares / (HEADS * HEAD_DIM)
    normed = (ssm_out * lax.rsqrt(mean_sq + epsilon)[:, None] * norm_gain).astype(jnp.bfloat16)
    partial_out = jnp.dot(
        normed, lax.all_gather(w_out, "seq", axis=1, tiled=True), preferred_element_type=jnp.float32
    )
    layer_out = lax.psum_scatter(
        partial_out.astype(jnp.bfloat16), "tensor", scatter_dimension=0, tiled=True
    )
    return (layer_out, abs_max)


PAIR = 2
LINE = 4
ROWS = 8
CUTS = 2
SMEM = pl.BlockSpec(memory_space=pltpu.SMEM)
VMEM = pl.BlockSpec(memory_space=pltpu.VMEM)
HBM = pl.BlockSpec(memory_space=pltpu.HBM)
HIGHEST = lax.Precision.HIGHEST


def splits(mesh):
    count, ranks = (mesh.shape["seq"], mesh.shape["tensor"])
    heads_all, groups_here = (HEADS // ranks, GROUPS // ranks)
    if count != PAIR * LINE or groups_here != PAIR or ranks & (ranks - 1):
        return False
    heads_here = heads_all // count
    return 2 * heads_here == ROWS and heads_here * HEAD_DIM == 2 * SPAN


def nt_dot(a, b, **kw):
    return lax.dot_general(
        a, b, (((1,), (1,)), ((), ())), preferred_element_type=jnp.float32, **kw
    )


def project_kernel(ranks, place_ref, factor_ref, *refs):
    hidden_in = [refs[x * ranks : (x + 1) * ranks] for x in range(PAIR)]
    refs = refs[PAIR * ranks :]
    w_in, x_far, own_bc, other_bc, own_dt, other_dt = refs[:6]
    far_refs = [refs[6 + m * CUTS : 6 + (m + 1) * CUTS] for m in range(LINE // 2)]
    refs = refs[6 + CUTS * (LINE // 2) :]
    near_refs, sent_refs = (refs[: LINE // 2], refs[LINE // 2 : LINE])
    bc_ref, largest_ref, hidden_buf, own_x, quant_ref, near_dt, all_dt, arrived = refs[LINE:]
    copies = [
        [
            pltpu.make_async_copy(
                hidden_in[x][j], hidden_buf.at[x, j], arrived.at[x * ranks + j]
            )
            for j in range(ranks)
        ]
        for x in range(PAIR)
    ]
    own_copy = pltpu.make_async_copy(w_in, own_x, arrived.at[PAIR * ranks])
    for row in copies:
        for copy in row:
            copy.start()
    own_copy.start()
    side, z = (place_ref[1], place_ref[2])
    factor = factor_ref[0]
    depth = own_x.shape[0]
    largest = None
    for x in range(PAIR):
        for j in range(ranks):
            copies[x][j].wait()
            for k in range(LINE):
                block = (k ^ z) * PAIR + (side ^ x)
                for half in range(PAIR):
                    cut = slice(half * depth, (half + 1) * depth)
                    values = hidden_buf[x, j, k, :, cut].astype(jnp.float32)
                    scaled = jnp.clip(values * factor, -quant_range, quant_range)
                    quant_ref[half, block, j] = scaled.astype(jnp.bfloat16)
                    top = jnp.max(jnp.abs(values).reshape(-1, ROWS, depth), axis=0)
                    largest = top if largest is None else jnp.maximum(largest, top)
    width = largest_ref.shape[1]
    top = largest[:, :width]
    for at in range(width, depth, width):
        top = jnp.maximum(top, largest[:, at : at + width])
    largest_ref[...] = top
    own_copy.wait()

    channels = near_refs[0].shape[1]
    tokens = bc_ref.shape[0]
    rows = tokens // CUTS
    blocks = quant_ref.shape[1] // CUTS
    extra = rows // channels * ROWS
    upper = lax.broadcasted_iota(jnp.int32, (ROWS, channels), 0) < ROWS // 2

    def steps_of(dt_ref, run):
        dt = dt_ref[run // 2]
        pieces = []
        for at in range(0, rows, channels):
            piece = dt[:, at : at + channels]
            turned = pltpu.roll(piece, ROWS // 2, 0)
            lower_run = jnp.where(upper, piece, turned)
            upper_run = jnp.where(upper, turned, piece)
            pieces.append(split_parts(jnp.where(run % 2 == 0, lower_run, upper_run), upper))
        return jnp.concatenate(pieces, axis=0).astype(jnp.bfloat16)

    def columns(run):
        return pl.ds(pl.multiple_of(run * channels, channels), channels)

    for cut in range(CUTS):
        part = slice(cut * blocks, (cut + 1) * blocks)
        near = quant_ref[side, part].reshape(rows, depth)
        far = quant_ref[1 - side, part].reshape(rows, depth)

        def both(own, other):
            return jnp.dot(near, own, preferred_element_type=jnp.float32) + jnp.dot(
                far, other, preferred_element_type=jnp.float32
            )

        at_rows = slice(cut * rows, (cut + 1) * rows)
        extra_rows = slice(tokens + cut * extra, tokens + (cut + 1) * extra)
        ours = nt_dot(own_dt[...], near)
        near_dt[...] = ours.reshape(near_dt.shape)
        all_dt[...] = (ours + nt_dot(other_dt[...], far)).reshape(all_dt.shape)
        bc_ref[at_rows] = both(own_bc[...], other_bc[...]).astype(jnp.bfloat16)
        for m in range(LINE // 2):
            owner = z ^ (m + LINE // 2)
            run = side * LINE + owner
            other = x_far[:, columns(owner % (LINE // 2))]
            far_ref = far_refs[m][cut]
            far_ref[:rows] = both(own_x[:, columns(run)], other).astype(jnp.bfloat16)
            far_ref[rows:] = steps_of(all_dt, run)
            for out_refs, way in ((near_refs, side), (sent_refs, 1 - side)):
                run = way * LINE + (z ^ m)
                product = jnp.dot(near, own_x[:, columns(run)], preferred_element_type=jnp.float32)
                out_refs[m][at_rows] = product.astype(jnp.bfloat16)
                out_refs[m][extra_rows] = steps_of(near_dt, run)


def split_parts(values, upper):
    top = values.astype(jnp.bfloat16).astype(jnp.float32)
    return jnp.where(upper, top, values - top)


def project(place, factor, hidden, w_x, weights):
    line, own, wide = hidden[0].shape
    ranks = len(hidden) // PAIR
    depth, x_wide = (weights[0].shape[0], 2 * weights[0].shape[1])
    channels, maps_wide = (x_wide // LINE, weights[1].shape[1])
    tokens = line * PAIR * ranks * own
    extra = tokens // channels * ROWS
    dt_shape = (weights[-1].shape[0] // ROWS, ROWS, tokens // CUTS)
    payload = jax.ShapeDtypeStruct((tokens + extra, channels), jnp.bfloat16)
    maps = jax.ShapeDtypeStruct((tokens, maps_wide), jnp.bfloat16)
    largest = jax.ShapeDtypeStruct((ROWS, 128), jnp.float32)
    run = jax.ShapeDtypeStruct(((tokens + extra) // CUTS, channels), jnp.bfloat16)
    outs = [run] * (CUTS * (LINE // 2)) + [payload] * LINE + [maps, largest]
    return pl.pallas_call(
        functools.partial(project_kernel, ranks),
        in_specs=[SMEM, SMEM] + [HBM] * (len(hidden) + 1) + [VMEM] * len(weights),
        out_specs=[VMEM] * len(outs),
        scratch_shapes=[
            pltpu.VMEM((PAIR, ranks, line, own, wide), jnp.bfloat16),
            pltpu.VMEM(w_x.shape, w_x.dtype),
            pltpu.VMEM((PAIR, line * PAIR, ranks, own, depth), jnp.bfloat16),
            pltpu.VMEM(dt_shape, jnp.float32),
            pltpu.VMEM(dt_shape, jnp.float32),
            pltpu.SemaphoreType.DMA((PAIR * ranks + 1,)),
        ],
        out_shape=outs,
        compiler_params=pltpu.CompilerParams(vmem_limit_bytes=32 * 2**20),
        cost_estimate=pl.CostEstimate(
            flops=2 * tokens * wide * (x_wide + maps_wide),
            bytes_accessed=2 * tokens * (wide + x_wide),
            transcendentals=0,
        ),
        name="project",
    )(place, factor, *hidden, w_x, *weights)


def onward_kernel(own_ref, received_ref, out_ref):
    rows, channels = own_ref.shape
    tokens = rows * channels // (channels + ROWS)
    total = own_ref[:tokens].astype(jnp.float32) + received_ref[:tokens].astype(jnp.float32)
    out_ref[:tokens] = total.astype(jnp.bfloat16)
    upper = lax.broadcasted_iota(jnp.int32, (ROWS, channels), 0) < ROWS // 2
    extra = own_ref[tokens:].astype(jnp.float32) + received_ref[tokens:].astype(jnp.float32)
    pieces = []
    for at in range(0, rows - tokens, ROWS):
        piece = extra[at : at + ROWS]
        pieces.append(split_parts(piece + pltpu.roll(piece, ROWS // 2, 0), upper))
    out_ref[tokens:] = jnp.concatenate(pieces, axis=0).astype(jnp.bfloat16)


def onward(own, received):
    return pl.pallas_call(
        onward_kernel,
        in_specs=[VMEM, VMEM],
        out_specs=VMEM,
        out_shape=jax.ShapeDtypeStruct(own.shape, own.dtype),
        compiler_params=pltpu.CompilerParams(vmem_limit_bytes=8 * 2**20),
        cost_estimate=pl.CostEstimate(
            flops=own.size, bytes_accessed=6 * own.size, transcendentals=0
        ),
        name="onward",
    )(own, received)


def turned_rank(rank, ranks):
    turned = 0
    while ranks > 1:
        turned, rank, ranks = (2 * turned + rank % 2, rank // 2, ranks // 2)
    return turned


def scan_kernel(wholes, place_ref, scale_ref, *refs):
    x_refs, run_refs, bc_refs = (refs[:wholes], refs[wholes:-9], refs[-9:-6])
    small_ref, largest_ref, state_ref, out_ref, x_buf, bc_buf = refs[-6:]
    tokens, channels = bc_refs[0].shape
    blocks = tokens // SPAN
    run_blocks = blocks // CUTS
    heads = channels // HEAD_DIM
    rank, z = (place_ref[0], place_ref[2])
    ranks = place_ref.shape[0] - 3
    own = SPAN // ranks
    edge = ROWS
    in_scale = scale_ref[0]
    at_end = (z == 0) | (z == LINE - 1)
    x_buf[:edge] = small_ref[:edge]
    bc_buf[:edge] = small_ref[edge : 2 * edge]
    state = state_ref[...].T

    for block in range(blocks):
        for true_rank in range(ranks):
            turn = (true_rank ^ rank) * own
            source = pl.ds(pl.multiple_of(block * SPAN + turn, own), own)
            at = edge + block * SPAN + true_rank * own
            at = slice(at, at + own)
            total = sum(ref[source].astype(jnp.float32) for ref in x_refs)
            inside = pl.ds(pl.multiple_of(block % run_blocks * SPAN + turn, own), own)
            for ref in run_refs[block // run_blocks :: CUTS]:
                total = total + ref[inside].astype(jnp.float32)
            total = total * in_scale
            x_buf[at] = total.astype(jnp.bfloat16).astype(jnp.float32)
            near, far, done = (ref[source].astype(jnp.float32) for ref in bc_refs)
            total = ((near + far) * in_scale).astype(jnp.bfloat16).astype(jnp.float32)
            bc_buf[at] = jnp.where(at_end, done, total)

    taps = 2 * edge

    def activate(buf, row, block):
        start = edge - (KERNEL - 1) + block * SPAN
        summed = small_ref[row : row + 1] * buf[start : start + SPAN]
        for k in range(1, KERNEL):
            summed = summed + small_ref[row + k : row + k + 1] * buf[start + k : start + k + SPAN]
        return (summed / (1.0 + jnp.exp(-summed))).astype(jnp.bfloat16)

    skip = small_ref[taps + 2 * KERNEL : taps + 2 * KERNEL + 1]
    gain = small_ref[taps + 2 * KERNEL + 1 : taps + 2 * KERNEL + 2]
    bias = small_ref[4 * edge :, :SPAN]
    rate = small_ref[4 * edge :, SPAN:]

    up = lax.broadcasted_iota(jnp.int32, (SPAN, SPAN), 0)
    across = lax.broadcasted_iota(jnp.int32, (SPAN, SPAN), 1)
    lane = lax.broadcasted_iota(jnp.int32, (SPAN, channels), 1)
    lower = up >= across
    upper = (up <= across).astype(jnp.float32)
    lanes = across[:ROWS]

    dt = sum(ref[tokens:].astype(jnp.float32) for ref in x_refs)
    run = tokens // CUTS
    runs = [
        sum(ref[run:].astype(jnp.float32) for ref in run_refs[cut::CUTS]) for cut in range(CUTS)
    ]
    dt = dt + jnp.concatenate(runs, axis=0)
    steps = []
    wide = channels // SPAN
    for block in range(blocks):
        tile = dt[block // wide * ROWS : (block // wide + 1) * ROWS]
        cut = tile[:, block % wide * SPAN : (block % wide + 1) * SPAN]
        cut = (cut + pltpu.roll(cut, ROWS // 2, 0)) * in_scale
        bit = 1
        while bit < ranks:
            shift = bit * own
            flipped = jnp.where(
                (lanes // shift) % 2 == 1,
                pltpu.roll(cut, shift, 1),
                pltpu.roll(cut, SPAN - shift, 1),
            )
            cut = jnp.where((rank & bit) != 0, flipped, cut)
            bit *= 2
        raw = cut + bias
        steps.append(jnp.maximum(raw, 0.0) + jnp.log1p(jnp.exp(-jnp.abs(raw))))
    drops = jnp.concatenate([-step * rate for step in steps], axis=0)
    cums = jnp.dot(drops, upper, precision=HIGHEST, preferred_element_type=jnp.float32)

    sums = jnp.zeros((SPAN, SPAN), jnp.float32)
    for block in range(blocks):
        x_act = activate(x_buf, taps, block)
        bc_act = activate(bc_buf, taps + KERNEL, block)
        in_map, out_map = (bc_act[:, :STATE], bc_act[:, STATE:])
        step, cum = (steps[block], cums[block * ROWS : (block + 1) * ROWS])
        last = cum[:, SPAN - 1 : SPAN]
        turned = jnp.concatenate(
            [
                cum,
                step * jnp.exp(last - cum),
                jnp.exp(cum),
                jnp.zeros((SPAN - 3 * ROWS, SPAN), jnp.float32),
            ],
            axis=0,
        ).T

        def spread(row):
            result = jnp.broadcast_to(turned[:, row : row + 1], (SPAN, channels))
            for h in range(1, heads):
                result = jnp.where(lane >= h * HEAD_DIM, turned[:, row + h : row + h + 1], result)
            return result

        inner = jnp.where(lower, nt_dot(out_map, in_map), 0.0)
        x_wide = x_act.astype(jnp.float32)
        weights, spaced = ([], [])
        for h in range(heads):
            gap = jnp.where(lower, turned[:, h : h + 1] - cum[h : h + 1], 0.0)
            weights.append((inner * jnp.exp(gap) * step[h : h + 1]).astype(jnp.bfloat16))
            inside = (lane >= h * HEAD_DIM) & (lane < (h + 1) * HEAD_DIM)
            spaced.append(jnp.where(inside, x_wide, 0.0).astype(jnp.bfloat16))
        local_part = jnp.dot(
            jnp.concatenate(weights, axis=1),
            jnp.concatenate(spaced, axis=0),
            preferred_element_type=jnp.float32,
        )
        grown = spread(2 * ROWS)
        x_weighted = (x_wide * spread(ROWS)).astype(jnp.bfloat16)
        added = lax.dot_general(
            in_map, x_weighted, (((0,), (0,)), ((), ())), preferred_element_type=jnp.float32
        )
        high = state.astype(jnp.bfloat16)
        rest = (state - high.astype(jnp.float32)).astype(jnp.bfloat16)
        carried = jnp.dot(
            jnp.concatenate([out_map, out_map], axis=1),
            jnp.concatenate([high, rest], axis=0),
            preferred_element_type=jnp.float32,
        )
        ssm_out = local_part + grown * carried + skip * x_wide
        state = grown[SPAN - 1 : SPAN] * state + added
        gained = (ssm_out * gain).astype(jnp.bfloat16)
        for true_rank in range(ranks):
            at = (turned_rank(true_rank, ranks) * blocks + block) * own
            out_ref[at : at + own] = gained[true_rank * own : (true_rank + 1) * own]
        summed = jnp.sum(ssm_out * ssm_out, axis=1, keepdims=True)
        sums = jnp.where(across == block, summed, sums)

    whole = sums.T[:ROWS]
    top = whole.astype(jnp.bfloat16).astype(jnp.float32)
    largest = jnp.broadcast_to(jnp.max(largest_ref[...]), (ROWS, channels))
    extra = jnp.concatenate([jnp.concatenate([top, whole - top], axis=1), largest], axis=0)
    out_ref[tokens:] = extra.astype(jnp.bfloat16)


def scan(place, in_scale, sums, runs, maps, small, largest, state):
    channels = sums[0].shape[1]
    tokens = maps[0].shape[0]

    out = jax.ShapeDtypeStruct((tokens + 2 * ROWS, channels), jnp.bfloat16)
    return pl.pallas_call(
        functools.partial(scan_kernel, len(sums)),
        in_specs=[SMEM, SMEM] + [VMEM] * (len(sums) + len(runs) + len(maps) + 3),
        out_specs=VMEM,
        scratch_shapes=[
            pltpu.VMEM((tokens + ROWS, channels), jnp.float32),
            pltpu.VMEM((tokens + ROWS, 2 * STATE), jnp.float32),
        ],
        out_shape=out,
        compiler_params=pltpu.CompilerParams(vmem_limit_bytes=20 * 2**20),
        cost_estimate=pl.CostEstimate(
            flops=8 * tokens * SPAN * channels,
            bytes_accessed=8 * tokens * channels,
            transcendentals=tokens * (channels + 8 * SPAN),
        ),
        name="scan",
    )(place, in_scale, *sums, *runs, *maps, small, largest, state)


def by_heads(
    hidden_in,
    prev_amax,
    w_x,
    w_bc,
    w_dt,
    conv_x,
    conv_bc,
    conv_state_x,
    conv_state_bc,
    dt_bias,
    decay_rate,
    skip,
    init_state,
    norm_gain,
    w_out,
):
    margin = KERNEL - 1
    count, here = (lax.axis_size("seq"), lax.axis_index("seq"))
    ranks, rank = (lax.axis_size("tensor"), lax.axis_index("tensor"))
    z, side = (here // PAIR, here % PAIR)
    place_of = side * LINE + z
    f32, bf16 = (jnp.float32, jnp.bfloat16)
    own, width = hidden_in.shape
    depth = w_x.shape[0]
    channels = w_x.shape[1] // count
    heads_here = w_dt.shape[1] // count
    in_scale = (prev_amax / quant_range).reshape(1)
    factor = (quant_range / prev_amax).reshape(1)
    place = jnp.stack([rank, side, z] + [rank] * ranks).astype(jnp.int32)

    def pick(array, axis, index):
        return lax.dynamic_index_in_dim(array, index, axis, keepdims=False)

    def along(value, pairs):
        moves = [(a * PAIR + x, b * PAIR + x) for a, b in pairs for x in range(PAIR)]
        return lax.ppermute(value, "seq", moves)

    def across(value):
        return lax.ppermute(value, "seq", [(s, s ^ 1) for s in range(count)])

    def of_heads(array):
        return jnp.repeat(array, HEAD_DIM)[None]

    by_channel = jnp.concatenate(
        [conv_state_x.astype(f32), conv_x, of_heads(skip), norm_gain[None]], axis=0
    )
    by_channel = lax.dynamic_slice_in_dim(by_channel, place_of * channels, channels, axis=1)
    by_map = jnp.concatenate([conv_state_bc.astype(f32), conv_bc], axis=0)
    by_map = pick(by_map, 1, side).reshape(margin + KERNEL, 2 * STATE)
    by_head = jnp.stack([dt_bias, decay_rate]).reshape(2, count, heads_here)
    by_head = jnp.tile(pick(by_head, 1, place_of).T, (ROWS // heads_here, 1))
    by_head = jnp.repeat(by_head, SPAN, axis=1)
    blank = jnp.zeros((ROWS - margin, channels), f32)
    small = jnp.concatenate(
        [
            blank,
            by_channel[:margin],
            blank,
            by_map[:margin],
            by_channel[margin : margin + KERNEL],
            by_map[margin:],
            by_channel[margin + KERNEL :],
            jnp.zeros((2 * ROWS - 2 * KERNEL - 2, channels), f32),
            by_head,
        ],
        axis=0,
    )

    start_state = lax.dynamic_slice_in_dim(
        init_state, place_of * heads_here, heads_here, axis=0
    ).reshape(channels, STATE)

    tie = lax.optimization_barrier
    half_run = LINE // 2 * channels
    opposite = (z // (LINE // 2)) ^ 1
    at = ((1 - side) * 2 + opposite) * half_run
    x_sent = lax.dynamic_slice_in_dim(w_x, at, half_run, axis=1)
    x_sent, hidden_in = tie((x_sent, hidden_in))
    x_far = across(x_sent)
    x_far, maps_sent, dt_sent = tie(
        (x_far, pick(w_bc, 1, 1 - side).reshape(depth, 2 * STATE), w_dt.T)
    )
    bc_other, dt_other = (across(maps_sent), across(dt_sent))
    bc_own = pick(w_bc, 1, side).reshape(depth, 2 * STATE)

    def line_columns(m):
        return lax.dynamic_slice_in_dim(hidden_in, (z ^ m) * PAIR * depth, PAIR * depth, axis=1)

    arrived = [line_columns(0)]
    for m in range(1, LINE):
        arrived.append(along(line_columns(m), [(s, s ^ m) for s in range(LINE)]))
    stacked = jnp.stack(arrived)
    beyond_pair = across(stacked)
    beyond_pair, small, start_state, bc_own, dt_sent = tie(
        (beyond_pair, small, start_state, bc_own, dt_sent)
    )
    rows = []
    for mine in (stacked, beyond_pair):
        ours = [mine]
        for j in range(1, ranks):
            bit = j & -j
            pairs = [(t, t ^ bit) for t in range(ranks)]
            if mine is beyond_pair and j == ranks - 1:
                ours[j - bit], dt_other = tie((ours[j - bit], dt_other))
            ours.append(lax.ppermute(ours[j - bit], "tensor", pairs))
        rows.extend(ours)

    start, end = (0, LINE - 1)
    at_end = (z == start) | (z == end)
    next_start, next_end = (1, LINE - 2)
    inward = [(start, next_start), (end, next_end)]
    outward = [(next_start, start), (next_end, end)]
    middle = [(next_start, next_end), (next_end, next_start)]
    over_middle = [(next_start, end), (next_end, start)]
    beside_pairs = [(s, s ^ 1) for s in range(LINE)]
    weights = (x_far, bc_own, bc_other, dt_sent, dt_other)
    shares = project(place, factor, rows, w_x, weights)
    over, far = (shares[:CUTS], shares[CUTS : 2 * CUTS])
    mine, near, mine_sent, near_sent, maps, largest = shares[2 * CUTS :]

    map_hop = along(maps, inward)
    hops_far = [along(run, inward) for run in far]
    hops_over = [along(run, inward) for run in over]
    near = onward(near, across(near_sent))
    got_mine = across(mine_sent)
    near_out = along(near, outward)
    map_sum = (maps.astype(f32) + map_hop.astype(f32)).astype(bf16)
    map_far = along(map_sum, middle)
    map_done = ((map_sum.astype(f32) + map_far.astype(f32)) * in_scale).astype(bf16)
    got_end, got_next = ([], [])
    for own_run, hop in zip(over, hops_far):
        value = onward(own_run, hop)
        got_end.append(along(value, over_middle))
    hops_over[0], near_out, unused = tie((hops_over[0], near_out, value))
    for own_run, hop in zip(far, hops_over):
        value = onward(own_run, hop)
        got_next.append(along(value, middle))
        if len(got_next) == 1:
            near, unused = tie((near, value))
            near_in = along(near, inward)
    map_done, got_end[0], got_mine = tie((map_done, got_end[0], got_mine))
    map_done = along(map_done, outward)
    gained = scan(
        place,
        in_scale,
        [mine, got_mine, near_out, near_in],
        [*got_end, *got_next],
        [map_sum, map_far, map_done],
        small,
        largest,
        start_state,
    )

    tokens = gained.shape[0] - 2 * ROWS
    beside = along(gained, beside_pairs)
    facing = along(gained, middle)
    second = jnp.where(at_end, along(facing, outward), facing)
    beyond = along(beside, middle)
    third = jnp.where(at_end, along(beyond, outward), beyond)
    far_own = across(gained)
    far_beside = across(beside)
    second, far_own = tie((second, far_own))
    far_second = across(second)
    third, far_beside = tie((third, far_beside))
    far_third = across(third)
    two, three = (jnp.where(at_end, 2, 3), jnp.where(at_end, 3, 2))

    def rows_for(x, m):
        at = ((side ^ x) * LINE + (z ^ m)) * channels
        return lax.dynamic_slice_in_dim(w_out, at, channels, axis=0)

    total = None
    tails = [far_third[tokens:]]
    for x, m, piece in (
        (0, 0, gained),
        (1, 0, far_own),
        (0, 1, beside),
        (1, 1, far_beside),
        (0, two, second),
        (1, two, far_second),
        (0, three, third),
    ):
        product = jnp.dot(piece, rows_for(x, m), preferred_element_type=f32)
        total = product if total is None else total + product
        tails.append(piece[tokens:])
    total, far_third = tie((total, far_third))
    last_rows = rows_for(1, three)
    tails = [tail.astype(f32) for tail in tails]
    squares = sum(tail[:ROWS, :SPAN] + tail[:ROWS, SPAN:] for tail in tails)
    top = functools.reduce(jnp.maximum, [tail[ROWS:, :SPAN] for tail in tails])

    def run_of(array, index, run):
        return lax.dynamic_slice_in_dim(array, index * run, run, axis=0)

    def first_sum(index):
        block, so_far = (run_of(far_third, index, run), run_of(total, index, run))
        return so_far + jnp.dot(block, last_rows, preferred_element_type=f32)

    run = tokens // 2
    keeps = rank % 2
    pairs = [(t, t ^ 1) for t in range(ranks)]
    received = lax.ppermute(first_sum(1 - keeps).astype(bf16), "tensor", pairs)
    kept = first_sum(keeps)
    squares = squares + lax.ppermute(squares, "tensor", pairs)
    bit = 2
    while bit < ranks:
        run //= 2
        keeps = (rank // bit) % 2
        pairs = [(t, t ^ bit) for t in range(ranks)]
        sent = run_of(kept, 1 - keeps, run) + run_of(received, 1 - keeps, run).astype(f32)
        kept = run_of(kept, keeps, run) + run_of(received, keeps, run).astype(f32)
        received = lax.ppermute(sent.astype(bf16), "tensor", pairs)
        squares = squares + lax.ppermute(squares, "tensor", pairs)
        bit *= 2
    mean_sq = squares.reshape(count, ranks, own) / (HEADS * HEAD_DIM)
    factors = lax.rsqrt(pick(mean_sq, 1, rank) + epsilon)
    final = (kept + received.astype(f32)).reshape(count, own, -1) * factors[:, :, None]
    final = lax.all_to_all(final.astype(bf16), "seq", split_axis=0, concat_axis=0, tiled=True)
    layer_out = final.transpose(1, 0, 2).reshape(own, count * final.shape[2])
    return (layer_out, jnp.max(top))


def solution(mesh):
    return jax.shard_map(
        by_heads if splits(mesh) else by_tokens,
        mesh=mesh,
        in_specs=(
            P(("seq", "tensor"), None),
            P(),
            P("seq", "tensor"),
            P("seq", "tensor", None, None),
            P("seq", "tensor"),
            P(None, "tensor"),
            P(None, "tensor", None, None),
            P(None, "tensor"),
            P(None, "tensor", None, None),
            P("tensor"),
            P("tensor"),
            P("tensor"),
            P("tensor", None, None),
            P("tensor"),
            P("tensor", "seq"),
        ),
        out_specs=(P(("seq", "tensor"), None), P()),
        check_vma=False,
    )
```

```python
import functools

import jax
import jax.numpy as jnp
from jax import lax
from jax.experimental import pallas as pl
from jax.experimental.pallas import tpu as pltpu
from jax.sharding import PartitionSpec as P

HEADS = 128
HEAD_DIM = 64
STATE = 128
GROUPS = 8
KERNEL = 4
SPAN = 128


epsilon = 1e-05
quant_range = 448.0


def from_behind(value, axis, steps):
    count = lax.axis_size(axis)
    first, last = (max(0, -steps), min(count, count - steps))
    return lax.ppermute(value, axis, [(source, source + steps) for source in range(first, last)])


def carried_in(shard, axis, combine, identity):
    count, here = (lax.axis_size(axis), lax.axis_index(axis))
    everything = jax.tree.map(
        lambda part, kind: lax.all_gather(part.astype(kind), axis),
        shard,
        (jnp.bfloat16, jnp.bfloat16),
    )
    start = jax.tree.map(
        lambda part, zero: jnp.broadcast_to(jnp.asarray(zero, part.dtype), part.shape),
        shard,
        identity,
    )

    def turn(k, before):
        reached = k < here
        new = combine(
            before, jax.tree.map(lambda part, own: part[k].astype(own.dtype), everything, shard)
        )
        return jax.tree.map(lambda a, b: jnp.where(reached, a, b), new, before)

    return lax.fori_loop(0, count, turn, start)


def depthwise(before, projected, conv_taps, length):
    extended = jnp.concatenate([before, projected], axis=0)
    summed = conv_taps[0] * extended[0:length]
    for offset in range(1, KERNEL):
        summed = summed + conv_taps[offset] * extended[offset : offset + length]
    return jax.nn.silu(summed).astype(jnp.bfloat16)


def combine(earlier, later):
    return (earlier[0] * later[0], later[0][:, None, None] * earlier[1] + later[1])


def by_tokens(
    hidden_in,
    prev_amax,
    w_x,
    w_bc,
    w_dt,
    conv_x,
    conv_bc,
    conv_state_x,
    conv_state_bc,
    dt_bias,
    decay_rate,
    skip,
    init_state,
    norm_gain,
    w_out,
):
    margin = KERNEL - 1
    gathered = lax.all_gather(hidden_in, "tensor", axis=0, tiled=True)
    abs_max = lax.pmax(jnp.max(jnp.abs(gathered.astype(jnp.float32))), "seq")
    in_scale = prev_amax / quant_range
    leading = lax.axis_index("seq") == 0
    row_count = gathered.shape[0]
    bc_width = w_bc.shape[1] * w_bc.shape[2] * w_bc.shape[3]
    bc_rows = jnp.reshape(w_bc, (w_bc.shape[0], bc_width))
    scaled = gathered.astype(jnp.float32) * (quant_range / prev_amax)
    quant = jnp.clip(scaled, -quant_range, quant_range).astype(jnp.bfloat16)
    pieces = (
        lax.all_gather(w_x, "seq", axis=0, tiled=True),
        lax.all_gather(bc_rows, "seq", axis=0, tiled=True),
        lax.all_gather(w_dt, "seq", axis=0, tiled=True),
    )
    x_proj, bc_proj, dt_proj = tuple(
        (
            jnp.dot(quant, weight_piece, preferred_element_type=jnp.float32)
            for weight_piece in pieces
        )
    )
    x_whole = (x_proj * in_scale).astype(jnp.bfloat16)
    bc_whole = (bc_proj * in_scale).astype(jnp.bfloat16)
    dt_raw = dt_proj * in_scale
    state_bc = jnp.reshape(conv_state_bc, (margin, bc_width))
    received = from_behind(
        (x_whole[row_count - margin :], bc_whole[row_count - margin :]), "seq", 1
    )
    x_edge = jnp.where(leading, conv_state_x, received[0])
    bc_edge = jnp.where(leading, state_bc, received[1])
    x_act = depthwise(x_edge, x_whole, conv_x, row_count)
    bc_act = depthwise(bc_edge, bc_whole, jnp.reshape(conv_bc, (KERNEL, bc_width)), row_count)
    step_size = jax.nn.softplus(dt_raw + dt_bias)
    heads_here = step_size.shape[1]
    groups_here = w_bc.shape[1]
    per_group = HEADS // GROUPS
    blocks = row_count // SPAN
    x_blocks = x_act.reshape(blocks, SPAN, heads_here, HEAD_DIM)
    bc_blocks = bc_act.reshape(blocks, SPAN, groups_here, 2, STATE)
    in_map = bc_blocks[:, :, :, 0]
    out_map = bc_blocks[:, :, :, 1]
    step_blocks = step_size.reshape(blocks, SPAN, heads_here)
    cum_blocks = jnp.cumsum(-step_blocks * decay_rate, axis=1)
    index_row = jnp.arange(SPAN, dtype=jnp.int32)
    lower_mask = index_row[:, None] >= index_row[None, :]
    intersection = jnp.einsum(
        "ctgn,cugn->cgtu", out_map, in_map, preferred_element_type=jnp.float32
    )
    intersection = jnp.repeat(intersection, per_group, axis=1)
    cum_heads = jnp.transpose(cum_blocks, (0, 2, 1))
    log_gap = cum_heads[:, :, :, None] - cum_heads[:, :, None, :]
    decay = jnp.exp(jnp.where(lower_mask[None, None], log_gap, -1e30))
    step_heads = jnp.transpose(step_blocks, (0, 2, 1))
    weights = (intersection * decay * step_heads[:, :, None, :]).astype(jnp.bfloat16)
    local_part = jnp.einsum(
        "chtu,cuhp->cthp", weights, x_blocks, preferred_element_type=jnp.float32
    )
    last_cum = cum_blocks[:, SPAN - 1, :]
    x_weighted = (
        x_blocks.astype(jnp.float32)
        * (step_blocks * jnp.exp(last_cum[:, None, :] - cum_blocks))[:, :, :, None]
    ).astype(jnp.bfloat16)
    in_heads = jnp.repeat(in_map, per_group, axis=2)
    added = jnp.einsum("cuhp,cuhn->chpn", x_weighted, in_heads, preferred_element_type=jnp.float32)

    def carry_on(carried, element):
        block_decay, block_added = element
        return (block_decay[:, None, None] * carried + block_added, carried)

    empty_state = jnp.zeros((heads_here, HEAD_DIM, STATE), jnp.float32)
    device_state, entering = lax.scan(carry_on, empty_state, (jnp.exp(last_cum), added))
    device_decay = jnp.exp(jnp.sum(last_cum, axis=0))
    seeded = device_state + jnp.where(leading, device_decay[:, None, None] * init_state, 0.0)
    identity = (jnp.ones_like(device_decay), jnp.zeros_like(device_state))
    scanned = carried_in((device_decay, seeded), "seq", combine, identity)
    incoming = jnp.where(leading, init_state, scanned[1])
    prefix = jnp.exp(jnp.cumsum(last_cum, axis=0) - last_cum)
    states_in = entering + prefix[:, :, None, None] * incoming[None]
    out_heads = jnp.repeat(out_map, per_group, axis=2).astype(jnp.float32)
    carried_part = (
        jnp.einsum("cthn,chpn->cthp", out_heads, states_in, precision=lax.Precision.HIGHEST)
        * jnp.exp(cum_blocks)[:, :, :, None]
    )
    ssm_out = local_part + carried_part + skip[None, None, :, None] * x_blocks.astype(jnp.float32)
    ssm_out = ssm_out.reshape(row_count, heads_here * HEAD_DIM)
    squares = lax.psum(jnp.sum(ssm_out * ssm_out, axis=1), "tensor")
    mean_sq = squares / (HEADS * HEAD_DIM)
    normed = (ssm_out * lax.rsqrt(mean_sq + epsilon)[:, None] * norm_gain).astype(jnp.bfloat16)
    partial_out = jnp.dot(
        normed, lax.all_gather(w_out, "seq", axis=1, tiled=True), preferred_element_type=jnp.float32
    )
    layer_out = lax.psum_scatter(
        partial_out.astype(jnp.bfloat16), "tensor", scatter_dimension=0, tiled=True
    )
    return (layer_out, abs_max)


PAIR = 2
LINE = 4
ROWS = 8
CUTS = 2
SMEM = pl.BlockSpec(memory_space=pltpu.SMEM)
VMEM = pl.BlockSpec(memory_space=pltpu.VMEM)
HIGHEST = lax.Precision.HIGHEST


def splits(mesh):
    count, ranks = (mesh.shape["seq"], mesh.shape["tensor"])
    heads_all, groups_here = (HEADS // ranks, GROUPS // ranks)
    if count != PAIR * LINE or groups_here != PAIR or ranks & (ranks - 1):
        return False
    heads_here = heads_all // count
    return 2 * heads_here == ROWS and heads_here * HEAD_DIM == 2 * SPAN


def nt_dot(a, b, **kw):
    return lax.dot_general(
        a, b, (((1,), (1,)), ((), ())), preferred_element_type=jnp.float32, **kw
    )


def pair_columns(owner, channels):
    at = owner % (LINE // 2) * channels
    return pl.ds(pl.multiple_of(at, channels), channels)


def steps_of(dt, run, upper):
    channels = upper.shape[1]
    dt = dt[run // 2]
    pieces = []
    for at in range(0, dt.shape[1], channels):
        piece = dt[:, at : at + channels]
        turned = pltpu.roll(piece, ROWS // 2, 0)
        lower_run = jnp.where(upper, piece, turned)
        upper_run = jnp.where(upper, turned, piece)
        pieces.append(split_parts(jnp.where(run % 2 == 0, lower_run, upper_run), upper))
    return jnp.concatenate(pieces, axis=0).astype(jnp.bfloat16)


def far_kernel(ranks, place_ref, factor_ref, *refs):
    hidden = [refs[x * ranks : (x + 1) * ranks] for x in range(PAIR)]
    refs = refs[PAIR * ranks :]
    own_x, other_x, own_bc, other_bc, own_dt, other_dt = refs[:6]
    x_refs = refs[6 : 6 + LINE // 2]
    bc_ref, largest_ref, quant_ref, dt_buf = refs[6 + LINE // 2 :]
    side, z = (place_ref[1], place_ref[2])
    factor = factor_ref[0]
    depth = own_x.shape[0]
    largest = None
    for x in range(PAIR):
        for k in range(LINE):
            block = (k ^ z) * PAIR + (side ^ x)
            for j in range(ranks):
                for half in range(PAIR):
                    cut = slice(half * depth, (half + 1) * depth)
                    values = hidden[x][j][k, :, cut].astype(jnp.float32)
                    scaled = jnp.clip(values * factor, -quant_range, quant_range)
                    quant_ref[half, block, j] = scaled.astype(jnp.bfloat16)
                    top = jnp.max(jnp.abs(values).reshape(-1, ROWS, depth), axis=0)
                    largest = top if largest is None else jnp.maximum(largest, top)
    width = largest_ref.shape[1]
    top = largest[:, :width]
    for at in range(width, depth, width):
        top = jnp.maximum(top, largest[:, at : at + width])
    largest_ref[...] = top

    channels = x_refs[0].shape[1]
    tokens = bc_ref.shape[0]
    rows = tokens // CUTS
    blocks = quant_ref.shape[1] // CUTS
    extra = rows // channels * ROWS
    upper = lax.broadcasted_iota(jnp.int32, (ROWS, channels), 0) < ROWS // 2
    for cut in range(CUTS):
        part = slice(cut * blocks, (cut + 1) * blocks)
        near = quant_ref[side, part].reshape(rows, depth)
        far = quant_ref[1 - side, part].reshape(rows, depth)

        def both(own, other):
            return jnp.dot(near, own, preferred_element_type=jnp.float32) + jnp.dot(
                far, other, preferred_element_type=jnp.float32
            )

        at_rows = slice(cut * rows, (cut + 1) * rows)
        extra_rows = slice(tokens + cut * extra, tokens + (cut + 1) * extra)
        bc_ref[at_rows] = both(own_bc[...], other_bc[...]).astype(jnp.bfloat16)
        dt = nt_dot(own_dt[...], near) + nt_dot(other_dt[...], far)
        dt_buf[...] = dt.reshape(dt_buf.shape)
        for m in range(LINE // 2):
            owner = z ^ (m + LINE // 2)
            columns = pair_columns(owner, channels)
            product = both(own_x[:, columns], other_x[:, columns])
            x_refs[m][at_rows] = product.astype(jnp.bfloat16)
            x_refs[m][extra_rows] = steps_of(dt_buf, side * LINE + owner, upper)


def near_kernel(place_ref, quant_ref, own_x, sent_x, own_dt, *refs):
    near_refs, sent_refs, dt_buf = (refs[: LINE // 2], refs[LINE // 2 : LINE], refs[LINE])
    side, z = (place_ref[1], place_ref[2])
    depth, channels = (own_x.shape[0], near_refs[0].shape[1])
    blocks = quant_ref.shape[1] // CUTS
    rows = blocks * quant_ref.shape[2] * quant_ref.shape[3]
    tokens = rows * CUTS
    extra = rows // channels * ROWS
    upper = lax.broadcasted_iota(jnp.int32, (ROWS, channels), 0) < ROWS // 2
    for cut in range(CUTS):
        near = quant_ref[side, cut * blocks : (cut + 1) * blocks].reshape(rows, depth)
        at_rows = slice(cut * rows, (cut + 1) * rows)
        extra_rows = slice(tokens + cut * extra, tokens + (cut + 1) * extra)
        dt_buf[...] = nt_dot(own_dt[...], near).reshape(dt_buf.shape)
        for x_ref, out_refs, way in ((own_x, near_refs, side), (sent_x, sent_refs, 1 - side)):
            for m in range(LINE // 2):
                owner = z ^ m
                weight = x_ref[:, pair_columns(owner, channels)]
                product = jnp.dot(near, weight, preferred_element_type=jnp.float32)
                out_refs[m][at_rows] = product.astype(jnp.bfloat16)
                out_refs[m][extra_rows] = steps_of(dt_buf, way * LINE + owner, upper)


def split_parts(values, upper):
    top = values.astype(jnp.bfloat16).astype(jnp.float32)
    return jnp.where(upper, top, values - top)


def project(place, factor, hidden, far_weights, near_weights):
    line, own, wide = hidden[0].shape
    ranks = len(hidden) // PAIR
    depth, x_wide = far_weights[0].shape
    channels, maps_wide = (x_wide // (LINE // 2), far_weights[2].shape[1])
    tokens = line * PAIR * ranks * own
    extra = tokens // channels * ROWS
    payload = jax.ShapeDtypeStruct((tokens + extra, channels), jnp.bfloat16)
    maps = jax.ShapeDtypeStruct((tokens, maps_wide), jnp.bfloat16)
    largest = jax.ShapeDtypeStruct((ROWS, 128), jnp.float32)
    quant = jax.ShapeDtypeStruct((PAIR, line * PAIR, ranks, own, depth), jnp.bfloat16)
    dt_buf = pltpu.VMEM((near_weights[-1].shape[0] // ROWS, ROWS, tokens // CUTS), jnp.float32)
    outs = [payload] * (LINE // 2) + [maps, largest, quant]
    over, far, maps, largest, quant = pl.pallas_call(
        functools.partial(far_kernel, ranks),
        in_specs=[SMEM, SMEM] + [VMEM] * (len(hidden) + len(far_weights)),
        out_specs=[VMEM] * len(outs),
        scratch_shapes=[dt_buf],
        out_shape=outs,
        compiler_params=pltpu.CompilerParams(vmem_limit_bytes=24 * 2**20),
        cost_estimate=pl.CostEstimate(
            flops=2 * tokens * wide * (x_wide + maps_wide),
            bytes_accessed=2 * tokens * (wide + x_wide),
            transcendentals=0,
        ),
        name="far",
    )(place, factor, *hidden, *far_weights)
    mine, near, mine_sent, near_sent = pl.pallas_call(
        near_kernel,
        in_specs=[SMEM] + [VMEM] * (1 + len(near_weights)),
        out_specs=[VMEM] * LINE,
        scratch_shapes=[dt_buf],
        out_shape=[payload] * LINE,
        compiler_params=pltpu.CompilerParams(vmem_limit_bytes=24 * 2**20),
        cost_estimate=pl.CostEstimate(
            flops=2 * tokens * wide * x_wide,
            bytes_accessed=2 * tokens * (wide + 2 * x_wide),
            transcendentals=0,
        ),
        name="near",
    )(place, quant, *near_weights)
    return over, far, mine, near, mine_sent, near_sent, maps, largest


def onward_kernel(own_ref, received_ref, out_ref):
    rows, channels = own_ref.shape
    tokens = rows * channels // (channels + ROWS)
    total = own_ref[:tokens].astype(jnp.float32) + received_ref[:tokens].astype(jnp.float32)
    out_ref[:tokens] = total.astype(jnp.bfloat16)
    upper = lax.broadcasted_iota(jnp.int32, (ROWS, channels), 0) < ROWS // 2
    extra = own_ref[tokens:].astype(jnp.float32) + received_ref[tokens:].astype(jnp.float32)
    pieces = []
    for at in range(0, rows - tokens, ROWS):
        piece = extra[at : at + ROWS]
        pieces.append(split_parts(piece + pltpu.roll(piece, ROWS // 2, 0), upper))
    out_ref[tokens:] = jnp.concatenate(pieces, axis=0).astype(jnp.bfloat16)


def onward(own, received):
    return pl.pallas_call(
        onward_kernel,
        in_specs=[VMEM, VMEM],
        out_specs=VMEM,
        out_shape=jax.ShapeDtypeStruct(own.shape, own.dtype),
        compiler_params=pltpu.CompilerParams(vmem_limit_bytes=8 * 2**20),
        cost_estimate=pl.CostEstimate(
            flops=own.size, bytes_accessed=6 * own.size, transcendentals=0
        ),
        name="onward",
    )(own, received)


def turned_rank(rank, ranks):
    turned = 0
    while ranks > 1:
        turned, rank, ranks = (2 * turned + rank % 2, rank // 2, ranks // 2)
    return turned


def scan_kernel(place_ref, scale_ref, *refs):
    x_refs, bc_refs = (refs[:-9], refs[-9:-6])
    small_ref, largest_ref, state_ref, out_ref, x_buf, bc_buf = refs[-6:]
    tokens, channels = bc_refs[0].shape
    blocks = tokens // SPAN
    heads = channels // HEAD_DIM
    rank, z = (place_ref[0], place_ref[2])
    ranks = place_ref.shape[0] - 3
    own = SPAN // ranks
    edge = ROWS
    in_scale = scale_ref[0]
    at_end = (z == 0) | (z == LINE - 1)
    x_buf[:edge] = small_ref[:edge]
    bc_buf[:edge] = small_ref[edge : 2 * edge]
    state = state_ref[...].T

    for block in range(blocks):
        for true_rank in range(ranks):
            source = block * SPAN + (true_rank ^ rank) * own
            source = pl.ds(pl.multiple_of(source, own), own)
            at = edge + block * SPAN + true_rank * own
            at = slice(at, at + own)
            total = sum(ref[source].astype(jnp.float32) for ref in x_refs) * in_scale
            x_buf[at] = total.astype(jnp.bfloat16).astype(jnp.float32)
            near, far, done = (ref[source].astype(jnp.float32) for ref in bc_refs)
            total = ((near + far) * in_scale).astype(jnp.bfloat16).astype(jnp.float32)
            bc_buf[at] = jnp.where(at_end, done, total)

    taps = 2 * edge

    def activate(buf, row, block):
        start = edge - (KERNEL - 1) + block * SPAN
        summed = small_ref[row : row + 1] * buf[start : start + SPAN]
        for k in range(1, KERNEL):
            summed = summed + small_ref[row + k : row + k + 1] * buf[start + k : start + k + SPAN]
        return (summed / (1.0 + jnp.exp(-summed))).astype(jnp.bfloat16)

    skip = small_ref[taps + 2 * KERNEL : taps + 2 * KERNEL + 1]
    gain = small_ref[taps + 2 * KERNEL + 1 : taps + 2 * KERNEL + 2]
    bias = small_ref[4 * edge :, :SPAN]
    rate = small_ref[4 * edge :, SPAN:]

    up = lax.broadcasted_iota(jnp.int32, (SPAN, SPAN), 0)
    across = lax.broadcasted_iota(jnp.int32, (SPAN, SPAN), 1)
    lane = lax.broadcasted_iota(jnp.int32, (SPAN, channels), 1)
    lower = up >= across
    upper = (up <= across).astype(jnp.float32)
    lanes = across[:ROWS]

    dt = sum(ref[tokens:].astype(jnp.float32) for ref in x_refs)
    steps = []
    wide = channels // SPAN
    for block in range(blocks):
        tile = dt[block // wide * ROWS : (block // wide + 1) * ROWS]
        cut = tile[:, block % wide * SPAN : (block % wide + 1) * SPAN]
        cut = (cut + pltpu.roll(cut, ROWS // 2, 0)) * in_scale
        bit = 1
        while bit < ranks:
            shift = bit * own
            flipped = jnp.where(
                (lanes // shift) % 2 == 1,
                pltpu.roll(cut, shift, 1),
                pltpu.roll(cut, SPAN - shift, 1),
            )
            cut = jnp.where((rank & bit) != 0, flipped, cut)
            bit *= 2
        raw = cut + bias
        steps.append(jnp.maximum(raw, 0.0) + jnp.log1p(jnp.exp(-jnp.abs(raw))))
    drops = jnp.concatenate([-step * rate for step in steps], axis=0)
    cums = jnp.dot(drops, upper, precision=HIGHEST, preferred_element_type=jnp.float32)

    sums = jnp.zeros((SPAN, SPAN), jnp.float32)
    for block in range(blocks):
        x_act = activate(x_buf, taps, block)
        bc_act = activate(bc_buf, taps + KERNEL, block)
        in_map, out_map = (bc_act[:, :STATE], bc_act[:, STATE:])
        step, cum = (steps[block], cums[block * ROWS : (block + 1) * ROWS])
        last = cum[:, SPAN - 1 : SPAN]
        turned = jnp.concatenate(
            [
                cum,
                step * jnp.exp(last - cum),
                jnp.exp(cum),
                jnp.zeros((SPAN - 3 * ROWS, SPAN), jnp.float32),
            ],
            axis=0,
        ).T

        def spread(row):
            result = jnp.broadcast_to(turned[:, row : row + 1], (SPAN, channels))
            for h in range(1, heads):
                result = jnp.where(lane >= h * HEAD_DIM, turned[:, row + h : row + h + 1], result)
            return result

        inner = jnp.where(lower, nt_dot(out_map, in_map), 0.0)
        x_wide = x_act.astype(jnp.float32)
        weights, spaced = ([], [])
        for h in range(heads):
            gap = jnp.where(lower, turned[:, h : h + 1] - cum[h : h + 1], 0.0)
            weights.append((inner * jnp.exp(gap) * step[h : h + 1]).astype(jnp.bfloat16))
            inside = (lane >= h * HEAD_DIM) & (lane < (h + 1) * HEAD_DIM)
            spaced.append(jnp.where(inside, x_wide, 0.0).astype(jnp.bfloat16))
        local_part = jnp.dot(
            jnp.concatenate(weights, axis=1),
            jnp.concatenate(spaced, axis=0),
            preferred_element_type=jnp.float32,
        )
        grown = spread(2 * ROWS)
        x_weighted = (x_wide * spread(ROWS)).astype(jnp.bfloat16)
        added = lax.dot_general(
            in_map, x_weighted, (((0,), (0,)), ((), ())), preferred_element_type=jnp.float32
        )
        high = state.astype(jnp.bfloat16)
        rest = (state - high.astype(jnp.float32)).astype(jnp.bfloat16)
        carried = jnp.dot(
            jnp.concatenate([out_map, out_map], axis=1),
            jnp.concatenate([high, rest], axis=0),
            preferred_element_type=jnp.float32,
        )
        ssm_out = local_part + grown * carried + skip * x_wide
        state = grown[SPAN - 1 : SPAN] * state + added
        gained = (ssm_out * gain).astype(jnp.bfloat16)
        for true_rank in range(ranks):
            at = (turned_rank(true_rank, ranks) * blocks + block) * own
            out_ref[at : at + own] = gained[true_rank * own : (true_rank + 1) * own]
        summed = jnp.sum(ssm_out * ssm_out, axis=1, keepdims=True)
        sums = jnp.where(across == block, summed, sums)

    whole = sums.T[:ROWS]
    top = whole.astype(jnp.bfloat16).astype(jnp.float32)
    largest = jnp.broadcast_to(jnp.max(largest_ref[...]), (ROWS, channels))
    extra = jnp.concatenate([jnp.concatenate([top, whole - top], axis=1), largest], axis=0)
    out_ref[tokens:] = extra.astype(jnp.bfloat16)


def scan(place, in_scale, sums, maps, small, largest, state):
    channels = sums[0].shape[1]
    tokens = maps[0].shape[0]

    out = jax.ShapeDtypeStruct((tokens + 2 * ROWS, channels), jnp.bfloat16)
    return pl.pallas_call(
        scan_kernel,
        in_specs=[SMEM, SMEM] + [VMEM] * (len(sums) + len(maps) + 3),
        out_specs=VMEM,
        scratch_shapes=[
            pltpu.VMEM((tokens + ROWS, channels), jnp.float32),
            pltpu.VMEM((tokens + ROWS, 2 * STATE), jnp.float32),
        ],
        out_shape=out,
        compiler_params=pltpu.CompilerParams(vmem_limit_bytes=20 * 2**20),
        cost_estimate=pl.CostEstimate(
            flops=8 * tokens * SPAN * channels,
            bytes_accessed=8 * tokens * channels,
            transcendentals=tokens * (channels + 8 * SPAN),
        ),
        name="scan",
    )(place, in_scale, *sums, *maps, small, largest, state)


def by_heads(
    hidden_in,
    prev_amax,
    w_x,
    w_bc,
    w_dt,
    conv_x,
    conv_bc,
    conv_state_x,
    conv_state_bc,
    dt_bias,
    decay_rate,
    skip,
    init_state,
    norm_gain,
    w_out,
):
    margin = KERNEL - 1
    count, here = (lax.axis_size("seq"), lax.axis_index("seq"))
    ranks, rank = (lax.axis_size("tensor"), lax.axis_index("tensor"))
    z, side = (here // PAIR, here % PAIR)
    place_of = side * LINE + z
    f32, bf16 = (jnp.float32, jnp.bfloat16)
    own, width = hidden_in.shape
    depth = w_x.shape[0]
    channels = w_x.shape[1] // count
    heads_here = w_dt.shape[1] // count
    in_scale = (prev_amax / quant_range).reshape(1)
    factor = (quant_range / prev_amax).reshape(1)
    place = jnp.stack([rank, side, z] + [rank] * ranks).astype(jnp.int32)

    def pick(array, axis, index):
        return lax.dynamic_index_in_dim(array, index, axis, keepdims=False)

    def along(value, pairs):
        moves = [(a * PAIR + x, b * PAIR + x) for a, b in pairs for x in range(PAIR)]
        return lax.ppermute(value, "seq", moves)

    def across(value):
        return lax.ppermute(value, "seq", [(s, s ^ 1) for s in range(count)])

    def of_heads(array):
        return jnp.repeat(array, HEAD_DIM)[None]

    by_channel = jnp.concatenate(
        [conv_state_x.astype(f32), conv_x, of_heads(skip), norm_gain[None]], axis=0
    )
    by_channel = lax.dynamic_slice_in_dim(by_channel, place_of * channels, channels, axis=1)
    by_map = jnp.concatenate([conv_state_bc.astype(f32), conv_bc], axis=0)
    by_map = pick(by_map, 1, side).reshape(margin + KERNEL, 2 * STATE)
    by_head = jnp.stack([dt_bias, decay_rate]).reshape(2, count, heads_here)
    by_head = jnp.tile(pick(by_head, 1, place_of).T, (ROWS // heads_here, 1))
    by_head = jnp.repeat(by_head, SPAN, axis=1)
    blank = jnp.zeros((ROWS - margin, channels), f32)
    small = jnp.concatenate(
        [
            blank,
            by_channel[:margin],
            blank,
            by_map[:margin],
            by_channel[margin : margin + KERNEL],
            by_map[margin:],
            by_channel[margin + KERNEL :],
            jnp.zeros((2 * ROWS - 2 * KERNEL - 2, channels), f32),
            by_head,
        ],
        axis=0,
    )

    start_state = lax.dynamic_slice_in_dim(
        init_state, place_of * heads_here, heads_here, axis=0
    ).reshape(channels, STATE)

    tie = lax.optimization_barrier
    half_run = LINE // 2 * channels
    opposite = (z // (LINE // 2)) ^ 1

    def half_columns(side_of, pair_of):
        return lax.dynamic_slice_in_dim(
            w_x, (side_of * 2 + pair_of) * half_run, half_run, axis=1
        )

    x_sent = half_columns(1 - side, opposite)
    x_sent, hidden_in = tie((x_sent, hidden_in))
    x_far = across(x_sent)
    x_far, maps_sent, dt_sent = tie(
        (x_far, pick(w_bc, 1, 1 - side).reshape(depth, 2 * STATE), w_dt.T)
    )
    bc_other, dt_other = (across(maps_sent), across(dt_sent))
    bc_own = pick(w_bc, 1, side).reshape(depth, 2 * STATE)

    def line_columns(m):
        return lax.dynamic_slice_in_dim(hidden_in, (z ^ m) * PAIR * depth, PAIR * depth, axis=1)

    arrived = [line_columns(0)]
    for m in range(1, LINE):
        arrived.append(along(line_columns(m), [(s, s ^ m) for s in range(LINE)]))
    stacked = jnp.stack(arrived)
    beyond_pair = across(stacked)
    w_far, w_near, w_near_sent = (
        half_columns(side, opposite),
        half_columns(side, 1 - opposite),
        half_columns(1 - side, 1 - opposite),
    )
    beyond_pair, small, start_state, bc_own, dt_sent, w_far, w_near, w_near_sent = tie(
        (beyond_pair, small, start_state, bc_own, dt_sent, w_far, w_near, w_near_sent)
    )
    rows = []
    for mine in (stacked, beyond_pair):
        ours = [mine]
        for j in range(1, ranks):
            bit = j & -j
            pairs = [(t, t ^ bit) for t in range(ranks)]
            ours.append(lax.ppermute(ours[j - bit], "tensor", pairs))
        rows.extend(ours)

    start, end = (0, LINE - 1)
    at_end = (z == start) | (z == end)
    next_start, next_end = (1, LINE - 2)
    inward = [(start, next_start), (end, next_end)]
    outward = [(next_start, start), (next_end, end)]
    middle = [(next_start, next_end), (next_end, next_start)]
    over_middle = [(next_start, end), (next_end, start)]
    beside_pairs = [(s, s ^ 1) for s in range(LINE)]
    over, far, mine, near, mine_sent, near_sent, maps, largest = project(
        place,
        factor,
        rows,
        (w_far, x_far, bc_own, bc_other, dt_sent, dt_other),
        (w_near, w_near_sent, dt_sent),
    )

    map_hop = along(maps, inward)
    hop_far = along(far, inward)
    hop_over = along(over, inward)
    near = onward(near, across(near_sent))
    got_mine = across(mine_sent)
    near_out = along(near, outward)
    map_sum = (maps.astype(f32) + map_hop.astype(f32)).astype(bf16)
    map_far = along(map_sum, middle)
    map_done = ((map_sum.astype(f32) + map_far.astype(f32)) * in_scale).astype(bf16)
    sent_end = onward(over, hop_far)
    got_end = along(sent_end, over_middle)
    hop_over, near_out, unused = tie((hop_over, near_out, sent_end))
    sent_next = onward(far, hop_over)
    got_next = along(sent_next, middle)
    near, unused = tie((near, sent_next))
    near_in = along(near, inward)
    map_done, got_end, got_mine = tie((map_done, got_end, got_mine))
    map_done = along(map_done, outward)
    gained = scan(
        place,
        in_scale,
        [mine, got_mine, near_out, near_in, got_end, got_next],
        [map_sum, map_far, map_done],
        small,
        largest,
        start_state,
    )

    tokens = gained.shape[0] - 2 * ROWS
    beside = along(gained, beside_pairs)
    facing = along(gained, middle)
    second = jnp.where(at_end, along(facing, outward), facing)
    beyond = along(beside, middle)
    third = jnp.where(at_end, along(beyond, outward), beyond)
    far_own = across(gained)
    far_beside = across(beside)
    second, far_own = tie((second, far_own))
    far_second = across(second)
    third, far_beside = tie((third, far_beside))
    far_third = across(third)
    two, three = (jnp.where(at_end, 2, 3), jnp.where(at_end, 3, 2))

    def rows_for(x, m):
        at = ((side ^ x) * LINE + (z ^ m)) * channels
        return lax.dynamic_slice_in_dim(w_out, at, channels, axis=0)

    total = None
    tails = [far_third[tokens:]]
    for x, m, piece in (
        (0, 0, gained),
        (1, 0, far_own),
        (0, 1, beside),
        (1, 1, far_beside),
        (0, two, second),
        (1, two, far_second),
        (0, three, third),
    ):
        product = jnp.dot(piece, rows_for(x, m), preferred_element_type=f32)
        total = product if total is None else total + product
        tails.append(piece[tokens:])
    total, far_third = tie((total, far_third))
    last_rows = rows_for(1, three)
    tails = [tail.astype(f32) for tail in tails]
    squares = sum(tail[:ROWS, :SPAN] + tail[:ROWS, SPAN:] for tail in tails)
    top = functools.reduce(jnp.maximum, [tail[ROWS:, :SPAN] for tail in tails])

    def run_of(array, index, run):
        return lax.dynamic_slice_in_dim(array, index * run, run, axis=0)

    def first_sum(index):
        block, so_far = (run_of(far_third, index, run), run_of(total, index, run))
        return so_far + jnp.dot(block, last_rows, preferred_element_type=f32)

    run = tokens // 2
    keeps = rank % 2
    pairs = [(t, t ^ 1) for t in range(ranks)]
    received = lax.ppermute(first_sum(1 - keeps).astype(bf16), "tensor", pairs)
    kept = first_sum(keeps)
    bit = 2
    while bit < ranks:
        run //= 2
        keeps = (rank // bit) % 2
        pairs = [(t, t ^ bit) for t in range(ranks)]
        sent = run_of(kept, 1 - keeps, run) + run_of(received, 1 - keeps, run).astype(f32)
        kept = run_of(kept, keeps, run) + run_of(received, keeps, run).astype(f32)
        sent = sent.astype(bf16)
        squares, unused = tie((squares, sent))
        received = lax.ppermute(sent, "tensor", pairs)
        bit *= 2
    bit = 1
    while bit < ranks:
        squares = squares + lax.ppermute(squares, "tensor", [(t, t ^ bit) for t in range(ranks)])
        bit *= 2
    mean_sq = squares.reshape(count, ranks, own) / (HEADS * HEAD_DIM)
    factors = lax.rsqrt(pick(mean_sq, 1, rank) + epsilon).reshape(run, 1)
    final = ((kept + received.astype(f32)) * factors).astype(bf16).reshape(count, own, -1)
    final = lax.all_to_all(final, "seq", split_axis=0, concat_axis=0, tiled=True)
    layer_out = final.transpose(1, 0, 2).reshape(own, count * final.shape[2])
    return (layer_out, jnp.max(top))


def solution(mesh):
    return jax.shard_map(
        by_heads if splits(mesh) else by_tokens,
        mesh=mesh,
        in_specs=(
            P(("seq", "tensor"), None),
            P(),
            P("seq", "tensor"),
            P("seq", "tensor", None, None),
            P("seq", "tensor"),
            P(None, "tensor"),
            P(None, "tensor", None, None),
            P(None, "tensor"),
            P(None, "tensor", None, None),
            P("tensor"),
            P("tensor"),
            P("tensor"),
            P("tensor", None, None),
            P("tensor"),
            P("tensor", "seq"),
        ),
        out_specs=(P(("seq", "tensor"), None), P()),
        check_vma=False,
    )
```

```python
import functools

import jax
import jax.numpy as jnp
from jax import lax
from jax.experimental import pallas as pl
from jax.experimental.pallas import tpu as pltpu
from jax.sharding import PartitionSpec as P

HEADS = 128
HEAD_DIM = 64
STATE = 128
GROUPS = 8
KERNEL = 4
SPAN = 128


epsilon = 1e-05
quant_range = 448.0


def from_behind(value, axis, steps):
    count = lax.axis_size(axis)
    first, last = (max(0, -steps), min(count, count - steps))
    return lax.ppermute(value, axis, [(source, source + steps) for source in range(first, last)])


def carried_in(shard, axis, combine, identity):
    count, here = (lax.axis_size(axis), lax.axis_index(axis))
    everything = jax.tree.map(
        lambda part, kind: lax.all_gather(part.astype(kind), axis),
        shard,
        (jnp.bfloat16, jnp.bfloat16),
    )
    start = jax.tree.map(
        lambda part, zero: jnp.broadcast_to(jnp.asarray(zero, part.dtype), part.shape),
        shard,
        identity,
    )

    def turn(k, before):
        reached = k < here
        new = combine(
            before, jax.tree.map(lambda part, own: part[k].astype(own.dtype), everything, shard)
        )
        return jax.tree.map(lambda a, b: jnp.where(reached, a, b), new, before)

    return lax.fori_loop(0, count, turn, start)


def depthwise(before, projected, conv_taps, length):
    extended = jnp.concatenate([before, projected], axis=0)
    summed = conv_taps[0] * extended[0:length]
    for offset in range(1, KERNEL):
        summed = summed + conv_taps[offset] * extended[offset : offset + length]
    return jax.nn.silu(summed).astype(jnp.bfloat16)


def combine(earlier, later):
    return (earlier[0] * later[0], later[0][:, None, None] * earlier[1] + later[1])


def by_tokens(
    hidden_in,
    prev_amax,
    w_x,
    w_bc,
    w_dt,
    conv_x,
    conv_bc,
    conv_state_x,
    conv_state_bc,
    dt_bias,
    decay_rate,
    skip,
    init_state,
    norm_gain,
    w_out,
):
    margin = KERNEL - 1
    gathered = lax.all_gather(hidden_in, "tensor", axis=0, tiled=True)
    abs_max = lax.pmax(jnp.max(jnp.abs(gathered.astype(jnp.float32))), "seq")
    in_scale = prev_amax / quant_range
    leading = lax.axis_index("seq") == 0
    row_count = gathered.shape[0]
    bc_width = w_bc.shape[1] * w_bc.shape[2] * w_bc.shape[3]
    bc_rows = jnp.reshape(w_bc, (w_bc.shape[0], bc_width))
    scaled = gathered.astype(jnp.float32) * (quant_range / prev_amax)
    quant = jnp.clip(scaled, -quant_range, quant_range).astype(jnp.bfloat16)
    pieces = (
        lax.all_gather(w_x, "seq", axis=0, tiled=True),
        lax.all_gather(bc_rows, "seq", axis=0, tiled=True),
        lax.all_gather(w_dt, "seq", axis=0, tiled=True),
    )
    x_proj, bc_proj, dt_proj = tuple(
        (
            jnp.dot(quant, weight_piece, preferred_element_type=jnp.float32)
            for weight_piece in pieces
        )
    )
    x_whole = (x_proj * in_scale).astype(jnp.bfloat16)
    bc_whole = (bc_proj * in_scale).astype(jnp.bfloat16)
    dt_raw = dt_proj * in_scale
    state_bc = jnp.reshape(conv_state_bc, (margin, bc_width))
    received = from_behind(
        (x_whole[row_count - margin :], bc_whole[row_count - margin :]), "seq", 1
    )
    x_edge = jnp.where(leading, conv_state_x, received[0])
    bc_edge = jnp.where(leading, state_bc, received[1])
    x_act = depthwise(x_edge, x_whole, conv_x, row_count)
    bc_act = depthwise(bc_edge, bc_whole, jnp.reshape(conv_bc, (KERNEL, bc_width)), row_count)
    step_size = jax.nn.softplus(dt_raw + dt_bias)
    heads_here = step_size.shape[1]
    groups_here = w_bc.shape[1]
    per_group = HEADS // GROUPS
    blocks = row_count // SPAN
    x_blocks = x_act.reshape(blocks, SPAN, heads_here, HEAD_DIM)
    bc_blocks = bc_act.reshape(blocks, SPAN, groups_here, 2, STATE)
    in_map = bc_blocks[:, :, :, 0]
    out_map = bc_blocks[:, :, :, 1]
    step_blocks = step_size.reshape(blocks, SPAN, heads_here)
    cum_blocks = jnp.cumsum(-step_blocks * decay_rate, axis=1)
    index_row = jnp.arange(SPAN, dtype=jnp.int32)
    lower_mask = index_row[:, None] >= index_row[None, :]
    intersection = jnp.einsum(
        "ctgn,cugn->cgtu", out_map, in_map, preferred_element_type=jnp.float32
    )
    intersection = jnp.repeat(intersection, per_group, axis=1)
    cum_heads = jnp.transpose(cum_blocks, (0, 2, 1))
    log_gap = cum_heads[:, :, :, None] - cum_heads[:, :, None, :]
    decay = jnp.exp(jnp.where(lower_mask[None, None], log_gap, -1e30))
    step_heads = jnp.transpose(step_blocks, (0, 2, 1))
    weights = (intersection * decay * step_heads[:, :, None, :]).astype(jnp.bfloat16)
    local_part = jnp.einsum(
        "chtu,cuhp->cthp", weights, x_blocks, preferred_element_type=jnp.float32
    )
    last_cum = cum_blocks[:, SPAN - 1, :]
    x_weighted = (
        x_blocks.astype(jnp.float32)
        * (step_blocks * jnp.exp(last_cum[:, None, :] - cum_blocks))[:, :, :, None]
    ).astype(jnp.bfloat16)
    in_heads = jnp.repeat(in_map, per_group, axis=2)
    added = jnp.einsum("cuhp,cuhn->chpn", x_weighted, in_heads, preferred_element_type=jnp.float32)

    def carry_on(carried, element):
        block_decay, block_added = element
        return (block_decay[:, None, None] * carried + block_added, carried)

    empty_state = jnp.zeros((heads_here, HEAD_DIM, STATE), jnp.float32)
    device_state, entering = lax.scan(carry_on, empty_state, (jnp.exp(last_cum), added))
    device_decay = jnp.exp(jnp.sum(last_cum, axis=0))
    seeded = device_state + jnp.where(leading, device_decay[:, None, None] * init_state, 0.0)
    identity = (jnp.ones_like(device_decay), jnp.zeros_like(device_state))
    scanned = carried_in((device_decay, seeded), "seq", combine, identity)
    incoming = jnp.where(leading, init_state, scanned[1])
    prefix = jnp.exp(jnp.cumsum(last_cum, axis=0) - last_cum)
    states_in = entering + prefix[:, :, None, None] * incoming[None]
    out_heads = jnp.repeat(out_map, per_group, axis=2).astype(jnp.float32)
    carried_part = (
        jnp.einsum("cthn,chpn->cthp", out_heads, states_in, precision=lax.Precision.HIGHEST)
        * jnp.exp(cum_blocks)[:, :, :, None]
    )
    ssm_out = local_part + carried_part + skip[None, None, :, None] * x_blocks.astype(jnp.float32)
    ssm_out = ssm_out.reshape(row_count, heads_here * HEAD_DIM)
    squares = lax.psum(jnp.sum(ssm_out * ssm_out, axis=1), "tensor")
    mean_sq = squares / (HEADS * HEAD_DIM)
    normed = (ssm_out * lax.rsqrt(mean_sq + epsilon)[:, None] * norm_gain).astype(jnp.bfloat16)
    partial_out = jnp.dot(
        normed, lax.all_gather(w_out, "seq", axis=1, tiled=True), preferred_element_type=jnp.float32
    )
    layer_out = lax.psum_scatter(
        partial_out.astype(jnp.bfloat16), "tensor", scatter_dimension=0, tiled=True
    )
    return (layer_out, abs_max)


PAIR = 2
LINE = 4
ROWS = 8
CUTS = 2
SMEM = pl.BlockSpec(memory_space=pltpu.SMEM)
VMEM = pl.BlockSpec(memory_space=pltpu.VMEM)
HIGHEST = lax.Precision.HIGHEST


def splits(mesh):
    count, ranks = (mesh.shape["seq"], mesh.shape["tensor"])
    heads_all, groups_here = (HEADS // ranks, GROUPS // ranks)
    if count != PAIR * LINE or groups_here != PAIR or ranks & (ranks - 1):
        return False
    heads_here = heads_all // count
    return 2 * heads_here == ROWS and heads_here * HEAD_DIM == 2 * SPAN


def nt_dot(a, b, **kw):
    return lax.dot_general(
        a, b, (((1,), (1,)), ((), ())), preferred_element_type=jnp.float32, **kw
    )


def project_kernel(ranks, place_ref, factor_ref, *refs):
    hidden = [refs[x * ranks : (x + 1) * ranks] for x in range(PAIR)]
    refs = refs[PAIR * ranks :]
    own_x, x_far, own_bc, other_bc, own_dt, other_dt = refs[:6]
    far_refs = refs[6 : 6 + LINE // 2]
    near_refs = refs[6 + LINE // 2 : 6 + LINE]
    sent_refs = refs[6 + LINE : 6 + LINE + LINE // 2]
    bc_ref, largest_ref, quant_ref, near_dt, all_dt = refs[6 + LINE + LINE // 2 :]
    side, z = (place_ref[1], place_ref[2])
    factor = factor_ref[0]
    depth = own_x.shape[0]
    largest = None
    for x in range(PAIR):
        for k in range(LINE):
            block = (k ^ z) * PAIR + (side ^ x)
            for j in range(ranks):
                for half in range(PAIR):
                    cut = slice(half * depth, (half + 1) * depth)
                    values = hidden[x][j][k, :, cut].astype(jnp.float32)
                    scaled = jnp.clip(values * factor, -quant_range, quant_range)
                    quant_ref[half, block, j] = scaled.astype(jnp.bfloat16)
                    top = jnp.max(jnp.abs(values).reshape(-1, ROWS, depth), axis=0)
                    largest = top if largest is None else jnp.maximum(largest, top)
    width = largest_ref.shape[1]
    top = largest[:, :width]
    for at in range(width, depth, width):
        top = jnp.maximum(top, largest[:, at : at + width])
    largest_ref[...] = top

    channels = near_refs[0].shape[1]
    tokens = bc_ref.shape[0]
    rows = tokens // CUTS
    blocks = quant_ref.shape[1] // CUTS
    extra = rows // channels * ROWS
    upper = lax.broadcasted_iota(jnp.int32, (ROWS, channels), 0) < ROWS // 2

    def steps_of(dt_ref, run):
        dt = dt_ref[run // 2]
        pieces = []
        for at in range(0, rows, channels):
            piece = dt[:, at : at + channels]
            turned = pltpu.roll(piece, ROWS // 2, 0)
            lower_run = jnp.where(upper, piece, turned)
            upper_run = jnp.where(upper, turned, piece)
            pieces.append(split_parts(jnp.where(run % 2 == 0, lower_run, upper_run), upper))
        return jnp.concatenate(pieces, axis=0).astype(jnp.bfloat16)

    def columns(run):
        return pl.ds(pl.multiple_of(run * channels, channels), channels)

    for cut in range(CUTS):
        part = slice(cut * blocks, (cut + 1) * blocks)
        near = quant_ref[side, part].reshape(rows, depth)
        far = quant_ref[1 - side, part].reshape(rows, depth)

        def both(own, other):
            return jnp.dot(near, own, preferred_element_type=jnp.float32) + jnp.dot(
                far, other, preferred_element_type=jnp.float32
            )

        at_rows = slice(cut * rows, (cut + 1) * rows)
        extra_rows = slice(tokens + cut * extra, tokens + (cut + 1) * extra)
        ours = nt_dot(own_dt[...], near)
        near_dt[...] = ours.reshape(near_dt.shape)
        all_dt[...] = (ours + nt_dot(other_dt[...], far)).reshape(all_dt.shape)
        bc_ref[at_rows] = both(own_bc[...], other_bc[...]).astype(jnp.bfloat16)
        for m in range(LINE // 2):
            owner = z ^ (m + LINE // 2)
            run = side * LINE + owner
            other = x_far[:, columns(owner % (LINE // 2))]
            far_refs[m][at_rows] = both(own_x[:, columns(run)], other).astype(jnp.bfloat16)
            far_refs[m][extra_rows] = steps_of(all_dt, run)
            for out_refs, way in ((near_refs, side), (sent_refs, 1 - side)):
                run = way * LINE + (z ^ m)
                product = jnp.dot(near, own_x[:, columns(run)], preferred_element_type=jnp.float32)
                out_refs[m][at_rows] = product.astype(jnp.bfloat16)
                out_refs[m][extra_rows] = steps_of(near_dt, run)


def split_parts(values, upper):
    top = values.astype(jnp.bfloat16).astype(jnp.float32)
    return jnp.where(upper, top, values - top)


def project(place, factor, hidden, w_x, weights):
    line, own, wide = hidden[0].shape
    ranks = len(hidden) // PAIR
    depth, x_wide = (weights[0].shape[0], 2 * weights[0].shape[1])
    channels, maps_wide = (x_wide // LINE, weights[1].shape[1])
    tokens = line * PAIR * ranks * own
    extra = tokens // channels * ROWS
    dt_shape = (weights[-1].shape[0] // ROWS, ROWS, tokens // CUTS)
    payload = jax.ShapeDtypeStruct((tokens + extra, channels), jnp.bfloat16)
    maps = jax.ShapeDtypeStruct((tokens, maps_wide), jnp.bfloat16)
    largest = jax.ShapeDtypeStruct((ROWS, 128), jnp.float32)
    outs = [payload] * (LINE + LINE // 2) + [maps, largest]
    return pl.pallas_call(
        functools.partial(project_kernel, ranks),
        in_specs=[SMEM, SMEM] + [VMEM] * (len(hidden) + 1 + len(weights)),
        out_specs=[VMEM] * len(outs),
        scratch_shapes=[
            pltpu.VMEM((PAIR, line * PAIR, ranks, own, depth), jnp.bfloat16),
            pltpu.VMEM(dt_shape, jnp.float32),
            pltpu.VMEM(dt_shape, jnp.float32),
        ],
        out_shape=outs,
        compiler_params=pltpu.CompilerParams(vmem_limit_bytes=10 * 2**20),
        cost_estimate=pl.CostEstimate(
            flops=2 * tokens * wide * (x_wide + maps_wide),
            bytes_accessed=2 * tokens * (wide + x_wide),
            transcendentals=0,
        ),
        name="project",
    )(place, factor, *hidden, w_x, *weights)


def onward_kernel(own_ref, received_ref, out_ref):
    rows, channels = own_ref.shape
    tokens = rows * channels // (channels + ROWS)
    total = own_ref[:tokens].astype(jnp.float32) + received_ref[:tokens].astype(jnp.float32)
    out_ref[:tokens] = total.astype(jnp.bfloat16)
    upper = lax.broadcasted_iota(jnp.int32, (ROWS, channels), 0) < ROWS // 2
    extra = own_ref[tokens:].astype(jnp.float32) + received_ref[tokens:].astype(jnp.float32)
    pieces = []
    for at in range(0, rows - tokens, ROWS):
        piece = extra[at : at + ROWS]
        pieces.append(split_parts(piece + pltpu.roll(piece, ROWS // 2, 0), upper))
    out_ref[tokens:] = jnp.concatenate(pieces, axis=0).astype(jnp.bfloat16)


def onward(own, received):
    return pl.pallas_call(
        onward_kernel,
        in_specs=[VMEM, VMEM],
        out_specs=VMEM,
        out_shape=jax.ShapeDtypeStruct(own.shape, own.dtype),
        compiler_params=pltpu.CompilerParams(vmem_limit_bytes=4 * 2**20),
        cost_estimate=pl.CostEstimate(
            flops=own.size, bytes_accessed=6 * own.size, transcendentals=0
        ),
        name="onward",
    )(own, received)


def turned_rank(rank, ranks):
    turned = 0
    while ranks > 1:
        turned, rank, ranks = (2 * turned + rank % 2, rank // 2, ranks // 2)
    return turned


def scan_kernel(place_ref, scale_ref, *refs):
    x_refs, bc_refs = (refs[:-9], refs[-9:-6])
    small_ref, largest_ref, state_ref, out_ref, x_buf, bc_buf = refs[-6:]
    tokens, channels = bc_refs[0].shape
    blocks = tokens // SPAN
    heads = channels // HEAD_DIM
    rank, z = (place_ref[0], place_ref[2])
    ranks = place_ref.shape[0] - 3
    own = SPAN // ranks
    edge = ROWS
    in_scale = scale_ref[0]
    at_end = (z == 0) | (z == LINE - 1)
    x_buf[:edge] = small_ref[:edge]
    bc_buf[:edge] = small_ref[edge : 2 * edge]
    state = state_ref[...].T

    for block in range(blocks):
        for true_rank in range(ranks):
            source = block * SPAN + (true_rank ^ rank) * own
            source = pl.ds(pl.multiple_of(source, own), own)
            at = edge + block * SPAN + true_rank * own
            at = slice(at, at + own)
            total = sum(ref[source].astype(jnp.float32) for ref in x_refs) * in_scale
            x_buf[at] = total.astype(jnp.bfloat16).astype(jnp.float32)
            near, far, done = (ref[source].astype(jnp.float32) for ref in bc_refs)
            total = ((near + far) * in_scale).astype(jnp.bfloat16).astype(jnp.float32)
            bc_buf[at] = jnp.where(at_end, done, total)

    taps = 2 * edge

    def activate(buf, row, block):
        start = edge - (KERNEL - 1) + block * SPAN
        summed = small_ref[row : row + 1] * buf[start : start + SPAN]
        for k in range(1, KERNEL):
            summed = summed + small_ref[row + k : row + k + 1] * buf[start + k : start + k + SPAN]
        return (summed / (1.0 + jnp.exp(-summed))).astype(jnp.bfloat16)

    skip = small_ref[taps + 2 * KERNEL : taps + 2 * KERNEL + 1]
    gain = small_ref[taps + 2 * KERNEL + 1 : taps + 2 * KERNEL + 2]
    bias = small_ref[4 * edge :, :SPAN]
    rate = small_ref[4 * edge :, SPAN:]

    up = lax.broadcasted_iota(jnp.int32, (SPAN, SPAN), 0)
    across = lax.broadcasted_iota(jnp.int32, (SPAN, SPAN), 1)
    lane = lax.broadcasted_iota(jnp.int32, (SPAN, channels), 1)
    lower = up >= across
    upper = (up <= across).astype(jnp.float32)
    lanes = across[:ROWS]

    dt = sum(ref[tokens:].astype(jnp.float32) for ref in x_refs)
    steps = []
    wide = channels // SPAN
    for block in range(blocks):
        tile = dt[block // wide * ROWS : (block // wide + 1) * ROWS]
        cut = tile[:, block % wide * SPAN : (block % wide + 1) * SPAN]
        cut = (cut + pltpu.roll(cut, ROWS // 2, 0)) * in_scale
        bit = 1
        while bit < ranks:
            shift = bit * own
            flipped = jnp.where(
                (lanes // shift) % 2 == 1,
                pltpu.roll(cut, shift, 1),
                pltpu.roll(cut, SPAN - shift, 1),
            )
            cut = jnp.where((rank & bit) != 0, flipped, cut)
            bit *= 2
        raw = cut + bias
        steps.append(jnp.maximum(raw, 0.0) + jnp.log1p(jnp.exp(-jnp.abs(raw))))
    drops = jnp.concatenate([-step * rate for step in steps], axis=0)
    cums = jnp.dot(drops, upper, precision=HIGHEST, preferred_element_type=jnp.float32)

    sums = jnp.zeros((SPAN, SPAN), jnp.float32)
    for block in range(blocks):
        x_act = activate(x_buf, taps, block)
        bc_act = activate(bc_buf, taps + KERNEL, block)
        in_map, out_map = (bc_act[:, :STATE], bc_act[:, STATE:])
        step, cum = (steps[block], cums[block * ROWS : (block + 1) * ROWS])
        last = cum[:, SPAN - 1 : SPAN]
        turned = jnp.concatenate(
            [
                cum,
                step * jnp.exp(last - cum),
                jnp.exp(cum),
                jnp.zeros((SPAN - 3 * ROWS, SPAN), jnp.float32),
            ],
            axis=0,
        ).T

        def spread(row):
            result = jnp.broadcast_to(turned[:, row : row + 1], (SPAN, channels))
            for h in range(1, heads):
                result = jnp.where(lane >= h * HEAD_DIM, turned[:, row + h : row + h + 1], result)
            return result

        inner = jnp.where(lower, nt_dot(out_map, in_map), 0.0)
        x_wide = x_act.astype(jnp.float32)
        weights, spaced = ([], [])
        for h in range(heads):
            gap = jnp.where(lower, turned[:, h : h + 1] - cum[h : h + 1], 0.0)
            weights.append((inner * jnp.exp(gap) * step[h : h + 1]).astype(jnp.bfloat16))
            inside = (lane >= h * HEAD_DIM) & (lane < (h + 1) * HEAD_DIM)
            spaced.append(jnp.where(inside, x_wide, 0.0).astype(jnp.bfloat16))
        local_part = jnp.dot(
            jnp.concatenate(weights, axis=1),
            jnp.concatenate(spaced, axis=0),
            preferred_element_type=jnp.float32,
        )
        grown = spread(2 * ROWS)
        x_weighted = (x_wide * spread(ROWS)).astype(jnp.bfloat16)
        added = lax.dot_general(
            in_map, x_weighted, (((0,), (0,)), ((), ())), preferred_element_type=jnp.float32
        )
        high = state.astype(jnp.bfloat16)
        rest = (state - high.astype(jnp.float32)).astype(jnp.bfloat16)
        carried = jnp.dot(
            jnp.concatenate([out_map, out_map], axis=1),
            jnp.concatenate([high, rest], axis=0),
            preferred_element_type=jnp.float32,
        )
        ssm_out = local_part + grown * carried + skip * x_wide
        state = grown[SPAN - 1 : SPAN] * state + added
        gained = (ssm_out * gain).astype(jnp.bfloat16)
        for true_rank in range(ranks):
            at = (turned_rank(true_rank, ranks) * blocks + block) * own
            out_ref[at : at + own] = gained[true_rank * own : (true_rank + 1) * own]
        summed = jnp.sum(ssm_out * ssm_out, axis=1, keepdims=True)
        sums = jnp.where(across == block, summed, sums)

    whole = sums.T[:ROWS]
    top = whole.astype(jnp.bfloat16).astype(jnp.float32)
    largest = jnp.broadcast_to(jnp.max(largest_ref[...]), (ROWS, channels))
    extra = jnp.concatenate([jnp.concatenate([top, whole - top], axis=1), largest], axis=0)
    out_ref[tokens:] = extra.astype(jnp.bfloat16)


def scan(place, in_scale, sums, maps, small, largest, state):
    channels = sums[0].shape[1]
    tokens = maps[0].shape[0]

    out = jax.ShapeDtypeStruct((tokens + 2 * ROWS, channels), jnp.bfloat16)
    return pl.pallas_call(
        scan_kernel,
        in_specs=[SMEM, SMEM] + [VMEM] * (len(sums) + len(maps) + 3),
        out_specs=VMEM,
        scratch_shapes=[
            pltpu.VMEM((tokens + ROWS, channels), jnp.float32),
            pltpu.VMEM((tokens + ROWS, 2 * STATE), jnp.float32),
        ],
        out_shape=out,
        compiler_params=pltpu.CompilerParams(vmem_limit_bytes=8 * 2**20),
        cost_estimate=pl.CostEstimate(
            flops=8 * tokens * SPAN * channels,
            bytes_accessed=8 * tokens * channels,
            transcendentals=tokens * (channels + 8 * SPAN),
        ),
        name="scan",
    )(place, in_scale, *sums, *maps, small, largest, state)


def by_heads(
    hidden_in,
    prev_amax,
    w_x,
    w_bc,
    w_dt,
    conv_x,
    conv_bc,
    conv_state_x,
    conv_state_bc,
    dt_bias,
    decay_rate,
    skip,
    init_state,
    norm_gain,
    w_out,
):
    margin = KERNEL - 1
    count, here = (lax.axis_size("seq"), lax.axis_index("seq"))
    ranks, rank = (lax.axis_size("tensor"), lax.axis_index("tensor"))
    z, side = (here // PAIR, here % PAIR)
    place_of = side * LINE + z
    f32, bf16 = (jnp.float32, jnp.bfloat16)
    own, width = hidden_in.shape
    depth = w_x.shape[0]
    channels = w_x.shape[1] // count
    heads_here = w_dt.shape[1] // count
    in_scale = (prev_amax / quant_range).reshape(1)
    factor = (quant_range / prev_amax).reshape(1)
    place = jnp.stack([rank, side, z] + [rank] * ranks).astype(jnp.int32)

    def pick(array, axis, index):
        return lax.dynamic_index_in_dim(array, index, axis, keepdims=False)

    def along(value, pairs):
        moves = [(a * PAIR + x, b * PAIR + x) for a, b in pairs for x in range(PAIR)]
        return lax.ppermute(value, "seq", moves)

    def across(value):
        return lax.ppermute(value, "seq", [(s, s ^ 1) for s in range(count)])

    def of_heads(array):
        return jnp.repeat(array, HEAD_DIM)[None]

    by_channel = jnp.concatenate(
        [conv_state_x.astype(f32), conv_x, of_heads(skip), norm_gain[None]], axis=0
    )
    by_channel = lax.dynamic_slice_in_dim(by_channel, place_of * channels, channels, axis=1)
    by_map = jnp.concatenate([conv_state_bc.astype(f32), conv_bc], axis=0)
    by_map = pick(by_map, 1, side).reshape(margin + KERNEL, 2 * STATE)
    by_head = jnp.stack([dt_bias, decay_rate]).reshape(2, count, heads_here)
    by_head = jnp.tile(pick(by_head, 1, place_of).T, (ROWS // heads_here, 1))
    by_head = jnp.repeat(by_head, SPAN, axis=1)
    blank = jnp.zeros((ROWS - margin, channels), f32)
    small = jnp.concatenate(
        [
            blank,
            by_channel[:margin],
            blank,
            by_map[:margin],
            by_channel[margin : margin + KERNEL],
            by_map[margin:],
            by_channel[margin + KERNEL :],
            jnp.zeros((2 * ROWS - 2 * KERNEL - 2, channels), f32),
            by_head,
        ],
        axis=0,
    )

    start_state = lax.dynamic_slice_in_dim(
        init_state, place_of * heads_here, heads_here, axis=0
    ).reshape(channels, STATE)

    tie = lax.optimization_barrier
    half_run = LINE // 2 * channels
    opposite = (z // (LINE // 2)) ^ 1
    at = ((1 - side) * 2 + opposite) * half_run
    x_sent = lax.dynamic_slice_in_dim(w_x, at, half_run, axis=1)
    x_sent, hidden_in = tie((x_sent, hidden_in))
    x_far = across(x_sent)
    x_far, maps_sent, dt_sent = tie(
        (x_far, pick(w_bc, 1, 1 - side).reshape(depth, 2 * STATE), w_dt.T)
    )
    bc_other, dt_other = (across(maps_sent), across(dt_sent))
    bc_own = pick(w_bc, 1, side).reshape(depth, 2 * STATE)

    def line_columns(m):
        return lax.dynamic_slice_in_dim(hidden_in, (z ^ m) * PAIR * depth, PAIR * depth, axis=1)

    arrived = [line_columns(0)]
    for m in range(1, LINE):
        arrived.append(along(line_columns(m), [(s, s ^ m) for s in range(LINE)]))
    stacked = jnp.stack(arrived)
    beyond_pair = across(stacked)
    beyond_pair, small, start_state, bc_own, dt_sent = tie(
        (beyond_pair, small, start_state, bc_own, dt_sent)
    )
    rows = []
    for mine in (stacked, beyond_pair):
        ours = [mine]
        for j in range(1, ranks):
            bit = j & -j
            pairs = [(t, t ^ bit) for t in range(ranks)]
            ours.append(lax.ppermute(ours[j - bit], "tensor", pairs))
        rows.extend(ours)

    start, end = (0, LINE - 1)
    at_end = (z == start) | (z == end)
    next_start, next_end = (1, LINE - 2)
    inward = [(start, next_start), (end, next_end)]
    outward = [(next_start, start), (next_end, end)]
    middle = [(next_start, next_end), (next_end, next_start)]
    over_middle = [(next_start, end), (next_end, start)]
    beside_pairs = [(s, s ^ 1) for s in range(LINE)]
    weights = (x_far, bc_own, bc_other, dt_sent, dt_other)
    over, far, mine, near, mine_sent, near_sent, maps, largest = project(
        place, factor, rows, w_x, weights
    )

    map_hop = along(maps, inward)
    hop_far = along(far, inward)
    hop_over = along(over, inward)
    near = onward(near, across(near_sent))
    got_mine = across(mine_sent)
    near_out = along(near, outward)
    map_sum = (maps.astype(f32) + map_hop.astype(f32)).astype(bf16)
    map_far = along(map_sum, middle)
    map_done = ((map_sum.astype(f32) + map_far.astype(f32)) * in_scale).astype(bf16)
    sent_end = onward(over, hop_far)
    got_end = along(sent_end, over_middle)
    hop_over, near_out, unused = tie((hop_over, near_out, sent_end))
    got_next = along(onward(far, hop_over), middle)
    near, got_end = tie((near, got_end))
    near_in = along(near, inward)
    map_done, got_mine, unused = tie((map_done, got_mine, hop_over))
    map_done = along(map_done, outward)
    gained = scan(
        place,
        in_scale,
        [mine, got_mine, near_out, near_in, got_end, got_next],
        [map_sum, map_far, map_done],
        small,
        largest,
        start_state,
    )

    tokens = gained.shape[0] - 2 * ROWS
    beside = along(gained, beside_pairs)
    facing = along(gained, middle)
    second = jnp.where(at_end, along(facing, outward), facing)
    beyond = along(beside, middle)
    third = jnp.where(at_end, along(beyond, outward), beyond)
    far_own = across(gained)
    far_beside = across(beside)
    second, far_own = tie((second, far_own))
    far_second = across(second)
    third, far_beside = tie((third, far_beside))
    far_third = across(third)
    two, three = (jnp.where(at_end, 2, 3), jnp.where(at_end, 3, 2))

    def rows_for(x, m):
        at = ((side ^ x) * LINE + (z ^ m)) * channels
        return lax.dynamic_slice_in_dim(w_out, at, channels, axis=0)

    total = None
    tails = [far_third[tokens:]]
    for x, m, piece in (
        (0, 0, gained),
        (1, 0, far_own),
        (0, 1, beside),
        (1, 1, far_beside),
        (0, two, second),
        (1, two, far_second),
        (0, three, third),
    ):
        product = jnp.dot(piece, rows_for(x, m), preferred_element_type=f32)
        total = product if total is None else total + product
        tails.append(piece[tokens:])
    total, far_third = tie((total, far_third))
    last_rows = rows_for(1, three)
    tails = [tail.astype(f32) for tail in tails]
    squares = sum(tail[:ROWS, :SPAN] + tail[:ROWS, SPAN:] for tail in tails)
    top = functools.reduce(jnp.maximum, [tail[ROWS:, :SPAN] for tail in tails])

    def run_of(array, index, run):
        return lax.dynamic_slice_in_dim(array, index * run, run, axis=0)

    def first_sum(index):
        block, so_far = (run_of(far_third, index, run), run_of(total, index, run))
        return so_far + jnp.dot(block, last_rows, preferred_element_type=f32)

    run = tokens // 2
    keeps = rank % 2
    pairs = [(t, t ^ 1) for t in range(ranks)]
    received = lax.ppermute(first_sum(1 - keeps).astype(bf16), "tensor", pairs)
    kept = first_sum(keeps)
    squares = squares + lax.ppermute(squares, "tensor", pairs)
    bit = 2
    while bit < ranks:
        run //= 2
        keeps = (rank // bit) % 2
        pairs = [(t, t ^ bit) for t in range(ranks)]
        sent = run_of(kept, 1 - keeps, run) + run_of(received, 1 - keeps, run).astype(f32)
        kept = run_of(kept, keeps, run) + run_of(received, keeps, run).astype(f32)
        received = lax.ppermute(sent.astype(bf16), "tensor", pairs)
        squares = squares + lax.ppermute(squares, "tensor", pairs)
        bit *= 2
    mean_sq = squares.reshape(count, ranks, own) / (HEADS * HEAD_DIM)
    factors = lax.rsqrt(pick(mean_sq, 1, rank) + epsilon)
    final = (kept + received.astype(f32)).reshape(count, own, -1) * factors[:, :, None]
    final = lax.all_to_all(final.astype(bf16), "seq", split_axis=0, concat_axis=0, tiled=True)
    layer_out = final.transpose(1, 0, 2).reshape(own, count * final.shape[2])
    return (layer_out, jnp.max(top))


def solution(mesh):
    return jax.shard_map(
        by_heads if splits(mesh) else by_tokens,
        mesh=mesh,
        in_specs=(
            P(("seq", "tensor"), None),
            P(),
            P("seq", "tensor"),
            P("seq", "tensor", None, None),
            P("seq", "tensor"),
            P(None, "tensor"),
            P(None, "tensor", None, None),
            P(None, "tensor"),
            P(None, "tensor", None, None),
            P("tensor"),
            P("tensor"),
            P("tensor"),
            P("tensor", None, None),
            P("tensor"),
            P("tensor", "seq"),
        ),
        out_specs=(P(("seq", "tensor"), None), P()),
        check_vma=False,
    )
```

```python
import functools

import jax
import jax.numpy as jnp
from jax import lax
from jax.experimental import pallas as pl
from jax.experimental.pallas import tpu as pltpu
from jax.sharding import PartitionSpec as P

HEADS = 128
HEAD_DIM = 64
STATE = 128
GROUPS = 8
KERNEL = 4
SPAN = 128


epsilon = 1e-05
quant_range = 448.0


def from_behind(value, axis, steps):
    count = lax.axis_size(axis)
    first, last = (max(0, -steps), min(count, count - steps))
    return lax.ppermute(value, axis, [(source, source + steps) for source in range(first, last)])


def carried_in(shard, axis, combine, identity):
    count, here = (lax.axis_size(axis), lax.axis_index(axis))
    everything = jax.tree.map(
        lambda part, kind: lax.all_gather(part.astype(kind), axis),
        shard,
        (jnp.bfloat16, jnp.bfloat16),
    )
    start = jax.tree.map(
        lambda part, zero: jnp.broadcast_to(jnp.asarray(zero, part.dtype), part.shape),
        shard,
        identity,
    )

    def turn(k, before):
        reached = k < here
        new = combine(
            before, jax.tree.map(lambda part, own: part[k].astype(own.dtype), everything, shard)
        )
        return jax.tree.map(lambda a, b: jnp.where(reached, a, b), new, before)

    return lax.fori_loop(0, count, turn, start)


def depthwise(before, projected, conv_taps, length):
    extended = jnp.concatenate([before, projected], axis=0)
    summed = conv_taps[0] * extended[0:length]
    for offset in range(1, KERNEL):
        summed = summed + conv_taps[offset] * extended[offset : offset + length]
    return jax.nn.silu(summed).astype(jnp.bfloat16)


def combine(earlier, later):
    return (earlier[0] * later[0], later[0][:, None, None] * earlier[1] + later[1])


def by_tokens(
    hidden_in,
    prev_amax,
    w_x,
    w_bc,
    w_dt,
    conv_x,
    conv_bc,
    conv_state_x,
    conv_state_bc,
    dt_bias,
    decay_rate,
    skip,
    init_state,
    norm_gain,
    w_out,
):
    margin = KERNEL - 1
    gathered = lax.all_gather(hidden_in, "tensor", axis=0, tiled=True)
    abs_max = lax.pmax(jnp.max(jnp.abs(gathered.astype(jnp.float32))), "seq")
    in_scale = prev_amax / quant_range
    leading = lax.axis_index("seq") == 0
    row_count = gathered.shape[0]
    bc_width = w_bc.shape[1] * w_bc.shape[2] * w_bc.shape[3]
    bc_rows = jnp.reshape(w_bc, (w_bc.shape[0], bc_width))
    scaled = gathered.astype(jnp.float32) * (quant_range / prev_amax)
    quant = jnp.clip(scaled, -quant_range, quant_range).astype(jnp.bfloat16)
    pieces = (
        lax.all_gather(w_x, "seq", axis=0, tiled=True),
        lax.all_gather(bc_rows, "seq", axis=0, tiled=True),
        lax.all_gather(w_dt, "seq", axis=0, tiled=True),
    )
    x_proj, bc_proj, dt_proj = tuple(
        (
            jnp.dot(quant, weight_piece, preferred_element_type=jnp.float32)
            for weight_piece in pieces
        )
    )
    x_whole = (x_proj * in_scale).astype(jnp.bfloat16)
    bc_whole = (bc_proj * in_scale).astype(jnp.bfloat16)
    dt_raw = dt_proj * in_scale
    state_bc = jnp.reshape(conv_state_bc, (margin, bc_width))
    received = from_behind(
        (x_whole[row_count - margin :], bc_whole[row_count - margin :]), "seq", 1
    )
    x_edge = jnp.where(leading, conv_state_x, received[0])
    bc_edge = jnp.where(leading, state_bc, received[1])
    x_act = depthwise(x_edge, x_whole, conv_x, row_count)
    bc_act = depthwise(bc_edge, bc_whole, jnp.reshape(conv_bc, (KERNEL, bc_width)), row_count)
    step_size = jax.nn.softplus(dt_raw + dt_bias)
    heads_here = step_size.shape[1]
    groups_here = w_bc.shape[1]
    per_group = HEADS // GROUPS
    blocks = row_count // SPAN
    x_blocks = x_act.reshape(blocks, SPAN, heads_here, HEAD_DIM)
    bc_blocks = bc_act.reshape(blocks, SPAN, groups_here, 2, STATE)
    in_map = bc_blocks[:, :, :, 0]
    out_map = bc_blocks[:, :, :, 1]
    step_blocks = step_size.reshape(blocks, SPAN, heads_here)
    cum_blocks = jnp.cumsum(-step_blocks * decay_rate, axis=1)
    index_row = jnp.arange(SPAN, dtype=jnp.int32)
    lower_mask = index_row[:, None] >= index_row[None, :]
    intersection = jnp.einsum(
        "ctgn,cugn->cgtu", out_map, in_map, preferred_element_type=jnp.float32
    )
    intersection = jnp.repeat(intersection, per_group, axis=1)
    cum_heads = jnp.transpose(cum_blocks, (0, 2, 1))
    log_gap = cum_heads[:, :, :, None] - cum_heads[:, :, None, :]
    decay = jnp.exp(jnp.where(lower_mask[None, None], log_gap, -1e30))
    step_heads = jnp.transpose(step_blocks, (0, 2, 1))
    weights = (intersection * decay * step_heads[:, :, None, :]).astype(jnp.bfloat16)
    local_part = jnp.einsum(
        "chtu,cuhp->cthp", weights, x_blocks, preferred_element_type=jnp.float32
    )
    last_cum = cum_blocks[:, SPAN - 1, :]
    x_weighted = (
        x_blocks.astype(jnp.float32)
        * (step_blocks * jnp.exp(last_cum[:, None, :] - cum_blocks))[:, :, :, None]
    ).astype(jnp.bfloat16)
    in_heads = jnp.repeat(in_map, per_group, axis=2)
    added = jnp.einsum("cuhp,cuhn->chpn", x_weighted, in_heads, preferred_element_type=jnp.float32)

    def carry_on(carried, element):
        block_decay, block_added = element
        return (block_decay[:, None, None] * carried + block_added, carried)

    empty_state = jnp.zeros((heads_here, HEAD_DIM, STATE), jnp.float32)
    device_state, entering = lax.scan(carry_on, empty_state, (jnp.exp(last_cum), added))
    device_decay = jnp.exp(jnp.sum(last_cum, axis=0))
    seeded = device_state + jnp.where(leading, device_decay[:, None, None] * init_state, 0.0)
    identity = (jnp.ones_like(device_decay), jnp.zeros_like(device_state))
    scanned = carried_in((device_decay, seeded), "seq", combine, identity)
    incoming = jnp.where(leading, init_state, scanned[1])
    prefix = jnp.exp(jnp.cumsum(last_cum, axis=0) - last_cum)
    states_in = entering + prefix[:, :, None, None] * incoming[None]
    out_heads = jnp.repeat(out_map, per_group, axis=2).astype(jnp.float32)
    carried_part = (
        jnp.einsum("cthn,chpn->cthp", out_heads, states_in, precision=lax.Precision.HIGHEST)
        * jnp.exp(cum_blocks)[:, :, :, None]
    )
    ssm_out = local_part + carried_part + skip[None, None, :, None] * x_blocks.astype(jnp.float32)
    ssm_out = ssm_out.reshape(row_count, heads_here * HEAD_DIM)
    squares = lax.psum(jnp.sum(ssm_out * ssm_out, axis=1), "tensor")
    mean_sq = squares / (HEADS * HEAD_DIM)
    normed = (ssm_out * lax.rsqrt(mean_sq + epsilon)[:, None] * norm_gain).astype(jnp.bfloat16)
    partial_out = jnp.dot(
        normed, lax.all_gather(w_out, "seq", axis=1, tiled=True), preferred_element_type=jnp.float32
    )
    layer_out = lax.psum_scatter(
        partial_out.astype(jnp.bfloat16), "tensor", scatter_dimension=0, tiled=True
    )
    return (layer_out, abs_max)


PAIR = 2
LINE = 4
ROWS = 8
CUTS = 2
SMEM = pl.BlockSpec(memory_space=pltpu.SMEM)
VMEM = pl.BlockSpec(memory_space=pltpu.VMEM)
HIGHEST = lax.Precision.HIGHEST


def splits(mesh):
    count, ranks = (mesh.shape["seq"], mesh.shape["tensor"])
    heads_all, groups_here = (HEADS // ranks, GROUPS // ranks)
    if count != PAIR * LINE or groups_here != PAIR or ranks & (ranks - 1):
        return False
    heads_here = heads_all // count
    return 2 * heads_here == ROWS and heads_here * HEAD_DIM == 2 * SPAN


def nt_dot(a, b, **kw):
    return lax.dot_general(
        a, b, (((1,), (1,)), ((), ())), preferred_element_type=jnp.float32, **kw
    )


def project_kernel(ranks, place_ref, factor_ref, *refs):
    hidden = [refs[x * ranks : (x + 1) * ranks] for x in range(PAIR)]
    refs = refs[PAIR * ranks :]
    own_x, x_far, own_bc, other_bc, own_dt, other_dt = refs[:6]
    far_refs = refs[6 : 6 + LINE // 2]
    near_refs = refs[6 + LINE // 2 : 6 + LINE]
    sent_refs = refs[6 + LINE : 6 + LINE + LINE // 2]
    bc_ref, largest_ref, quant_ref, near_dt, all_dt = refs[6 + LINE + LINE // 2 :]
    side, z = (place_ref[1], place_ref[2])
    factor = factor_ref[0]
    depth = own_x.shape[0]
    largest = None
    for x in range(PAIR):
        for k in range(LINE):
            block = (k ^ z) * PAIR + (side ^ x)
            for j in range(ranks):
                for half in range(PAIR):
                    cut = slice(half * depth, (half + 1) * depth)
                    values = hidden[x][j][k, :, cut].astype(jnp.float32)
                    scaled = jnp.clip(values * factor, -quant_range, quant_range)
                    quant_ref[half, block, j] = scaled.astype(jnp.bfloat16)
                    top = jnp.max(jnp.abs(values).reshape(-1, ROWS, depth), axis=0)
                    largest = top if largest is None else jnp.maximum(largest, top)
    width = largest_ref.shape[1]
    top = largest[:, :width]
    for at in range(width, depth, width):
        top = jnp.maximum(top, largest[:, at : at + width])
    largest_ref[...] = top

    channels = near_refs[0].shape[1]
    tokens = bc_ref.shape[0]
    rows = tokens // CUTS
    blocks = quant_ref.shape[1] // CUTS
    extra = rows // channels * ROWS
    upper = lax.broadcasted_iota(jnp.int32, (ROWS, channels), 0) < ROWS // 2

    def steps_of(dt_ref, run):
        dt = dt_ref[run // 2]
        pieces = []
        for at in range(0, rows, channels):
            piece = dt[:, at : at + channels]
            turned = pltpu.roll(piece, ROWS // 2, 0)
            lower_run = jnp.where(upper, piece, turned)
            upper_run = jnp.where(upper, turned, piece)
            pieces.append(split_parts(jnp.where(run % 2 == 0, lower_run, upper_run), upper))
        return jnp.concatenate(pieces, axis=0).astype(jnp.bfloat16)

    def columns(run):
        return pl.ds(pl.multiple_of(run * channels, channels), channels)

    for cut in range(CUTS):
        part = slice(cut * blocks, (cut + 1) * blocks)
        near = quant_ref[side, part].reshape(rows, depth)
        far = quant_ref[1 - side, part].reshape(rows, depth)

        def both(own, other):
            return jnp.dot(near, own, preferred_element_type=jnp.float32) + jnp.dot(
                far, other, preferred_element_type=jnp.float32
            )

        at_rows = slice(cut * rows, (cut + 1) * rows)
        extra_rows = slice(tokens + cut * extra, tokens + (cut + 1) * extra)
        ours = nt_dot(own_dt[...], near)
        near_dt[...] = ours.reshape(near_dt.shape)
        all_dt[...] = (ours + nt_dot(other_dt[...], far)).reshape(all_dt.shape)
        bc_ref[at_rows] = both(own_bc[...], other_bc[...]).astype(jnp.bfloat16)
        for m in range(LINE // 2):
            owner = z ^ (m + LINE // 2)
            run = side * LINE + owner
            other = x_far[:, columns(owner % (LINE // 2))]
            far_refs[m][at_rows] = both(own_x[:, columns(run)], other).astype(jnp.bfloat16)
            far_refs[m][extra_rows] = steps_of(all_dt, run)
            for out_refs, way in ((near_refs, side), (sent_refs, 1 - side)):
                run = way * LINE + (z ^ m)
                product = jnp.dot(near, own_x[:, columns(run)], preferred_element_type=jnp.float32)
                out_refs[m][at_rows] = product.astype(jnp.bfloat16)
                out_refs[m][extra_rows] = steps_of(near_dt, run)


def split_parts(values, upper):
    top = values.astype(jnp.bfloat16).astype(jnp.float32)
    return jnp.where(upper, top, values - top)


def project(place, factor, hidden, w_x, weights):
    line, own, wide = hidden[0].shape
    ranks = len(hidden) // PAIR
    depth, x_wide = (weights[0].shape[0], 2 * weights[0].shape[1])
    channels, maps_wide = (x_wide // LINE, weights[1].shape[1])
    tokens = line * PAIR * ranks * own
    extra = tokens // channels * ROWS
    dt_shape = (weights[-1].shape[0] // ROWS, ROWS, tokens // CUTS)
    payload = jax.ShapeDtypeStruct((tokens + extra, channels), jnp.bfloat16)
    maps = jax.ShapeDtypeStruct((tokens, maps_wide), jnp.bfloat16)
    largest = jax.ShapeDtypeStruct((ROWS, 128), jnp.float32)
    outs = [payload] * (LINE + LINE // 2) + [maps, largest]
    return pl.pallas_call(
        functools.partial(project_kernel, ranks),
        in_specs=[SMEM, SMEM] + [VMEM] * (len(hidden) + 1 + len(weights)),
        out_specs=[VMEM] * len(outs),
        scratch_shapes=[
            pltpu.VMEM((PAIR, line * PAIR, ranks, own, depth), jnp.bfloat16),
            pltpu.VMEM(dt_shape, jnp.float32),
            pltpu.VMEM(dt_shape, jnp.float32),
        ],
        out_shape=outs,
        compiler_params=pltpu.CompilerParams(vmem_limit_bytes=32 * 2**20),
        cost_estimate=pl.CostEstimate(
            flops=2 * tokens * wide * (x_wide + maps_wide),
            bytes_accessed=2 * tokens * (wide + x_wide),
            transcendentals=0,
        ),
        name="project",
    )(place, factor, *hidden, w_x, *weights)


def onward_kernel(own_ref, received_ref, out_ref):
    rows, channels = own_ref.shape
    tokens = rows * channels // (channels + ROWS)
    total = own_ref[:tokens].astype(jnp.float32) + received_ref[:tokens].astype(jnp.float32)
    out_ref[:tokens] = total.astype(jnp.bfloat16)
    upper = lax.broadcasted_iota(jnp.int32, (ROWS, channels), 0) < ROWS // 2
    extra = own_ref[tokens:].astype(jnp.float32) + received_ref[tokens:].astype(jnp.float32)
    pieces = []
    for at in range(0, rows - tokens, ROWS):
        piece = extra[at : at + ROWS]
        pieces.append(split_parts(piece + pltpu.roll(piece, ROWS // 2, 0), upper))
    out_ref[tokens:] = jnp.concatenate(pieces, axis=0).astype(jnp.bfloat16)


def onward(own, received):
    return pl.pallas_call(
        onward_kernel,
        in_specs=[VMEM, VMEM],
        out_specs=VMEM,
        out_shape=jax.ShapeDtypeStruct(own.shape, own.dtype),
        compiler_params=pltpu.CompilerParams(vmem_limit_bytes=8 * 2**20),
        cost_estimate=pl.CostEstimate(
            flops=own.size, bytes_accessed=6 * own.size, transcendentals=0
        ),
        name="onward",
    )(own, received)


def turned_rank(rank, ranks):
    turned = 0
    while ranks > 1:
        turned, rank, ranks = (2 * turned + rank % 2, rank // 2, ranks // 2)
    return turned


def scan_kernel(place_ref, scale_ref, *refs):
    x_refs, bc_refs = (refs[:-10], refs[-10:-7])
    small_ref, largest_ref, state_ref = refs[-7:-4]
    out_refs, x_buf, bc_buf = (refs[-4:-2], *refs[-2:])
    tokens, channels = bc_refs[0].shape
    blocks = tokens // SPAN
    run_blocks = blocks // CUTS
    heads = channels // HEAD_DIM
    rank, z = (place_ref[0], place_ref[2])
    ranks = place_ref.shape[0] - 3
    own = SPAN // ranks
    edge = ROWS
    in_scale = scale_ref[0]
    at_end = (z == 0) | (z == LINE - 1)
    x_buf[:edge] = small_ref[:edge]
    bc_buf[:edge] = small_ref[edge : 2 * edge]
    state = state_ref[...].T

    for block in range(blocks):
        for true_rank in range(ranks):
            source = block * SPAN + (true_rank ^ rank) * own
            source = pl.ds(pl.multiple_of(source, own), own)
            at = edge + block * SPAN + true_rank * own
            at = slice(at, at + own)
            total = sum(ref[source].astype(jnp.float32) for ref in x_refs) * in_scale
            x_buf[at] = total.astype(jnp.bfloat16).astype(jnp.float32)
            near, far, done = (ref[source].astype(jnp.float32) for ref in bc_refs)
            total = ((near + far) * in_scale).astype(jnp.bfloat16).astype(jnp.float32)
            bc_buf[at] = jnp.where(at_end, done, total)

    taps = 2 * edge

    def activate(buf, row, block):
        start = edge - (KERNEL - 1) + block * SPAN
        summed = small_ref[row : row + 1] * buf[start : start + SPAN]
        for k in range(1, KERNEL):
            summed = summed + small_ref[row + k : row + k + 1] * buf[start + k : start + k + SPAN]
        return (summed / (1.0 + jnp.exp(-summed))).astype(jnp.bfloat16)

    skip = small_ref[taps + 2 * KERNEL : taps + 2 * KERNEL + 1]
    gain = small_ref[taps + 2 * KERNEL + 1 : taps + 2 * KERNEL + 2]
    bias = small_ref[4 * edge :, :SPAN]
    rate = small_ref[4 * edge :, SPAN:]

    up = lax.broadcasted_iota(jnp.int32, (SPAN, SPAN), 0)
    across = lax.broadcasted_iota(jnp.int32, (SPAN, SPAN), 1)
    lane = lax.broadcasted_iota(jnp.int32, (SPAN, channels), 1)
    lower = up >= across
    upper = (up <= across).astype(jnp.float32)
    lanes = across[:ROWS]

    dt = sum(ref[tokens:].astype(jnp.float32) for ref in x_refs)
    steps = []
    wide = channels // SPAN
    for block in range(blocks):
        tile = dt[block // wide * ROWS : (block // wide + 1) * ROWS]
        cut = tile[:, block % wide * SPAN : (block % wide + 1) * SPAN]
        cut = (cut + pltpu.roll(cut, ROWS // 2, 0)) * in_scale
        bit = 1
        while bit < ranks:
            shift = bit * own
            flipped = jnp.where(
                (lanes // shift) % 2 == 1,
                pltpu.roll(cut, shift, 1),
                pltpu.roll(cut, SPAN - shift, 1),
            )
            cut = jnp.where((rank & bit) != 0, flipped, cut)
            bit *= 2
        raw = cut + bias
        steps.append(jnp.maximum(raw, 0.0) + jnp.log1p(jnp.exp(-jnp.abs(raw))))
    drops = jnp.concatenate([-step * rate for step in steps], axis=0)
    cums = jnp.dot(drops, upper, precision=HIGHEST, preferred_element_type=jnp.float32)

    sums = jnp.zeros((SPAN, SPAN), jnp.float32)
    for block in range(blocks):
        x_act = activate(x_buf, taps, block)
        bc_act = activate(bc_buf, taps + KERNEL, block)
        in_map, out_map = (bc_act[:, :STATE], bc_act[:, STATE:])
        step, cum = (steps[block], cums[block * ROWS : (block + 1) * ROWS])
        last = cum[:, SPAN - 1 : SPAN]
        turned = jnp.concatenate(
            [
                cum,
                step * jnp.exp(last - cum),
                jnp.exp(cum),
                jnp.zeros((SPAN - 3 * ROWS, SPAN), jnp.float32),
            ],
            axis=0,
        ).T

        def spread(row):
            result = jnp.broadcast_to(turned[:, row : row + 1], (SPAN, channels))
            for h in range(1, heads):
                result = jnp.where(lane >= h * HEAD_DIM, turned[:, row + h : row + h + 1], result)
            return result

        inner = jnp.where(lower, nt_dot(out_map, in_map), 0.0)
        x_wide = x_act.astype(jnp.float32)
        weights, spaced = ([], [])
        for h in range(heads):
            gap = jnp.where(lower, turned[:, h : h + 1] - cum[h : h + 1], 0.0)
            weights.append((inner * jnp.exp(gap) * step[h : h + 1]).astype(jnp.bfloat16))
            inside = (lane >= h * HEAD_DIM) & (lane < (h + 1) * HEAD_DIM)
            spaced.append(jnp.where(inside, x_wide, 0.0).astype(jnp.bfloat16))
        local_part = jnp.dot(
            jnp.concatenate(weights, axis=1),
            jnp.concatenate(spaced, axis=0),
            preferred_element_type=jnp.float32,
        )
        grown = spread(2 * ROWS)
        x_weighted = (x_wide * spread(ROWS)).astype(jnp.bfloat16)
        added = lax.dot_general(
            in_map, x_weighted, (((0,), (0,)), ((), ())), preferred_element_type=jnp.float32
        )
        high = state.astype(jnp.bfloat16)
        rest = (state - high.astype(jnp.float32)).astype(jnp.bfloat16)
        carried = jnp.dot(
            jnp.concatenate([out_map, out_map], axis=1),
            jnp.concatenate([high, rest], axis=0),
            preferred_element_type=jnp.float32,
        )
        ssm_out = local_part + grown * carried + skip * x_wide
        state = grown[SPAN - 1 : SPAN] * state + added
        gained = (ssm_out * gain).astype(jnp.bfloat16)
        for true_rank in range(ranks):
            at = (turned_rank(true_rank, ranks) * run_blocks + block % run_blocks) * own
            out_ref = out_refs[block // run_blocks]
            out_ref[at : at + own] = gained[true_rank * own : (true_rank + 1) * own]
        summed = jnp.sum(ssm_out * ssm_out, axis=1, keepdims=True)
        sums = jnp.where(across == block, summed, sums)

    whole = sums.T[:ROWS]
    top = whole.astype(jnp.bfloat16).astype(jnp.float32)
    largest = jnp.broadcast_to(jnp.max(largest_ref[...]), (ROWS, channels))
    extra = jnp.concatenate([jnp.concatenate([top, whole - top], axis=1), largest], axis=0)
    out_refs[-1][tokens // CUTS :] = extra.astype(jnp.bfloat16)


def scan(place, in_scale, sums, maps, small, largest, state):
    channels = sums[0].shape[1]
    tokens = maps[0].shape[0]

    outs = [
        jax.ShapeDtypeStruct((tokens // CUTS + 2 * ROWS * last, channels), jnp.bfloat16)
        for last in (False, True)
    ]
    return pl.pallas_call(
        scan_kernel,
        in_specs=[SMEM, SMEM] + [VMEM] * (len(sums) + len(maps) + 3),
        out_specs=[VMEM] * len(outs),
        scratch_shapes=[
            pltpu.VMEM((tokens + ROWS, channels), jnp.float32),
            pltpu.VMEM((tokens + ROWS, 2 * STATE), jnp.float32),
        ],
        out_shape=outs,
        compiler_params=pltpu.CompilerParams(vmem_limit_bytes=20 * 2**20),
        cost_estimate=pl.CostEstimate(
            flops=8 * tokens * SPAN * channels,
            bytes_accessed=8 * tokens * channels,
            transcendentals=tokens * (channels + 8 * SPAN),
        ),
        name="scan",
    )(place, in_scale, *sums, *maps, small, largest, state)


def by_heads(
    hidden_in,
    prev_amax,
    w_x,
    w_bc,
    w_dt,
    conv_x,
    conv_bc,
    conv_state_x,
    conv_state_bc,
    dt_bias,
    decay_rate,
    skip,
    init_state,
    norm_gain,
    w_out,
):
    margin = KERNEL - 1
    count, here = (lax.axis_size("seq"), lax.axis_index("seq"))
    ranks, rank = (lax.axis_size("tensor"), lax.axis_index("tensor"))
    z, side = (here // PAIR, here % PAIR)
    place_of = side * LINE + z
    f32, bf16 = (jnp.float32, jnp.bfloat16)
    own, width = hidden_in.shape
    depth = w_x.shape[0]
    channels = w_x.shape[1] // count
    heads_here = w_dt.shape[1] // count
    in_scale = (prev_amax / quant_range).reshape(1)
    factor = (quant_range / prev_amax).reshape(1)
    place = jnp.stack([rank, side, z] + [rank] * ranks).astype(jnp.int32)

    def pick(array, axis, index):
        return lax.dynamic_index_in_dim(array, index, axis, keepdims=False)

    def along(value, pairs):
        moves = [(a * PAIR + x, b * PAIR + x) for a, b in pairs for x in range(PAIR)]
        return lax.ppermute(value, "seq", moves)

    def across(value):
        return lax.ppermute(value, "seq", [(s, s ^ 1) for s in range(count)])

    def of_heads(array):
        return jnp.repeat(array, HEAD_DIM)[None]

    by_channel = jnp.concatenate(
        [conv_state_x.astype(f32), conv_x, of_heads(skip), norm_gain[None]], axis=0
    )
    by_channel = lax.dynamic_slice_in_dim(by_channel, place_of * channels, channels, axis=1)
    by_map = jnp.concatenate([conv_state_bc.astype(f32), conv_bc], axis=0)
    by_map = pick(by_map, 1, side).reshape(margin + KERNEL, 2 * STATE)
    by_head = jnp.stack([dt_bias, decay_rate]).reshape(2, count, heads_here)
    by_head = jnp.tile(pick(by_head, 1, place_of).T, (ROWS // heads_here, 1))
    by_head = jnp.repeat(by_head, SPAN, axis=1)
    blank = jnp.zeros((ROWS - margin, channels), f32)
    small = jnp.concatenate(
        [
            blank,
            by_channel[:margin],
            blank,
            by_map[:margin],
            by_channel[margin : margin + KERNEL],
            by_map[margin:],
            by_channel[margin + KERNEL :],
            jnp.zeros((2 * ROWS - 2 * KERNEL - 2, channels), f32),
            by_head,
        ],
        axis=0,
    )

    start_state = lax.dynamic_slice_in_dim(
        init_state, place_of * heads_here, heads_here, axis=0
    ).reshape(channels, STATE)

    tie = lax.optimization_barrier
    half_run = LINE // 2 * channels
    opposite = (z // (LINE // 2)) ^ 1
    at = ((1 - side) * 2 + opposite) * half_run
    x_sent = lax.dynamic_slice_in_dim(w_x, at, half_run, axis=1)
    x_sent, hidden_in = tie((x_sent, hidden_in))
    x_far = across(x_sent)
    x_far, maps_sent, dt_sent = tie(
        (x_far, pick(w_bc, 1, 1 - side).reshape(depth, 2 * STATE), w_dt.T)
    )
    bc_other, dt_other = (across(maps_sent), across(dt_sent))
    bc_own = pick(w_bc, 1, side).reshape(depth, 2 * STATE)

    def line_columns(m):
        return lax.dynamic_slice_in_dim(hidden_in, (z ^ m) * PAIR * depth, PAIR * depth, axis=1)

    arrived = [line_columns(0)]
    for m in range(1, LINE):
        arrived.append(along(line_columns(m), [(s, s ^ m) for s in range(LINE)]))
    stacked = jnp.stack(arrived)
    beyond_pair = across(stacked)
    beyond_pair, small, start_state, bc_own, dt_sent = tie(
        (beyond_pair, small, start_state, bc_own, dt_sent)
    )
    rows = []
    for mine in (stacked, beyond_pair):
        ours = [mine]
        for j in range(1, ranks):
            bit = j & -j
            pairs = [(t, t ^ bit) for t in range(ranks)]
            ours.append(lax.ppermute(ours[j - bit], "tensor", pairs))
        rows.extend(ours)

    start, end = (0, LINE - 1)
    at_end = (z == start) | (z == end)
    next_start, next_end = (1, LINE - 2)
    inward = [(start, next_start), (end, next_end)]
    outward = [(next_start, start), (next_end, end)]
    middle = [(next_start, next_end), (next_end, next_start)]
    over_middle = [(next_start, end), (next_end, start)]
    beside_pairs = [(s, s ^ 1) for s in range(LINE)]
    weights = (x_far, bc_own, bc_other, dt_sent, dt_other)
    over, far, mine, near, mine_sent, near_sent, maps, largest = project(
        place, factor, rows, w_x, weights
    )

    map_hop = along(maps, inward)
    hop_far = along(far, inward)
    hop_over = along(over, inward)
    near = onward(near, across(near_sent))
    got_mine = across(mine_sent)
    near_out = along(near, outward)
    near_in = along(near, inward)
    map_sum = (maps.astype(f32) + map_hop.astype(f32)).astype(bf16)
    map_far = along(map_sum, middle)
    map_done = ((map_sum.astype(f32) + map_far.astype(f32)) * in_scale).astype(bf16)
    sent_end = onward(over, hop_far)
    got_end = along(sent_end, over_middle)
    hop_over, near_out, unused = tie((hop_over, near_out, sent_end))
    got_next = along(onward(far, hop_over), middle)
    map_done, got_end, got_mine = tie((map_done, got_end, got_mine))
    map_done = along(map_done, outward)
    gained = scan(
        place,
        in_scale,
        [mine, got_mine, near_out, near_in, got_end, got_next],
        [map_sum, map_far, map_done],
        small,
        largest,
        start_state,
    )

    run = maps.shape[0] // CUTS
    two, three = (jnp.where(at_end, 2, 3), jnp.where(at_end, 3, 2))

    def rows_for(x, m):
        at = ((side ^ x) * LINE + (z ^ m)) * channels
        return lax.dynamic_slice_in_dim(w_out, at, channels, axis=0)

    def gather(block):
        beside = along(block, beside_pairs)
        facing = along(block, middle)
        outer = along(facing, outward)
        second = jnp.where(at_end, outer, facing)
        beyond = along(beside, middle)
        beyond, unused = tie((beyond, outer))
        third = jnp.where(at_end, along(beyond, outward), beyond)
        far_own = across(block)
        far_beside = across(beside)
        second, far_own = tie((second, far_own))
        far_second = across(second)
        third, far_beside = tie((third, far_beside))
        far_third = across(third)
        return (
            (0, 0, block),
            (1, 0, far_own),
            (0, 1, beside),
            (1, 1, far_beside),
            (0, two, second),
            (1, two, far_second),
            (0, three, third),
            (1, three, far_third),
        )

    def run_of(array, index, length):
        return lax.dynamic_slice_in_dim(array, index * length, length, axis=0)

    def reduced(pieces, after):
        total = None
        for x, m, piece in pieces[:-1]:
            product = jnp.dot(piece, rows_for(x, m), preferred_element_type=f32)
            total = product if total is None else total + product
        x, m, last = pieces[-1]
        total, last, unused = tie((total, last, after))
        length = run // 2

        def first_sum(index):
            product = jnp.dot(
                run_of(last, index, length), rows_for(x, m), preferred_element_type=f32
            )
            return run_of(total, index, length) + product

        keeps = rank % 2
        pairs = [(t, t ^ 1) for t in range(ranks)]
        received = lax.ppermute(first_sum(1 - keeps).astype(bf16), "tensor", pairs)
        kept = first_sum(keeps)
        bit = 2
        while bit < ranks:
            length //= 2
            keeps = (rank // bit) % 2
            pairs = [(t, t ^ bit) for t in range(ranks)]
            sent = run_of(kept, 1 - keeps, length) + run_of(received, 1 - keeps, length)
            kept = run_of(kept, keeps, length) + run_of(received, keeps, length)
            sent = sent.astype(bf16)
            received = lax.ppermute(sent, "tensor", pairs)
            bit *= 2
        return kept, received, sent

    gathered = [gather(block) for block in gained]
    halves = []
    for pieces in gathered:
        halves.append(reduced(pieces, halves[-1][-1] if halves else ()))
    tails = [piece[run:].astype(f32) for x, m, piece in gathered[-1]]
    squares = sum(tail[:ROWS, :SPAN] + tail[:ROWS, SPAN:] for tail in tails)
    top = functools.reduce(jnp.maximum, [tail[ROWS:, :SPAN] for tail in tails])
    bit = 1
    while bit < ranks:
        squares = squares + lax.ppermute(squares, "tensor", [(t, t ^ bit) for t in range(ranks)])
        bit *= 2
    mean_sq = squares.reshape(count, ranks, own) / (HEADS * HEAD_DIM)
    factors = lax.rsqrt(pick(mean_sq, 1, rank) + epsilon)[:, :, None]
    final = jnp.concatenate([kept + received.astype(f32) for kept, received, _ in halves], axis=0)
    final = (final.reshape(count, own, -1) * factors).astype(bf16)
    final = lax.all_to_all(final, "seq", split_axis=0, concat_axis=0, tiled=True)
    layer_out = final.transpose(1, 0, 2).reshape(own, count * final.shape[2])
    return (layer_out, jnp.max(top))


def solution(mesh):
    return jax.shard_map(
        by_heads if splits(mesh) else by_tokens,
        mesh=mesh,
        in_specs=(
            P(("seq", "tensor"), None),
            P(),
            P("seq", "tensor"),
            P("seq", "tensor", None, None),
            P("seq", "tensor"),
            P(None, "tensor"),
            P(None, "tensor", None, None),
            P(None, "tensor"),
            P(None, "tensor", None, None),
            P("tensor"),
            P("tensor"),
            P("tensor"),
            P("tensor", None, None),
            P("tensor"),
            P("tensor", "seq"),
        ),
        out_specs=(P(("seq", "tensor"), None), P()),
        check_vma=False,
    )
```

```python
import functools

import jax
import jax.numpy as jnp
from jax import lax
from jax.experimental import pallas as pl
from jax.experimental.pallas import tpu as pltpu
from jax.sharding import PartitionSpec as P

HEADS = 128
HEAD_DIM = 64
STATE = 128
GROUPS = 8
KERNEL = 4
SPAN = 128


epsilon = 1e-05
quant_range = 448.0


def from_behind(value, axis, steps):
    count = lax.axis_size(axis)
    first, last = (max(0, -steps), min(count, count - steps))
    return lax.ppermute(value, axis, [(source, source + steps) for source in range(first, last)])


def carried_in(shard, axis, combine, identity):
    count, here = (lax.axis_size(axis), lax.axis_index(axis))
    everything = jax.tree.map(
        lambda part, kind: lax.all_gather(part.astype(kind), axis),
        shard,
        (jnp.bfloat16, jnp.bfloat16),
    )
    start = jax.tree.map(
        lambda part, zero: jnp.broadcast_to(jnp.asarray(zero, part.dtype), part.shape),
        shard,
        identity,
    )

    def turn(k, before):
        reached = k < here
        new = combine(
            before, jax.tree.map(lambda part, own: part[k].astype(own.dtype), everything, shard)
        )
        return jax.tree.map(lambda a, b: jnp.where(reached, a, b), new, before)

    return lax.fori_loop(0, count, turn, start)


def depthwise(before, projected, conv_taps, length):
    extended = jnp.concatenate([before, projected], axis=0)
    summed = conv_taps[0] * extended[0:length]
    for offset in range(1, KERNEL):
        summed = summed + conv_taps[offset] * extended[offset : offset + length]
    return jax.nn.silu(summed).astype(jnp.bfloat16)


def combine(earlier, later):
    return (earlier[0] * later[0], later[0][:, None, None] * earlier[1] + later[1])


def by_tokens(
    hidden_in,
    prev_amax,
    w_x,
    w_bc,
    w_dt,
    conv_x,
    conv_bc,
    conv_state_x,
    conv_state_bc,
    dt_bias,
    decay_rate,
    skip,
    init_state,
    norm_gain,
    w_out,
):
    margin = KERNEL - 1
    gathered = lax.all_gather(hidden_in, "tensor", axis=0, tiled=True)
    abs_max = lax.pmax(jnp.max(jnp.abs(gathered.astype(jnp.float32))), "seq")
    in_scale = prev_amax / quant_range
    leading = lax.axis_index("seq") == 0
    row_count = gathered.shape[0]
    bc_width = w_bc.shape[1] * w_bc.shape[2] * w_bc.shape[3]
    bc_rows = jnp.reshape(w_bc, (w_bc.shape[0], bc_width))
    scaled = gathered.astype(jnp.float32) * (quant_range / prev_amax)
    quant = jnp.clip(scaled, -quant_range, quant_range).astype(jnp.bfloat16)
    pieces = (
        lax.all_gather(w_x, "seq", axis=0, tiled=True),
        lax.all_gather(bc_rows, "seq", axis=0, tiled=True),
        lax.all_gather(w_dt, "seq", axis=0, tiled=True),
    )
    x_proj, bc_proj, dt_proj = tuple(
        (
            jnp.dot(quant, weight_piece, preferred_element_type=jnp.float32)
            for weight_piece in pieces
        )
    )
    x_whole = (x_proj * in_scale).astype(jnp.bfloat16)
    bc_whole = (bc_proj * in_scale).astype(jnp.bfloat16)
    dt_raw = dt_proj * in_scale
    state_bc = jnp.reshape(conv_state_bc, (margin, bc_width))
    received = from_behind(
        (x_whole[row_count - margin :], bc_whole[row_count - margin :]), "seq", 1
    )
    x_edge = jnp.where(leading, conv_state_x, received[0])
    bc_edge = jnp.where(leading, state_bc, received[1])
    x_act = depthwise(x_edge, x_whole, conv_x, row_count)
    bc_act = depthwise(bc_edge, bc_whole, jnp.reshape(conv_bc, (KERNEL, bc_width)), row_count)
    step_size = jax.nn.softplus(dt_raw + dt_bias)
    heads_here = step_size.shape[1]
    groups_here = w_bc.shape[1]
    per_group = HEADS // GROUPS
    blocks = row_count // SPAN
    x_blocks = x_act.reshape(blocks, SPAN, heads_here, HEAD_DIM)
    bc_blocks = bc_act.reshape(blocks, SPAN, groups_here, 2, STATE)
    in_map = bc_blocks[:, :, :, 0]
    out_map = bc_blocks[:, :, :, 1]
    step_blocks = step_size.reshape(blocks, SPAN, heads_here)
    cum_blocks = jnp.cumsum(-step_blocks * decay_rate, axis=1)
    index_row = jnp.arange(SPAN, dtype=jnp.int32)
    lower_mask = index_row[:, None] >= index_row[None, :]
    intersection = jnp.einsum(
        "ctgn,cugn->cgtu", out_map, in_map, preferred_element_type=jnp.float32
    )
    intersection = jnp.repeat(intersection, per_group, axis=1)
    cum_heads = jnp.transpose(cum_blocks, (0, 2, 1))
    log_gap = cum_heads[:, :, :, None] - cum_heads[:, :, None, :]
    decay = jnp.exp(jnp.where(lower_mask[None, None], log_gap, -1e30))
    step_heads = jnp.transpose(step_blocks, (0, 2, 1))
    weights = (intersection * decay * step_heads[:, :, None, :]).astype(jnp.bfloat16)
    local_part = jnp.einsum(
        "chtu,cuhp->cthp", weights, x_blocks, preferred_element_type=jnp.float32
    )
    last_cum = cum_blocks[:, SPAN - 1, :]
    x_weighted = (
        x_blocks.astype(jnp.float32)
        * (step_blocks * jnp.exp(last_cum[:, None, :] - cum_blocks))[:, :, :, None]
    ).astype(jnp.bfloat16)
    in_heads = jnp.repeat(in_map, per_group, axis=2)
    added = jnp.einsum("cuhp,cuhn->chpn", x_weighted, in_heads, preferred_element_type=jnp.float32)

    def carry_on(carried, element):
        block_decay, block_added = element
        return (block_decay[:, None, None] * carried + block_added, carried)

    empty_state = jnp.zeros((heads_here, HEAD_DIM, STATE), jnp.float32)
    device_state, entering = lax.scan(carry_on, empty_state, (jnp.exp(last_cum), added))
    device_decay = jnp.exp(jnp.sum(last_cum, axis=0))
    seeded = device_state + jnp.where(leading, device_decay[:, None, None] * init_state, 0.0)
    identity = (jnp.ones_like(device_decay), jnp.zeros_like(device_state))
    scanned = carried_in((device_decay, seeded), "seq", combine, identity)
    incoming = jnp.where(leading, init_state, scanned[1])
    prefix = jnp.exp(jnp.cumsum(last_cum, axis=0) - last_cum)
    states_in = entering + prefix[:, :, None, None] * incoming[None]
    out_heads = jnp.repeat(out_map, per_group, axis=2).astype(jnp.float32)
    carried_part = (
        jnp.einsum("cthn,chpn->cthp", out_heads, states_in, precision=lax.Precision.HIGHEST)
        * jnp.exp(cum_blocks)[:, :, :, None]
    )
    ssm_out = local_part + carried_part + skip[None, None, :, None] * x_blocks.astype(jnp.float32)
    ssm_out = ssm_out.reshape(row_count, heads_here * HEAD_DIM)
    squares = lax.psum(jnp.sum(ssm_out * ssm_out, axis=1), "tensor")
    mean_sq = squares / (HEADS * HEAD_DIM)
    normed = (ssm_out * lax.rsqrt(mean_sq + epsilon)[:, None] * norm_gain).astype(jnp.bfloat16)
    partial_out = jnp.dot(
        normed, lax.all_gather(w_out, "seq", axis=1, tiled=True), preferred_element_type=jnp.float32
    )
    layer_out = lax.psum_scatter(
        partial_out.astype(jnp.bfloat16), "tensor", scatter_dimension=0, tiled=True
    )
    return (layer_out, abs_max)


PAIR = 2
LINE = 4
ROWS = 8
CUTS = 2
SMEM = pl.BlockSpec(memory_space=pltpu.SMEM)
VMEM = pl.BlockSpec(memory_space=pltpu.VMEM)
HIGHEST = lax.Precision.HIGHEST


def splits(mesh):
    count, ranks = (mesh.shape["seq"], mesh.shape["tensor"])
    heads_all, groups_here = (HEADS // ranks, GROUPS // ranks)
    if count != PAIR * LINE or groups_here != PAIR or ranks & (ranks - 1):
        return False
    heads_here = heads_all // count
    return 2 * heads_here == ROWS and heads_here * HEAD_DIM == 2 * SPAN


def nt_dot(a, b, **kw):
    return lax.dot_general(
        a, b, (((1,), (1,)), ((), ())), preferred_element_type=jnp.float32, **kw
    )


def project_kernel(ranks, place_ref, factor_ref, *refs):
    hidden = [refs[x * ranks : (x + 1) * ranks] for x in range(PAIR)]
    refs = refs[PAIR * ranks :]
    own_x, other_x, refs = (refs[0], refs[1 : 1 + LINE // 2], refs[1 + LINE // 2 :])
    own_bc, other_bc, own_dt, other_dt = refs[:4]
    far_refs, near_refs, sent_refs = (
        refs[4 + at : 4 + at + LINE // 2] for at in range(0, 3 * LINE // 2, LINE // 2)
    )
    bc_ref, largest_ref, quant_ref, near_dt, all_dt = refs[4 + 3 * LINE // 2 :]
    side, z = (place_ref[1], place_ref[2])
    factor = factor_ref[0]
    depth = own_x.shape[0]
    largest = None
    for x in range(PAIR):
        for k in range(LINE):
            block = (k ^ z) * PAIR + (side ^ x)
            for j in range(ranks):
                for half in range(PAIR):
                    cut = slice(half * depth, (half + 1) * depth)
                    values = hidden[x][j][k, :, cut].astype(jnp.float32)
                    scaled = jnp.clip(values * factor, -quant_range, quant_range)
                    quant_ref[half, block, j] = scaled.astype(jnp.bfloat16)
                    top = jnp.max(jnp.abs(values).reshape(-1, ROWS, depth), axis=0)
                    largest = top if largest is None else jnp.maximum(largest, top)
    width = largest_ref.shape[1]
    top = largest[:, :width]
    for at in range(width, depth, width):
        top = jnp.maximum(top, largest[:, at : at + width])
    largest_ref[...] = top

    channels = near_refs[0].shape[1]
    tokens = bc_ref.shape[0]
    rows = tokens // CUTS
    blocks = quant_ref.shape[1] // CUTS
    extra = rows // channels * ROWS
    upper = lax.broadcasted_iota(jnp.int32, (ROWS, channels), 0) < ROWS // 2

    def steps_of(dt_ref, run):
        dt = dt_ref[run // 2]
        pieces = []
        for at in range(0, rows, channels):
            piece = dt[:, at : at + channels]
            turned = pltpu.roll(piece, ROWS // 2, 0)
            lower_run = jnp.where(upper, piece, turned)
            upper_run = jnp.where(upper, turned, piece)
            pieces.append(split_parts(jnp.where(run % 2 == 0, lower_run, upper_run), upper))
        return jnp.concatenate(pieces, axis=0).astype(jnp.bfloat16)

    def columns(run):
        return pl.ds(pl.multiple_of(run * channels, channels), channels)

    for cut in range(CUTS):
        part = slice(cut * blocks, (cut + 1) * blocks)
        near = quant_ref[side, part].reshape(rows, depth)
        far = quant_ref[1 - side, part].reshape(rows, depth)

        def both(own, other):
            return jnp.dot(near, own, preferred_element_type=jnp.float32) + jnp.dot(
                far, other, preferred_element_type=jnp.float32
            )

        at_rows = slice(cut * rows, (cut + 1) * rows)
        extra_rows = slice(tokens + cut * extra, tokens + (cut + 1) * extra)
        ours = nt_dot(own_dt[...], near)
        near_dt[...] = ours.reshape(near_dt.shape)
        all_dt[...] = (ours + nt_dot(other_dt[...], far)).reshape(all_dt.shape)
        bc_ref[at_rows] = both(own_bc[...], other_bc[...]).astype(jnp.bfloat16)
        for m in range(LINE // 2):
            owner = z ^ (m + LINE // 2)
            run = side * LINE + owner
            product = both(own_x[:, columns(run)], other_x[m][...])
            far_refs[m][at_rows] = product.astype(jnp.bfloat16)
            far_refs[m][extra_rows] = steps_of(all_dt, run)
            for out_refs, way in ((near_refs, side), (sent_refs, 1 - side)):
                run = way * LINE + (z ^ m)
                product = jnp.dot(near, own_x[:, columns(run)], preferred_element_type=jnp.float32)
                out_refs[m][at_rows] = product.astype(jnp.bfloat16)
                out_refs[m][extra_rows] = steps_of(near_dt, run)


def split_parts(values, upper):
    top = values.astype(jnp.bfloat16).astype(jnp.float32)
    return jnp.where(upper, top, values - top)


def project(place, factor, hidden, w_x, weights):
    line, own, wide = hidden[0].shape
    ranks = len(hidden) // PAIR
    depth, channels = weights[0].shape
    x_wide, maps_wide = (LINE * channels, weights[LINE // 2].shape[1])
    tokens = line * PAIR * ranks * own
    extra = tokens // channels * ROWS
    dt_shape = (weights[-1].shape[0] // ROWS, ROWS, tokens // CUTS)
    payload = jax.ShapeDtypeStruct((tokens + extra, channels), jnp.bfloat16)
    maps = jax.ShapeDtypeStruct((tokens, maps_wide), jnp.bfloat16)
    largest = jax.ShapeDtypeStruct((ROWS, 128), jnp.float32)
    outs = [payload] * (LINE + LINE // 2) + [maps, largest]
    return pl.pallas_call(
        functools.partial(project_kernel, ranks),
        in_specs=[SMEM, SMEM] + [VMEM] * (len(hidden) + 1 + len(weights)),
        out_specs=[VMEM] * len(outs),
        scratch_shapes=[
            pltpu.VMEM((PAIR, line * PAIR, ranks, own, depth), jnp.bfloat16),
            pltpu.VMEM(dt_shape, jnp.float32),
            pltpu.VMEM(dt_shape, jnp.float32),
        ],
        out_shape=outs,
        compiler_params=pltpu.CompilerParams(vmem_limit_bytes=32 * 2**20),
        cost_estimate=pl.CostEstimate(
            flops=2 * tokens * wide * (x_wide + maps_wide),
            bytes_accessed=2 * tokens * (wide + x_wide),
            transcendentals=0,
        ),
        name="project",
    )(place, factor, *hidden, w_x, *weights)


def onward_kernel(own_ref, received_ref, out_ref):
    rows, channels = own_ref.shape
    tokens = rows * channels // (channels + ROWS)
    total = own_ref[:tokens].astype(jnp.float32) + received_ref[:tokens].astype(jnp.float32)
    out_ref[:tokens] = total.astype(jnp.bfloat16)
    upper = lax.broadcasted_iota(jnp.int32, (ROWS, channels), 0) < ROWS // 2
    extra = own_ref[tokens:].astype(jnp.float32) + received_ref[tokens:].astype(jnp.float32)
    pieces = []
    for at in range(0, rows - tokens, ROWS):
        piece = extra[at : at + ROWS]
        pieces.append(split_parts(piece + pltpu.roll(piece, ROWS // 2, 0), upper))
    out_ref[tokens:] = jnp.concatenate(pieces, axis=0).astype(jnp.bfloat16)


def onward(own, received):
    return pl.pallas_call(
        onward_kernel,
        in_specs=[VMEM, VMEM],
        out_specs=VMEM,
        out_shape=jax.ShapeDtypeStruct(own.shape, own.dtype),
        compiler_params=pltpu.CompilerParams(vmem_limit_bytes=8 * 2**20),
        cost_estimate=pl.CostEstimate(
            flops=own.size, bytes_accessed=6 * own.size, transcendentals=0
        ),
        name="onward",
    )(own, received)


def turned_rank(rank, ranks):
    turned = 0
    while ranks > 1:
        turned, rank, ranks = (2 * turned + rank % 2, rank // 2, ranks // 2)
    return turned


def scan_kernel(place_ref, scale_ref, *refs):
    x_refs, bc_refs = (refs[:-9], refs[-9:-6])
    small_ref, largest_ref, state_ref, out_ref, x_buf, bc_buf = refs[-6:]
    tokens, channels = bc_refs[0].shape
    blocks = tokens // SPAN
    heads = channels // HEAD_DIM
    rank, z = (place_ref[0], place_ref[2])
    ranks = place_ref.shape[0] - 3
    own = SPAN // ranks
    edge = ROWS
    in_scale = scale_ref[0]
    at_end = (z == 0) | (z == LINE - 1)
    x_buf[:edge] = small_ref[:edge]
    bc_buf[:edge] = small_ref[edge : 2 * edge]
    state = state_ref[...].T

    for block in range(blocks):
        for true_rank in range(ranks):
            source = block * SPAN + (true_rank ^ rank) * own
            source = pl.ds(pl.multiple_of(source, own), own)
            at = edge + block * SPAN + true_rank * own
            at = slice(at, at + own)
            total = sum(ref[source].astype(jnp.float32) for ref in x_refs) * in_scale
            x_buf[at] = total.astype(jnp.bfloat16).astype(jnp.float32)
            near, far, done = (ref[source].astype(jnp.float32) for ref in bc_refs)
            total = ((near + far) * in_scale).astype(jnp.bfloat16).astype(jnp.float32)
            bc_buf[at] = jnp.where(at_end, done, total)

    taps = 2 * edge

    def activate(buf, row, block):
        start = edge - (KERNEL - 1) + block * SPAN
        summed = small_ref[row : row + 1] * buf[start : start + SPAN]
        for k in range(1, KERNEL):
            summed = summed + small_ref[row + k : row + k + 1] * buf[start + k : start + k + SPAN]
        return (summed / (1.0 + jnp.exp(-summed))).astype(jnp.bfloat16)

    skip = small_ref[taps + 2 * KERNEL : taps + 2 * KERNEL + 1]
    gain = small_ref[taps + 2 * KERNEL + 1 : taps + 2 * KERNEL + 2]
    bias = small_ref[4 * edge :, :SPAN]
    rate = small_ref[4 * edge :, SPAN:]

    up = lax.broadcasted_iota(jnp.int32, (SPAN, SPAN), 0)
    across = lax.broadcasted_iota(jnp.int32, (SPAN, SPAN), 1)
    lane = lax.broadcasted_iota(jnp.int32, (SPAN, channels), 1)
    lower = up >= across
    upper = (up <= across).astype(jnp.float32)
    lanes = across[:ROWS]

    dt = sum(ref[tokens:].astype(jnp.float32) for ref in x_refs)
    steps = []
    wide = channels // SPAN
    for block in range(blocks):
        tile = dt[block // wide * ROWS : (block // wide + 1) * ROWS]
        cut = tile[:, block % wide * SPAN : (block % wide + 1) * SPAN]
        cut = (cut + pltpu.roll(cut, ROWS // 2, 0)) * in_scale
        bit = 1
        while bit < ranks:
            shift = bit * own
            flipped = jnp.where(
                (lanes // shift) % 2 == 1,
                pltpu.roll(cut, shift, 1),
                pltpu.roll(cut, SPAN - shift, 1),
            )
            cut = jnp.where((rank & bit) != 0, flipped, cut)
            bit *= 2
        raw = cut + bias
        steps.append(jnp.maximum(raw, 0.0) + jnp.log1p(jnp.exp(-jnp.abs(raw))))
    drops = jnp.concatenate([-step * rate for step in steps], axis=0)
    cums = jnp.dot(drops, upper, precision=HIGHEST, preferred_element_type=jnp.float32)

    sums = jnp.zeros((SPAN, SPAN), jnp.float32)
    for block in range(blocks):
        x_act = activate(x_buf, taps, block)
        bc_act = activate(bc_buf, taps + KERNEL, block)
        in_map, out_map = (bc_act[:, :STATE], bc_act[:, STATE:])
        step, cum = (steps[block], cums[block * ROWS : (block + 1) * ROWS])
        last = cum[:, SPAN - 1 : SPAN]
        turned = jnp.concatenate(
            [
                cum,
                step * jnp.exp(last - cum),
                jnp.exp(cum),
                jnp.zeros((SPAN - 3 * ROWS, SPAN), jnp.float32),
            ],
            axis=0,
        ).T

        def spread(row):
            result = jnp.broadcast_to(turned[:, row : row + 1], (SPAN, channels))
            for h in range(1, heads):
                result = jnp.where(lane >= h * HEAD_DIM, turned[:, row + h : row + h + 1], result)
            return result

        inner = jnp.where(lower, nt_dot(out_map, in_map), 0.0)
        x_wide = x_act.astype(jnp.float32)
        weights, spaced = ([], [])
        for h in range(heads):
            gap = jnp.where(lower, turned[:, h : h + 1] - cum[h : h + 1], 0.0)
            weights.append((inner * jnp.exp(gap) * step[h : h + 1]).astype(jnp.bfloat16))
            inside = (lane >= h * HEAD_DIM) & (lane < (h + 1) * HEAD_DIM)
            spaced.append(jnp.where(inside, x_wide, 0.0).astype(jnp.bfloat16))
        local_part = jnp.dot(
            jnp.concatenate(weights, axis=1),
            jnp.concatenate(spaced, axis=0),
            preferred_element_type=jnp.float32,
        )
        grown = spread(2 * ROWS)
        x_weighted = (x_wide * spread(ROWS)).astype(jnp.bfloat16)
        added = lax.dot_general(
            in_map, x_weighted, (((0,), (0,)), ((), ())), preferred_element_type=jnp.float32
        )
        high = state.astype(jnp.bfloat16)
        rest = (state - high.astype(jnp.float32)).astype(jnp.bfloat16)
        carried = jnp.dot(
            jnp.concatenate([out_map, out_map], axis=1),
            jnp.concatenate([high, rest], axis=0),
            preferred_element_type=jnp.float32,
        )
        ssm_out = local_part + grown * carried + skip * x_wide
        state = grown[SPAN - 1 : SPAN] * state + added
        gained = (ssm_out * gain).astype(jnp.bfloat16)
        for true_rank in range(ranks):
            at = (turned_rank(true_rank, ranks) * blocks + block) * own
            out_ref[at : at + own] = gained[true_rank * own : (true_rank + 1) * own]
        summed = jnp.sum(ssm_out * ssm_out, axis=1, keepdims=True)
        sums = jnp.where(across == block, summed, sums)

    whole = sums.T[:ROWS]
    top = whole.astype(jnp.bfloat16).astype(jnp.float32)
    largest = jnp.broadcast_to(jnp.max(largest_ref[...]), (ROWS, channels))
    extra = jnp.concatenate([jnp.concatenate([top, whole - top], axis=1), largest], axis=0)
    out_ref[tokens:] = extra.astype(jnp.bfloat16)


def scan(place, in_scale, sums, maps, small, largest, state):
    channels = sums[0].shape[1]
    tokens = maps[0].shape[0]

    out = jax.ShapeDtypeStruct((tokens + 2 * ROWS, channels), jnp.bfloat16)
    return pl.pallas_call(
        scan_kernel,
        in_specs=[SMEM, SMEM] + [VMEM] * (len(sums) + len(maps) + 3),
        out_specs=VMEM,
        scratch_shapes=[
            pltpu.VMEM((tokens + ROWS, channels), jnp.float32),
            pltpu.VMEM((tokens + ROWS, 2 * STATE), jnp.float32),
        ],
        out_shape=out,
        compiler_params=pltpu.CompilerParams(vmem_limit_bytes=20 * 2**20),
        cost_estimate=pl.CostEstimate(
            flops=8 * tokens * SPAN * channels,
            bytes_accessed=8 * tokens * channels,
            transcendentals=tokens * (channels + 8 * SPAN),
        ),
        name="scan",
    )(place, in_scale, *sums, *maps, small, largest, state)


def by_heads(
    hidden_in,
    prev_amax,
    w_x,
    w_bc,
    w_dt,
    conv_x,
    conv_bc,
    conv_state_x,
    conv_state_bc,
    dt_bias,
    decay_rate,
    skip,
    init_state,
    norm_gain,
    w_out,
):
    margin = KERNEL - 1
    count, here = (lax.axis_size("seq"), lax.axis_index("seq"))
    ranks, rank = (lax.axis_size("tensor"), lax.axis_index("tensor"))
    z, side = (here // PAIR, here % PAIR)
    place_of = side * LINE + z
    f32, bf16 = (jnp.float32, jnp.bfloat16)
    own, width = hidden_in.shape
    depth = w_x.shape[0]
    channels = w_x.shape[1] // count
    heads_here = w_dt.shape[1] // count
    in_scale = (prev_amax / quant_range).reshape(1)
    factor = (quant_range / prev_amax).reshape(1)
    place = jnp.stack([rank, side, z] + [rank] * ranks).astype(jnp.int32)

    def pick(array, axis, index):
        return lax.dynamic_index_in_dim(array, index, axis, keepdims=False)

    def along(value, pairs):
        moves = [(a * PAIR + x, b * PAIR + x) for a, b in pairs for x in range(PAIR)]
        return lax.ppermute(value, "seq", moves)

    def across(value):
        return lax.ppermute(value, "seq", [(s, s ^ 1) for s in range(count)])

    def of_heads(array):
        return jnp.repeat(array, HEAD_DIM)[None]

    by_channel = jnp.concatenate(
        [conv_state_x.astype(f32), conv_x, of_heads(skip), norm_gain[None]], axis=0
    )
    by_channel = lax.dynamic_slice_in_dim(by_channel, place_of * channels, channels, axis=1)
    by_map = jnp.concatenate([conv_state_bc.astype(f32), conv_bc], axis=0)
    by_map = pick(by_map, 1, side).reshape(margin + KERNEL, 2 * STATE)
    by_head = jnp.stack([dt_bias, decay_rate]).reshape(2, count, heads_here)
    by_head = jnp.tile(pick(by_head, 1, place_of).T, (ROWS // heads_here, 1))
    by_head = jnp.repeat(by_head, SPAN, axis=1)
    blank = jnp.zeros((ROWS - margin, channels), f32)
    small = jnp.concatenate(
        [
            blank,
            by_channel[:margin],
            blank,
            by_map[:margin],
            by_channel[margin : margin + KERNEL],
            by_map[margin:],
            by_channel[margin + KERNEL :],
            jnp.zeros((2 * ROWS - 2 * KERNEL - 2, channels), f32),
            by_head,
        ],
        axis=0,
    )

    start_state = lax.dynamic_slice_in_dim(
        init_state, place_of * heads_here, heads_here, axis=0
    ).reshape(channels, STATE)

    tie = lax.optimization_barrier
    def sent_columns(m):
        run = (1 - side) * LINE + (z ^ m)
        return lax.dynamic_slice_in_dim(w_x, run * channels, channels, axis=1)

    x_sent, hidden_in = tie((sent_columns(LINE - 1), hidden_in))
    swapped = [across(x_sent)]
    bc_own = pick(w_bc, 1, side).reshape(depth, 2 * STATE)
    maps_sent = pick(w_bc, 1, 1 - side).reshape(depth, 2 * STATE)
    dt_sent = w_dt.T

    def line_columns(m):
        return lax.dynamic_slice_in_dim(hidden_in, (z ^ m) * PAIR * depth, PAIR * depth, axis=1)

    arrived = [line_columns(0)]
    for m in range(1, LINE):
        arrived.append(along(line_columns(m), [(s, s ^ m) for s in range(LINE)]))
    stacked = jnp.stack(arrived)
    stacked, x_sent, maps_sent, dt_sent = tie(
        (stacked, sent_columns(LINE - 2), maps_sent, dt_sent)
    )
    beyond_pair = across(stacked)
    swapped.insert(0, across(x_sent))
    bc_other, dt_other = (across(maps_sent), across(dt_sent))
    beyond_pair, small, start_state, bc_own, dt_sent = tie(
        (beyond_pair, small, start_state, bc_own, dt_sent)
    )
    rows = []
    for mine in (stacked, beyond_pair):
        ours = [mine]
        for j in range(1, ranks):
            bit = j & -j
            pairs = [(t, t ^ bit) for t in range(ranks)]
            ours.append(lax.ppermute(ours[j - bit], "tensor", pairs))
        rows.extend(ours)

    start, end = (0, LINE - 1)
    at_end = (z == start) | (z == end)
    next_start, next_end = (1, LINE - 2)
    inward = [(start, next_start), (end, next_end)]
    outward = [(next_start, start), (next_end, end)]
    middle = [(next_start, next_end), (next_end, next_start)]
    over_middle = [(next_start, end), (next_end, start)]
    beside_pairs = [(s, s ^ 1) for s in range(LINE)]
    weights = (*swapped, bc_own, bc_other, dt_sent, dt_other)
    over, far, mine, near, mine_sent, near_sent, maps, largest = project(
        place, factor, rows, w_x, weights
    )

    map_hop = along(maps, inward)
    hop_far = along(far, inward)
    hop_over = along(over, inward)
    near = onward(near, across(near_sent))
    got_mine = across(mine_sent)
    near_out = along(near, outward)
    near_in = along(near, inward)
    map_sum = (maps.astype(f32) + map_hop.astype(f32)).astype(bf16)
    map_far = along(map_sum, middle)
    map_done = ((map_sum.astype(f32) + map_far.astype(f32)) * in_scale).astype(bf16)
    sent_end = onward(over, hop_far)
    got_end = along(sent_end, over_middle)
    hop_over, near_out, unused = tie((hop_over, near_out, sent_end))
    got_next = along(onward(far, hop_over), middle)
    map_done, got_end, got_mine = tie((map_done, got_end, got_mine))
    map_done = along(map_done, outward)
    gained = scan(
        place,
        in_scale,
        [mine, got_mine, near_out, near_in, got_end, got_next],
        [map_sum, map_far, map_done],
        small,
        largest,
        start_state,
    )

    tokens = gained.shape[0] - 2 * ROWS
    beside = along(gained, beside_pairs)
    facing = along(gained, middle)
    second = jnp.where(at_end, along(facing, outward), facing)
    beyond = along(beside, middle)
    third = jnp.where(at_end, along(beyond, outward), beyond)
    far_own = across(gained)
    far_beside = across(beside)
    second, far_own = tie((second, far_own))
    far_second = across(second)
    third, far_beside = tie((third, far_beside))
    far_third = across(third)
    two, three = (jnp.where(at_end, 2, 3), jnp.where(at_end, 3, 2))

    def rows_for(x, m):
        at = ((side ^ x) * LINE + (z ^ m)) * channels
        return lax.dynamic_slice_in_dim(w_out, at, channels, axis=0)

    total = None
    tails = [far_third[tokens:]]
    for x, m, piece in (
        (0, 0, gained),
        (1, 0, far_own),
        (0, 1, beside),
        (1, 1, far_beside),
        (0, two, second),
        (1, two, far_second),
        (0, three, third),
    ):
        product = jnp.dot(piece, rows_for(x, m), preferred_element_type=f32)
        total = product if total is None else total + product
        tails.append(piece[tokens:])
    total, far_third = tie((total, far_third))
    last_rows = rows_for(1, three)
    tails = [tail.astype(f32) for tail in tails]
    squares = sum(tail[:ROWS, :SPAN] + tail[:ROWS, SPAN:] for tail in tails)
    top = functools.reduce(jnp.maximum, [tail[ROWS:, :SPAN] for tail in tails])

    def run_of(array, index, run):
        return lax.dynamic_slice_in_dim(array, index * run, run, axis=0)

    def first_sum(index):
        block, so_far = (run_of(far_third, index, run), run_of(total, index, run))
        return so_far + jnp.dot(block, last_rows, preferred_element_type=f32)

    run = tokens // 2
    keeps = rank % 2
    pairs = [(t, t ^ 1) for t in range(ranks)]
    received = lax.ppermute(first_sum(1 - keeps).astype(bf16), "tensor", pairs)
    kept = first_sum(keeps)
    squares = squares + lax.ppermute(squares, "tensor", pairs)
    bit = 2
    while bit < ranks:
        run //= 2
        keeps = (rank // bit) % 2
        pairs = [(t, t ^ bit) for t in range(ranks)]
        sent = run_of(kept, 1 - keeps, run) + run_of(received, 1 - keeps, run).astype(f32)
        kept = run_of(kept, keeps, run) + run_of(received, keeps, run).astype(f32)
        received = lax.ppermute(sent.astype(bf16), "tensor", pairs)
        squares = squares + lax.ppermute(squares, "tensor", pairs)
        bit *= 2
    mean_sq = squares.reshape(count, ranks, own) / (HEADS * HEAD_DIM)
    factors = lax.rsqrt(pick(mean_sq, 1, rank) + epsilon)
    final = (kept + received.astype(f32)).reshape(count, own, -1) * factors[:, :, None]
    final = lax.all_to_all(final.astype(bf16), "seq", split_axis=0, concat_axis=0, tiled=True)
    layer_out = final.transpose(1, 0, 2).reshape(own, count * final.shape[2])
    return (layer_out, jnp.max(top))


def solution(mesh):
    return jax.shard_map(
        by_heads if splits(mesh) else by_tokens,
        mesh=mesh,
        in_specs=(
            P(("seq", "tensor"), None),
            P(),
            P("seq", "tensor"),
            P("seq", "tensor", None, None),
            P("seq", "tensor"),
            P(None, "tensor"),
            P(None, "tensor", None, None),
            P(None, "tensor"),
            P(None, "tensor", None, None),
            P("tensor"),
            P("tensor"),
            P("tensor"),
            P("tensor", None, None),
            P("tensor"),
            P("tensor", "seq"),
        ),
        out_specs=(P(("seq", "tensor"), None), P()),
        check_vma=False,
    )
```

```python
import functools

import jax
import jax.numpy as jnp
from jax import lax
from jax.experimental import pallas as pl
from jax.experimental.pallas import tpu as pltpu
from jax.sharding import PartitionSpec as P

HEADS = 128
HEAD_DIM = 64
STATE = 128
GROUPS = 8
KERNEL = 4
SPAN = 128


epsilon = 1e-05
quant_range = 448.0


def from_behind(value, axis, steps):
    count = lax.axis_size(axis)
    first, last = (max(0, -steps), min(count, count - steps))
    return lax.ppermute(value, axis, [(source, source + steps) for source in range(first, last)])


def carried_in(shard, axis, combine, identity):
    count, here = (lax.axis_size(axis), lax.axis_index(axis))
    everything = jax.tree.map(
        lambda part, kind: lax.all_gather(part.astype(kind), axis),
        shard,
        (jnp.bfloat16, jnp.bfloat16),
    )
    start = jax.tree.map(
        lambda part, zero: jnp.broadcast_to(jnp.asarray(zero, part.dtype), part.shape),
        shard,
        identity,
    )

    def turn(k, before):
        reached = k < here
        new = combine(
            before, jax.tree.map(lambda part, own: part[k].astype(own.dtype), everything, shard)
        )
        return jax.tree.map(lambda a, b: jnp.where(reached, a, b), new, before)

    return lax.fori_loop(0, count, turn, start)


def depthwise(before, projected, conv_taps, length):
    extended = jnp.concatenate([before, projected], axis=0)
    summed = conv_taps[0] * extended[0:length]
    for offset in range(1, KERNEL):
        summed = summed + conv_taps[offset] * extended[offset : offset + length]
    return jax.nn.silu(summed).astype(jnp.bfloat16)


def combine(earlier, later):
    return (earlier[0] * later[0], later[0][:, None, None] * earlier[1] + later[1])


def by_tokens(
    hidden_in,
    prev_amax,
    w_x,
    w_bc,
    w_dt,
    conv_x,
    conv_bc,
    conv_state_x,
    conv_state_bc,
    dt_bias,
    decay_rate,
    skip,
    init_state,
    norm_gain,
    w_out,
):
    margin = KERNEL - 1
    gathered = lax.all_gather(hidden_in, "tensor", axis=0, tiled=True)
    abs_max = lax.pmax(jnp.max(jnp.abs(gathered.astype(jnp.float32))), "seq")
    in_scale = prev_amax / quant_range
    leading = lax.axis_index("seq") == 0
    row_count = gathered.shape[0]
    bc_width = w_bc.shape[1] * w_bc.shape[2] * w_bc.shape[3]
    bc_rows = jnp.reshape(w_bc, (w_bc.shape[0], bc_width))
    scaled = gathered.astype(jnp.float32) * (quant_range / prev_amax)
    quant = jnp.clip(scaled, -quant_range, quant_range).astype(jnp.bfloat16)
    pieces = (
        lax.all_gather(w_x, "seq", axis=0, tiled=True),
        lax.all_gather(bc_rows, "seq", axis=0, tiled=True),
        lax.all_gather(w_dt, "seq", axis=0, tiled=True),
    )
    x_proj, bc_proj, dt_proj = tuple(
        (
            jnp.dot(quant, weight_piece, preferred_element_type=jnp.float32)
            for weight_piece in pieces
        )
    )
    x_whole = (x_proj * in_scale).astype(jnp.bfloat16)
    bc_whole = (bc_proj * in_scale).astype(jnp.bfloat16)
    dt_raw = dt_proj * in_scale
    state_bc = jnp.reshape(conv_state_bc, (margin, bc_width))
    received = from_behind(
        (x_whole[row_count - margin :], bc_whole[row_count - margin :]), "seq", 1
    )
    x_edge = jnp.where(leading, conv_state_x, received[0])
    bc_edge = jnp.where(leading, state_bc, received[1])
    x_act = depthwise(x_edge, x_whole, conv_x, row_count)
    bc_act = depthwise(bc_edge, bc_whole, jnp.reshape(conv_bc, (KERNEL, bc_width)), row_count)
    step_size = jax.nn.softplus(dt_raw + dt_bias)
    heads_here = step_size.shape[1]
    groups_here = w_bc.shape[1]
    per_group = HEADS // GROUPS
    blocks = row_count // SPAN
    x_blocks = x_act.reshape(blocks, SPAN, heads_here, HEAD_DIM)
    bc_blocks = bc_act.reshape(blocks, SPAN, groups_here, 2, STATE)
    in_map = bc_blocks[:, :, :, 0]
    out_map = bc_blocks[:, :, :, 1]
    step_blocks = step_size.reshape(blocks, SPAN, heads_here)
    cum_blocks = jnp.cumsum(-step_blocks * decay_rate, axis=1)
    index_row = jnp.arange(SPAN, dtype=jnp.int32)
    lower_mask = index_row[:, None] >= index_row[None, :]
    intersection = jnp.einsum(
        "ctgn,cugn->cgtu", out_map, in_map, preferred_element_type=jnp.float32
    )
    intersection = jnp.repeat(intersection, per_group, axis=1)
    cum_heads = jnp.transpose(cum_blocks, (0, 2, 1))
    log_gap = cum_heads[:, :, :, None] - cum_heads[:, :, None, :]
    decay = jnp.exp(jnp.where(lower_mask[None, None], log_gap, -1e30))
    step_heads = jnp.transpose(step_blocks, (0, 2, 1))
    weights = (intersection * decay * step_heads[:, :, None, :]).astype(jnp.bfloat16)
    local_part = jnp.einsum(
        "chtu,cuhp->cthp", weights, x_blocks, preferred_element_type=jnp.float32
    )
    last_cum = cum_blocks[:, SPAN - 1, :]
    x_weighted = (
        x_blocks.astype(jnp.float32)
        * (step_blocks * jnp.exp(last_cum[:, None, :] - cum_blocks))[:, :, :, None]
    ).astype(jnp.bfloat16)
    in_heads = jnp.repeat(in_map, per_group, axis=2)
    added = jnp.einsum("cuhp,cuhn->chpn", x_weighted, in_heads, preferred_element_type=jnp.float32)

    def carry_on(carried, element):
        block_decay, block_added = element
        return (block_decay[:, None, None] * carried + block_added, carried)

    empty_state = jnp.zeros((heads_here, HEAD_DIM, STATE), jnp.float32)
    device_state, entering = lax.scan(carry_on, empty_state, (jnp.exp(last_cum), added))
    device_decay = jnp.exp(jnp.sum(last_cum, axis=0))
    seeded = device_state + jnp.where(leading, device_decay[:, None, None] * init_state, 0.0)
    identity = (jnp.ones_like(device_decay), jnp.zeros_like(device_state))
    scanned = carried_in((device_decay, seeded), "seq", combine, identity)
    incoming = jnp.where(leading, init_state, scanned[1])
    prefix = jnp.exp(jnp.cumsum(last_cum, axis=0) - last_cum)
    states_in = entering + prefix[:, :, None, None] * incoming[None]
    out_heads = jnp.repeat(out_map, per_group, axis=2).astype(jnp.float32)
    carried_part = (
        jnp.einsum("cthn,chpn->cthp", out_heads, states_in, precision=lax.Precision.HIGHEST)
        * jnp.exp(cum_blocks)[:, :, :, None]
    )
    ssm_out = local_part + carried_part + skip[None, None, :, None] * x_blocks.astype(jnp.float32)
    ssm_out = ssm_out.reshape(row_count, heads_here * HEAD_DIM)
    squares = lax.psum(jnp.sum(ssm_out * ssm_out, axis=1), "tensor")
    mean_sq = squares / (HEADS * HEAD_DIM)
    normed = (ssm_out * lax.rsqrt(mean_sq + epsilon)[:, None] * norm_gain).astype(jnp.bfloat16)
    partial_out = jnp.dot(
        normed, lax.all_gather(w_out, "seq", axis=1, tiled=True), preferred_element_type=jnp.float32
    )
    layer_out = lax.psum_scatter(
        partial_out.astype(jnp.bfloat16), "tensor", scatter_dimension=0, tiled=True
    )
    return (layer_out, abs_max)


PAIR = 2
LINE = 4
ROWS = 8
CUTS = 2
SMEM = pl.BlockSpec(memory_space=pltpu.SMEM)
VMEM = pl.BlockSpec(memory_space=pltpu.VMEM)
HIGHEST = lax.Precision.HIGHEST


def splits(mesh):
    count, ranks = (mesh.shape["seq"], mesh.shape["tensor"])
    heads_all, groups_here = (HEADS // ranks, GROUPS // ranks)
    if count != PAIR * LINE or groups_here != PAIR or ranks & (ranks - 1):
        return False
    heads_here = heads_all // count
    return 2 * heads_here == ROWS and heads_here * HEAD_DIM == 2 * SPAN


def nt_dot(a, b, **kw):
    return lax.dot_general(
        a, b, (((1,), (1,)), ((), ())), preferred_element_type=jnp.float32, **kw
    )


def project_kernel(ranks, place_ref, factor_ref, *refs):
    hidden = [refs[x * ranks : (x + 1) * ranks] for x in range(PAIR)]
    refs = refs[PAIR * ranks :]
    own_x, x_far, own_bc, own_dt, rest = refs[:5]
    far_refs, near_refs, sent_refs = (
        refs[5 + at : 5 + at + LINE // 2] for at in range(0, 3 * LINE // 2, LINE // 2)
    )
    bc_ref, largest_ref, quant_ref, near_dt, all_dt = refs[5 + 3 * LINE // 2 :]
    side, z = (place_ref[1], place_ref[2])
    factor = factor_ref[0]
    depth = own_x.shape[0]
    largest = None
    for x in range(PAIR):
        for k in range(LINE):
            block = (k ^ z) * PAIR + (side ^ x)
            for j in range(ranks):
                for half in range(PAIR):
                    cut = slice(half * depth, (half + 1) * depth)
                    values = hidden[x][j][k, :, cut].astype(jnp.float32)
                    scaled = jnp.clip(values * factor, -quant_range, quant_range)
                    quant_ref[half, block, j] = scaled.astype(jnp.bfloat16)
                    top = jnp.max(jnp.abs(values).reshape(-1, ROWS, depth), axis=0)
                    largest = top if largest is None else jnp.maximum(largest, top)
    step_rows = own_dt.shape[0]
    other_dt = jnp.concatenate(
        [rest[at : at + step_rows] for at in range(depth, rest.shape[0], step_rows)], axis=1
    )
    width = largest_ref.shape[1]
    top = largest[:, :width]
    for at in range(width, depth, width):
        top = jnp.maximum(top, largest[:, at : at + width])
    largest_ref[...] = top

    channels = near_refs[0].shape[1]
    tokens = bc_ref.shape[0]
    rows = tokens // CUTS
    blocks = quant_ref.shape[1] // CUTS
    extra = rows // channels * ROWS
    upper = lax.broadcasted_iota(jnp.int32, (ROWS, channels), 0) < ROWS // 2

    def steps_of(dt_ref, run):
        dt = dt_ref[run // 2]
        pieces = []
        for at in range(0, rows, channels):
            piece = dt[:, at : at + channels]
            turned = pltpu.roll(piece, ROWS // 2, 0)
            lower_run = jnp.where(upper, piece, turned)
            upper_run = jnp.where(upper, turned, piece)
            pieces.append(split_parts(jnp.where(run % 2 == 0, lower_run, upper_run), upper))
        return jnp.concatenate(pieces, axis=0).astype(jnp.bfloat16)

    def columns(run):
        return pl.ds(pl.multiple_of(run * channels, channels), channels)

    for cut in range(CUTS):
        part = slice(cut * blocks, (cut + 1) * blocks)
        near = quant_ref[side, part].reshape(rows, depth)
        far = quant_ref[1 - side, part].reshape(rows, depth)

        def both(own, other):
            return jnp.dot(near, own, preferred_element_type=jnp.float32) + jnp.dot(
                far, other, preferred_element_type=jnp.float32
            )

        at_rows = slice(cut * rows, (cut + 1) * rows)
        extra_rows = slice(tokens + cut * extra, tokens + (cut + 1) * extra)
        ours = nt_dot(own_dt[...], near)
        near_dt[...] = ours.reshape(near_dt.shape)
        all_dt[...] = (ours + nt_dot(other_dt, far)).reshape(all_dt.shape)
        bc_ref[at_rows] = both(own_bc[...], rest[:depth]).astype(jnp.bfloat16)
        for m in range(LINE // 2):
            owner = z ^ (m + LINE // 2)
            run = side * LINE + owner
            other = x_far[:, columns(owner % (LINE // 2))]
            far_refs[m][at_rows] = both(own_x[:, columns(run)], other).astype(jnp.bfloat16)
            far_refs[m][extra_rows] = steps_of(all_dt, run)
            for out_refs, way in ((near_refs, side), (sent_refs, 1 - side)):
                run = way * LINE + (z ^ m)
                product = jnp.dot(near, own_x[:, columns(run)], preferred_element_type=jnp.float32)
                out_refs[m][at_rows] = product.astype(jnp.bfloat16)
                out_refs[m][extra_rows] = steps_of(near_dt, run)


def split_parts(values, upper):
    top = values.astype(jnp.bfloat16).astype(jnp.float32)
    return jnp.where(upper, top, values - top)


def project(place, factor, hidden, w_x, weights):
    line, own, wide = hidden[0].shape
    ranks = len(hidden) // PAIR
    depth, x_wide = (weights[0].shape[0], 2 * weights[0].shape[1])
    channels, maps_wide = (x_wide // LINE, weights[1].shape[1])
    tokens = line * PAIR * ranks * own
    extra = tokens // channels * ROWS
    dt_shape = (weights[2].shape[0] // ROWS, ROWS, tokens // CUTS)
    payload = jax.ShapeDtypeStruct((tokens + extra, channels), jnp.bfloat16)
    maps = jax.ShapeDtypeStruct((tokens, maps_wide), jnp.bfloat16)
    largest = jax.ShapeDtypeStruct((ROWS, 128), jnp.float32)
    outs = [payload] * (LINE + LINE // 2) + [maps, largest]
    return pl.pallas_call(
        functools.partial(project_kernel, ranks),
        in_specs=[SMEM, SMEM] + [VMEM] * (len(hidden) + 1 + len(weights)),
        out_specs=[VMEM] * len(outs),
        scratch_shapes=[
            pltpu.VMEM((PAIR, line * PAIR, ranks, own, depth), jnp.bfloat16),
            pltpu.VMEM(dt_shape, jnp.float32),
            pltpu.VMEM(dt_shape, jnp.float32),
        ],
        out_shape=outs,
        compiler_params=pltpu.CompilerParams(vmem_limit_bytes=32 * 2**20),
        cost_estimate=pl.CostEstimate(
            flops=2 * tokens * wide * (x_wide + maps_wide),
            bytes_accessed=2 * tokens * (wide + x_wide),
            transcendentals=0,
        ),
        name="project",
    )(place, factor, *hidden, w_x, *weights)


def onward_kernel(own_ref, received_ref, out_ref):
    rows, channels = own_ref.shape
    tokens = rows * channels // (channels + ROWS)
    total = own_ref[:tokens].astype(jnp.float32) + received_ref[:tokens].astype(jnp.float32)
    out_ref[:tokens] = total.astype(jnp.bfloat16)
    upper = lax.broadcasted_iota(jnp.int32, (ROWS, channels), 0) < ROWS // 2
    extra = own_ref[tokens:].astype(jnp.float32) + received_ref[tokens:].astype(jnp.float32)
    pieces = []
    for at in range(0, rows - tokens, ROWS):
        piece = extra[at : at + ROWS]
        pieces.append(split_parts(piece + pltpu.roll(piece, ROWS // 2, 0), upper))
    out_ref[tokens:] = jnp.concatenate(pieces, axis=0).astype(jnp.bfloat16)


def onward(own, received):
    return pl.pallas_call(
        onward_kernel,
        in_specs=[VMEM, VMEM],
        out_specs=VMEM,
        out_shape=jax.ShapeDtypeStruct(own.shape, own.dtype),
        compiler_params=pltpu.CompilerParams(vmem_limit_bytes=8 * 2**20),
        cost_estimate=pl.CostEstimate(
            flops=own.size, bytes_accessed=6 * own.size, transcendentals=0
        ),
        name="onward",
    )(own, received)


def turned_rank(rank, ranks):
    turned = 0
    while ranks > 1:
        turned, rank, ranks = (2 * turned + rank % 2, rank // 2, ranks // 2)
    return turned


def scan_kernel(place_ref, scale_ref, *refs):
    x_refs, bc_refs = (refs[:-9], refs[-9:-6])
    small_ref, largest_ref, state_ref, out_ref, x_buf, bc_buf = refs[-6:]
    tokens, channels = bc_refs[0].shape
    blocks = tokens // SPAN
    heads = channels // HEAD_DIM
    rank, z = (place_ref[0], place_ref[2])
    ranks = place_ref.shape[0] - 3
    own = SPAN // ranks
    edge = ROWS
    in_scale = scale_ref[0]
    at_end = (z == 0) | (z == LINE - 1)
    x_buf[:edge] = small_ref[:edge]
    bc_buf[:edge] = small_ref[edge : 2 * edge]
    state = state_ref[...].T

    for block in range(blocks):
        for true_rank in range(ranks):
            source = block * SPAN + (true_rank ^ rank) * own
            source = pl.ds(pl.multiple_of(source, own), own)
            at = edge + block * SPAN + true_rank * own
            at = slice(at, at + own)
            total = sum(ref[source].astype(jnp.float32) for ref in x_refs) * in_scale
            x_buf[at] = total.astype(jnp.bfloat16).astype(jnp.float32)
            near, far, done = (ref[source].astype(jnp.float32) for ref in bc_refs)
            total = ((near + far) * in_scale).astype(jnp.bfloat16).astype(jnp.float32)
            bc_buf[at] = jnp.where(at_end, done, total)

    taps = 2 * edge

    def activate(buf, row, block):
        start = edge - (KERNEL - 1) + block * SPAN
        summed = small_ref[row : row + 1] * buf[start : start + SPAN]
        for k in range(1, KERNEL):
            summed = summed + small_ref[row + k : row + k + 1] * buf[start + k : start + k + SPAN]
        return (summed / (1.0 + jnp.exp(-summed))).astype(jnp.bfloat16)

    skip = small_ref[taps + 2 * KERNEL : taps + 2 * KERNEL + 1]
    gain = small_ref[taps + 2 * KERNEL + 1 : taps + 2 * KERNEL + 2]
    bias = small_ref[4 * edge :, :SPAN]
    rate = small_ref[4 * edge :, SPAN:]

    up = lax.broadcasted_iota(jnp.int32, (SPAN, SPAN), 0)
    across = lax.broadcasted_iota(jnp.int32, (SPAN, SPAN), 1)
    together = SPAN // HEAD_DIM
    insides = [
        ((across >= h * HEAD_DIM) & (across < (h + 1) * HEAD_DIM))
        .astype(jnp.float32)
        .astype(jnp.bfloat16)
        for h in range(together)
    ]
    lower = up >= across
    upper = (up <= across).astype(jnp.float32)
    lanes = across[:ROWS]

    dt = sum(ref[tokens:].astype(jnp.float32) for ref in x_refs)
    steps = []
    wide = channels // SPAN
    for block in range(blocks):
        tile = dt[block // wide * ROWS : (block // wide + 1) * ROWS]
        cut = tile[:, block % wide * SPAN : (block % wide + 1) * SPAN]
        cut = (cut + pltpu.roll(cut, ROWS // 2, 0)) * in_scale
        bit = 1
        while bit < ranks:
            shift = bit * own
            flipped = jnp.where(
                (lanes // shift) % 2 == 1,
                pltpu.roll(cut, shift, 1),
                pltpu.roll(cut, SPAN - shift, 1),
            )
            cut = jnp.where((rank & bit) != 0, flipped, cut)
            bit *= 2
        raw = cut + bias
        steps.append(jnp.maximum(raw, 0.0) + jnp.log1p(jnp.exp(-jnp.abs(raw))))
    drops = jnp.concatenate([-step * rate for step in steps], axis=0)
    cums = jnp.dot(drops, upper, precision=HIGHEST, preferred_element_type=jnp.float32)

    sums = jnp.zeros((SPAN, SPAN), jnp.float32)
    for block in range(blocks):
        x_act = activate(x_buf, taps, block)
        bc_act = activate(bc_buf, taps + KERNEL, block)
        in_map, out_map = (bc_act[:, :STATE], bc_act[:, STATE:])
        step, cum = (steps[block], cums[block * ROWS : (block + 1) * ROWS])
        last = cum[:, SPAN - 1 : SPAN]
        turned = jnp.concatenate(
            [
                cum,
                step * jnp.exp(last - cum),
                jnp.exp(cum),
                jnp.zeros((SPAN - 3 * ROWS, SPAN), jnp.float32),
            ],
            axis=0,
        ).T

        def spread(row):
            tiles = []
            for first in range(row, row + heads, together):
                tile = jnp.broadcast_to(turned[:, first : first + 1], across.shape)
                for h in range(1, together):
                    column = turned[:, first + h : first + h + 1]
                    tile = jnp.where(across >= h * HEAD_DIM, column, tile)
                tiles.append(tile)
            return jnp.concatenate(tiles, axis=1)

        inner = jnp.where(lower, nt_dot(out_map, in_map), 0.0)
        x_wide = x_act.astype(jnp.float32)
        local_tiles = []
        for first in range(0, heads, together):
            weights, spaced = ([], [])
            tile = x_act[:, first * HEAD_DIM : (first + together) * HEAD_DIM]
            for h in range(first, first + together):
                gap = jnp.where(lower, turned[:, h : h + 1] - cum[h : h + 1], 0.0)
                weights.append((inner * jnp.exp(gap) * step[h : h + 1]).astype(jnp.bfloat16))
                spaced.append(tile * insides[h - first])
            local_tiles.append(
                jnp.dot(
                    jnp.concatenate(weights, axis=1),
                    jnp.concatenate(spaced, axis=0),
                    preferred_element_type=jnp.float32,
                )
            )
        local_part = jnp.concatenate(local_tiles, axis=1)
        grown = spread(2 * ROWS)
        x_weighted = (x_wide * spread(ROWS)).astype(jnp.bfloat16)
        added = lax.dot_general(
            in_map, x_weighted, (((0,), (0,)), ((), ())), preferred_element_type=jnp.float32
        )
        high = state.astype(jnp.bfloat16)
        rest = (state - high.astype(jnp.float32)).astype(jnp.bfloat16)
        carried = jnp.dot(
            jnp.concatenate([out_map, out_map], axis=1),
            jnp.concatenate([high, rest], axis=0),
            preferred_element_type=jnp.float32,
        )
        ssm_out = local_part + grown * carried + skip * x_wide
        state = grown[SPAN - 1 : SPAN] * state + added
        gained = (ssm_out * gain).astype(jnp.bfloat16)
        for true_rank in range(ranks):
            at = (turned_rank(true_rank, ranks) * blocks + block) * own
            out_ref[at : at + own] = gained[true_rank * own : (true_rank + 1) * own]
        summed = jnp.sum(ssm_out * ssm_out, axis=1, keepdims=True)
        sums = jnp.where(across == block, summed, sums)

    whole = sums.T[:ROWS]
    top = whole.astype(jnp.bfloat16).astype(jnp.float32)
    largest = jnp.broadcast_to(jnp.max(largest_ref[...]), (ROWS, channels))
    extra = jnp.concatenate([jnp.concatenate([top, whole - top], axis=1), largest], axis=0)
    out_ref[tokens:] = extra.astype(jnp.bfloat16)


def scan(place, in_scale, sums, maps, small, largest, state):
    channels = sums[0].shape[1]
    tokens = maps[0].shape[0]

    out = jax.ShapeDtypeStruct((tokens + 2 * ROWS, channels), jnp.bfloat16)
    return pl.pallas_call(
        scan_kernel,
        in_specs=[SMEM, SMEM] + [VMEM] * (len(sums) + len(maps) + 3),
        out_specs=VMEM,
        scratch_shapes=[
            pltpu.VMEM((tokens + ROWS, channels), jnp.float32),
            pltpu.VMEM((tokens + ROWS, 2 * STATE), jnp.float32),
        ],
        out_shape=out,
        compiler_params=pltpu.CompilerParams(vmem_limit_bytes=20 * 2**20),
        cost_estimate=pl.CostEstimate(
            flops=8 * tokens * SPAN * channels,
            bytes_accessed=8 * tokens * channels,
            transcendentals=tokens * (channels + 8 * SPAN),
        ),
        name="scan",
    )(place, in_scale, *sums, *maps, small, largest, state)


def by_heads(
    hidden_in,
    prev_amax,
    w_x,
    w_bc,
    w_dt,
    conv_x,
    conv_bc,
    conv_state_x,
    conv_state_bc,
    dt_bias,
    decay_rate,
    skip,
    init_state,
    norm_gain,
    w_out,
):
    margin = KERNEL - 1
    count, here = (lax.axis_size("seq"), lax.axis_index("seq"))
    ranks, rank = (lax.axis_size("tensor"), lax.axis_index("tensor"))
    z, side = (here // PAIR, here % PAIR)
    place_of = side * LINE + z
    f32, bf16 = (jnp.float32, jnp.bfloat16)
    own, width = hidden_in.shape
    depth = w_x.shape[0]
    channels = w_x.shape[1] // count
    heads_here = w_dt.shape[1] // count
    in_scale = (prev_amax / quant_range).reshape(1)
    factor = (quant_range / prev_amax).reshape(1)
    place = jnp.stack([rank, side, z] + [rank] * ranks).astype(jnp.int32)

    def pick(array, axis, index):
        return lax.dynamic_index_in_dim(array, index, axis, keepdims=False)

    def along(value, pairs):
        moves = [(a * PAIR + x, b * PAIR + x) for a, b in pairs for x in range(PAIR)]
        return lax.ppermute(value, "seq", moves)

    def across(value):
        return lax.ppermute(value, "seq", [(s, s ^ 1) for s in range(count)])

    def of_heads(array):
        return jnp.repeat(array, HEAD_DIM)[None]

    by_channel = jnp.concatenate(
        [conv_state_x.astype(f32), conv_x, of_heads(skip), norm_gain[None]], axis=0
    )
    by_channel = lax.dynamic_slice_in_dim(by_channel, place_of * channels, channels, axis=1)
    by_map = jnp.concatenate([conv_state_bc.astype(f32), conv_bc], axis=0)
    by_map = pick(by_map, 1, side).reshape(margin + KERNEL, 2 * STATE)
    by_head = jnp.stack([dt_bias, decay_rate]).reshape(2, count, heads_here)
    by_head = jnp.tile(pick(by_head, 1, place_of).T, (ROWS // heads_here, 1))
    by_head = jnp.repeat(by_head, SPAN, axis=1)
    blank = jnp.zeros((ROWS - margin, channels), f32)
    small = jnp.concatenate(
        [
            blank,
            by_channel[:margin],
            blank,
            by_map[:margin],
            by_channel[margin : margin + KERNEL],
            by_map[margin:],
            by_channel[margin + KERNEL :],
            jnp.zeros((2 * ROWS - 2 * KERNEL - 2, channels), f32),
            by_head,
        ],
        axis=0,
    )

    start_state = lax.dynamic_slice_in_dim(
        init_state, place_of * heads_here, heads_here, axis=0
    ).reshape(channels, STATE)

    tie = lax.optimization_barrier
    half_run = LINE // 2 * channels
    opposite = (z // (LINE // 2)) ^ 1
    at = ((1 - side) * 2 + opposite) * half_run
    x_sent = lax.dynamic_slice_in_dim(w_x, at, half_run, axis=1)
    x_sent, hidden_in = tie((x_sent, hidden_in))
    x_far = across(x_sent)
    dt_rows = w_dt.T
    dt_cut = [dt_rows[:, at : at + 2 * STATE] for at in range(0, depth, 2 * STATE)]
    maps_sent = pick(w_bc, 1, 1 - side).reshape(depth, 2 * STATE)
    x_far, rest_sent = tie((x_far, jnp.concatenate([maps_sent, *dt_cut], axis=0)))
    rest_other = across(rest_sent)
    bc_own = pick(w_bc, 1, side).reshape(depth, 2 * STATE)

    def line_columns(m):
        return lax.dynamic_slice_in_dim(hidden_in, (z ^ m) * PAIR * depth, PAIR * depth, axis=1)

    arrived = [line_columns(0)]
    for m in range(1, LINE):
        arrived.append(along(line_columns(m), [(s, s ^ m) for s in range(LINE)]))
    stacked = jnp.stack(arrived)
    beyond_pair = across(stacked)
    beyond_pair, small, start_state, bc_own, dt_rows = tie(
        (beyond_pair, small, start_state, bc_own, dt_rows)
    )
    rows = []
    for mine in (stacked, beyond_pair):
        ours = [mine]
        for j in range(1, ranks):
            bit = j & -j
            pairs = [(t, t ^ bit) for t in range(ranks)]
            ours.append(lax.ppermute(ours[j - bit], "tensor", pairs))
        rows.extend(ours)

    start, end = (0, LINE - 1)
    at_end = (z == start) | (z == end)
    next_start, next_end = (1, LINE - 2)
    inward = [(start, next_start), (end, next_end)]
    outward = [(next_start, start), (next_end, end)]
    middle = [(next_start, next_end), (next_end, next_start)]
    over_middle = [(next_start, end), (next_end, start)]
    beside_pairs = [(s, s ^ 1) for s in range(LINE)]
    weights = (x_far, bc_own, dt_rows, rest_other)
    over, far, mine, near, mine_sent, near_sent, maps, largest = project(
        place, factor, rows, w_x, weights
    )

    map_hop = along(maps, inward)
    hop_far = along(far, inward)
    hop_over = along(over, inward)
    near = onward(near, across(near_sent))
    got_mine = across(mine_sent)
    near_out = along(near, outward)
    near_in = along(near, inward)
    map_sum = (maps.astype(f32) + map_hop.astype(f32)).astype(bf16)
    map_far = along(map_sum, middle)
    map_done = ((map_sum.astype(f32) + map_far.astype(f32)) * in_scale).astype(bf16)
    sent_end = onward(over, hop_far)
    got_end = along(sent_end, over_middle)
    hop_over, near_out, unused = tie((hop_over, near_out, sent_end))
    got_next = along(onward(far, hop_over), middle)
    map_done, got_end, got_mine = tie((map_done, got_end, got_mine))
    map_done = along(map_done, outward)
    gained = scan(
        place,
        in_scale,
        [mine, got_mine, near_out, near_in, got_end, got_next],
        [map_sum, map_far, map_done],
        small,
        largest,
        start_state,
    )

    tokens = gained.shape[0] - 2 * ROWS
    beside = along(gained, beside_pairs)
    facing = along(gained, middle)
    second = jnp.where(at_end, along(facing, outward), facing)
    beyond = along(beside, middle)
    third = jnp.where(at_end, along(beyond, outward), beyond)
    far_own = across(gained)
    far_beside = across(beside)
    second, far_own = tie((second, far_own))
    far_second = across(second)
    third, far_beside = tie((third, far_beside))
    far_third = across(third)
    two, three = (jnp.where(at_end, 2, 3), jnp.where(at_end, 3, 2))

    def rows_for(x, m):
        at = ((side ^ x) * LINE + (z ^ m)) * channels
        return lax.dynamic_slice_in_dim(w_out, at, channels, axis=0)

    total = None
    tails = [far_third[tokens:]]
    for x, m, piece in (
        (0, 0, gained),
        (1, 0, far_own),
        (0, 1, beside),
        (1, 1, far_beside),
        (0, two, second),
        (1, two, far_second),
        (0, three, third),
    ):
        product = jnp.dot(piece, rows_for(x, m), preferred_element_type=f32)
        total = product if total is None else total + product
        tails.append(piece[tokens:])
    total, far_third = tie((total, far_third))
    last_rows = rows_for(1, three)
    tails = [tail.astype(f32) for tail in tails]
    squares = sum(tail[:ROWS, :SPAN] + tail[:ROWS, SPAN:] for tail in tails)
    top = functools.reduce(jnp.maximum, [tail[ROWS:, :SPAN] for tail in tails])

    def run_of(array, index, run):
        return lax.dynamic_slice_in_dim(array, index * run, run, axis=0)

    def first_sum(index):
        block, so_far = (run_of(far_third, index, run), run_of(total, index, run))
        return so_far + jnp.dot(block, last_rows, preferred_element_type=f32)

    run = tokens // 2
    keeps = rank % 2
    pairs = [(t, t ^ 1) for t in range(ranks)]
    received = lax.ppermute(first_sum(1 - keeps).astype(bf16), "tensor", pairs)
    kept = first_sum(keeps)
    squares = squares + lax.ppermute(squares, "tensor", pairs)
    bit = 2
    while bit < ranks:
        run //= 2
        keeps = (rank // bit) % 2
        pairs = [(t, t ^ bit) for t in range(ranks)]
        sent = run_of(kept, 1 - keeps, run) + run_of(received, 1 - keeps, run).astype(f32)
        kept = run_of(kept, keeps, run) + run_of(received, keeps, run).astype(f32)
        received = lax.ppermute(sent.astype(bf16), "tensor", pairs)
        squares = squares + lax.ppermute(squares, "tensor", pairs)
        bit *= 2
    mean_sq = squares.reshape(count, ranks, own) / (HEADS * HEAD_DIM)
    factors = lax.rsqrt(pick(mean_sq, 1, rank) + epsilon)
    final = (kept + received.astype(f32)).reshape(count, own, -1) * factors[:, :, None]
    final = lax.all_to_all(final.astype(bf16), "seq", split_axis=0, concat_axis=0, tiled=True)
    layer_out = final.transpose(1, 0, 2).reshape(own, count * final.shape[2])
    return (layer_out, jnp.max(top))


def solution(mesh):
    return jax.shard_map(
        by_heads if splits(mesh) else by_tokens,
        mesh=mesh,
        in_specs=(
            P(("seq", "tensor"), None),
            P(),
            P("seq", "tensor"),
            P("seq", "tensor", None, None),
            P("seq", "tensor"),
            P(None, "tensor"),
            P(None, "tensor", None, None),
            P(None, "tensor"),
            P(None, "tensor", None, None),
            P("tensor"),
            P("tensor"),
            P("tensor"),
            P("tensor", None, None),
            P("tensor"),
            P("tensor", "seq"),
        ),
        out_specs=(P(("seq", "tensor"), None), P()),
        check_vma=False,
    )
```

```python
import functools

import jax
import jax.numpy as jnp
from jax import lax
from jax.experimental import pallas as pl
from jax.experimental.pallas import tpu as pltpu
from jax.sharding import PartitionSpec as P

HEADS = 128
HEAD_DIM = 64
STATE = 128
GROUPS = 8
KERNEL = 4
SPAN = 128


epsilon = 1e-05
quant_range = 448.0


def from_behind(value, axis, steps):
    count = lax.axis_size(axis)
    first, last = (max(0, -steps), min(count, count - steps))
    return lax.ppermute(value, axis, [(source, source + steps) for source in range(first, last)])


def carried_in(shard, axis, combine, identity):
    count, here = (lax.axis_size(axis), lax.axis_index(axis))
    everything = jax.tree.map(
        lambda part, kind: lax.all_gather(part.astype(kind), axis),
        shard,
        (jnp.bfloat16, jnp.bfloat16),
    )
    start = jax.tree.map(
        lambda part, zero: jnp.broadcast_to(jnp.asarray(zero, part.dtype), part.shape),
        shard,
        identity,
    )

    def turn(k, before):
        reached = k < here
        new = combine(
            before, jax.tree.map(lambda part, own: part[k].astype(own.dtype), everything, shard)
        )
        return jax.tree.map(lambda a, b: jnp.where(reached, a, b), new, before)

    return lax.fori_loop(0, count, turn, start)


def depthwise(before, projected, conv_taps, length):
    extended = jnp.concatenate([before, projected], axis=0)
    summed = conv_taps[0] * extended[0:length]
    for offset in range(1, KERNEL):
        summed = summed + conv_taps[offset] * extended[offset : offset + length]
    return jax.nn.silu(summed).astype(jnp.bfloat16)


def combine(earlier, later):
    return (earlier[0] * later[0], later[0][:, None, None] * earlier[1] + later[1])


def by_tokens(
    hidden_in,
    prev_amax,
    w_x,
    w_bc,
    w_dt,
    conv_x,
    conv_bc,
    conv_state_x,
    conv_state_bc,
    dt_bias,
    decay_rate,
    skip,
    init_state,
    norm_gain,
    w_out,
):
    margin = KERNEL - 1
    gathered = lax.all_gather(hidden_in, "tensor", axis=0, tiled=True)
    abs_max = lax.pmax(jnp.max(jnp.abs(gathered.astype(jnp.float32))), "seq")
    in_scale = prev_amax / quant_range
    leading = lax.axis_index("seq") == 0
    row_count = gathered.shape[0]
    bc_width = w_bc.shape[1] * w_bc.shape[2] * w_bc.shape[3]
    bc_rows = jnp.reshape(w_bc, (w_bc.shape[0], bc_width))
    scaled = gathered.astype(jnp.float32) * (quant_range / prev_amax)
    quant = jnp.clip(scaled, -quant_range, quant_range).astype(jnp.bfloat16)
    pieces = (
        lax.all_gather(w_x, "seq", axis=0, tiled=True),
        lax.all_gather(bc_rows, "seq", axis=0, tiled=True),
        lax.all_gather(w_dt, "seq", axis=0, tiled=True),
    )
    x_proj, bc_proj, dt_proj = tuple(
        (
            jnp.dot(quant, weight_piece, preferred_element_type=jnp.float32)
            for weight_piece in pieces
        )
    )
    x_whole = (x_proj * in_scale).astype(jnp.bfloat16)
    bc_whole = (bc_proj * in_scale).astype(jnp.bfloat16)
    dt_raw = dt_proj * in_scale
    state_bc = jnp.reshape(conv_state_bc, (margin, bc_width))
    received = from_behind(
        (x_whole[row_count - margin :], bc_whole[row_count - margin :]), "seq", 1
    )
    x_edge = jnp.where(leading, conv_state_x, received[0])
    bc_edge = jnp.where(leading, state_bc, received[1])
    x_act = depthwise(x_edge, x_whole, conv_x, row_count)
    bc_act = depthwise(bc_edge, bc_whole, jnp.reshape(conv_bc, (KERNEL, bc_width)), row_count)
    step_size = jax.nn.softplus(dt_raw + dt_bias)
    heads_here = step_size.shape[1]
    groups_here = w_bc.shape[1]
    per_group = HEADS // GROUPS
    blocks = row_count // SPAN
    x_blocks = x_act.reshape(blocks, SPAN, heads_here, HEAD_DIM)
    bc_blocks = bc_act.reshape(blocks, SPAN, groups_here, 2, STATE)
    in_map = bc_blocks[:, :, :, 0]
    out_map = bc_blocks[:, :, :, 1]
    step_blocks = step_size.reshape(blocks, SPAN, heads_here)
    cum_blocks = jnp.cumsum(-step_blocks * decay_rate, axis=1)
    index_row = jnp.arange(SPAN, dtype=jnp.int32)
    lower_mask = index_row[:, None] >= index_row[None, :]
    intersection = jnp.einsum(
        "ctgn,cugn->cgtu", out_map, in_map, preferred_element_type=jnp.float32
    )
    intersection = jnp.repeat(intersection, per_group, axis=1)
    cum_heads = jnp.transpose(cum_blocks, (0, 2, 1))
    log_gap = cum_heads[:, :, :, None] - cum_heads[:, :, None, :]
    decay = jnp.exp(jnp.where(lower_mask[None, None], log_gap, -1e30))
    step_heads = jnp.transpose(step_blocks, (0, 2, 1))
    weights = (intersection * decay * step_heads[:, :, None, :]).astype(jnp.bfloat16)
    local_part = jnp.einsum(
        "chtu,cuhp->cthp", weights, x_blocks, preferred_element_type=jnp.float32
    )
    last_cum = cum_blocks[:, SPAN - 1, :]
    x_weighted = (
        x_blocks.astype(jnp.float32)
        * (step_blocks * jnp.exp(last_cum[:, None, :] - cum_blocks))[:, :, :, None]
    ).astype(jnp.bfloat16)
    in_heads = jnp.repeat(in_map, per_group, axis=2)
    added = jnp.einsum("cuhp,cuhn->chpn", x_weighted, in_heads, preferred_element_type=jnp.float32)

    def carry_on(carried, element):
        block_decay, block_added = element
        return (block_decay[:, None, None] * carried + block_added, carried)

    empty_state = jnp.zeros((heads_here, HEAD_DIM, STATE), jnp.float32)
    device_state, entering = lax.scan(carry_on, empty_state, (jnp.exp(last_cum), added))
    device_decay = jnp.exp(jnp.sum(last_cum, axis=0))
    seeded = device_state + jnp.where(leading, device_decay[:, None, None] * init_state, 0.0)
    identity = (jnp.ones_like(device_decay), jnp.zeros_like(device_state))
    scanned = carried_in((device_decay, seeded), "seq", combine, identity)
    incoming = jnp.where(leading, init_state, scanned[1])
    prefix = jnp.exp(jnp.cumsum(last_cum, axis=0) - last_cum)
    states_in = entering + prefix[:, :, None, None] * incoming[None]
    out_heads = jnp.repeat(out_map, per_group, axis=2).astype(jnp.float32)
    carried_part = (
        jnp.einsum("cthn,chpn->cthp", out_heads, states_in, precision=lax.Precision.HIGHEST)
        * jnp.exp(cum_blocks)[:, :, :, None]
    )
    ssm_out = local_part + carried_part + skip[None, None, :, None] * x_blocks.astype(jnp.float32)
    ssm_out = ssm_out.reshape(row_count, heads_here * HEAD_DIM)
    squares = lax.psum(jnp.sum(ssm_out * ssm_out, axis=1), "tensor")
    mean_sq = squares / (HEADS * HEAD_DIM)
    normed = (ssm_out * lax.rsqrt(mean_sq + epsilon)[:, None] * norm_gain).astype(jnp.bfloat16)
    partial_out = jnp.dot(
        normed, lax.all_gather(w_out, "seq", axis=1, tiled=True), preferred_element_type=jnp.float32
    )
    layer_out = lax.psum_scatter(
        partial_out.astype(jnp.bfloat16), "tensor", scatter_dimension=0, tiled=True
    )
    return (layer_out, abs_max)


PAIR = 2
LINE = 4
ROWS = 8
CUTS = 2
SMEM = pl.BlockSpec(memory_space=pltpu.SMEM)
VMEM = pl.BlockSpec(memory_space=pltpu.VMEM)
HIGHEST = lax.Precision.HIGHEST


def splits(mesh):
    count, ranks = (mesh.shape["seq"], mesh.shape["tensor"])
    heads_all, groups_here = (HEADS // ranks, GROUPS // ranks)
    if count != PAIR * LINE or groups_here != PAIR or ranks & (ranks - 1):
        return False
    heads_here = heads_all // count
    return 2 * heads_here == ROWS and heads_here * HEAD_DIM == 2 * SPAN


def nt_dot(a, b, **kw):
    return lax.dot_general(
        a, b, (((1,), (1,)), ((), ())), preferred_element_type=jnp.float32, **kw
    )


def project_kernel(ranks, place_ref, factor_ref, *refs):
    hidden = [refs[x * ranks : (x + 1) * ranks] for x in range(PAIR)]
    refs = refs[PAIR * ranks :]
    own_x, x_far, own_bc, own_dt, rest = refs[:5]
    far_refs, near_refs, sent_refs = (
        refs[5 + at : 5 + at + LINE // 2] for at in range(0, 3 * LINE // 2, LINE // 2)
    )
    bc_ref, largest_ref, quant_ref, near_dt, all_dt = refs[5 + 3 * LINE // 2 :]
    side, z = (place_ref[1], place_ref[2])
    factor = factor_ref[0]
    depth = own_x.shape[0]
    largest = None
    for x in range(PAIR):
        for k in range(LINE):
            block = (k ^ z) * PAIR + (side ^ x)
            for j in range(ranks):
                for half in range(PAIR):
                    cut = slice(half * depth, (half + 1) * depth)
                    values = hidden[x][j][k, :, cut].astype(jnp.float32)
                    scaled = jnp.clip(values * factor, -quant_range, quant_range)
                    quant_ref[half, block, j] = scaled.astype(jnp.bfloat16)
                    top = jnp.max(jnp.abs(values).reshape(-1, ROWS, depth), axis=0)
                    largest = top if largest is None else jnp.maximum(largest, top)
    step_rows = own_dt.shape[0]
    other_dt = jnp.concatenate(
        [rest[at : at + step_rows] for at in range(depth, rest.shape[0], step_rows)], axis=1
    )
    width = largest_ref.shape[1]
    top = largest[:, :width]
    for at in range(width, depth, width):
        top = jnp.maximum(top, largest[:, at : at + width])
    largest_ref[...] = top

    channels = near_refs[0].shape[1]
    tokens = bc_ref.shape[0]
    rows = tokens // CUTS
    blocks = quant_ref.shape[1] // CUTS
    extra = rows // channels * ROWS
    upper = lax.broadcasted_iota(jnp.int32, (ROWS, channels), 0) < ROWS // 2

    def steps_of(dt_ref, run):
        dt = dt_ref[run // 2]
        pieces = []
        for at in range(0, rows, channels):
            piece = dt[:, at : at + channels]
            turned = pltpu.roll(piece, ROWS // 2, 0)
            lower_run = jnp.where(upper, piece, turned)
            upper_run = jnp.where(upper, turned, piece)
            pieces.append(split_parts(jnp.where(run % 2 == 0, lower_run, upper_run), upper))
        return jnp.concatenate(pieces, axis=0).astype(jnp.bfloat16)

    def columns(run):
        return pl.ds(pl.multiple_of(run * channels, channels), channels)

    for cut in range(CUTS):
        part = slice(cut * blocks, (cut + 1) * blocks)
        near = quant_ref[side, part].reshape(rows, depth)
        far = quant_ref[1 - side, part].reshape(rows, depth)

        def both(own, other):
            return jnp.dot(near, own, preferred_element_type=jnp.float32) + jnp.dot(
                far, other, preferred_element_type=jnp.float32
            )

        at_rows = slice(cut * rows, (cut + 1) * rows)
        extra_rows = slice(tokens + cut * extra, tokens + (cut + 1) * extra)
        ours = nt_dot(own_dt[...], near)
        near_dt[...] = ours.reshape(near_dt.shape)
        all_dt[...] = (ours + nt_dot(other_dt, far)).reshape(all_dt.shape)
        bc_ref[at_rows] = both(own_bc[...], rest[:depth]).astype(jnp.bfloat16)
        for m in range(LINE // 2):
            owner = z ^ (m + LINE // 2)
            run = side * LINE + owner
            other = x_far[:, columns(owner % (LINE // 2))]
            far_refs[m][at_rows] = both(own_x[:, columns(run)], other).astype(jnp.bfloat16)
            far_refs[m][extra_rows] = steps_of(all_dt, run)
            for out_refs, way in ((near_refs, side), (sent_refs, 1 - side)):
                run = way * LINE + (z ^ m)
                product = jnp.dot(near, own_x[:, columns(run)], preferred_element_type=jnp.float32)
                out_refs[m][at_rows] = product.astype(jnp.bfloat16)
                out_refs[m][extra_rows] = steps_of(near_dt, run)


def split_parts(values, upper):
    top = values.astype(jnp.bfloat16).astype(jnp.float32)
    return jnp.where(upper, top, values - top)


def project(place, factor, hidden, w_x, weights):
    line, own, wide = hidden[0].shape
    ranks = len(hidden) // PAIR
    depth, x_wide = (weights[0].shape[0], 2 * weights[0].shape[1])
    channels, maps_wide = (x_wide // LINE, weights[1].shape[1])
    tokens = line * PAIR * ranks * own
    extra = tokens // channels * ROWS
    dt_shape = (weights[2].shape[0] // ROWS, ROWS, tokens // CUTS)
    payload = jax.ShapeDtypeStruct((tokens + extra, channels), jnp.bfloat16)
    maps = jax.ShapeDtypeStruct((tokens, maps_wide), jnp.bfloat16)
    largest = jax.ShapeDtypeStruct((ROWS, 128), jnp.float32)
    outs = [payload] * (LINE + LINE // 2) + [maps, largest]
    return pl.pallas_call(
        functools.partial(project_kernel, ranks),
        in_specs=[SMEM, SMEM] + [VMEM] * (len(hidden) + 1 + len(weights)),
        out_specs=[VMEM] * len(outs),
        scratch_shapes=[
            pltpu.VMEM((PAIR, line * PAIR, ranks, own, depth), jnp.bfloat16),
            pltpu.VMEM(dt_shape, jnp.float32),
            pltpu.VMEM(dt_shape, jnp.float32),
        ],
        out_shape=outs,
        compiler_params=pltpu.CompilerParams(vmem_limit_bytes=32 * 2**20),
        cost_estimate=pl.CostEstimate(
            flops=2 * tokens * wide * (x_wide + maps_wide),
            bytes_accessed=2 * tokens * (wide + x_wide),
            transcendentals=0,
        ),
        name="project",
    )(place, factor, *hidden, w_x, *weights)


def onward_kernel(*refs):
    share_refs, out_ref = (refs[:-1], refs[-1])
    rows, channels = out_ref.shape
    tokens = rows * channels // (channels + ROWS)
    total = sum(ref[:tokens].astype(jnp.float32) for ref in share_refs)
    out_ref[:tokens] = total.astype(jnp.bfloat16)
    upper = lax.broadcasted_iota(jnp.int32, (ROWS, channels), 0) < ROWS // 2
    extra = sum(ref[tokens:].astype(jnp.float32) for ref in share_refs)
    pieces = []
    for at in range(0, rows - tokens, ROWS):
        piece = extra[at : at + ROWS]
        pieces.append(split_parts(piece + pltpu.roll(piece, ROWS // 2, 0), upper))
    out_ref[tokens:] = jnp.concatenate(pieces, axis=0).astype(jnp.bfloat16)


def onward(*shares):
    own = shares[0]
    return pl.pallas_call(
        onward_kernel,
        in_specs=[VMEM] * len(shares),
        out_specs=VMEM,
        out_shape=jax.ShapeDtypeStruct(own.shape, own.dtype),
        compiler_params=pltpu.CompilerParams(vmem_limit_bytes=8 * 2**20),
        cost_estimate=pl.CostEstimate(
            flops=len(shares) * own.size,
            bytes_accessed=2 * (len(shares) + 1) * own.size,
            transcendentals=0,
        ),
        name="onward",
    )(*shares)


def turned_rank(rank, ranks):
    turned = 0
    while ranks > 1:
        turned, rank, ranks = (2 * turned + rank % 2, rank // 2, ranks // 2)
    return turned


def scan_kernel(place_ref, scale_ref, *refs):
    x_refs, bc_refs = (refs[:-9], refs[-9:-6])
    small_ref, largest_ref, state_ref, out_ref, x_buf, bc_buf = refs[-6:]
    tokens, channels = bc_refs[0].shape
    blocks = tokens // SPAN
    heads = channels // HEAD_DIM
    rank, z = (place_ref[0], place_ref[2])
    ranks = place_ref.shape[0] - 3
    own = SPAN // ranks
    edge = ROWS
    in_scale = scale_ref[0]
    at_end = (z == 0) | (z == LINE - 1)
    x_buf[:edge] = small_ref[:edge]
    bc_buf[:edge] = small_ref[edge : 2 * edge]
    state = state_ref[...].T

    for block in range(blocks):
        for true_rank in range(ranks):
            source = block * SPAN + (true_rank ^ rank) * own
            source = pl.ds(pl.multiple_of(source, own), own)
            at = edge + block * SPAN + true_rank * own
            at = slice(at, at + own)
            total = sum(ref[source].astype(jnp.float32) for ref in x_refs) * in_scale
            x_buf[at] = total.astype(jnp.bfloat16).astype(jnp.float32)
            near, far, done = (ref[source].astype(jnp.float32) for ref in bc_refs)
            total = ((near + far) * in_scale).astype(jnp.bfloat16).astype(jnp.float32)
            bc_buf[at] = jnp.where(at_end, done, total)

    taps = 2 * edge

    def activate(buf, row, block):
        start = edge - (KERNEL - 1) + block * SPAN
        summed = small_ref[row : row + 1] * buf[start : start + SPAN]
        for k in range(1, KERNEL):
            summed = summed + small_ref[row + k : row + k + 1] * buf[start + k : start + k + SPAN]
        return (summed / (1.0 + jnp.exp(-summed))).astype(jnp.bfloat16)

    skip = small_ref[taps + 2 * KERNEL : taps + 2 * KERNEL + 1]
    gain = small_ref[taps + 2 * KERNEL + 1 : taps + 2 * KERNEL + 2]
    bias = small_ref[4 * edge :, :SPAN]
    rate = small_ref[4 * edge :, SPAN:]

    up = lax.broadcasted_iota(jnp.int32, (SPAN, SPAN), 0)
    across = lax.broadcasted_iota(jnp.int32, (SPAN, SPAN), 1)
    together = SPAN // HEAD_DIM
    insides = [
        ((across >= h * HEAD_DIM) & (across < (h + 1) * HEAD_DIM))
        .astype(jnp.float32)
        .astype(jnp.bfloat16)
        for h in range(together)
    ]
    lower = up >= across
    upper = (up <= across).astype(jnp.float32)
    lanes = across[:ROWS]

    dt = sum(ref[tokens:].astype(jnp.float32) for ref in x_refs)
    steps = []
    wide = channels // SPAN
    for block in range(blocks):
        tile = dt[block // wide * ROWS : (block // wide + 1) * ROWS]
        cut = tile[:, block % wide * SPAN : (block % wide + 1) * SPAN]
        cut = (cut + pltpu.roll(cut, ROWS // 2, 0)) * in_scale
        bit = 1
        while bit < ranks:
            shift = bit * own
            flipped = jnp.where(
                (lanes // shift) % 2 == 1,
                pltpu.roll(cut, shift, 1),
                pltpu.roll(cut, SPAN - shift, 1),
            )
            cut = jnp.where((rank & bit) != 0, flipped, cut)
            bit *= 2
        raw = cut + bias
        steps.append(jnp.maximum(raw, 0.0) + jnp.log1p(jnp.exp(-jnp.abs(raw))))
    drops = jnp.concatenate([-step * rate for step in steps], axis=0)
    cums = jnp.dot(drops, upper, precision=HIGHEST, preferred_element_type=jnp.float32)

    sums = jnp.zeros((SPAN, SPAN), jnp.float32)
    for block in range(blocks):
        x_act = activate(x_buf, taps, block)
        bc_act = activate(bc_buf, taps + KERNEL, block)
        in_map, out_map = (bc_act[:, :STATE], bc_act[:, STATE:])
        step, cum = (steps[block], cums[block * ROWS : (block + 1) * ROWS])
        last = cum[:, SPAN - 1 : SPAN]
        turned = jnp.concatenate(
            [
                cum,
                step * jnp.exp(last - cum),
                jnp.exp(cum),
                jnp.zeros((SPAN - 3 * ROWS, SPAN), jnp.float32),
            ],
            axis=0,
        ).T

        def spread(row):
            tiles = []
            for first in range(row, row + heads, together):
                tile = jnp.broadcast_to(turned[:, first : first + 1], across.shape)
                for h in range(1, together):
                    column = turned[:, first + h : first + h + 1]
                    tile = jnp.where(across >= h * HEAD_DIM, column, tile)
                tiles.append(tile)
            return jnp.concatenate(tiles, axis=1)

        inner = jnp.where(lower, nt_dot(out_map, in_map), 0.0)
        x_wide = x_act.astype(jnp.float32)
        local_tiles = []
        for first in range(0, heads, together):
            weights, spaced = ([], [])
            tile = x_act[:, first * HEAD_DIM : (first + together) * HEAD_DIM]
            for h in range(first, first + together):
                gap = jnp.where(lower, turned[:, h : h + 1] - cum[h : h + 1], 0.0)
                weights.append((inner * jnp.exp(gap) * step[h : h + 1]).astype(jnp.bfloat16))
                spaced.append(tile * insides[h - first])
            local_tiles.append(
                jnp.dot(
                    jnp.concatenate(weights, axis=1),
                    jnp.concatenate(spaced, axis=0),
                    preferred_element_type=jnp.float32,
                )
            )
        local_part = jnp.concatenate(local_tiles, axis=1)
        grown = spread(2 * ROWS)
        x_weighted = (x_wide * spread(ROWS)).astype(jnp.bfloat16)
        added = lax.dot_general(
            in_map, x_weighted, (((0,), (0,)), ((), ())), preferred_element_type=jnp.float32
        )
        high = state.astype(jnp.bfloat16)
        rest = (state - high.astype(jnp.float32)).astype(jnp.bfloat16)
        carried = jnp.dot(
            jnp.concatenate([out_map, out_map], axis=1),
            jnp.concatenate([high, rest], axis=0),
            preferred_element_type=jnp.float32,
        )
        ssm_out = local_part + grown * carried + skip * x_wide
        state = grown[SPAN - 1 : SPAN] * state + added
        gained = (ssm_out * gain).astype(jnp.bfloat16)
        for true_rank in range(ranks):
            at = (turned_rank(true_rank, ranks) * blocks + block) * own
            out_ref[at : at + own] = gained[true_rank * own : (true_rank + 1) * own]
        summed = jnp.sum(ssm_out * ssm_out, axis=1, keepdims=True)
        sums = jnp.where(across == block, summed, sums)

    whole = sums.T[:ROWS]
    top = whole.astype(jnp.bfloat16).astype(jnp.float32)
    largest = jnp.broadcast_to(jnp.max(largest_ref[...]), (ROWS, channels))
    extra = jnp.concatenate([jnp.concatenate([top, whole - top], axis=1), largest], axis=0)
    out_ref[tokens:] = extra.astype(jnp.bfloat16)


def scan(place, in_scale, sums, maps, small, largest, state):
    channels = sums[0].shape[1]
    tokens = maps[0].shape[0]

    out = jax.ShapeDtypeStruct((tokens + 2 * ROWS, channels), jnp.bfloat16)
    return pl.pallas_call(
        scan_kernel,
        in_specs=[SMEM, SMEM] + [VMEM] * (len(sums) + len(maps) + 3),
        out_specs=VMEM,
        scratch_shapes=[
            pltpu.VMEM((tokens + ROWS, channels), jnp.float32),
            pltpu.VMEM((tokens + ROWS, 2 * STATE), jnp.float32),
        ],
        out_shape=out,
        compiler_params=pltpu.CompilerParams(vmem_limit_bytes=20 * 2**20),
        cost_estimate=pl.CostEstimate(
            flops=8 * tokens * SPAN * channels,
            bytes_accessed=8 * tokens * channels,
            transcendentals=tokens * (channels + 8 * SPAN),
        ),
        name="scan",
    )(place, in_scale, *sums, *maps, small, largest, state)


def by_heads(
    hidden_in,
    prev_amax,
    w_x,
    w_bc,
    w_dt,
    conv_x,
    conv_bc,
    conv_state_x,
    conv_state_bc,
    dt_bias,
    decay_rate,
    skip,
    init_state,
    norm_gain,
    w_out,
):
    margin = KERNEL - 1
    count, here = (lax.axis_size("seq"), lax.axis_index("seq"))
    ranks, rank = (lax.axis_size("tensor"), lax.axis_index("tensor"))
    z, side = (here // PAIR, here % PAIR)
    place_of = side * LINE + z
    f32, bf16 = (jnp.float32, jnp.bfloat16)
    own, width = hidden_in.shape
    depth = w_x.shape[0]
    channels = w_x.shape[1] // count
    heads_here = w_dt.shape[1] // count
    in_scale = (prev_amax / quant_range).reshape(1)
    factor = (quant_range / prev_amax).reshape(1)
    place = jnp.stack([rank, side, z] + [rank] * ranks).astype(jnp.int32)

    def pick(array, axis, index):
        return lax.dynamic_index_in_dim(array, index, axis, keepdims=False)

    def along(value, pairs):
        moves = [(a * PAIR + x, b * PAIR + x) for a, b in pairs for x in range(PAIR)]
        return lax.ppermute(value, "seq", moves)

    def across(value):
        return lax.ppermute(value, "seq", [(s, s ^ 1) for s in range(count)])

    def of_heads(array):
        return jnp.repeat(array, HEAD_DIM)[None]

    by_channel = jnp.concatenate(
        [conv_state_x.astype(f32), conv_x, of_heads(skip), norm_gain[None]], axis=0
    )
    by_channel = lax.dynamic_slice_in_dim(by_channel, place_of * channels, channels, axis=1)
    by_map = jnp.concatenate([conv_state_bc.astype(f32), conv_bc], axis=0)
    by_map = pick(by_map, 1, side).reshape(margin + KERNEL, 2 * STATE)
    by_head = jnp.stack([dt_bias, decay_rate]).reshape(2, count, heads_here)
    by_head = jnp.tile(pick(by_head, 1, place_of).T, (ROWS // heads_here, 1))
    by_head = jnp.repeat(by_head, SPAN, axis=1)
    blank = jnp.zeros((ROWS - margin, channels), f32)
    small = jnp.concatenate(
        [
            blank,
            by_channel[:margin],
            blank,
            by_map[:margin],
            by_channel[margin : margin + KERNEL],
            by_map[margin:],
            by_channel[margin + KERNEL :],
            jnp.zeros((2 * ROWS - 2 * KERNEL - 2, channels), f32),
            by_head,
        ],
        axis=0,
    )

    start_state = lax.dynamic_slice_in_dim(
        init_state, place_of * heads_here, heads_here, axis=0
    ).reshape(channels, STATE)

    tie = lax.optimization_barrier
    half_run = LINE // 2 * channels
    opposite = (z // (LINE // 2)) ^ 1
    at = ((1 - side) * 2 + opposite) * half_run
    x_sent = lax.dynamic_slice_in_dim(w_x, at, half_run, axis=1)
    x_sent, hidden_in = tie((x_sent, hidden_in))
    x_far = across(x_sent)
    dt_rows = w_dt.T
    dt_cut = [dt_rows[:, at : at + 2 * STATE] for at in range(0, depth, 2 * STATE)]
    maps_sent = pick(w_bc, 1, 1 - side).reshape(depth, 2 * STATE)
    x_far, rest_sent = tie((x_far, jnp.concatenate([maps_sent, *dt_cut], axis=0)))
    rest_other = across(rest_sent)
    bc_own = pick(w_bc, 1, side).reshape(depth, 2 * STATE)

    def line_columns(m):
        return lax.dynamic_slice_in_dim(hidden_in, (z ^ m) * PAIR * depth, PAIR * depth, axis=1)

    arrived = [line_columns(0)]
    for m in range(1, LINE):
        arrived.append(along(line_columns(m), [(s, s ^ m) for s in range(LINE)]))
    stacked = jnp.stack(arrived)
    beyond_pair = across(stacked)
    beyond_pair, small, start_state, bc_own, dt_rows = tie(
        (beyond_pair, small, start_state, bc_own, dt_rows)
    )
    rows = []
    for mine in (stacked, beyond_pair):
        ours = [mine]
        for j in range(1, ranks):
            bit = j & -j
            pairs = [(t, t ^ bit) for t in range(ranks)]
            ours.append(lax.ppermute(ours[j - bit], "tensor", pairs))
        rows.extend(ours)

    start, end = (0, LINE - 1)
    at_end = (z == start) | (z == end)
    next_start, next_end = (1, LINE - 2)
    inward = [(start, next_start), (end, next_end)]
    outward = [(next_start, start), (next_end, end)]
    middle = [(next_start, next_end), (next_end, next_start)]
    over_middle = [(next_start, end), (next_end, start)]
    beside_pairs = [(s, s ^ 1) for s in range(LINE)]
    weights = (x_far, bc_own, dt_rows, rest_other)
    over, far, mine, near, mine_sent, near_sent, maps, largest = project(
        place, factor, rows, w_x, weights
    )

    map_hop = along(maps, inward)
    hop_far = along(far, inward)
    hop_over = along(over, inward)
    near = onward(near, across(near_sent))
    got_mine = across(mine_sent)
    near_out = along(near, outward)
    near_in = along(near, inward)
    map_sum = (maps.astype(f32) + map_hop.astype(f32)).astype(bf16)
    map_far = along(map_sum, middle)
    map_done = ((map_sum.astype(f32) + map_far.astype(f32)) * in_scale).astype(bf16)
    sent_end = onward(over, hop_far)
    got_end = along(sent_end, over_middle)
    hop_over, near_out, unused = tie((hop_over, near_out, sent_end))
    sent_next = onward(far, hop_over)
    got_next = along(sent_next, middle)
    near_sum = onward(mine, got_mine, near_out, near_in)
    map_done, unused = tie((map_done, sent_next))
    map_done = along(map_done, outward)
    gained = scan(
        place,
        in_scale,
        [near_sum, got_end, got_next],
        [map_sum, map_far, map_done],
        small,
        largest,
        start_state,
    )

    tokens = gained.shape[0] - 2 * ROWS
    beside = along(gained, beside_pairs)
    facing = along(gained, middle)
    second = jnp.where(at_end, along(facing, outward), facing)
    beyond = along(beside, middle)
    third = jnp.where(at_end, along(beyond, outward), beyond)
    far_own = across(gained)
    far_beside = across(beside)
    second, far_own = tie((second, far_own))
    far_second = across(second)
    third, far_beside = tie((third, far_beside))
    far_third = across(third)
    two, three = (jnp.where(at_end, 2, 3), jnp.where(at_end, 3, 2))

    def rows_for(x, m):
        at = ((side ^ x) * LINE + (z ^ m)) * channels
        return lax.dynamic_slice_in_dim(w_out, at, channels, axis=0)

    total = None
    tails = [far_third[tokens:]]
    for x, m, piece in (
        (0, 0, gained),
        (1, 0, far_own),
        (0, 1, beside),
        (1, 1, far_beside),
        (0, two, second),
        (1, two, far_second),
        (0, three, third),
    ):
        product = jnp.dot(piece, rows_for(x, m), preferred_element_type=f32)
        total = product if total is None else total + product
        tails.append(piece[tokens:])
    total, far_third = tie((total, far_third))
    last_rows = rows_for(1, three)
    tails = [tail.astype(f32) for tail in tails]
    squares = sum(tail[:ROWS, :SPAN] + tail[:ROWS, SPAN:] for tail in tails)
    top = functools.reduce(jnp.maximum, [tail[ROWS:, :SPAN] for tail in tails])

    def run_of(array, index, run):
        return lax.dynamic_slice_in_dim(array, index * run, run, axis=0)

    def first_sum(index):
        block, so_far = (run_of(far_third, index, run), run_of(total, index, run))
        return so_far + jnp.dot(block, last_rows, preferred_element_type=f32)

    run = tokens // 2
    keeps = rank % 2
    pairs = [(t, t ^ 1) for t in range(ranks)]
    received = lax.ppermute(first_sum(1 - keeps).astype(bf16), "tensor", pairs)
    kept = first_sum(keeps)
    squares = squares + lax.ppermute(squares, "tensor", pairs)
    bit = 2
    while bit < ranks:
        run //= 2
        keeps = (rank // bit) % 2
        pairs = [(t, t ^ bit) for t in range(ranks)]
        sent = run_of(kept, 1 - keeps, run) + run_of(received, 1 - keeps, run).astype(f32)
        kept = run_of(kept, keeps, run) + run_of(received, keeps, run).astype(f32)
        received = lax.ppermute(sent.astype(bf16), "tensor", pairs)
        squares = squares + lax.ppermute(squares, "tensor", pairs)
        bit *= 2
    mean_sq = squares.reshape(count, ranks, own) / (HEADS * HEAD_DIM)
    factors = lax.rsqrt(pick(mean_sq, 1, rank) + epsilon)
    final = (kept + received.astype(f32)).reshape(count, own, -1) * factors[:, :, None]
    final = lax.all_to_all(final.astype(bf16), "seq", split_axis=0, concat_axis=0, tiled=True)
    layer_out = final.transpose(1, 0, 2).reshape(own, count * final.shape[2])
    return (layer_out, jnp.max(top))


def solution(mesh):
    return jax.shard_map(
        by_heads if splits(mesh) else by_tokens,
        mesh=mesh,
        in_specs=(
            P(("seq", "tensor"), None),
            P(),
            P("seq", "tensor"),
            P("seq", "tensor", None, None),
            P("seq", "tensor"),
            P(None, "tensor"),
            P(None, "tensor", None, None),
            P(None, "tensor"),
            P(None, "tensor", None, None),
            P("tensor"),
            P("tensor"),
            P("tensor"),
            P("tensor", None, None),
            P("tensor"),
            P("tensor", "seq"),
        ),
        out_specs=(P(("seq", "tensor"), None), P()),
        check_vma=False,
    )
```

```python
import functools

import jax
import jax.numpy as jnp
from jax import lax
from jax.experimental import pallas as pl
from jax.experimental.pallas import tpu as pltpu
from jax.sharding import PartitionSpec as P

HEADS = 128
HEAD_DIM = 64
STATE = 128
GROUPS = 8
KERNEL = 4
SPAN = 128


epsilon = 1e-05
quant_range = 448.0


def from_behind(value, axis, steps):
    count = lax.axis_size(axis)
    first, last = (max(0, -steps), min(count, count - steps))
    return lax.ppermute(value, axis, [(source, source + steps) for source in range(first, last)])


def carried_in(shard, axis, combine, identity):
    count, here = (lax.axis_size(axis), lax.axis_index(axis))
    everything = jax.tree.map(
        lambda part, kind: lax.all_gather(part.astype(kind), axis),
        shard,
        (jnp.bfloat16, jnp.bfloat16),
    )
    start = jax.tree.map(
        lambda part, zero: jnp.broadcast_to(jnp.asarray(zero, part.dtype), part.shape),
        shard,
        identity,
    )

    def turn(k, before):
        reached = k < here
        new = combine(
            before, jax.tree.map(lambda part, own: part[k].astype(own.dtype), everything, shard)
        )
        return jax.tree.map(lambda a, b: jnp.where(reached, a, b), new, before)

    return lax.fori_loop(0, count, turn, start)


def depthwise(before, projected, conv_taps, length):
    extended = jnp.concatenate([before, projected], axis=0)
    summed = conv_taps[0] * extended[0:length]
    for offset in range(1, KERNEL):
        summed = summed + conv_taps[offset] * extended[offset : offset + length]
    return jax.nn.silu(summed).astype(jnp.bfloat16)


def combine(earlier, later):
    return (earlier[0] * later[0], later[0][:, None, None] * earlier[1] + later[1])


def by_tokens(
    hidden_in,
    prev_amax,
    w_x,
    w_bc,
    w_dt,
    conv_x,
    conv_bc,
    conv_state_x,
    conv_state_bc,
    dt_bias,
    decay_rate,
    skip,
    init_state,
    norm_gain,
    w_out,
):
    margin = KERNEL - 1
    gathered = lax.all_gather(hidden_in, "tensor", axis=0, tiled=True)
    abs_max = lax.pmax(jnp.max(jnp.abs(gathered.astype(jnp.float32))), "seq")
    in_scale = prev_amax / quant_range
    leading = lax.axis_index("seq") == 0
    row_count = gathered.shape[0]
    bc_width = w_bc.shape[1] * w_bc.shape[2] * w_bc.shape[3]
    bc_rows = jnp.reshape(w_bc, (w_bc.shape[0], bc_width))
    scaled = gathered.astype(jnp.float32) * (quant_range / prev_amax)
    quant = jnp.clip(scaled, -quant_range, quant_range).astype(jnp.bfloat16)
    pieces = (
        lax.all_gather(w_x, "seq", axis=0, tiled=True),
        lax.all_gather(bc_rows, "seq", axis=0, tiled=True),
        lax.all_gather(w_dt, "seq", axis=0, tiled=True),
    )
    x_proj, bc_proj, dt_proj = tuple(
        (
            jnp.dot(quant, weight_piece, preferred_element_type=jnp.float32)
            for weight_piece in pieces
        )
    )
    x_whole = (x_proj * in_scale).astype(jnp.bfloat16)
    bc_whole = (bc_proj * in_scale).astype(jnp.bfloat16)
    dt_raw = dt_proj * in_scale
    state_bc = jnp.reshape(conv_state_bc, (margin, bc_width))
    received = from_behind(
        (x_whole[row_count - margin :], bc_whole[row_count - margin :]), "seq", 1
    )
    x_edge = jnp.where(leading, conv_state_x, received[0])
    bc_edge = jnp.where(leading, state_bc, received[1])
    x_act = depthwise(x_edge, x_whole, conv_x, row_count)
    bc_act = depthwise(bc_edge, bc_whole, jnp.reshape(conv_bc, (KERNEL, bc_width)), row_count)
    step_size = jax.nn.softplus(dt_raw + dt_bias)
    heads_here = step_size.shape[1]
    groups_here = w_bc.shape[1]
    per_group = HEADS // GROUPS
    blocks = row_count // SPAN
    x_blocks = x_act.reshape(blocks, SPAN, heads_here, HEAD_DIM)
    bc_blocks = bc_act.reshape(blocks, SPAN, groups_here, 2, STATE)
    in_map = bc_blocks[:, :, :, 0]
    out_map = bc_blocks[:, :, :, 1]
    step_blocks = step_size.reshape(blocks, SPAN, heads_here)
    cum_blocks = jnp.cumsum(-step_blocks * decay_rate, axis=1)
    index_row = jnp.arange(SPAN, dtype=jnp.int32)
    lower_mask = index_row[:, None] >= index_row[None, :]
    intersection = jnp.einsum(
        "ctgn,cugn->cgtu", out_map, in_map, preferred_element_type=jnp.float32
    )
    intersection = jnp.repeat(intersection, per_group, axis=1)
    cum_heads = jnp.transpose(cum_blocks, (0, 2, 1))
    log_gap = cum_heads[:, :, :, None] - cum_heads[:, :, None, :]
    decay = jnp.exp(jnp.where(lower_mask[None, None], log_gap, -1e30))
    step_heads = jnp.transpose(step_blocks, (0, 2, 1))
    weights = (intersection * decay * step_heads[:, :, None, :]).astype(jnp.bfloat16)
    local_part = jnp.einsum(
        "chtu,cuhp->cthp", weights, x_blocks, preferred_element_type=jnp.float32
    )
    last_cum = cum_blocks[:, SPAN - 1, :]
    x_weighted = (
        x_blocks.astype(jnp.float32)
        * (step_blocks * jnp.exp(last_cum[:, None, :] - cum_blocks))[:, :, :, None]
    ).astype(jnp.bfloat16)
    in_heads = jnp.repeat(in_map, per_group, axis=2)
    added = jnp.einsum("cuhp,cuhn->chpn", x_weighted, in_heads, preferred_element_type=jnp.float32)

    def carry_on(carried, element):
        block_decay, block_added = element
        return (block_decay[:, None, None] * carried + block_added, carried)

    empty_state = jnp.zeros((heads_here, HEAD_DIM, STATE), jnp.float32)
    device_state, entering = lax.scan(carry_on, empty_state, (jnp.exp(last_cum), added))
    device_decay = jnp.exp(jnp.sum(last_cum, axis=0))
    seeded = device_state + jnp.where(leading, device_decay[:, None, None] * init_state, 0.0)
    identity = (jnp.ones_like(device_decay), jnp.zeros_like(device_state))
    scanned = carried_in((device_decay, seeded), "seq", combine, identity)
    incoming = jnp.where(leading, init_state, scanned[1])
    prefix = jnp.exp(jnp.cumsum(last_cum, axis=0) - last_cum)
    states_in = entering + prefix[:, :, None, None] * incoming[None]
    out_heads = jnp.repeat(out_map, per_group, axis=2).astype(jnp.float32)
    carried_part = (
        jnp.einsum("cthn,chpn->cthp", out_heads, states_in, precision=lax.Precision.HIGHEST)
        * jnp.exp(cum_blocks)[:, :, :, None]
    )
    ssm_out = local_part + carried_part + skip[None, None, :, None] * x_blocks.astype(jnp.float32)
    ssm_out = ssm_out.reshape(row_count, heads_here * HEAD_DIM)
    squares = lax.psum(jnp.sum(ssm_out * ssm_out, axis=1), "tensor")
    mean_sq = squares / (HEADS * HEAD_DIM)
    normed = (ssm_out * lax.rsqrt(mean_sq + epsilon)[:, None] * norm_gain).astype(jnp.bfloat16)
    partial_out = jnp.dot(
        normed, lax.all_gather(w_out, "seq", axis=1, tiled=True), preferred_element_type=jnp.float32
    )
    layer_out = lax.psum_scatter(
        partial_out.astype(jnp.bfloat16), "tensor", scatter_dimension=0, tiled=True
    )
    return (layer_out, abs_max)


PAIR = 2
LINE = 4
ROWS = 8
CUTS = 2
SMEM = pl.BlockSpec(memory_space=pltpu.SMEM)
VMEM = pl.BlockSpec(memory_space=pltpu.VMEM)
HIGHEST = lax.Precision.HIGHEST


def splits(mesh):
    count, ranks = (mesh.shape["seq"], mesh.shape["tensor"])
    heads_all, groups_here = (HEADS // ranks, GROUPS // ranks)
    if count != PAIR * LINE or groups_here != PAIR or ranks & (ranks - 1):
        return False
    heads_here = heads_all // count
    return 2 * heads_here == ROWS and heads_here * HEAD_DIM == 2 * SPAN


def nt_dot(a, b, **kw):
    return lax.dot_general(
        a, b, (((1,), (1,)), ((), ())), preferred_element_type=jnp.float32, **kw
    )


def project_kernel(ranks, place_ref, factor_ref, *refs):
    hidden = [refs[x * ranks : (x + 1) * ranks] for x in range(PAIR)]
    refs = refs[PAIR * ranks :]
    own_x, x_far, own_bc, own_dt, rest = refs[:5]
    far_refs, near_refs, sent_refs = (
        refs[5 + at : 5 + at + LINE // 2] for at in range(0, 3 * LINE // 2, LINE // 2)
    )
    bc_ref, largest_ref, quant_ref, near_dt, all_dt = refs[5 + 3 * LINE // 2 :]
    side, z = (place_ref[1], place_ref[2])
    factor = factor_ref[0]
    depth = own_x.shape[0]
    largest = None
    for x in range(PAIR):
        for k in range(LINE):
            block = (k ^ z) * PAIR + (side ^ x)
            for j in range(ranks):
                for half in range(PAIR):
                    cut = slice(half * depth, (half + 1) * depth)
                    values = hidden[x][j][k, :, cut].astype(jnp.float32)
                    scaled = jnp.clip(values * factor, -quant_range, quant_range)
                    quant_ref[half, block, j] = scaled.astype(jnp.bfloat16)
                    top = jnp.max(jnp.abs(values).reshape(-1, ROWS, depth), axis=0)
                    largest = top if largest is None else jnp.maximum(largest, top)
    step_rows = own_dt.shape[0]
    other_dt = jnp.concatenate(
        [rest[at : at + step_rows] for at in range(depth, rest.shape[0], step_rows)], axis=1
    )
    width = largest_ref.shape[1]
    top = largest[:, :width]
    for at in range(width, depth, width):
        top = jnp.maximum(top, largest[:, at : at + width])
    largest_ref[...] = top

    channels = near_refs[0].shape[1]
    tokens = bc_ref.shape[0]
    rows = tokens // CUTS
    blocks = quant_ref.shape[1] // CUTS
    extra = rows // channels * ROWS
    upper = lax.broadcasted_iota(jnp.int32, (ROWS, channels), 0) < ROWS // 2

    def steps_of(dt_ref, run):
        dt = dt_ref[run // 2]
        pieces = []
        for at in range(0, rows, channels):
            piece = dt[:, at : at + channels]
            turned = pltpu.roll(piece, ROWS // 2, 0)
            lower_run = jnp.where(upper, piece, turned)
            upper_run = jnp.where(upper, turned, piece)
            pieces.append(split_parts(jnp.where(run % 2 == 0, lower_run, upper_run), upper))
        return jnp.concatenate(pieces, axis=0).astype(jnp.bfloat16)

    def columns(run):
        return pl.ds(pl.multiple_of(run * channels, channels), channels)

    for cut in range(CUTS):
        part = slice(cut * blocks, (cut + 1) * blocks)
        near = quant_ref[side, part].reshape(rows, depth)
        far = quant_ref[1 - side, part].reshape(rows, depth)

        def both(own, other):
            return jnp.dot(near, own, preferred_element_type=jnp.float32) + jnp.dot(
                far, other, preferred_element_type=jnp.float32
            )

        at_rows = slice(cut * rows, (cut + 1) * rows)
        extra_rows = slice(tokens + cut * extra, tokens + (cut + 1) * extra)
        ours = nt_dot(own_dt[...], near)
        near_dt[...] = ours.reshape(near_dt.shape)
        all_dt[...] = (ours + nt_dot(other_dt, far)).reshape(all_dt.shape)
        bc_ref[at_rows] = both(own_bc[...], rest[:depth]).astype(jnp.bfloat16)
        for m in range(LINE // 2):
            owner = z ^ (m + LINE // 2)
            run = side * LINE + owner
            other = x_far[:, columns(owner % (LINE // 2))]
            far_refs[m][at_rows] = both(own_x[:, columns(run)], other).astype(jnp.bfloat16)
            far_refs[m][extra_rows] = steps_of(all_dt, run)
            for out_refs, way in ((near_refs, side), (sent_refs, 1 - side)):
                run = way * LINE + (z ^ m)
                product = jnp.dot(near, own_x[:, columns(run)], preferred_element_type=jnp.float32)
                out_refs[m][at_rows] = product.astype(jnp.bfloat16)
                out_refs[m][extra_rows] = steps_of(near_dt, run)


def split_parts(values, upper):
    top = values.astype(jnp.bfloat16).astype(jnp.float32)
    return jnp.where(upper, top, values - top)


def project(place, factor, hidden, w_x, weights):
    line, own, wide = hidden[0].shape
    ranks = len(hidden) // PAIR
    depth, x_wide = (weights[0].shape[0], 2 * weights[0].shape[1])
    channels, maps_wide = (x_wide // LINE, weights[1].shape[1])
    tokens = line * PAIR * ranks * own
    extra = tokens // channels * ROWS
    dt_shape = (weights[2].shape[0] // ROWS, ROWS, tokens // CUTS)
    payload = jax.ShapeDtypeStruct((tokens + extra, channels), jnp.bfloat16)
    maps = jax.ShapeDtypeStruct((tokens, maps_wide), jnp.bfloat16)
    largest = jax.ShapeDtypeStruct((ROWS, 128), jnp.float32)
    outs = [payload] * (LINE + LINE // 2) + [maps, largest]
    return pl.pallas_call(
        functools.partial(project_kernel, ranks),
        in_specs=[SMEM, SMEM] + [VMEM] * (len(hidden) + 1 + len(weights)),
        out_specs=[VMEM] * len(outs),
        scratch_shapes=[
            pltpu.VMEM((PAIR, line * PAIR, ranks, own, depth), jnp.bfloat16),
            pltpu.VMEM(dt_shape, jnp.float32),
            pltpu.VMEM(dt_shape, jnp.float32),
        ],
        out_shape=outs,
        compiler_params=pltpu.CompilerParams(vmem_limit_bytes=32 * 2**20),
        cost_estimate=pl.CostEstimate(
            flops=2 * tokens * wide * (x_wide + maps_wide),
            bytes_accessed=2 * tokens * (wide + x_wide),
            transcendentals=0,
        ),
        name="project",
    )(place, factor, *hidden, w_x, *weights)


def onward_kernel(*refs):
    share_refs, out_ref = (refs[:-1], refs[-1])
    rows, channels = out_ref.shape
    tokens = rows * channels // (channels + ROWS)
    total = sum(ref[:tokens].astype(jnp.float32) for ref in share_refs)
    out_ref[:tokens] = total.astype(jnp.bfloat16)
    upper = lax.broadcasted_iota(jnp.int32, (ROWS, channels), 0) < ROWS // 2
    extra = sum(ref[tokens:].astype(jnp.float32) for ref in share_refs)
    pieces = []
    for at in range(0, rows - tokens, ROWS):
        piece = extra[at : at + ROWS]
        pieces.append(split_parts(piece + pltpu.roll(piece, ROWS // 2, 0), upper))
    out_ref[tokens:] = jnp.concatenate(pieces, axis=0).astype(jnp.bfloat16)


def onward(*shares):
    own = shares[0]
    return pl.pallas_call(
        onward_kernel,
        in_specs=[VMEM] * len(shares),
        out_specs=VMEM,
        out_shape=jax.ShapeDtypeStruct(own.shape, own.dtype),
        compiler_params=pltpu.CompilerParams(vmem_limit_bytes=8 * 2**20),
        cost_estimate=pl.CostEstimate(
            flops=len(shares) * own.size,
            bytes_accessed=2 * (len(shares) + 1) * own.size,
            transcendentals=0,
        ),
        name="onward",
    )(*shares)


def turned_rank(rank, ranks):
    turned = 0
    while ranks > 1:
        turned, rank, ranks = (2 * turned + rank % 2, rank // 2, ranks // 2)
    return turned


def scan_kernel(place_ref, scale_ref, *refs):
    x_refs, bc_refs = (refs[:-9], refs[-9:-6])
    small_ref, largest_ref, state_ref, out_ref, x_buf, bc_buf = refs[-6:]
    tokens, channels = bc_refs[0].shape
    blocks = tokens // SPAN
    heads = channels // HEAD_DIM
    rank, z = (place_ref[0], place_ref[2])
    ranks = place_ref.shape[0] - 3
    own = SPAN // ranks
    edge = ROWS
    in_scale = scale_ref[0]
    at_end = (z == 0) | (z == LINE - 1)
    x_buf[:edge] = small_ref[:edge]
    bc_buf[:edge] = small_ref[edge : 2 * edge]
    state = state_ref[...].T

    for block in range(blocks):
        for true_rank in range(ranks):
            source = block * SPAN + (true_rank ^ rank) * own
            source = pl.ds(pl.multiple_of(source, own), own)
            at = edge + block * SPAN + true_rank * own
            at = slice(at, at + own)
            total = sum(ref[source].astype(jnp.float32) for ref in x_refs) * in_scale
            x_buf[at] = total.astype(jnp.bfloat16).astype(jnp.float32)
            near, far, done = (ref[source].astype(jnp.float32) for ref in bc_refs)
            total = ((near + far) * in_scale).astype(jnp.bfloat16).astype(jnp.float32)
            bc_buf[at] = jnp.where(at_end, done, total)

    taps = 2 * edge

    def activate(buf, row, block):
        start = edge - (KERNEL - 1) + block * SPAN
        summed = small_ref[row : row + 1] * buf[start : start + SPAN]
        for k in range(1, KERNEL):
            summed = summed + small_ref[row + k : row + k + 1] * buf[start + k : start + k + SPAN]
        return (summed / (1.0 + jnp.exp(-summed))).astype(jnp.bfloat16)

    skip = small_ref[taps + 2 * KERNEL : taps + 2 * KERNEL + 1]
    gain = small_ref[taps + 2 * KERNEL + 1 : taps + 2 * KERNEL + 2]
    bias = small_ref[4 * edge :, :SPAN]
    rate = small_ref[4 * edge :, SPAN:]

    up = lax.broadcasted_iota(jnp.int32, (SPAN, SPAN), 0)
    across = lax.broadcasted_iota(jnp.int32, (SPAN, SPAN), 1)
    together = SPAN // HEAD_DIM
    insides = [
        ((across >= h * HEAD_DIM) & (across < (h + 1) * HEAD_DIM))
        .astype(jnp.float32)
        .astype(jnp.bfloat16)
        for h in range(together)
    ]
    lower = up >= across
    upper = (up <= across).astype(jnp.float32)
    lanes = across[:ROWS]

    dt = sum(ref[tokens:].astype(jnp.float32) for ref in x_refs)
    steps = []
    wide = channels // SPAN
    for block in range(blocks):
        tile = dt[block // wide * ROWS : (block // wide + 1) * ROWS]
        cut = tile[:, block % wide * SPAN : (block % wide + 1) * SPAN]
        cut = (cut + pltpu.roll(cut, ROWS // 2, 0)) * in_scale
        bit = 1
        while bit < ranks:
            shift = bit * own
            flipped = jnp.where(
                (lanes // shift) % 2 == 1,
                pltpu.roll(cut, shift, 1),
                pltpu.roll(cut, SPAN - shift, 1),
            )
            cut = jnp.where((rank & bit) != 0, flipped, cut)
            bit *= 2
        raw = cut + bias
        steps.append(jnp.maximum(raw, 0.0) + jnp.log1p(jnp.exp(-jnp.abs(raw))))
    drops = jnp.concatenate([-step * rate for step in steps], axis=0)
    cums = jnp.dot(drops, upper, precision=HIGHEST, preferred_element_type=jnp.float32)

    sums = jnp.zeros((SPAN, SPAN), jnp.float32)
    for block in range(blocks):
        x_act = activate(x_buf, taps, block)
        bc_act = activate(bc_buf, taps + KERNEL, block)
        in_map, out_map = (bc_act[:, :STATE], bc_act[:, STATE:])
        step, cum = (steps[block], cums[block * ROWS : (block + 1) * ROWS])
        last = cum[:, SPAN - 1 : SPAN]
        turned = jnp.concatenate(
            [
                cum,
                step * jnp.exp(last - cum),
                jnp.exp(cum),
                jnp.zeros((SPAN - 3 * ROWS, SPAN), jnp.float32),
            ],
            axis=0,
        ).T

        def spread(row):
            tiles = []
            for first in range(row, row + heads, together):
                tile = jnp.broadcast_to(turned[:, first : first + 1], across.shape)
                for h in range(1, together):
                    column = turned[:, first + h : first + h + 1]
                    tile = jnp.where(across >= h * HEAD_DIM, column, tile)
                tiles.append(tile)
            return jnp.concatenate(tiles, axis=1)

        inner = jnp.where(lower, nt_dot(out_map, in_map), 0.0)
        x_wide = x_act.astype(jnp.float32)
        local_tiles = []
        for first in range(0, heads, together):
            weights, spaced = ([], [])
            tile = x_act[:, first * HEAD_DIM : (first + together) * HEAD_DIM]
            for h in range(first, first + together):
                gap = jnp.where(lower, turned[:, h : h + 1] - cum[h : h + 1], 0.0)
                weights.append((inner * jnp.exp(gap) * step[h : h + 1]).astype(jnp.bfloat16))
                spaced.append(tile * insides[h - first])
            local_tiles.append(
                jnp.dot(
                    jnp.concatenate(weights, axis=1),
                    jnp.concatenate(spaced, axis=0),
                    preferred_element_type=jnp.float32,
                )
            )
        local_part = jnp.concatenate(local_tiles, axis=1)
        grown = spread(2 * ROWS)
        x_weighted = (x_wide * spread(ROWS)).astype(jnp.bfloat16)
        added = lax.dot_general(
            in_map, x_weighted, (((0,), (0,)), ((), ())), preferred_element_type=jnp.float32
        )
        high = state.astype(jnp.bfloat16)
        rest = (state - high.astype(jnp.float32)).astype(jnp.bfloat16)
        carried = jnp.dot(
            jnp.concatenate([out_map, out_map], axis=1),
            jnp.concatenate([high, rest], axis=0),
            preferred_element_type=jnp.float32,
        )
        ssm_out = local_part + grown * carried + skip * x_wide
        state = grown[SPAN - 1 : SPAN] * state + added
        gained = (ssm_out * gain).astype(jnp.bfloat16)
        for true_rank in range(ranks):
            at = (turned_rank(true_rank, ranks) * blocks + block) * own
            out_ref[at : at + own] = gained[true_rank * own : (true_rank + 1) * own]
        summed = jnp.sum(ssm_out * ssm_out, axis=1, keepdims=True)
        sums = jnp.where(across == block, summed, sums)

    whole = sums.T[:ROWS]
    top = whole.astype(jnp.bfloat16).astype(jnp.float32)
    largest = jnp.broadcast_to(jnp.max(largest_ref[...]), (ROWS, channels))
    extra = jnp.concatenate([jnp.concatenate([top, whole - top], axis=1), largest], axis=0)
    out_ref[tokens:] = extra.astype(jnp.bfloat16)


def scan(place, in_scale, sums, maps, small, largest, state):
    channels = sums[0].shape[1]
    tokens = maps[0].shape[0]

    out = jax.ShapeDtypeStruct((tokens + 2 * ROWS, channels), jnp.bfloat16)
    return pl.pallas_call(
        scan_kernel,
        in_specs=[SMEM, SMEM] + [VMEM] * (len(sums) + len(maps) + 3),
        out_specs=VMEM,
        scratch_shapes=[
            pltpu.VMEM((tokens + ROWS, channels), jnp.float32),
            pltpu.VMEM((tokens + ROWS, 2 * STATE), jnp.float32),
        ],
        out_shape=out,
        compiler_params=pltpu.CompilerParams(vmem_limit_bytes=20 * 2**20),
        cost_estimate=pl.CostEstimate(
            flops=8 * tokens * SPAN * channels,
            bytes_accessed=8 * tokens * channels,
            transcendentals=tokens * (channels + 8 * SPAN),
        ),
        name="scan",
    )(place, in_scale, *sums, *maps, small, largest, state)


def by_heads(
    hidden_in,
    prev_amax,
    w_x,
    w_bc,
    w_dt,
    conv_x,
    conv_bc,
    conv_state_x,
    conv_state_bc,
    dt_bias,
    decay_rate,
    skip,
    init_state,
    norm_gain,
    w_out,
):
    margin = KERNEL - 1
    count, here = (lax.axis_size("seq"), lax.axis_index("seq"))
    ranks, rank = (lax.axis_size("tensor"), lax.axis_index("tensor"))
    z, side = (here // PAIR, here % PAIR)
    place_of = side * LINE + z
    f32, bf16 = (jnp.float32, jnp.bfloat16)
    own, width = hidden_in.shape
    depth = w_x.shape[0]
    channels = w_x.shape[1] // count
    heads_here = w_dt.shape[1] // count
    in_scale = (prev_amax / quant_range).reshape(1)
    factor = (quant_range / prev_amax).reshape(1)
    place = jnp.stack([rank, side, z] + [rank] * ranks).astype(jnp.int32)

    def pick(array, axis, index):
        return lax.dynamic_index_in_dim(array, index, axis, keepdims=False)

    def along(value, pairs):
        moves = [(a * PAIR + x, b * PAIR + x) for a, b in pairs for x in range(PAIR)]
        return lax.ppermute(value, "seq", moves)

    def across(value):
        return lax.ppermute(value, "seq", [(s, s ^ 1) for s in range(count)])

    def of_heads(array):
        return jnp.repeat(array, HEAD_DIM)[None]

    by_channel = jnp.concatenate(
        [conv_state_x.astype(f32), conv_x, of_heads(skip), norm_gain[None]], axis=0
    )
    by_channel = lax.dynamic_slice_in_dim(by_channel, place_of * channels, channels, axis=1)
    by_map = jnp.concatenate([conv_state_bc.astype(f32), conv_bc], axis=0)
    by_map = pick(by_map, 1, side).reshape(margin + KERNEL, 2 * STATE)
    by_head = jnp.stack([dt_bias, decay_rate]).reshape(2, count, heads_here)
    by_head = jnp.tile(pick(by_head, 1, place_of).T, (ROWS // heads_here, 1))
    by_head = jnp.repeat(by_head, SPAN, axis=1)
    blank = jnp.zeros((ROWS - margin, channels), f32)
    small = jnp.concatenate(
        [
            blank,
            by_channel[:margin],
            blank,
            by_map[:margin],
            by_channel[margin : margin + KERNEL],
            by_map[margin:],
            by_channel[margin + KERNEL :],
            jnp.zeros((2 * ROWS - 2 * KERNEL - 2, channels), f32),
            by_head,
        ],
        axis=0,
    )

    start_state = lax.dynamic_slice_in_dim(
        init_state, place_of * heads_here, heads_here, axis=0
    ).reshape(channels, STATE)

    tie = lax.optimization_barrier
    half_run = LINE // 2 * channels
    opposite = (z // (LINE // 2)) ^ 1
    at = ((1 - side) * 2 + opposite) * half_run
    x_sent = lax.dynamic_slice_in_dim(w_x, at, half_run, axis=1)
    x_sent, hidden_in = tie((x_sent, hidden_in))
    x_far = across(x_sent)
    dt_rows = w_dt.T
    dt_cut = [dt_rows[:, at : at + 2 * STATE] for at in range(0, depth, 2 * STATE)]
    maps_sent = pick(w_bc, 1, 1 - side).reshape(depth, 2 * STATE)
    x_far, rest_sent = tie((x_far, jnp.concatenate([maps_sent, *dt_cut], axis=0)))
    rest_other = across(rest_sent)
    bc_own = pick(w_bc, 1, side).reshape(depth, 2 * STATE)

    def line_columns(m):
        return lax.dynamic_slice_in_dim(hidden_in, (z ^ m) * PAIR * depth, PAIR * depth, axis=1)

    arrived = [line_columns(0)]
    for m in range(1, LINE):
        arrived.append(along(line_columns(m), [(s, s ^ m) for s in range(LINE)]))
    stacked = jnp.stack(arrived)
    beyond_pair = across(stacked)
    beyond_pair, small, start_state, bc_own, dt_rows = tie(
        (beyond_pair, small, start_state, bc_own, dt_rows)
    )
    rows = []
    for mine in (stacked, beyond_pair):
        ours = [mine]
        for j in range(1, ranks):
            bit = j & -j
            pairs = [(t, t ^ bit) for t in range(ranks)]
            ours.append(lax.ppermute(ours[j - bit], "tensor", pairs))
        rows.extend(ours)

    start, end = (0, LINE - 1)
    at_end = (z == start) | (z == end)
    next_start, next_end = (1, LINE - 2)
    inward = [(start, next_start), (end, next_end)]
    outward = [(next_start, start), (next_end, end)]
    middle = [(next_start, next_end), (next_end, next_start)]
    over_middle = [(next_start, end), (next_end, start)]
    beside_pairs = [(s, s ^ 1) for s in range(LINE)]
    weights = (x_far, bc_own, dt_rows, rest_other)
    over, far, mine, near, mine_sent, near_sent, maps, largest = project(
        place, factor, rows, w_x, weights
    )

    map_hop = along(maps, inward)
    hop_far = along(far, inward)
    hop_over = along(over, inward)
    near = onward(near, across(near_sent))
    got_mine = across(mine_sent)
    near_out = along(near, outward)
    map_sum = (maps.astype(f32) + map_hop.astype(f32)).astype(bf16)
    map_far = along(map_sum, middle)
    map_done = ((map_sum.astype(f32) + map_far.astype(f32)) * in_scale).astype(bf16)
    sent_end = onward(over, hop_far)
    got_end = along(sent_end, over_middle)
    near, unused = tie((near, sent_end))
    near_in = along(near, inward)
    hop_over, near_out, unused = tie((hop_over, near_out, sent_end))
    sent_next = onward(far, hop_over)
    got_next = along(sent_next, middle)
    got_end, near_in = tie((got_end, near_in))
    near_sum = onward(mine, got_mine, near_out, near_in)
    map_done, unused = tie((map_done, sent_next))
    map_done = along(map_done, outward)
    gained = scan(
        place,
        in_scale,
        [near_sum, got_end, got_next],
        [map_sum, map_far, map_done],
        small,
        largest,
        start_state,
    )

    tokens = gained.shape[0] - 2 * ROWS
    beside = along(gained, beside_pairs)
    facing = along(gained, middle)
    second = jnp.where(at_end, along(facing, outward), facing)
    beyond = along(beside, middle)
    third = jnp.where(at_end, along(beyond, outward), beyond)
    far_own = across(gained)
    far_beside = across(beside)
    second, far_own = tie((second, far_own))
    far_second = across(second)
    third, far_beside = tie((third, far_beside))
    far_third = across(third)
    two, three = (jnp.where(at_end, 2, 3), jnp.where(at_end, 3, 2))

    def rows_for(x, m):
        at = ((side ^ x) * LINE + (z ^ m)) * channels
        return lax.dynamic_slice_in_dim(w_out, at, channels, axis=0)

    total = None
    tails = [far_third[tokens:]]
    for x, m, piece in (
        (0, 0, gained),
        (1, 0, far_own),
        (0, 1, beside),
        (1, 1, far_beside),
        (0, two, second),
        (1, two, far_second),
        (0, three, third),
    ):
        product = jnp.dot(piece, rows_for(x, m), preferred_element_type=f32)
        total = product if total is None else total + product
        tails.append(piece[tokens:])
    total, far_third = tie((total, far_third))
    last_rows = rows_for(1, three)
    tails = [tail.astype(f32) for tail in tails]
    squares = sum(tail[:ROWS, :SPAN] + tail[:ROWS, SPAN:] for tail in tails)
    top = functools.reduce(jnp.maximum, [tail[ROWS:, :SPAN] for tail in tails])

    def run_of(array, index, run):
        return lax.dynamic_slice_in_dim(array, index * run, run, axis=0)

    def first_sum(index):
        block, so_far = (run_of(far_third, index, run), run_of(total, index, run))
        return so_far + jnp.dot(block, last_rows, preferred_element_type=f32)

    run = tokens // 2
    keeps = rank % 2
    pairs = [(t, t ^ 1) for t in range(ranks)]
    received = lax.ppermute(first_sum(1 - keeps).astype(bf16), "tensor", pairs)
    kept = first_sum(keeps)
    squares = squares + lax.ppermute(squares, "tensor", pairs)
    bit = 2
    while bit < ranks:
        run //= 2
        keeps = (rank // bit) % 2
        pairs = [(t, t ^ bit) for t in range(ranks)]
        sent = run_of(kept, 1 - keeps, run) + run_of(received, 1 - keeps, run).astype(f32)
        kept = run_of(kept, keeps, run) + run_of(received, keeps, run).astype(f32)
        received = lax.ppermute(sent.astype(bf16), "tensor", pairs)
        squares = squares + lax.ppermute(squares, "tensor", pairs)
        bit *= 2
    mean_sq = squares.reshape(count, ranks, own) / (HEADS * HEAD_DIM)
    factors = lax.rsqrt(pick(mean_sq, 1, rank) + epsilon)
    final = (kept + received.astype(f32)).reshape(count, own, -1) * factors[:, :, None]
    final = lax.all_to_all(final.astype(bf16), "seq", split_axis=0, concat_axis=0, tiled=True)
    layer_out = final.transpose(1, 0, 2).reshape(own, count * final.shape[2])
    return (layer_out, jnp.max(top))


def solution(mesh):
    return jax.shard_map(
        by_heads if splits(mesh) else by_tokens,
        mesh=mesh,
        in_specs=(
            P(("seq", "tensor"), None),
            P(),
            P("seq", "tensor"),
            P("seq", "tensor", None, None),
            P("seq", "tensor"),
            P(None, "tensor"),
            P(None, "tensor", None, None),
            P(None, "tensor"),
            P(None, "tensor", None, None),
            P("tensor"),
            P("tensor"),
            P("tensor"),
            P("tensor", None, None),
            P("tensor"),
            P("tensor", "seq"),
        ),
        out_specs=(P(("seq", "tensor"), None), P()),
        check_vma=False,
    )
```

```python
import functools

import jax
import jax.numpy as jnp
from jax import lax
from jax.experimental import pallas as pl
from jax.experimental.pallas import tpu as pltpu
from jax.sharding import PartitionSpec as P

HEADS = 128
HEAD_DIM = 64
STATE = 128
GROUPS = 8
KERNEL = 4
SPAN = 128


epsilon = 1e-05
quant_range = 448.0


def from_behind(value, axis, steps):
    count = lax.axis_size(axis)
    first, last = (max(0, -steps), min(count, count - steps))
    return lax.ppermute(value, axis, [(source, source + steps) for source in range(first, last)])


def carried_in(shard, axis, combine, identity):
    count, here = (lax.axis_size(axis), lax.axis_index(axis))
    everything = jax.tree.map(
        lambda part, kind: lax.all_gather(part.astype(kind), axis),
        shard,
        (jnp.bfloat16, jnp.bfloat16),
    )
    start = jax.tree.map(
        lambda part, zero: jnp.broadcast_to(jnp.asarray(zero, part.dtype), part.shape),
        shard,
        identity,
    )

    def turn(k, before):
        reached = k < here
        new = combine(
            before, jax.tree.map(lambda part, own: part[k].astype(own.dtype), everything, shard)
        )
        return jax.tree.map(lambda a, b: jnp.where(reached, a, b), new, before)

    return lax.fori_loop(0, count, turn, start)


def depthwise(before, projected, conv_taps, length):
    extended = jnp.concatenate([before, projected], axis=0)
    summed = conv_taps[0] * extended[0:length]
    for offset in range(1, KERNEL):
        summed = summed + conv_taps[offset] * extended[offset : offset + length]
    return jax.nn.silu(summed).astype(jnp.bfloat16)


def combine(earlier, later):
    return (earlier[0] * later[0], later[0][:, None, None] * earlier[1] + later[1])


def by_tokens(
    hidden_in,
    prev_amax,
    w_x,
    w_bc,
    w_dt,
    conv_x,
    conv_bc,
    conv_state_x,
    conv_state_bc,
    dt_bias,
    decay_rate,
    skip,
    init_state,
    norm_gain,
    w_out,
):
    margin = KERNEL - 1
    gathered = lax.all_gather(hidden_in, "tensor", axis=0, tiled=True)
    abs_max = lax.pmax(jnp.max(jnp.abs(gathered.astype(jnp.float32))), "seq")
    in_scale = prev_amax / quant_range
    leading = lax.axis_index("seq") == 0
    row_count = gathered.shape[0]
    bc_width = w_bc.shape[1] * w_bc.shape[2] * w_bc.shape[3]
    bc_rows = jnp.reshape(w_bc, (w_bc.shape[0], bc_width))
    scaled = gathered.astype(jnp.float32) * (quant_range / prev_amax)
    quant = jnp.clip(scaled, -quant_range, quant_range).astype(jnp.bfloat16)
    pieces = (
        lax.all_gather(w_x, "seq", axis=0, tiled=True),
        lax.all_gather(bc_rows, "seq", axis=0, tiled=True),
        lax.all_gather(w_dt, "seq", axis=0, tiled=True),
    )
    x_proj, bc_proj, dt_proj = tuple(
        (
            jnp.dot(quant, weight_piece, preferred_element_type=jnp.float32)
            for weight_piece in pieces
        )
    )
    x_whole = (x_proj * in_scale).astype(jnp.bfloat16)
    bc_whole = (bc_proj * in_scale).astype(jnp.bfloat16)
    dt_raw = dt_proj * in_scale
    state_bc = jnp.reshape(conv_state_bc, (margin, bc_width))
    received = from_behind(
        (x_whole[row_count - margin :], bc_whole[row_count - margin :]), "seq", 1
    )
    x_edge = jnp.where(leading, conv_state_x, received[0])
    bc_edge = jnp.where(leading, state_bc, received[1])
    x_act = depthwise(x_edge, x_whole, conv_x, row_count)
    bc_act = depthwise(bc_edge, bc_whole, jnp.reshape(conv_bc, (KERNEL, bc_width)), row_count)
    step_size = jax.nn.softplus(dt_raw + dt_bias)
    heads_here = step_size.shape[1]
    groups_here = w_bc.shape[1]
    per_group = HEADS // GROUPS
    blocks = row_count // SPAN
    x_blocks = x_act.reshape(blocks, SPAN, heads_here, HEAD_DIM)
    bc_blocks = bc_act.reshape(blocks, SPAN, groups_here, 2, STATE)
    in_map = bc_blocks[:, :, :, 0]
    out_map = bc_blocks[:, :, :, 1]
    step_blocks = step_size.reshape(blocks, SPAN, heads_here)
    cum_blocks = jnp.cumsum(-step_blocks * decay_rate, axis=1)
    index_row = jnp.arange(SPAN, dtype=jnp.int32)
    lower_mask = index_row[:, None] >= index_row[None, :]
    intersection = jnp.einsum(
        "ctgn,cugn->cgtu", out_map, in_map, preferred_element_type=jnp.float32
    )
    intersection = jnp.repeat(intersection, per_group, axis=1)
    cum_heads = jnp.transpose(cum_blocks, (0, 2, 1))
    log_gap = cum_heads[:, :, :, None] - cum_heads[:, :, None, :]
    decay = jnp.exp(jnp.where(lower_mask[None, None], log_gap, -1e30))
    step_heads = jnp.transpose(step_blocks, (0, 2, 1))
    weights = (intersection * decay * step_heads[:, :, None, :]).astype(jnp.bfloat16)
    local_part = jnp.einsum(
        "chtu,cuhp->cthp", weights, x_blocks, preferred_element_type=jnp.float32
    )
    last_cum = cum_blocks[:, SPAN - 1, :]
    x_weighted = (
        x_blocks.astype(jnp.float32)
        * (step_blocks * jnp.exp(last_cum[:, None, :] - cum_blocks))[:, :, :, None]
    ).astype(jnp.bfloat16)
    in_heads = jnp.repeat(in_map, per_group, axis=2)
    added = jnp.einsum("cuhp,cuhn->chpn", x_weighted, in_heads, preferred_element_type=jnp.float32)

    def carry_on(carried, element):
        block_decay, block_added = element
        return (block_decay[:, None, None] * carried + block_added, carried)

    empty_state = jnp.zeros((heads_here, HEAD_DIM, STATE), jnp.float32)
    device_state, entering = lax.scan(carry_on, empty_state, (jnp.exp(last_cum), added))
    device_decay = jnp.exp(jnp.sum(last_cum, axis=0))
    seeded = device_state + jnp.where(leading, device_decay[:, None, None] * init_state, 0.0)
    identity = (jnp.ones_like(device_decay), jnp.zeros_like(device_state))
    scanned = carried_in((device_decay, seeded), "seq", combine, identity)
    incoming = jnp.where(leading, init_state, scanned[1])
    prefix = jnp.exp(jnp.cumsum(last_cum, axis=0) - last_cum)
    states_in = entering + prefix[:, :, None, None] * incoming[None]
    out_heads = jnp.repeat(out_map, per_group, axis=2).astype(jnp.float32)
    carried_part = (
        jnp.einsum("cthn,chpn->cthp", out_heads, states_in, precision=lax.Precision.HIGHEST)
        * jnp.exp(cum_blocks)[:, :, :, None]
    )
    ssm_out = local_part + carried_part + skip[None, None, :, None] * x_blocks.astype(jnp.float32)
    ssm_out = ssm_out.reshape(row_count, heads_here * HEAD_DIM)
    squares = lax.psum(jnp.sum(ssm_out * ssm_out, axis=1), "tensor")
    mean_sq = squares / (HEADS * HEAD_DIM)
    normed = (ssm_out * lax.rsqrt(mean_sq + epsilon)[:, None] * norm_gain).astype(jnp.bfloat16)
    partial_out = jnp.dot(
        normed, lax.all_gather(w_out, "seq", axis=1, tiled=True), preferred_element_type=jnp.float32
    )
    layer_out = lax.psum_scatter(
        partial_out.astype(jnp.bfloat16), "tensor", scatter_dimension=0, tiled=True
    )
    return (layer_out, abs_max)


PAIR = 2
LINE = 4
ROWS = 8
CUTS = 2
SMEM = pl.BlockSpec(memory_space=pltpu.SMEM)
VMEM = pl.BlockSpec(memory_space=pltpu.VMEM)
HIGHEST = lax.Precision.HIGHEST


def splits(mesh):
    count, ranks = (mesh.shape["seq"], mesh.shape["tensor"])
    heads_all, groups_here = (HEADS // ranks, GROUPS // ranks)
    if count != PAIR * LINE or groups_here != PAIR or ranks & (ranks - 1):
        return False
    heads_here = heads_all // count
    return 2 * heads_here == ROWS and heads_here * HEAD_DIM == 2 * SPAN


def nt_dot(a, b, **kw):
    return lax.dot_general(
        a, b, (((1,), (1,)), ((), ())), preferred_element_type=jnp.float32, **kw
    )


def project_kernel(ranks, place_ref, factor_ref, *refs):
    hidden = [refs[x * ranks : (x + 1) * ranks] for x in range(PAIR)]
    refs = refs[PAIR * ranks :]
    own_x, x_far, own_bc, own_dt, rest = refs[:5]
    far_refs, near_refs, sent_refs = (
        refs[5 + at : 5 + at + LINE // 2] for at in range(0, 3 * LINE // 2, LINE // 2)
    )
    bc_ref, largest_ref, quant_ref, near_dt, all_dt = refs[5 + 3 * LINE // 2 :]
    side, z = (place_ref[1], place_ref[2])
    factor = factor_ref[0]
    depth = own_x.shape[0]
    largest = None
    for x in range(PAIR):
        for k in range(LINE):
            block = (k ^ z) * PAIR + (side ^ x)
            for j in range(ranks):
                for half in range(PAIR):
                    cut = slice(half * depth, (half + 1) * depth)
                    values = hidden[x][j][k, :, cut].astype(jnp.float32)
                    scaled = jnp.clip(values * factor, -quant_range, quant_range)
                    quant_ref[half, block, j] = scaled.astype(jnp.bfloat16)
                    top = jnp.max(jnp.abs(values).reshape(-1, ROWS, depth), axis=0)
                    largest = top if largest is None else jnp.maximum(largest, top)
    step_rows = own_dt.shape[0]
    other_dt = jnp.concatenate(
        [rest[at : at + step_rows] for at in range(depth, rest.shape[0], step_rows)], axis=1
    )
    width = largest_ref.shape[1]
    top = largest[:, :width]
    for at in range(width, depth, width):
        top = jnp.maximum(top, largest[:, at : at + width])
    largest_ref[...] = top

    channels = near_refs[0].shape[1]
    tokens = bc_ref.shape[0]
    rows = tokens // CUTS
    blocks = quant_ref.shape[1] // CUTS
    extra = rows // channels * ROWS
    upper = lax.broadcasted_iota(jnp.int32, (ROWS, channels), 0) < ROWS // 2

    def steps_of(dt_ref, run):
        dt = dt_ref[run // 2]
        pieces = []
        for at in range(0, rows, channels):
            piece = dt[:, at : at + channels]
            turned = pltpu.roll(piece, ROWS // 2, 0)
            lower_run = jnp.where(upper, piece, turned)
            upper_run = jnp.where(upper, turned, piece)
            pieces.append(split_parts(jnp.where(run % 2 == 0, lower_run, upper_run), upper))
        return jnp.concatenate(pieces, axis=0).astype(jnp.bfloat16)

    def columns(run):
        return pl.ds(pl.multiple_of(run * channels, channels), channels)

    for cut in range(CUTS):
        part = slice(cut * blocks, (cut + 1) * blocks)
        near = quant_ref[side, part].reshape(rows, depth)
        far = quant_ref[1 - side, part].reshape(rows, depth)

        def both(own, other):
            return jnp.dot(near, own, preferred_element_type=jnp.float32) + jnp.dot(
                far, other, preferred_element_type=jnp.float32
            )

        at_rows = slice(cut * rows, (cut + 1) * rows)
        extra_rows = slice(tokens + cut * extra, tokens + (cut + 1) * extra)
        ours = nt_dot(own_dt[...], near)
        near_dt[...] = ours.reshape(near_dt.shape)
        all_dt[...] = (ours + nt_dot(other_dt, far)).reshape(all_dt.shape)
        bc_ref[at_rows] = both(own_bc[...], rest[:depth]).astype(jnp.bfloat16)
        for m in range(LINE // 2):
            owner = z ^ (m + LINE // 2)
            run = side * LINE + owner
            other = x_far[:, columns(owner % (LINE // 2))]
            far_refs[m][at_rows] = both(own_x[:, columns(run)], other).astype(jnp.bfloat16)
            far_refs[m][extra_rows] = steps_of(all_dt, run)
            for out_refs, way in ((near_refs, side), (sent_refs, 1 - side)):
                run = way * LINE + (z ^ m)
                product = jnp.dot(near, own_x[:, columns(run)], preferred_element_type=jnp.float32)
                out_refs[m][at_rows] = product.astype(jnp.bfloat16)
                out_refs[m][extra_rows] = steps_of(near_dt, run)


def split_parts(values, upper):
    top = values.astype(jnp.bfloat16).astype(jnp.float32)
    return jnp.where(upper, top, values - top)


def project(place, factor, hidden, w_x, weights):
    line, own, wide = hidden[0].shape
    ranks = len(hidden) // PAIR
    depth, x_wide = (weights[0].shape[0], 2 * weights[0].shape[1])
    channels, maps_wide = (x_wide // LINE, weights[1].shape[1])
    tokens = line * PAIR * ranks * own
    extra = tokens // channels * ROWS
    dt_shape = (weights[2].shape[0] // ROWS, ROWS, tokens // CUTS)
    payload = jax.ShapeDtypeStruct((tokens + extra, channels), jnp.bfloat16)
    maps = jax.ShapeDtypeStruct((tokens, maps_wide), jnp.bfloat16)
    largest = jax.ShapeDtypeStruct((ROWS, 128), jnp.float32)
    outs = [payload] * (LINE + LINE // 2) + [maps, largest]
    return pl.pallas_call(
        functools.partial(project_kernel, ranks),
        in_specs=[SMEM, SMEM] + [VMEM] * (len(hidden) + 1 + len(weights)),
        out_specs=[VMEM] * len(outs),
        scratch_shapes=[
            pltpu.VMEM((PAIR, line * PAIR, ranks, own, depth), jnp.bfloat16),
            pltpu.VMEM(dt_shape, jnp.float32),
            pltpu.VMEM(dt_shape, jnp.float32),
        ],
        out_shape=outs,
        compiler_params=pltpu.CompilerParams(vmem_limit_bytes=32 * 2**20),
        cost_estimate=pl.CostEstimate(
            flops=2 * tokens * wide * (x_wide + maps_wide),
            bytes_accessed=2 * tokens * (wide + x_wide),
            transcendentals=0,
        ),
        name="project",
    )(place, factor, *hidden, w_x, *weights)


def onward_kernel(*refs):
    share_refs, out_ref = (refs[:-1], refs[-1])
    rows, channels = out_ref.shape
    tokens = rows * channels // (channels + ROWS)
    total = sum(ref[:tokens].astype(jnp.float32) for ref in share_refs)
    out_ref[:tokens] = total.astype(jnp.bfloat16)
    upper = lax.broadcasted_iota(jnp.int32, (ROWS, channels), 0) < ROWS // 2
    extra = sum(ref[tokens:].astype(jnp.float32) for ref in share_refs)
    pieces = []
    for at in range(0, rows - tokens, ROWS):
        piece = extra[at : at + ROWS]
        pieces.append(split_parts(piece + pltpu.roll(piece, ROWS // 2, 0), upper))
    out_ref[tokens:] = jnp.concatenate(pieces, axis=0).astype(jnp.bfloat16)


def onward(*shares):
    own = shares[0]
    return pl.pallas_call(
        onward_kernel,
        in_specs=[VMEM] * len(shares),
        out_specs=VMEM,
        out_shape=jax.ShapeDtypeStruct(own.shape, own.dtype),
        compiler_params=pltpu.CompilerParams(vmem_limit_bytes=8 * 2**20),
        cost_estimate=pl.CostEstimate(
            flops=len(shares) * own.size,
            bytes_accessed=2 * (len(shares) + 1) * own.size,
            transcendentals=0,
        ),
        name="onward",
    )(*shares)


def turned_rank(rank, ranks):
    turned = 0
    while ranks > 1:
        turned, rank, ranks = (2 * turned + rank % 2, rank // 2, ranks // 2)
    return turned


def scan_kernel(place_ref, scale_ref, *refs):
    x_refs, bc_refs = (refs[:-9], refs[-9:-6])
    small_ref, largest_ref, state_ref, out_ref, x_buf, bc_buf = refs[-6:]
    tokens, channels = bc_refs[0].shape
    blocks = tokens // SPAN
    heads = channels // HEAD_DIM
    rank, z = (place_ref[0], place_ref[2])
    ranks = place_ref.shape[0] - 3
    own = SPAN // ranks
    edge = ROWS
    in_scale = scale_ref[0]
    at_end = (z == 0) | (z == LINE - 1)
    x_buf[:edge] = small_ref[:edge]
    bc_buf[:edge] = small_ref[edge : 2 * edge]
    state = state_ref[...].T

    for block in range(blocks):
        for true_rank in range(ranks):
            source = block * SPAN + (true_rank ^ rank) * own
            source = pl.ds(pl.multiple_of(source, own), own)
            at = edge + block * SPAN + true_rank * own
            at = slice(at, at + own)
            total = sum(ref[source].astype(jnp.float32) for ref in x_refs) * in_scale
            x_buf[at] = total.astype(jnp.bfloat16).astype(jnp.float32)
            near, far, done = (ref[source].astype(jnp.float32) for ref in bc_refs)
            total = ((near + far) * in_scale).astype(jnp.bfloat16).astype(jnp.float32)
            bc_buf[at] = jnp.where(at_end, done, total)

    taps = 2 * edge

    def activate(buf, row, block):
        start = edge - (KERNEL - 1) + block * SPAN
        summed = small_ref[row : row + 1] * buf[start : start + SPAN]
        for k in range(1, KERNEL):
            summed = summed + small_ref[row + k : row + k + 1] * buf[start + k : start + k + SPAN]
        return (summed / (1.0 + jnp.exp(-summed))).astype(jnp.bfloat16)

    skip = small_ref[taps + 2 * KERNEL : taps + 2 * KERNEL + 1]
    gain = small_ref[taps + 2 * KERNEL + 1 : taps + 2 * KERNEL + 2]
    bias = small_ref[4 * edge :, :SPAN]
    rate = small_ref[4 * edge :, SPAN:]

    up = lax.broadcasted_iota(jnp.int32, (SPAN, SPAN), 0)
    across = lax.broadcasted_iota(jnp.int32, (SPAN, SPAN), 1)
    together = SPAN // HEAD_DIM
    insides = [
        ((across >= h * HEAD_DIM) & (across < (h + 1) * HEAD_DIM))
        .astype(jnp.float32)
        .astype(jnp.bfloat16)
        for h in range(together)
    ]
    lower = up >= across
    upper = (up <= across).astype(jnp.float32)
    lanes = across[:ROWS]

    dt = sum(ref[tokens:].astype(jnp.float32) for ref in x_refs)
    steps = []
    wide = channels // SPAN
    for block in range(blocks):
        tile = dt[block // wide * ROWS : (block // wide + 1) * ROWS]
        cut = tile[:, block % wide * SPAN : (block % wide + 1) * SPAN]
        cut = (cut + pltpu.roll(cut, ROWS // 2, 0)) * in_scale
        bit = 1
        while bit < ranks:
            shift = bit * own
            flipped = jnp.where(
                (lanes // shift) % 2 == 1,
                pltpu.roll(cut, shift, 1),
                pltpu.roll(cut, SPAN - shift, 1),
            )
            cut = jnp.where((rank & bit) != 0, flipped, cut)
            bit *= 2
        raw = cut + bias
        steps.append(jnp.maximum(raw, 0.0) + jnp.log1p(jnp.exp(-jnp.abs(raw))))
    drops = jnp.concatenate([-step * rate for step in steps], axis=0)
    cums = jnp.dot(drops, upper, precision=HIGHEST, preferred_element_type=jnp.float32)

    sums = jnp.zeros((SPAN, SPAN), jnp.float32)
    for block in range(blocks):
        x_act = activate(x_buf, taps, block)
        bc_act = activate(bc_buf, taps + KERNEL, block)
        in_map, out_map = (bc_act[:, :STATE], bc_act[:, STATE:])
        step, cum = (steps[block], cums[block * ROWS : (block + 1) * ROWS])
        last = cum[:, SPAN - 1 : SPAN]
        turned = jnp.concatenate(
            [
                cum,
                step * jnp.exp(last - cum),
                jnp.exp(cum),
                jnp.zeros((SPAN - 3 * ROWS, SPAN), jnp.float32),
            ],
            axis=0,
        ).T

        def spread(row):
            tiles = []
            for first in range(row, row + heads, together):
                tile = jnp.broadcast_to(turned[:, first : first + 1], across.shape)
                for h in range(1, together):
                    column = turned[:, first + h : first + h + 1]
                    tile = jnp.where(across >= h * HEAD_DIM, column, tile)
                tiles.append(tile)
            return jnp.concatenate(tiles, axis=1)

        inner = jnp.where(lower, nt_dot(out_map, in_map), 0.0)
        x_wide = x_act.astype(jnp.float32)
        local_tiles = []
        for first in range(0, heads, together):
            weights, spaced = ([], [])
            tile = x_act[:, first * HEAD_DIM : (first + together) * HEAD_DIM]
            for h in range(first, first + together):
                gap = jnp.where(lower, turned[:, h : h + 1] - cum[h : h + 1], 0.0)
                weights.append((inner * jnp.exp(gap) * step[h : h + 1]).astype(jnp.bfloat16))
                spaced.append(tile * insides[h - first])
            local_tiles.append(
                jnp.dot(
                    jnp.concatenate(weights, axis=1),
                    jnp.concatenate(spaced, axis=0),
                    preferred_element_type=jnp.float32,
                )
            )
        local_part = jnp.concatenate(local_tiles, axis=1)
        grown = spread(2 * ROWS)
        x_weighted = (x_wide * spread(ROWS)).astype(jnp.bfloat16)
        added = lax.dot_general(
            in_map, x_weighted, (((0,), (0,)), ((), ())), preferred_element_type=jnp.float32
        )
        high = state.astype(jnp.bfloat16)
        rest = (state - high.astype(jnp.float32)).astype(jnp.bfloat16)
        carried = jnp.dot(
            jnp.concatenate([out_map, out_map], axis=1),
            jnp.concatenate([high, rest], axis=0),
            preferred_element_type=jnp.float32,
        )
        ssm_out = local_part + grown * carried + skip * x_wide
        state = grown[SPAN - 1 : SPAN] * state + added
        gained = (ssm_out * gain).astype(jnp.bfloat16)
        for true_rank in range(ranks):
            at = (turned_rank(true_rank, ranks) * blocks + block) * own
            out_ref[at : at + own] = gained[true_rank * own : (true_rank + 1) * own]
        summed = jnp.sum(ssm_out * ssm_out, axis=1, keepdims=True)
        sums = jnp.where(across == block, summed, sums)

    whole = sums.T[:ROWS]
    top = whole.astype(jnp.bfloat16).astype(jnp.float32)
    largest = jnp.broadcast_to(jnp.max(largest_ref[...]), (ROWS, channels))
    extra = jnp.concatenate([jnp.concatenate([top, whole - top], axis=1), largest], axis=0)
    out_ref[tokens:] = extra.astype(jnp.bfloat16)


def scan(place, in_scale, sums, maps, small, largest, state):
    channels = sums[0].shape[1]
    tokens = maps[0].shape[0]

    out = jax.ShapeDtypeStruct((tokens + 2 * ROWS, channels), jnp.bfloat16)
    return pl.pallas_call(
        scan_kernel,
        in_specs=[SMEM, SMEM] + [VMEM] * (len(sums) + len(maps) + 3),
        out_specs=VMEM,
        scratch_shapes=[
            pltpu.VMEM((tokens + ROWS, channels), jnp.float32),
            pltpu.VMEM((tokens + ROWS, 2 * STATE), jnp.float32),
        ],
        out_shape=out,
        compiler_params=pltpu.CompilerParams(vmem_limit_bytes=20 * 2**20),
        cost_estimate=pl.CostEstimate(
            flops=8 * tokens * SPAN * channels,
            bytes_accessed=8 * tokens * channels,
            transcendentals=tokens * (channels + 8 * SPAN),
        ),
        name="scan",
    )(place, in_scale, *sums, *maps, small, largest, state)


def by_heads(
    hidden_in,
    prev_amax,
    w_x,
    w_bc,
    w_dt,
    conv_x,
    conv_bc,
    conv_state_x,
    conv_state_bc,
    dt_bias,
    decay_rate,
    skip,
    init_state,
    norm_gain,
    w_out,
):
    margin = KERNEL - 1
    count, here = (lax.axis_size("seq"), lax.axis_index("seq"))
    ranks, rank = (lax.axis_size("tensor"), lax.axis_index("tensor"))
    z, side = (here // PAIR, here % PAIR)
    place_of = side * LINE + z
    f32, bf16 = (jnp.float32, jnp.bfloat16)
    own, width = hidden_in.shape
    depth = w_x.shape[0]
    channels = w_x.shape[1] // count
    heads_here = w_dt.shape[1] // count
    in_scale = (prev_amax / quant_range).reshape(1)
    factor = (quant_range / prev_amax).reshape(1)
    place = jnp.stack([rank, side, z] + [rank] * ranks).astype(jnp.int32)

    def pick(array, axis, index):
        return lax.dynamic_index_in_dim(array, index, axis, keepdims=False)

    def along(value, pairs):
        moves = [(a * PAIR + x, b * PAIR + x) for a, b in pairs for x in range(PAIR)]
        return lax.ppermute(value, "seq", moves)

    def across(value):
        return lax.ppermute(value, "seq", [(s, s ^ 1) for s in range(count)])

    def of_heads(array):
        return jnp.repeat(array, HEAD_DIM)[None]

    by_channel = jnp.concatenate(
        [conv_state_x.astype(f32), conv_x, of_heads(skip), norm_gain[None]], axis=0
    )
    by_channel = lax.dynamic_slice_in_dim(by_channel, place_of * channels, channels, axis=1)
    by_map = jnp.concatenate([conv_state_bc.astype(f32), conv_bc], axis=0)
    by_map = pick(by_map, 1, side).reshape(margin + KERNEL, 2 * STATE)
    by_head = jnp.stack([dt_bias, decay_rate]).reshape(2, count, heads_here)
    by_head = jnp.tile(pick(by_head, 1, place_of).T, (ROWS // heads_here, 1))
    by_head = jnp.repeat(by_head, SPAN, axis=1)
    blank = jnp.zeros((ROWS - margin, channels), f32)
    small = jnp.concatenate(
        [
            blank,
            by_channel[:margin],
            blank,
            by_map[:margin],
            by_channel[margin : margin + KERNEL],
            by_map[margin:],
            by_channel[margin + KERNEL :],
            jnp.zeros((2 * ROWS - 2 * KERNEL - 2, channels), f32),
            by_head,
        ],
        axis=0,
    )

    start_state = lax.dynamic_slice_in_dim(
        init_state, place_of * heads_here, heads_here, axis=0
    ).reshape(channels, STATE)

    tie = lax.optimization_barrier
    half_run = LINE // 2 * channels
    opposite = (z // (LINE // 2)) ^ 1
    at = ((1 - side) * 2 + opposite) * half_run
    x_sent = lax.dynamic_slice_in_dim(w_x, at, half_run, axis=1)
    x_sent, hidden_in = tie((x_sent, hidden_in))
    x_far = across(x_sent)
    dt_rows = w_dt.T
    dt_cut = [dt_rows[:, at : at + 2 * STATE] for at in range(0, depth, 2 * STATE)]
    maps_sent = pick(w_bc, 1, 1 - side).reshape(depth, 2 * STATE)
    x_far, rest_sent = tie((x_far, jnp.concatenate([maps_sent, *dt_cut], axis=0)))
    rest_other = across(rest_sent)
    bc_own = pick(w_bc, 1, side).reshape(depth, 2 * STATE)

    def line_columns(m):
        return lax.dynamic_slice_in_dim(hidden_in, (z ^ m) * PAIR * depth, PAIR * depth, axis=1)

    arrived = [line_columns(0)]
    for m in range(1, LINE):
        arrived.append(along(line_columns(m), [(s, s ^ m) for s in range(LINE)]))
    stacked = jnp.stack(arrived)
    beyond_pair = across(stacked)
    beyond_pair, small, start_state, bc_own, dt_rows = tie(
        (beyond_pair, small, start_state, bc_own, dt_rows)
    )
    rows = []
    for mine in (stacked, beyond_pair):
        ours = [mine]
        for j in range(1, ranks):
            bit = j & -j
            pairs = [(t, t ^ bit) for t in range(ranks)]
            ours.append(lax.ppermute(ours[j - bit], "tensor", pairs))
        rows.extend(ours)

    start, end = (0, LINE - 1)
    at_end = (z == start) | (z == end)
    next_start, next_end = (1, LINE - 2)
    inward = [(start, next_start), (end, next_end)]
    outward = [(next_start, start), (next_end, end)]
    middle = [(next_start, next_end), (next_end, next_start)]
    over_middle = [(next_start, end), (next_end, start)]
    beside_pairs = [(s, s ^ 1) for s in range(LINE)]
    weights = (x_far, bc_own, dt_rows, rest_other)
    over, far, mine, near, mine_sent, near_sent, maps, largest = project(
        place, factor, rows, w_x, weights
    )

    map_hop = along(maps, inward)
    hop_far = along(far, inward)
    hop_over = along(over, inward)
    near = onward(near, across(near_sent))
    got_mine = across(mine_sent)
    near_out = along(near, outward)
    map_sum = (maps.astype(f32) + map_hop.astype(f32)).astype(bf16)
    map_far = along(map_sum, middle)
    map_done = ((map_sum.astype(f32) + map_far.astype(f32)) * in_scale).astype(bf16)
    sent_end = onward(over, hop_far)
    got_end = along(sent_end, over_middle)
    near, unused = tie((near, sent_end))
    near_in = along(near, inward)
    hop_over, near_out, unused = tie((hop_over, near_out, sent_end))
    sent_next = onward(far, hop_over)
    got_next = along(sent_next, middle)
    got_end, near_in = tie((got_end, near_in))
    near_sum = onward(mine, got_mine, near_out, near_in)
    map_done, unused = tie((map_done, sent_next))
    map_done = along(map_done, outward)
    gained = scan(
        place,
        in_scale,
        [near_sum, got_end, got_next],
        [map_sum, map_far, map_done],
        small,
        largest,
        start_state,
    )

    tokens = gained.shape[0] - 2 * ROWS
    beside = along(gained, beside_pairs)
    facing = along(gained, middle)
    second = jnp.where(at_end, along(facing, outward), facing)
    beyond = along(beside, middle)
    third = jnp.where(at_end, along(beyond, outward), beyond)
    far_own = across(gained)
    far_beside = across(beside)
    second, far_own = tie((second, far_own))
    far_second = across(second)
    third, far_beside = tie((third, far_beside))
    far_third = across(third)
    two, three = (jnp.where(at_end, 2, 3), jnp.where(at_end, 3, 2))

    def rows_for(x, m):
        at = ((side ^ x) * LINE + (z ^ m)) * channels
        return lax.dynamic_slice_in_dim(w_out, at, channels, axis=0)

    total = None
    tails = [far_third[tokens:]]
    for x, m, piece in (
        (0, 0, gained),
        (1, 0, far_own),
        (0, 1, beside),
        (1, 1, far_beside),
        (0, two, second),
        (1, two, far_second),
        (0, three, third),
    ):
        product = jnp.dot(piece, rows_for(x, m), preferred_element_type=f32)
        total = product if total is None else total + product
        tails.append(piece[tokens:])
    total, far_third = tie((total, far_third))
    last_rows = rows_for(1, three)
    tails = [tail.astype(f32) for tail in tails]
    squares = sum(tail[:ROWS, :SPAN] + tail[:ROWS, SPAN:] for tail in tails)
    top = functools.reduce(jnp.maximum, [tail[ROWS:, :SPAN] for tail in tails])

    def run_of(array, index, run):
        return lax.dynamic_slice_in_dim(array, index * run, run, axis=0)

    def first_sum(index):
        block, so_far = (run_of(far_third, index, run), run_of(total, index, run))
        return so_far + jnp.dot(block, last_rows, preferred_element_type=f32)

    run = tokens // 2
    keeps = rank % 2
    pairs = [(t, t ^ 1) for t in range(ranks)]
    received = lax.ppermute(first_sum(1 - keeps).astype(bf16), "tensor", pairs)
    kept = first_sum(keeps)
    bit = 2
    while bit < ranks:
        run //= 2
        keeps = (rank // bit) % 2
        pairs = [(t, t ^ bit) for t in range(ranks)]
        sent = run_of(kept, 1 - keeps, run) + run_of(received, 1 - keeps, run).astype(f32)
        kept = run_of(kept, keeps, run) + run_of(received, keeps, run).astype(f32)
        sent = sent.astype(bf16)
        squares = squares + lax.ppermute(squares, "tensor", pairs)
        squares, unused = tie((squares, sent))
        received = lax.ppermute(sent, "tensor", pairs)
        bit *= 2
    squares = squares + lax.ppermute(squares, "tensor", [(t, t ^ 1) for t in range(ranks)])
    mean_sq = squares.reshape(count, ranks, own) / (HEADS * HEAD_DIM)
    factors = lax.rsqrt(pick(mean_sq, 1, rank) + epsilon)
    final = (kept + received.astype(f32)).reshape(count, own, -1) * factors[:, :, None]
    final = lax.all_to_all(final.astype(bf16), "seq", split_axis=0, concat_axis=0, tiled=True)
    layer_out = final.transpose(1, 0, 2).reshape(own, count * final.shape[2])
    return (layer_out, jnp.max(top))


def solution(mesh):
    return jax.shard_map(
        by_heads if splits(mesh) else by_tokens,
        mesh=mesh,
        in_specs=(
            P(("seq", "tensor"), None),
            P(),
            P("seq", "tensor"),
            P("seq", "tensor", None, None),
            P("seq", "tensor"),
            P(None, "tensor"),
            P(None, "tensor", None, None),
            P(None, "tensor"),
            P(None, "tensor", None, None),
            P("tensor"),
            P("tensor"),
            P("tensor"),
            P("tensor", None, None),
            P("tensor"),
            P("tensor", "seq"),
        ),
        out_specs=(P(("seq", "tensor"), None), P()),
        check_vma=False,
    )
```

```python
import functools

import jax
import jax.numpy as jnp
from jax import lax
from jax.experimental import pallas as pl
from jax.experimental.pallas import tpu as pltpu
from jax.sharding import PartitionSpec as P

HEADS = 128
HEAD_DIM = 64
STATE = 128
GROUPS = 8
KERNEL = 4
SPAN = 128


epsilon = 1e-05
quant_range = 448.0


def from_behind(value, axis, steps):
    count = lax.axis_size(axis)
    first, last = (max(0, -steps), min(count, count - steps))
    return lax.ppermute(value, axis, [(source, source + steps) for source in range(first, last)])


def carried_in(shard, axis, combine, identity):
    count, here = (lax.axis_size(axis), lax.axis_index(axis))
    everything = jax.tree.map(
        lambda part, kind: lax.all_gather(part.astype(kind), axis),
        shard,
        (jnp.bfloat16, jnp.bfloat16),
    )
    start = jax.tree.map(
        lambda part, zero: jnp.broadcast_to(jnp.asarray(zero, part.dtype), part.shape),
        shard,
        identity,
    )

    def turn(k, before):
        reached = k < here
        new = combine(
            before, jax.tree.map(lambda part, own: part[k].astype(own.dtype), everything, shard)
        )
        return jax.tree.map(lambda a, b: jnp.where(reached, a, b), new, before)

    return lax.fori_loop(0, count, turn, start)


def depthwise(before, projected, conv_taps, length):
    extended = jnp.concatenate([before, projected], axis=0)
    summed = conv_taps[0] * extended[0:length]
    for offset in range(1, KERNEL):
        summed = summed + conv_taps[offset] * extended[offset : offset + length]
    return jax.nn.silu(summed).astype(jnp.bfloat16)


def combine(earlier, later):
    return (earlier[0] * later[0], later[0][:, None, None] * earlier[1] + later[1])


def by_tokens(
    hidden_in,
    prev_amax,
    w_x,
    w_bc,
    w_dt,
    conv_x,
    conv_bc,
    conv_state_x,
    conv_state_bc,
    dt_bias,
    decay_rate,
    skip,
    init_state,
    norm_gain,
    w_out,
):
    margin = KERNEL - 1
    gathered = lax.all_gather(hidden_in, "tensor", axis=0, tiled=True)
    abs_max = lax.pmax(jnp.max(jnp.abs(gathered.astype(jnp.float32))), "seq")
    in_scale = prev_amax / quant_range
    leading = lax.axis_index("seq") == 0
    row_count = gathered.shape[0]
    bc_width = w_bc.shape[1] * w_bc.shape[2] * w_bc.shape[3]
    bc_rows = jnp.reshape(w_bc, (w_bc.shape[0], bc_width))
    scaled = gathered.astype(jnp.float32) * (quant_range / prev_amax)
    quant = jnp.clip(scaled, -quant_range, quant_range).astype(jnp.bfloat16)
    pieces = (
        lax.all_gather(w_x, "seq", axis=0, tiled=True),
        lax.all_gather(bc_rows, "seq", axis=0, tiled=True),
        lax.all_gather(w_dt, "seq", axis=0, tiled=True),
    )
    x_proj, bc_proj, dt_proj = tuple(
        (
            jnp.dot(quant, weight_piece, preferred_element_type=jnp.float32)
            for weight_piece in pieces
        )
    )
    x_whole = (x_proj * in_scale).astype(jnp.bfloat16)
    bc_whole = (bc_proj * in_scale).astype(jnp.bfloat16)
    dt_raw = dt_proj * in_scale
    state_bc = jnp.reshape(conv_state_bc, (margin, bc_width))
    received = from_behind(
        (x_whole[row_count - margin :], bc_whole[row_count - margin :]), "seq", 1
    )
    x_edge = jnp.where(leading, conv_state_x, received[0])
    bc_edge = jnp.where(leading, state_bc, received[1])
    x_act = depthwise(x_edge, x_whole, conv_x, row_count)
    bc_act = depthwise(bc_edge, bc_whole, jnp.reshape(conv_bc, (KERNEL, bc_width)), row_count)
    step_size = jax.nn.softplus(dt_raw + dt_bias)
    heads_here = step_size.shape[1]
    groups_here = w_bc.shape[1]
    per_group = HEADS // GROUPS
    blocks = row_count // SPAN
    x_blocks = x_act.reshape(blocks, SPAN, heads_here, HEAD_DIM)
    bc_blocks = bc_act.reshape(blocks, SPAN, groups_here, 2, STATE)
    in_map = bc_blocks[:, :, :, 0]
    out_map = bc_blocks[:, :, :, 1]
    step_blocks = step_size.reshape(blocks, SPAN, heads_here)
    cum_blocks = jnp.cumsum(-step_blocks * decay_rate, axis=1)
    index_row = jnp.arange(SPAN, dtype=jnp.int32)
    lower_mask = index_row[:, None] >= index_row[None, :]
    intersection = jnp.einsum(
        "ctgn,cugn->cgtu", out_map, in_map, preferred_element_type=jnp.float32
    )
    intersection = jnp.repeat(intersection, per_group, axis=1)
    cum_heads = jnp.transpose(cum_blocks, (0, 2, 1))
    log_gap = cum_heads[:, :, :, None] - cum_heads[:, :, None, :]
    decay = jnp.exp(jnp.where(lower_mask[None, None], log_gap, -1e30))
    step_heads = jnp.transpose(step_blocks, (0, 2, 1))
    weights = (intersection * decay * step_heads[:, :, None, :]).astype(jnp.bfloat16)
    local_part = jnp.einsum(
        "chtu,cuhp->cthp", weights, x_blocks, preferred_element_type=jnp.float32
    )
    last_cum = cum_blocks[:, SPAN - 1, :]
    x_weighted = (
        x_blocks.astype(jnp.float32)
        * (step_blocks * jnp.exp(last_cum[:, None, :] - cum_blocks))[:, :, :, None]
    ).astype(jnp.bfloat16)
    in_heads = jnp.repeat(in_map, per_group, axis=2)
    added = jnp.einsum("cuhp,cuhn->chpn", x_weighted, in_heads, preferred_element_type=jnp.float32)

    def carry_on(carried, element):
        block_decay, block_added = element
        return (block_decay[:, None, None] * carried + block_added, carried)

    empty_state = jnp.zeros((heads_here, HEAD_DIM, STATE), jnp.float32)
    device_state, entering = lax.scan(carry_on, empty_state, (jnp.exp(last_cum), added))
    device_decay = jnp.exp(jnp.sum(last_cum, axis=0))
    seeded = device_state + jnp.where(leading, device_decay[:, None, None] * init_state, 0.0)
    identity = (jnp.ones_like(device_decay), jnp.zeros_like(device_state))
    scanned = carried_in((device_decay, seeded), "seq", combine, identity)
    incoming = jnp.where(leading, init_state, scanned[1])
    prefix = jnp.exp(jnp.cumsum(last_cum, axis=0) - last_cum)
    states_in = entering + prefix[:, :, None, None] * incoming[None]
    out_heads = jnp.repeat(out_map, per_group, axis=2).astype(jnp.float32)
    carried_part = (
        jnp.einsum("cthn,chpn->cthp", out_heads, states_in, precision=lax.Precision.HIGHEST)
        * jnp.exp(cum_blocks)[:, :, :, None]
    )
    ssm_out = local_part + carried_part + skip[None, None, :, None] * x_blocks.astype(jnp.float32)
    ssm_out = ssm_out.reshape(row_count, heads_here * HEAD_DIM)
    squares = lax.psum(jnp.sum(ssm_out * ssm_out, axis=1), "tensor")
    mean_sq = squares / (HEADS * HEAD_DIM)
    normed = (ssm_out * lax.rsqrt(mean_sq + epsilon)[:, None] * norm_gain).astype(jnp.bfloat16)
    partial_out = jnp.dot(
        normed, lax.all_gather(w_out, "seq", axis=1, tiled=True), preferred_element_type=jnp.float32
    )
    layer_out = lax.psum_scatter(
        partial_out.astype(jnp.bfloat16), "tensor", scatter_dimension=0, tiled=True
    )
    return (layer_out, abs_max)


PAIR = 2
LINE = 4
ROWS = 8
CUTS = 2
SMEM = pl.BlockSpec(memory_space=pltpu.SMEM)
VMEM = pl.BlockSpec(memory_space=pltpu.VMEM)
HIGHEST = lax.Precision.HIGHEST


def splits(mesh):
    count, ranks = (mesh.shape["seq"], mesh.shape["tensor"])
    heads_all, groups_here = (HEADS // ranks, GROUPS // ranks)
    if count != PAIR * LINE or groups_here != PAIR or ranks & (ranks - 1):
        return False
    heads_here = heads_all // count
    return 2 * heads_here == ROWS and heads_here * HEAD_DIM == 2 * SPAN


def nt_dot(a, b, **kw):
    return lax.dot_general(
        a, b, (((1,), (1,)), ((), ())), preferred_element_type=jnp.float32, **kw
    )


def project_kernel(ranks, place_ref, factor_ref, *refs):
    hidden = [refs[x * ranks : (x + 1) * ranks] for x in range(PAIR)]
    refs = refs[PAIR * ranks :]
    own_x, x_far, own_bc, own_dt, rest = refs[:5]
    far_refs, near_refs, sent_refs = (
        refs[5 + at : 5 + at + LINE // 2] for at in range(0, 3 * LINE // 2, LINE // 2)
    )
    bc_ref, largest_ref, quant_ref, near_dt, all_dt = refs[5 + 3 * LINE // 2 :]
    side, z = (place_ref[1], place_ref[2])
    factor = factor_ref[0]
    depth = own_x.shape[0]
    largest = None
    for x in range(PAIR):
        for k in range(LINE):
            block = (k ^ z) * PAIR + (side ^ x)
            for j in range(ranks):
                for half in range(PAIR):
                    cut = slice(half * depth, (half + 1) * depth)
                    values = hidden[x][j][k, :, cut].astype(jnp.float32)
                    scaled = jnp.clip(values * factor, -quant_range, quant_range)
                    quant_ref[half, block, j] = scaled.astype(jnp.bfloat16)
                    top = jnp.max(jnp.abs(values).reshape(-1, ROWS, depth), axis=0)
                    largest = top if largest is None else jnp.maximum(largest, top)
    step_rows = own_dt.shape[0]
    other_dt = jnp.concatenate(
        [rest[at : at + step_rows] for at in range(depth, rest.shape[0], step_rows)], axis=1
    )
    width = largest_ref.shape[1]
    top = largest[:, :width]
    for at in range(width, depth, width):
        top = jnp.maximum(top, largest[:, at : at + width])
    largest_ref[...] = top

    channels = near_refs[0].shape[1]
    tokens = bc_ref.shape[0]
    rows = tokens // CUTS
    blocks = quant_ref.shape[1] // CUTS
    extra = rows // channels * ROWS
    upper = lax.broadcasted_iota(jnp.int32, (ROWS, channels), 0) < ROWS // 2

    def steps_of(dt_ref, run):
        dt = dt_ref[run // 2]
        pieces = []
        for at in range(0, rows, channels):
            piece = dt[:, at : at + channels]
            turned = pltpu.roll(piece, ROWS // 2, 0)
            lower_run = jnp.where(upper, piece, turned)
            upper_run = jnp.where(upper, turned, piece)
            pieces.append(split_parts(jnp.where(run % 2 == 0, lower_run, upper_run), upper))
        return jnp.concatenate(pieces, axis=0).astype(jnp.bfloat16)

    def columns(run):
        return pl.ds(pl.multiple_of(run * channels, channels), channels)

    for cut in range(CUTS):
        part = slice(cut * blocks, (cut + 1) * blocks)
        near = quant_ref[side, part].reshape(rows, depth)
        far = quant_ref[1 - side, part].reshape(rows, depth)

        def both(own, other):
            return jnp.dot(near, own, preferred_element_type=jnp.float32) + jnp.dot(
                far, other, preferred_element_type=jnp.float32
            )

        at_rows = slice(cut * rows, (cut + 1) * rows)
        extra_rows = slice(tokens + cut * extra, tokens + (cut + 1) * extra)
        ours = nt_dot(own_dt[...], near)
        near_dt[...] = ours.reshape(near_dt.shape)
        all_dt[...] = (ours + nt_dot(other_dt, far)).reshape(all_dt.shape)
        bc_ref[at_rows] = both(own_bc[...], rest[:depth]).astype(jnp.bfloat16)
        for m in range(LINE // 2):
            owner = z ^ (m + LINE // 2)
            run = side * LINE + owner
            other = x_far[:, columns(owner % (LINE // 2))]
            far_refs[m][at_rows] = both(own_x[:, columns(run)], other).astype(jnp.bfloat16)
            far_refs[m][extra_rows] = steps_of(all_dt, run)
            for out_refs, way in ((near_refs, side), (sent_refs, 1 - side)):
                run = way * LINE + (z ^ m)
                product = jnp.dot(near, own_x[:, columns(run)], preferred_element_type=jnp.float32)
                out_refs[m][at_rows] = product.astype(jnp.bfloat16)
                out_refs[m][extra_rows] = steps_of(near_dt, run)


def split_parts(values, upper):
    top = values.astype(jnp.bfloat16).astype(jnp.float32)
    return jnp.where(upper, top, values - top)


def project(place, factor, hidden, w_x, weights):
    line, own, wide = hidden[0].shape
    ranks = len(hidden) // PAIR
    depth, x_wide = (weights[0].shape[0], 2 * weights[0].shape[1])
    channels, maps_wide = (x_wide // LINE, weights[1].shape[1])
    tokens = line * PAIR * ranks * own
    extra = tokens // channels * ROWS
    dt_shape = (weights[2].shape[0] // ROWS, ROWS, tokens // CUTS)
    payload = jax.ShapeDtypeStruct((tokens + extra, channels), jnp.bfloat16)
    maps = jax.ShapeDtypeStruct((tokens, maps_wide), jnp.bfloat16)
    largest = jax.ShapeDtypeStruct((ROWS, 128), jnp.float32)
    outs = [payload] * (LINE + LINE // 2) + [maps, largest]
    return pl.pallas_call(
        functools.partial(project_kernel, ranks),
        in_specs=[SMEM, SMEM] + [VMEM] * (len(hidden) + 1 + len(weights)),
        out_specs=[VMEM] * len(outs),
        scratch_shapes=[
            pltpu.VMEM((PAIR, line * PAIR, ranks, own, depth), jnp.bfloat16),
            pltpu.VMEM(dt_shape, jnp.float32),
            pltpu.VMEM(dt_shape, jnp.float32),
        ],
        out_shape=outs,
        compiler_params=pltpu.CompilerParams(vmem_limit_bytes=32 * 2**20),
        cost_estimate=pl.CostEstimate(
            flops=2 * tokens * wide * (x_wide + maps_wide),
            bytes_accessed=2 * tokens * (wide + x_wide),
            transcendentals=0,
        ),
        name="project",
    )(place, factor, *hidden, w_x, *weights)


def onward_kernel(*refs):
    share_refs, out_ref = (refs[:-1], refs[-1])
    rows, channels = out_ref.shape
    tokens = rows * channels // (channels + ROWS)
    total = sum(ref[:tokens].astype(jnp.float32) for ref in share_refs)
    out_ref[:tokens] = total.astype(jnp.bfloat16)
    upper = lax.broadcasted_iota(jnp.int32, (ROWS, channels), 0) < ROWS // 2
    extra = sum(ref[tokens:].astype(jnp.float32) for ref in share_refs)
    pieces = []
    for at in range(0, rows - tokens, ROWS):
        piece = extra[at : at + ROWS]
        pieces.append(split_parts(piece + pltpu.roll(piece, ROWS // 2, 0), upper))
    out_ref[tokens:] = jnp.concatenate(pieces, axis=0).astype(jnp.bfloat16)


def onward(*shares):
    own = shares[0]
    return pl.pallas_call(
        onward_kernel,
        in_specs=[VMEM] * len(shares),
        out_specs=VMEM,
        out_shape=jax.ShapeDtypeStruct(own.shape, own.dtype),
        compiler_params=pltpu.CompilerParams(vmem_limit_bytes=8 * 2**20),
        cost_estimate=pl.CostEstimate(
            flops=len(shares) * own.size,
            bytes_accessed=2 * (len(shares) + 1) * own.size,
            transcendentals=0,
        ),
        name="onward",
    )(*shares)


def turned_rank(rank, ranks):
    turned = 0
    while ranks > 1:
        turned, rank, ranks = (2 * turned + rank % 2, rank // 2, ranks // 2)
    return turned


def scan_kernel(place_ref, scale_ref, *refs):
    x_refs, bc_refs = (refs[:-9], refs[-9:-6])
    small_ref, largest_ref, state_ref, out_ref, x_buf, bc_buf = refs[-6:]
    tokens, channels = bc_refs[0].shape
    blocks = tokens // SPAN
    heads = channels // HEAD_DIM
    rank, z = (place_ref[0], place_ref[2])
    ranks = place_ref.shape[0] - 3
    own = SPAN // ranks
    edge = ROWS
    in_scale = scale_ref[0]
    at_end = (z == 0) | (z == LINE - 1)
    x_buf[:edge] = small_ref[:edge]
    bc_buf[:edge] = small_ref[edge : 2 * edge]
    state = state_ref[...].T

    for block in range(blocks):
        for true_rank in range(ranks):
            source = block * SPAN + (true_rank ^ rank) * own
            source = pl.ds(pl.multiple_of(source, own), own)
            at = edge + block * SPAN + true_rank * own
            at = slice(at, at + own)
            total = sum(ref[source].astype(jnp.float32) for ref in x_refs) * in_scale
            x_buf[at] = total.astype(jnp.bfloat16).astype(jnp.float32)
            near, far, done = (ref[source].astype(jnp.float32) for ref in bc_refs)
            total = ((near + far) * in_scale).astype(jnp.bfloat16).astype(jnp.float32)
            bc_buf[at] = jnp.where(at_end, done, total)

    taps = 2 * edge

    def activate(buf, row, block):
        start = edge - (KERNEL - 1) + block * SPAN
        summed = small_ref[row : row + 1] * buf[start : start + SPAN]
        for k in range(1, KERNEL):
            summed = summed + small_ref[row + k : row + k + 1] * buf[start + k : start + k + SPAN]
        return (summed / (1.0 + jnp.exp(-summed))).astype(jnp.bfloat16)

    skip = small_ref[taps + 2 * KERNEL : taps + 2 * KERNEL + 1]
    gain = small_ref[taps + 2 * KERNEL + 1 : taps + 2 * KERNEL + 2]
    bias = small_ref[4 * edge :, :SPAN]
    rate = small_ref[4 * edge :, SPAN:]

    up = lax.broadcasted_iota(jnp.int32, (SPAN, SPAN), 0)
    across = lax.broadcasted_iota(jnp.int32, (SPAN, SPAN), 1)
    together = SPAN // HEAD_DIM
    insides = [
        ((across >= h * HEAD_DIM) & (across < (h + 1) * HEAD_DIM))
        .astype(jnp.float32)
        .astype(jnp.bfloat16)
        for h in range(together)
    ]
    lower = up >= across
    upper = (up <= across).astype(jnp.float32)
    lanes = across[:ROWS]

    dt = sum(ref[tokens:].astype(jnp.float32) for ref in x_refs)
    steps = []
    wide = channels // SPAN
    for block in range(blocks):
        tile = dt[block // wide * ROWS : (block // wide + 1) * ROWS]
        cut = tile[:, block % wide * SPAN : (block % wide + 1) * SPAN]
        cut = (cut + pltpu.roll(cut, ROWS // 2, 0)) * in_scale
        bit = 1
        while bit < ranks:
            shift = bit * own
            flipped = jnp.where(
                (lanes // shift) % 2 == 1,
                pltpu.roll(cut, shift, 1),
                pltpu.roll(cut, SPAN - shift, 1),
            )
            cut = jnp.where((rank & bit) != 0, flipped, cut)
            bit *= 2
        raw = cut + bias
        steps.append(jnp.maximum(raw, 0.0) + jnp.log1p(jnp.exp(-jnp.abs(raw))))
    drops = jnp.concatenate([-step * rate for step in steps], axis=0)
    cums = jnp.dot(drops, upper, precision=HIGHEST, preferred_element_type=jnp.float32)

    sums = jnp.zeros((SPAN, SPAN), jnp.float32)
    for block in range(blocks):
        x_act = activate(x_buf, taps, block)
        bc_act = activate(bc_buf, taps + KERNEL, block)
        in_map, out_map = (bc_act[:, :STATE], bc_act[:, STATE:])
        step, cum = (steps[block], cums[block * ROWS : (block + 1) * ROWS])
        last = cum[:, SPAN - 1 : SPAN]
        turned = jnp.concatenate(
            [
                cum,
                step * jnp.exp(last - cum),
                jnp.exp(cum),
                jnp.zeros((SPAN - 3 * ROWS, SPAN), jnp.float32),
            ],
            axis=0,
        ).T

        def spread(row):
            tiles = []
            for first in range(row, row + heads, together):
                tile = jnp.broadcast_to(turned[:, first : first + 1], across.shape)
                for h in range(1, together):
                    column = turned[:, first + h : first + h + 1]
                    tile = jnp.where(across >= h * HEAD_DIM, column, tile)
                tiles.append(tile)
            return jnp.concatenate(tiles, axis=1)

        inner = jnp.where(lower, nt_dot(out_map, in_map), 0.0)
        x_wide = x_act.astype(jnp.float32)
        local_tiles = []
        for first in range(0, heads, together):
            weights, spaced = ([], [])
            tile = x_act[:, first * HEAD_DIM : (first + together) * HEAD_DIM]
            for h in range(first, first + together):
                gap = jnp.where(lower, turned[:, h : h + 1] - cum[h : h + 1], 0.0)
                weights.append((inner * jnp.exp(gap) * step[h : h + 1]).astype(jnp.bfloat16))
                spaced.append(tile * insides[h - first])
            local_tiles.append(
                jnp.dot(
                    jnp.concatenate(weights, axis=1),
                    jnp.concatenate(spaced, axis=0),
                    preferred_element_type=jnp.float32,
                )
            )
        local_part = jnp.concatenate(local_tiles, axis=1)
        grown = spread(2 * ROWS)
        x_weighted = (x_wide * spread(ROWS)).astype(jnp.bfloat16)
        added = lax.dot_general(
            in_map, x_weighted, (((0,), (0,)), ((), ())), preferred_element_type=jnp.float32
        )
        high = state.astype(jnp.bfloat16)
        rest = (state - high.astype(jnp.float32)).astype(jnp.bfloat16)
        carried = jnp.dot(
            jnp.concatenate([out_map, out_map], axis=1),
            jnp.concatenate([high, rest], axis=0),
            preferred_element_type=jnp.float32,
        )
        ssm_out = local_part + grown * carried + skip * x_wide
        state = grown[SPAN - 1 : SPAN] * state + added
        gained = (ssm_out * gain).astype(jnp.bfloat16)
        for true_rank in range(ranks):
            at = (turned_rank(true_rank, ranks) * blocks + block) * own
            out_ref[at : at + own] = gained[true_rank * own : (true_rank + 1) * own]
        summed = jnp.sum(ssm_out * ssm_out, axis=1, keepdims=True)
        sums = jnp.where(across == block, summed, sums)

    whole = sums.T[:ROWS]
    top = whole.astype(jnp.bfloat16).astype(jnp.float32)
    largest = jnp.broadcast_to(jnp.max(largest_ref[...]), (ROWS, channels))
    extra = jnp.concatenate([jnp.concatenate([top, whole - top], axis=1), largest], axis=0)
    out_ref[tokens:] = extra.astype(jnp.bfloat16)


def scan(place, in_scale, sums, maps, small, largest, state):
    channels = sums[0].shape[1]
    tokens = maps[0].shape[0]

    out = jax.ShapeDtypeStruct((tokens + 2 * ROWS, channels), jnp.bfloat16)
    return pl.pallas_call(
        scan_kernel,
        in_specs=[SMEM, SMEM] + [VMEM] * (len(sums) + len(maps) + 3),
        out_specs=VMEM,
        scratch_shapes=[
            pltpu.VMEM((tokens + ROWS, channels), jnp.float32),
            pltpu.VMEM((tokens + ROWS, 2 * STATE), jnp.float32),
        ],
        out_shape=out,
        compiler_params=pltpu.CompilerParams(vmem_limit_bytes=20 * 2**20),
        cost_estimate=pl.CostEstimate(
            flops=8 * tokens * SPAN * channels,
            bytes_accessed=8 * tokens * channels,
            transcendentals=tokens * (channels + 8 * SPAN),
        ),
        name="scan",
    )(place, in_scale, *sums, *maps, small, largest, state)


def by_heads(
    hidden_in,
    prev_amax,
    w_x,
    w_bc,
    w_dt,
    conv_x,
    conv_bc,
    conv_state_x,
    conv_state_bc,
    dt_bias,
    decay_rate,
    skip,
    init_state,
    norm_gain,
    w_out,
):
    margin = KERNEL - 1
    count, here = (lax.axis_size("seq"), lax.axis_index("seq"))
    ranks, rank = (lax.axis_size("tensor"), lax.axis_index("tensor"))
    z, side = (here // PAIR, here % PAIR)
    place_of = side * LINE + z
    f32, bf16 = (jnp.float32, jnp.bfloat16)
    own, width = hidden_in.shape
    depth = w_x.shape[0]
    channels = w_x.shape[1] // count
    heads_here = w_dt.shape[1] // count
    in_scale = (prev_amax / quant_range).reshape(1)
    factor = (quant_range / prev_amax).reshape(1)
    place = jnp.stack([rank, side, z] + [rank] * ranks).astype(jnp.int32)

    def pick(array, axis, index):
        return lax.dynamic_index_in_dim(array, index, axis, keepdims=False)

    def along(value, pairs):
        moves = [(a * PAIR + x, b * PAIR + x) for a, b in pairs for x in range(PAIR)]
        return lax.ppermute(value, "seq", moves)

    def across(value):
        return lax.ppermute(value, "seq", [(s, s ^ 1) for s in range(count)])

    def of_heads(array):
        return jnp.repeat(array, HEAD_DIM)[None]

    by_channel = jnp.concatenate(
        [conv_state_x.astype(f32), conv_x, of_heads(skip), norm_gain[None]], axis=0
    )
    by_channel = lax.dynamic_slice_in_dim(by_channel, place_of * channels, channels, axis=1)
    by_map = jnp.concatenate([conv_state_bc.astype(f32), conv_bc], axis=0)
    by_map = pick(by_map, 1, side).reshape(margin + KERNEL, 2 * STATE)
    by_head = jnp.stack([dt_bias, decay_rate]).reshape(2, count, heads_here)
    by_head = jnp.tile(pick(by_head, 1, place_of).T, (ROWS // heads_here, 1))
    by_head = jnp.repeat(by_head, SPAN, axis=1)
    blank = jnp.zeros((ROWS - margin, channels), f32)
    small = jnp.concatenate(
        [
            blank,
            by_channel[:margin],
            blank,
            by_map[:margin],
            by_channel[margin : margin + KERNEL],
            by_map[margin:],
            by_channel[margin + KERNEL :],
            jnp.zeros((2 * ROWS - 2 * KERNEL - 2, channels), f32),
            by_head,
        ],
        axis=0,
    )

    start_state = lax.dynamic_slice_in_dim(
        init_state, place_of * heads_here, heads_here, axis=0
    ).reshape(channels, STATE)

    tie = lax.optimization_barrier
    half_run = LINE // 2 * channels
    opposite = (z // (LINE // 2)) ^ 1
    at = ((1 - side) * 2 + opposite) * half_run
    x_sent = lax.dynamic_slice_in_dim(w_x, at, half_run, axis=1)
    x_sent, hidden_in = tie((x_sent, hidden_in))
    x_far = across(x_sent)
    dt_rows = w_dt.T
    dt_cut = [dt_rows[:, at : at + 2 * STATE] for at in range(0, depth, 2 * STATE)]
    maps_sent = pick(w_bc, 1, 1 - side).reshape(depth, 2 * STATE)
    rest_other = across(jnp.concatenate([maps_sent, *dt_cut], axis=0))
    bc_own = pick(w_bc, 1, side).reshape(depth, 2 * STATE)

    def line_columns(m):
        return lax.dynamic_slice_in_dim(hidden_in, (z ^ m) * PAIR * depth, PAIR * depth, axis=1)

    arrived = [line_columns(0)]
    for m in range(1, LINE):
        arrived.append(along(line_columns(m), [(s, s ^ m) for s in range(LINE)]))
    stacked = jnp.stack(arrived)
    beyond_pair = across(stacked)
    beyond_pair, small, start_state, bc_own, dt_rows = tie(
        (beyond_pair, small, start_state, bc_own, dt_rows)
    )
    rows = []
    for mine in (stacked, beyond_pair):
        ours = [mine]
        for j in range(1, ranks):
            bit = j & -j
            pairs = [(t, t ^ bit) for t in range(ranks)]
            ours.append(lax.ppermute(ours[j - bit], "tensor", pairs))
        rows.extend(ours)

    start, end = (0, LINE - 1)
    at_end = (z == start) | (z == end)
    next_start, next_end = (1, LINE - 2)
    inward = [(start, next_start), (end, next_end)]
    outward = [(next_start, start), (next_end, end)]
    middle = [(next_start, next_end), (next_end, next_start)]
    over_middle = [(next_start, end), (next_end, start)]
    beside_pairs = [(s, s ^ 1) for s in range(LINE)]
    weights = (x_far, bc_own, dt_rows, rest_other)
    over, far, mine, near, mine_sent, near_sent, maps, largest = project(
        place, factor, rows, w_x, weights
    )

    map_hop = along(maps, inward)
    hop_far = along(far, inward)
    hop_over = along(over, inward)
    near = onward(near, across(near_sent))
    got_mine = across(mine_sent)
    near_out = along(near, outward)
    map_sum = (maps.astype(f32) + map_hop.astype(f32)).astype(bf16)
    map_far = along(map_sum, middle)
    map_done = ((map_sum.astype(f32) + map_far.astype(f32)) * in_scale).astype(bf16)
    sent_end = onward(over, hop_far)
    got_end = along(sent_end, over_middle)
    near, unused = tie((near, sent_end))
    near_in = along(near, inward)
    hop_over, near_out, unused = tie((hop_over, near_out, sent_end))
    sent_next = onward(far, hop_over)
    got_next = along(sent_next, middle)
    got_end, near_in = tie((got_end, near_in))
    near_sum = onward(mine, got_mine, near_out, near_in)
    map_done, unused = tie((map_done, sent_next))
    map_done = along(map_done, outward)
    gained = scan(
        place,
        in_scale,
        [near_sum, got_end, got_next],
        [map_sum, map_far, map_done],
        small,
        largest,
        start_state,
    )

    tokens = gained.shape[0] - 2 * ROWS
    beside = along(gained, beside_pairs)
    facing = along(gained, middle)
    second = jnp.where(at_end, along(facing, outward), facing)
    beyond = along(beside, middle)
    third = jnp.where(at_end, along(beyond, outward), beyond)
    far_own = across(gained)
    far_beside = across(beside)
    second, far_own = tie((second, far_own))
    far_second = across(second)
    third, far_beside = tie((third, far_beside))
    far_third = across(third)
    two, three = (jnp.where(at_end, 2, 3), jnp.where(at_end, 3, 2))

    def rows_for(x, m):
        at = ((side ^ x) * LINE + (z ^ m)) * channels
        return lax.dynamic_slice_in_dim(w_out, at, channels, axis=0)

    total = None
    tails = [far_third[tokens:]]
    for x, m, piece in (
        (0, 0, gained),
        (1, 0, far_own),
        (0, 1, beside),
        (1, 1, far_beside),
        (0, two, second),
        (1, two, far_second),
        (0, three, third),
    ):
        product = jnp.dot(piece, rows_for(x, m), preferred_element_type=f32)
        total = product if total is None else total + product
        tails.append(piece[tokens:])
    total, far_third = tie((total, far_third))
    last_rows = rows_for(1, three)
    tails = [tail.astype(f32) for tail in tails]
    squares = sum(tail[:ROWS, :SPAN] + tail[:ROWS, SPAN:] for tail in tails)
    top = functools.reduce(jnp.maximum, [tail[ROWS:, :SPAN] for tail in tails])

    def run_of(array, index, run):
        return lax.dynamic_slice_in_dim(array, index * run, run, axis=0)

    def first_sum(index):
        block, so_far = (run_of(far_third, index, run), run_of(total, index, run))
        return so_far + jnp.dot(block, last_rows, preferred_element_type=f32)

    run = tokens // 2
    keeps = rank % 2
    pairs = [(t, t ^ 1) for t in range(ranks)]
    received = lax.ppermute(first_sum(1 - keeps).astype(bf16), "tensor", pairs)
    kept = first_sum(keeps)
    squares = squares + lax.ppermute(squares, "tensor", pairs)
    bit = 2
    while bit < ranks:
        run //= 2
        keeps = (rank // bit) % 2
        pairs = [(t, t ^ bit) for t in range(ranks)]
        sent = run_of(kept, 1 - keeps, run) + run_of(received, 1 - keeps, run).astype(f32)
        kept = run_of(kept, keeps, run) + run_of(received, keeps, run).astype(f32)
        received = lax.ppermute(sent.astype(bf16), "tensor", pairs)
        squares = squares + lax.ppermute(squares, "tensor", pairs)
        bit *= 2
    mean_sq = squares.reshape(count, ranks, own) / (HEADS * HEAD_DIM)
    factors = lax.rsqrt(pick(mean_sq, 1, rank) + epsilon)
    final = (kept + received.astype(f32)).reshape(count, own, -1) * factors[:, :, None]
    final = lax.all_to_all(final.astype(bf16), "seq", split_axis=0, concat_axis=0, tiled=True)
    layer_out = final.transpose(1, 0, 2).reshape(own, count * final.shape[2])
    return (layer_out, jnp.max(top))


def solution(mesh):
    return jax.shard_map(
        by_heads if splits(mesh) else by_tokens,
        mesh=mesh,
        in_specs=(
            P(("seq", "tensor"), None),
            P(),
            P("seq", "tensor"),
            P("seq", "tensor", None, None),
            P("seq", "tensor"),
            P(None, "tensor"),
            P(None, "tensor", None, None),
            P(None, "tensor"),
            P(None, "tensor", None, None),
            P("tensor"),
            P("tensor"),
            P("tensor"),
            P("tensor", None, None),
            P("tensor"),
            P("tensor", "seq"),
        ),
        out_specs=(P(("seq", "tensor"), None), P()),
        check_vma=False,
    )
```

```python
import functools

import jax
import jax.numpy as jnp
from jax import lax
from jax.experimental import pallas as pl
from jax.experimental.pallas import tpu as pltpu
from jax.sharding import PartitionSpec as P

HEADS = 128
HEAD_DIM = 64
STATE = 128
GROUPS = 8
KERNEL = 4
SPAN = 128


epsilon = 1e-05
quant_range = 448.0


def from_behind(value, axis, steps):
    count = lax.axis_size(axis)
    first, last = (max(0, -steps), min(count, count - steps))
    return lax.ppermute(value, axis, [(source, source + steps) for source in range(first, last)])


def carried_in(shard, axis, combine, identity):
    count, here = (lax.axis_size(axis), lax.axis_index(axis))
    everything = jax.tree.map(
        lambda part, kind: lax.all_gather(part.astype(kind), axis),
        shard,
        (jnp.bfloat16, jnp.bfloat16),
    )
    start = jax.tree.map(
        lambda part, zero: jnp.broadcast_to(jnp.asarray(zero, part.dtype), part.shape),
        shard,
        identity,
    )

    def turn(k, before):
        reached = k < here
        new = combine(
            before, jax.tree.map(lambda part, own: part[k].astype(own.dtype), everything, shard)
        )
        return jax.tree.map(lambda a, b: jnp.where(reached, a, b), new, before)

    return lax.fori_loop(0, count, turn, start)


def depthwise(before, projected, conv_taps, length):
    extended = jnp.concatenate([before, projected], axis=0)
    summed = conv_taps[0] * extended[0:length]
    for offset in range(1, KERNEL):
        summed = summed + conv_taps[offset] * extended[offset : offset + length]
    return jax.nn.silu(summed).astype(jnp.bfloat16)


def combine(earlier, later):
    return (earlier[0] * later[0], later[0][:, None, None] * earlier[1] + later[1])


def by_tokens(
    hidden_in,
    prev_amax,
    w_x,
    w_bc,
    w_dt,
    conv_x,
    conv_bc,
    conv_state_x,
    conv_state_bc,
    dt_bias,
    decay_rate,
    skip,
    init_state,
    norm_gain,
    w_out,
):
    margin = KERNEL - 1
    gathered = lax.all_gather(hidden_in, "tensor", axis=0, tiled=True)
    abs_max = lax.pmax(jnp.max(jnp.abs(gathered.astype(jnp.float32))), "seq")
    in_scale = prev_amax / quant_range
    leading = lax.axis_index("seq") == 0
    row_count = gathered.shape[0]
    bc_width = w_bc.shape[1] * w_bc.shape[2] * w_bc.shape[3]
    bc_rows = jnp.reshape(w_bc, (w_bc.shape[0], bc_width))
    scaled = gathered.astype(jnp.float32) * (quant_range / prev_amax)
    quant = jnp.clip(scaled, -quant_range, quant_range).astype(jnp.bfloat16)
    pieces = (
        lax.all_gather(w_x, "seq", axis=0, tiled=True),
        lax.all_gather(bc_rows, "seq", axis=0, tiled=True),
        lax.all_gather(w_dt, "seq", axis=0, tiled=True),
    )
    x_proj, bc_proj, dt_proj = tuple(
        (
            jnp.dot(quant, weight_piece, preferred_element_type=jnp.float32)
            for weight_piece in pieces
        )
    )
    x_whole = (x_proj * in_scale).astype(jnp.bfloat16)
    bc_whole = (bc_proj * in_scale).astype(jnp.bfloat16)
    dt_raw = dt_proj * in_scale
    state_bc = jnp.reshape(conv_state_bc, (margin, bc_width))
    received = from_behind(
        (x_whole[row_count - margin :], bc_whole[row_count - margin :]), "seq", 1
    )
    x_edge = jnp.where(leading, conv_state_x, received[0])
    bc_edge = jnp.where(leading, state_bc, received[1])
    x_act = depthwise(x_edge, x_whole, conv_x, row_count)
    bc_act = depthwise(bc_edge, bc_whole, jnp.reshape(conv_bc, (KERNEL, bc_width)), row_count)
    step_size = jax.nn.softplus(dt_raw + dt_bias)
    heads_here = step_size.shape[1]
    groups_here = w_bc.shape[1]
    per_group = HEADS // GROUPS
    blocks = row_count // SPAN
    x_blocks = x_act.reshape(blocks, SPAN, heads_here, HEAD_DIM)
    bc_blocks = bc_act.reshape(blocks, SPAN, groups_here, 2, STATE)
    in_map = bc_blocks[:, :, :, 0]
    out_map = bc_blocks[:, :, :, 1]
    step_blocks = step_size.reshape(blocks, SPAN, heads_here)
    cum_blocks = jnp.cumsum(-step_blocks * decay_rate, axis=1)
    index_row = jnp.arange(SPAN, dtype=jnp.int32)
    lower_mask = index_row[:, None] >= index_row[None, :]
    intersection = jnp.einsum(
        "ctgn,cugn->cgtu", out_map, in_map, preferred_element_type=jnp.float32
    )
    intersection = jnp.repeat(intersection, per_group, axis=1)
    cum_heads = jnp.transpose(cum_blocks, (0, 2, 1))
    log_gap = cum_heads[:, :, :, None] - cum_heads[:, :, None, :]
    decay = jnp.exp(jnp.where(lower_mask[None, None], log_gap, -1e30))
    step_heads = jnp.transpose(step_blocks, (0, 2, 1))
    weights = (intersection * decay * step_heads[:, :, None, :]).astype(jnp.bfloat16)
    local_part = jnp.einsum(
        "chtu,cuhp->cthp", weights, x_blocks, preferred_element_type=jnp.float32
    )
    last_cum = cum_blocks[:, SPAN - 1, :]
    x_weighted = (
        x_blocks.astype(jnp.float32)
        * (step_blocks * jnp.exp(last_cum[:, None, :] - cum_blocks))[:, :, :, None]
    ).astype(jnp.bfloat16)
    in_heads = jnp.repeat(in_map, per_group, axis=2)
    added = jnp.einsum("cuhp,cuhn->chpn", x_weighted, in_heads, preferred_element_type=jnp.float32)

    def carry_on(carried, element):
        block_decay, block_added = element
        return (block_decay[:, None, None] * carried + block_added, carried)

    empty_state = jnp.zeros((heads_here, HEAD_DIM, STATE), jnp.float32)
    device_state, entering = lax.scan(carry_on, empty_state, (jnp.exp(last_cum), added))
    device_decay = jnp.exp(jnp.sum(last_cum, axis=0))
    seeded = device_state + jnp.where(leading, device_decay[:, None, None] * init_state, 0.0)
    identity = (jnp.ones_like(device_decay), jnp.zeros_like(device_state))
    scanned = carried_in((device_decay, seeded), "seq", combine, identity)
    incoming = jnp.where(leading, init_state, scanned[1])
    prefix = jnp.exp(jnp.cumsum(last_cum, axis=0) - last_cum)
    states_in = entering + prefix[:, :, None, None] * incoming[None]
    out_heads = jnp.repeat(out_map, per_group, axis=2).astype(jnp.float32)
    carried_part = (
        jnp.einsum("cthn,chpn->cthp", out_heads, states_in, precision=lax.Precision.HIGHEST)
        * jnp.exp(cum_blocks)[:, :, :, None]
    )
    ssm_out = local_part + carried_part + skip[None, None, :, None] * x_blocks.astype(jnp.float32)
    ssm_out = ssm_out.reshape(row_count, heads_here * HEAD_DIM)
    squares = lax.psum(jnp.sum(ssm_out * ssm_out, axis=1), "tensor")
    mean_sq = squares / (HEADS * HEAD_DIM)
    normed = (ssm_out * lax.rsqrt(mean_sq + epsilon)[:, None] * norm_gain).astype(jnp.bfloat16)
    partial_out = jnp.dot(
        normed, lax.all_gather(w_out, "seq", axis=1, tiled=True), preferred_element_type=jnp.float32
    )
    layer_out = lax.psum_scatter(
        partial_out.astype(jnp.bfloat16), "tensor", scatter_dimension=0, tiled=True
    )
    return (layer_out, abs_max)


PAIR = 2
LINE = 4
ROWS = 8
CUTS = 2
SMEM = pl.BlockSpec(memory_space=pltpu.SMEM)
VMEM = pl.BlockSpec(memory_space=pltpu.VMEM)
HIGHEST = lax.Precision.HIGHEST


def splits(mesh):
    count, ranks = (mesh.shape["seq"], mesh.shape["tensor"])
    heads_all, groups_here = (HEADS // ranks, GROUPS // ranks)
    if count != PAIR * LINE or groups_here != PAIR or ranks & (ranks - 1):
        return False
    heads_here = heads_all // count
    return 2 * heads_here == ROWS and heads_here * HEAD_DIM == 2 * SPAN


def nt_dot(a, b, **kw):
    return lax.dot_general(
        a, b, (((1,), (1,)), ((), ())), preferred_element_type=jnp.float32, **kw
    )


def project_kernel(ranks, place_ref, factor_ref, *refs):
    hidden = [refs[x * ranks : (x + 1) * ranks] for x in range(PAIR)]
    refs = refs[PAIR * ranks :]
    own_x, x_far, own_bc, own_dt, rest = refs[:5]
    far_refs, near_refs, sent_refs = (
        refs[5 + at : 5 + at + LINE // 2] for at in range(0, 3 * LINE // 2, LINE // 2)
    )
    bc_ref, largest_ref, quant_ref, near_dt, all_dt = refs[5 + 3 * LINE // 2 :]
    side, z = (place_ref[1], place_ref[2])
    factor = factor_ref[0]
    depth = own_x.shape[0]
    largest = None
    for x in range(PAIR):
        for k in range(LINE):
            block = (k ^ z) * PAIR + (side ^ x)
            for j in range(ranks):
                for half in range(PAIR):
                    cut = slice(half * depth, (half + 1) * depth)
                    values = hidden[x][j][k, :, cut].astype(jnp.float32)
                    scaled = jnp.clip(values * factor, -quant_range, quant_range)
                    quant_ref[half, block, j] = scaled.astype(jnp.bfloat16)
                    top = jnp.max(jnp.abs(values).reshape(-1, ROWS, depth), axis=0)
                    largest = top if largest is None else jnp.maximum(largest, top)
    step_rows = own_dt.shape[0]
    other_dt = jnp.concatenate(
        [rest[at : at + step_rows] for at in range(depth, rest.shape[0], step_rows)], axis=1
    )
    width = largest_ref.shape[1]
    top = largest[:, :width]
    for at in range(width, depth, width):
        top = jnp.maximum(top, largest[:, at : at + width])
    largest_ref[...] = top

    channels = near_refs[0].shape[1]
    tokens = bc_ref.shape[0]
    rows = tokens // CUTS
    blocks = quant_ref.shape[1] // CUTS
    extra = rows // channels * ROWS
    upper = lax.broadcasted_iota(jnp.int32, (ROWS, channels), 0) < ROWS // 2

    def steps_of(dt_ref, run):
        dt = dt_ref[run // 2]
        pieces = []
        for at in range(0, rows, channels):
            piece = dt[:, at : at + channels]
            turned = pltpu.roll(piece, ROWS // 2, 0)
            lower_run = jnp.where(upper, piece, turned)
            upper_run = jnp.where(upper, turned, piece)
            pieces.append(split_parts(jnp.where(run % 2 == 0, lower_run, upper_run), upper))
        return jnp.concatenate(pieces, axis=0).astype(jnp.bfloat16)

    def columns(run):
        return pl.ds(pl.multiple_of(run * channels, channels), channels)

    for cut in range(CUTS):
        part = slice(cut * blocks, (cut + 1) * blocks)
        near = quant_ref[side, part].reshape(rows, depth)
        far = quant_ref[1 - side, part].reshape(rows, depth)

        def both(own, other):
            return jnp.dot(near, own, preferred_element_type=jnp.float32) + jnp.dot(
                far, other, preferred_element_type=jnp.float32
            )

        at_rows = slice(cut * rows, (cut + 1) * rows)
        extra_rows = slice(tokens + cut * extra, tokens + (cut + 1) * extra)
        ours = nt_dot(own_dt[...], near)
        near_dt[...] = ours.reshape(near_dt.shape)
        all_dt[...] = (ours + nt_dot(other_dt, far)).reshape(all_dt.shape)
        bc_ref[at_rows] = both(own_bc[...], rest[:depth]).astype(jnp.bfloat16)
        for m in range(LINE // 2):
            owner = z ^ (m + LINE // 2)
            run = side * LINE + owner
            other = x_far[:, columns(owner % (LINE // 2))]
            far_refs[m][at_rows] = both(own_x[:, columns(run)], other).astype(jnp.bfloat16)
            far_refs[m][extra_rows] = steps_of(all_dt, run)
            for out_refs, way in ((near_refs, side), (sent_refs, 1 - side)):
                run = way * LINE + (z ^ m)
                product = jnp.dot(near, own_x[:, columns(run)], preferred_element_type=jnp.float32)
                out_refs[m][at_rows] = product.astype(jnp.bfloat16)
                out_refs[m][extra_rows] = steps_of(near_dt, run)


def split_parts(values, upper):
    top = values.astype(jnp.bfloat16).astype(jnp.float32)
    return jnp.where(upper, top, values - top)


def project(place, factor, hidden, w_x, weights):
    line, own, wide = hidden[0].shape
    ranks = len(hidden) // PAIR
    depth, x_wide = (weights[0].shape[0], 2 * weights[0].shape[1])
    channels, maps_wide = (x_wide // LINE, weights[1].shape[1])
    tokens = line * PAIR * ranks * own
    extra = tokens // channels * ROWS
    dt_shape = (weights[2].shape[0] // ROWS, ROWS, tokens // CUTS)
    payload = jax.ShapeDtypeStruct((tokens + extra, channels), jnp.bfloat16)
    maps = jax.ShapeDtypeStruct((tokens, maps_wide), jnp.bfloat16)
    largest = jax.ShapeDtypeStruct((ROWS, 128), jnp.float32)
    outs = [payload] * (LINE + LINE // 2) + [maps, largest]
    return pl.pallas_call(
        functools.partial(project_kernel, ranks),
        in_specs=[SMEM, SMEM] + [VMEM] * (len(hidden) + 1 + len(weights)),
        out_specs=[VMEM] * len(outs),
        scratch_shapes=[
            pltpu.VMEM((PAIR, line * PAIR, ranks, own, depth), jnp.bfloat16),
            pltpu.VMEM(dt_shape, jnp.float32),
            pltpu.VMEM(dt_shape, jnp.float32),
        ],
        out_shape=outs,
        compiler_params=pltpu.CompilerParams(vmem_limit_bytes=32 * 2**20),
        cost_estimate=pl.CostEstimate(
            flops=2 * tokens * wide * (x_wide + maps_wide),
            bytes_accessed=2 * tokens * (wide + x_wide),
            transcendentals=0,
        ),
        name="project",
    )(place, factor, *hidden, w_x, *weights)


def onward_kernel(*refs):
    share_refs, out_ref = (refs[:-1], refs[-1])
    rows, channels = out_ref.shape
    tokens = rows * channels // (channels + ROWS)
    total = sum(ref[:tokens].astype(jnp.float32) for ref in share_refs)
    out_ref[:tokens] = total.astype(jnp.bfloat16)
    upper = lax.broadcasted_iota(jnp.int32, (ROWS, channels), 0) < ROWS // 2
    extra = sum(ref[tokens:].astype(jnp.float32) for ref in share_refs)
    pieces = []
    for at in range(0, rows - tokens, ROWS):
        piece = extra[at : at + ROWS]
        pieces.append(split_parts(piece + pltpu.roll(piece, ROWS // 2, 0), upper))
    out_ref[tokens:] = jnp.concatenate(pieces, axis=0).astype(jnp.bfloat16)


def onward(*shares):
    own = shares[0]
    return pl.pallas_call(
        onward_kernel,
        in_specs=[VMEM] * len(shares),
        out_specs=VMEM,
        out_shape=jax.ShapeDtypeStruct(own.shape, own.dtype),
        compiler_params=pltpu.CompilerParams(vmem_limit_bytes=8 * 2**20),
        cost_estimate=pl.CostEstimate(
            flops=len(shares) * own.size,
            bytes_accessed=2 * (len(shares) + 1) * own.size,
            transcendentals=0,
        ),
        name="onward",
    )(*shares)


def turned_rank(rank, ranks):
    turned = 0
    while ranks > 1:
        turned, rank, ranks = (2 * turned + rank % 2, rank // 2, ranks // 2)
    return turned


def scan_kernel(place_ref, scale_ref, *refs):
    x_refs, bc_refs = (refs[:-9], refs[-9:-6])
    small_ref, largest_ref, state_ref, out_ref, x_buf, bc_buf = refs[-6:]
    tokens, channels = bc_refs[0].shape
    blocks = tokens // SPAN
    heads = channels // HEAD_DIM
    rank, z = (place_ref[0], place_ref[2])
    ranks = place_ref.shape[0] - 3
    own = SPAN // ranks
    edge = ROWS
    in_scale = scale_ref[0]
    at_end = (z == 0) | (z == LINE - 1)
    x_buf[:edge] = small_ref[:edge]
    bc_buf[:edge] = small_ref[edge : 2 * edge]
    state = state_ref[...].T

    for block in range(blocks):
        for true_rank in range(ranks):
            source = block * SPAN + (true_rank ^ rank) * own
            source = pl.ds(pl.multiple_of(source, own), own)
            at = edge + block * SPAN + true_rank * own
            at = slice(at, at + own)
            total = sum(ref[source].astype(jnp.float32) for ref in x_refs) * in_scale
            x_buf[at] = total.astype(jnp.bfloat16).astype(jnp.float32)
            near, far, done = (ref[source].astype(jnp.float32) for ref in bc_refs)
            total = ((near + far) * in_scale).astype(jnp.bfloat16).astype(jnp.float32)
            bc_buf[at] = jnp.where(at_end, done, total)

    taps = 2 * edge

    def activate(buf, row, block):
        start = edge - (KERNEL - 1) + block * SPAN
        summed = small_ref[row : row + 1] * buf[start : start + SPAN]
        for k in range(1, KERNEL):
            summed = summed + small_ref[row + k : row + k + 1] * buf[start + k : start + k + SPAN]
        return (summed / (1.0 + jnp.exp(-summed))).astype(jnp.bfloat16)

    skip = small_ref[taps + 2 * KERNEL : taps + 2 * KERNEL + 1]
    gain = small_ref[taps + 2 * KERNEL + 1 : taps + 2 * KERNEL + 2]
    bias = small_ref[4 * edge :, :SPAN]
    rate = small_ref[4 * edge :, SPAN:]

    up = lax.broadcasted_iota(jnp.int32, (SPAN, SPAN), 0)
    across = lax.broadcasted_iota(jnp.int32, (SPAN, SPAN), 1)
    together = SPAN // HEAD_DIM
    insides = [
        ((across >= h * HEAD_DIM) & (across < (h + 1) * HEAD_DIM))
        .astype(jnp.float32)
        .astype(jnp.bfloat16)
        for h in range(together)
    ]
    lower = up >= across
    upper = (up <= across).astype(jnp.float32)
    lanes = across[:ROWS]

    dt = sum(ref[tokens:].astype(jnp.float32) for ref in x_refs)
    steps = []
    wide = channels // SPAN
    for block in range(blocks):
        tile = dt[block // wide * ROWS : (block // wide + 1) * ROWS]
        cut = tile[:, block % wide * SPAN : (block % wide + 1) * SPAN]
        cut = (cut + pltpu.roll(cut, ROWS // 2, 0)) * in_scale
        bit = 1
        while bit < ranks:
            shift = bit * own
            flipped = jnp.where(
                (lanes // shift) % 2 == 1,
                pltpu.roll(cut, shift, 1),
                pltpu.roll(cut, SPAN - shift, 1),
            )
            cut = jnp.where((rank & bit) != 0, flipped, cut)
            bit *= 2
        raw = cut + bias
        steps.append(jnp.maximum(raw, 0.0) + jnp.log1p(jnp.exp(-jnp.abs(raw))))
    drops = jnp.concatenate([-step * rate for step in steps], axis=0)
    cums = jnp.dot(drops, upper, precision=HIGHEST, preferred_element_type=jnp.float32)

    sums = jnp.zeros((SPAN, SPAN), jnp.float32)
    for block in range(blocks):
        x_act = activate(x_buf, taps, block)
        bc_act = activate(bc_buf, taps + KERNEL, block)
        in_map, out_map = (bc_act[:, :STATE], bc_act[:, STATE:])
        step, cum = (steps[block], cums[block * ROWS : (block + 1) * ROWS])
        last = cum[:, SPAN - 1 : SPAN]
        turned = jnp.concatenate(
            [
                cum,
                step * jnp.exp(last - cum),
                jnp.exp(cum),
                jnp.zeros((SPAN - 3 * ROWS, SPAN), jnp.float32),
            ],
            axis=0,
        ).T

        def spread(row):
            tiles = []
            for first in range(row, row + heads, together):
                tile = jnp.broadcast_to(turned[:, first : first + 1], across.shape)
                for h in range(1, together):
                    column = turned[:, first + h : first + h + 1]
                    tile = jnp.where(across >= h * HEAD_DIM, column, tile)
                tiles.append(tile)
            return jnp.concatenate(tiles, axis=1)

        inner = jnp.where(lower, nt_dot(out_map, in_map), 0.0)
        x_wide = x_act.astype(jnp.float32)
        local_tiles = []
        for first in range(0, heads, together):
            weights, spaced = ([], [])
            tile = x_act[:, first * HEAD_DIM : (first + together) * HEAD_DIM]
            for h in range(first, first + together):
                gap = jnp.where(lower, turned[:, h : h + 1] - cum[h : h + 1], 0.0)
                weights.append((inner * jnp.exp(gap) * step[h : h + 1]).astype(jnp.bfloat16))
                spaced.append(tile * insides[h - first])
            local_tiles.append(
                jnp.dot(
                    jnp.concatenate(weights, axis=1),
                    jnp.concatenate(spaced, axis=0),
                    preferred_element_type=jnp.float32,
                )
            )
        local_part = jnp.concatenate(local_tiles, axis=1)
        grown = spread(2 * ROWS)
        x_weighted = (x_wide * spread(ROWS)).astype(jnp.bfloat16)
        added = lax.dot_general(
            in_map, x_weighted, (((0,), (0,)), ((), ())), preferred_element_type=jnp.float32
        )
        high = state.astype(jnp.bfloat16)
        rest = (state - high.astype(jnp.float32)).astype(jnp.bfloat16)
        carried = jnp.dot(
            jnp.concatenate([out_map, out_map], axis=1),
            jnp.concatenate([high, rest], axis=0),
            preferred_element_type=jnp.float32,
        )
        ssm_out = local_part + grown * carried + skip * x_wide
        state = grown[SPAN - 1 : SPAN] * state + added
        gained = (ssm_out * gain).astype(jnp.bfloat16)
        for true_rank in range(ranks):
            at = (turned_rank(true_rank, ranks) * blocks + block) * own
            out_ref[at : at + own] = gained[true_rank * own : (true_rank + 1) * own]
        summed = jnp.sum(ssm_out * ssm_out, axis=1, keepdims=True)
        sums = jnp.where(across == block, summed, sums)

    whole = sums.T[:ROWS]
    top = whole.astype(jnp.bfloat16).astype(jnp.float32)
    largest = jnp.broadcast_to(jnp.max(largest_ref[...]), (ROWS, channels))
    extra = jnp.concatenate([jnp.concatenate([top, whole - top], axis=1), largest], axis=0)
    out_ref[tokens:] = extra.astype(jnp.bfloat16)


def scan(place, in_scale, sums, maps, small, largest, state):
    channels = sums[0].shape[1]
    tokens = maps[0].shape[0]

    out = jax.ShapeDtypeStruct((tokens + 2 * ROWS, channels), jnp.bfloat16)
    return pl.pallas_call(
        scan_kernel,
        in_specs=[SMEM, SMEM] + [VMEM] * (len(sums) + len(maps) + 3),
        out_specs=VMEM,
        scratch_shapes=[
            pltpu.VMEM((tokens + ROWS, channels), jnp.float32),
            pltpu.VMEM((tokens + ROWS, 2 * STATE), jnp.float32),
        ],
        out_shape=out,
        compiler_params=pltpu.CompilerParams(vmem_limit_bytes=20 * 2**20),
        cost_estimate=pl.CostEstimate(
            flops=8 * tokens * SPAN * channels,
            bytes_accessed=8 * tokens * channels,
            transcendentals=tokens * (channels + 8 * SPAN),
        ),
        name="scan",
    )(place, in_scale, *sums, *maps, small, largest, state)


def by_heads(
    hidden_in,
    prev_amax,
    w_x,
    w_bc,
    w_dt,
    conv_x,
    conv_bc,
    conv_state_x,
    conv_state_bc,
    dt_bias,
    decay_rate,
    skip,
    init_state,
    norm_gain,
    w_out,
):
    margin = KERNEL - 1
    count, here = (lax.axis_size("seq"), lax.axis_index("seq"))
    ranks, rank = (lax.axis_size("tensor"), lax.axis_index("tensor"))
    z, side = (here // PAIR, here % PAIR)
    place_of = side * LINE + z
    f32, bf16 = (jnp.float32, jnp.bfloat16)
    own, width = hidden_in.shape
    depth = w_x.shape[0]
    channels = w_x.shape[1] // count
    heads_here = w_dt.shape[1] // count
    in_scale = (prev_amax / quant_range).reshape(1)
    factor = (quant_range / prev_amax).reshape(1)
    place = jnp.stack([rank, side, z] + [rank] * ranks).astype(jnp.int32)

    def pick(array, axis, index):
        return lax.dynamic_index_in_dim(array, index, axis, keepdims=False)

    def along(value, pairs):
        moves = [(a * PAIR + x, b * PAIR + x) for a, b in pairs for x in range(PAIR)]
        return lax.ppermute(value, "seq", moves)

    def across(value):
        return lax.ppermute(value, "seq", [(s, s ^ 1) for s in range(count)])

    def of_heads(array):
        return jnp.repeat(array, HEAD_DIM)[None]

    by_channel = jnp.concatenate(
        [conv_state_x.astype(f32), conv_x, of_heads(skip), norm_gain[None]], axis=0
    )
    by_channel = lax.dynamic_slice_in_dim(by_channel, place_of * channels, channels, axis=1)
    by_map = jnp.concatenate([conv_state_bc.astype(f32), conv_bc], axis=0)
    by_map = pick(by_map, 1, side).reshape(margin + KERNEL, 2 * STATE)
    by_head = jnp.stack([dt_bias, decay_rate]).reshape(2, count, heads_here)
    by_head = jnp.tile(pick(by_head, 1, place_of).T, (ROWS // heads_here, 1))
    by_head = jnp.repeat(by_head, SPAN, axis=1)
    blank = jnp.zeros((ROWS - margin, channels), f32)
    small = jnp.concatenate(
        [
            blank,
            by_channel[:margin],
            blank,
            by_map[:margin],
            by_channel[margin : margin + KERNEL],
            by_map[margin:],
            by_channel[margin + KERNEL :],
            jnp.zeros((2 * ROWS - 2 * KERNEL - 2, channels), f32),
            by_head,
        ],
        axis=0,
    )

    start_state = lax.dynamic_slice_in_dim(
        init_state, place_of * heads_here, heads_here, axis=0
    ).reshape(channels, STATE)

    tie = lax.optimization_barrier
    half_run = LINE // 2 * channels
    opposite = (z // (LINE // 2)) ^ 1
    at = ((1 - side) * 2 + opposite) * half_run
    x_sent = lax.dynamic_slice_in_dim(w_x, at, half_run, axis=1)
    dt_rows = w_dt.T
    dt_cut = [dt_rows[:, at : at + 2 * STATE] for at in range(0, depth, 2 * STATE)]
    maps_sent = pick(w_bc, 1, 1 - side).reshape(depth, 2 * STATE)
    rest_other = across(jnp.concatenate([maps_sent, *dt_cut], axis=0))
    bc_own = pick(w_bc, 1, side).reshape(depth, 2 * STATE)

    def line_columns(m):
        return lax.dynamic_slice_in_dim(hidden_in, (z ^ m) * PAIR * depth, PAIR * depth, axis=1)

    arrived = [line_columns(0)]
    for m in range(1, LINE):
        arrived.append(along(line_columns(m), [(s, s ^ m) for s in range(LINE)]))
    stacked = jnp.stack(arrived)
    stacked, x_sent = tie((stacked, x_sent))
    beyond_pair = across(stacked)
    x_far = across(x_sent)
    beyond_pair, small, start_state, bc_own, dt_rows = tie(
        (beyond_pair, small, start_state, bc_own, dt_rows)
    )
    rows = []
    for mine in (stacked, beyond_pair):
        ours = [mine]
        for j in range(1, ranks):
            bit = j & -j
            pairs = [(t, t ^ bit) for t in range(ranks)]
            ours.append(lax.ppermute(ours[j - bit], "tensor", pairs))
        rows.extend(ours)

    start, end = (0, LINE - 1)
    at_end = (z == start) | (z == end)
    next_start, next_end = (1, LINE - 2)
    inward = [(start, next_start), (end, next_end)]
    outward = [(next_start, start), (next_end, end)]
    middle = [(next_start, next_end), (next_end, next_start)]
    over_middle = [(next_start, end), (next_end, start)]
    beside_pairs = [(s, s ^ 1) for s in range(LINE)]
    weights = (x_far, bc_own, dt_rows, rest_other)
    over, far, mine, near, mine_sent, near_sent, maps, largest = project(
        place, factor, rows, w_x, weights
    )

    map_hop = along(maps, inward)
    hop_far = along(far, inward)
    hop_over = along(over, inward)
    near = onward(near, across(near_sent))
    got_mine = across(mine_sent)
    near_out = along(near, outward)
    map_sum = (maps.astype(f32) + map_hop.astype(f32)).astype(bf16)
    map_far = along(map_sum, middle)
    map_done = ((map_sum.astype(f32) + map_far.astype(f32)) * in_scale).astype(bf16)
    sent_end = onward(over, hop_far)
    got_end = along(sent_end, over_middle)
    near, unused = tie((near, sent_end))
    near_in = along(near, inward)
    hop_over, near_out, unused = tie((hop_over, near_out, sent_end))
    sent_next = onward(far, hop_over)
    got_next = along(sent_next, middle)
    got_end, near_in = tie((got_end, near_in))
    near_sum = onward(mine, got_mine, near_out, near_in)
    map_done, unused = tie((map_done, sent_next))
    map_done = along(map_done, outward)
    gained = scan(
        place,
        in_scale,
        [near_sum, got_end, got_next],
        [map_sum, map_far, map_done],
        small,
        largest,
        start_state,
    )

    tokens = gained.shape[0] - 2 * ROWS
    beside = along(gained, beside_pairs)
    facing = along(gained, middle)
    second = jnp.where(at_end, along(facing, outward), facing)
    beyond = along(beside, middle)
    third = jnp.where(at_end, along(beyond, outward), beyond)
    far_own = across(gained)
    far_beside = across(beside)
    second, far_own = tie((second, far_own))
    far_second = across(second)
    third, far_beside = tie((third, far_beside))
    far_third = across(third)
    two, three = (jnp.where(at_end, 2, 3), jnp.where(at_end, 3, 2))

    def rows_for(x, m):
        at = ((side ^ x) * LINE + (z ^ m)) * channels
        return lax.dynamic_slice_in_dim(w_out, at, channels, axis=0)

    total = None
    tails = [far_third[tokens:]]
    for x, m, piece in (
        (0, 0, gained),
        (1, 0, far_own),
        (0, 1, beside),
        (1, 1, far_beside),
        (0, two, second),
        (1, two, far_second),
        (0, three, third),
    ):
        product = jnp.dot(piece, rows_for(x, m), preferred_element_type=f32)
        total = product if total is None else total + product
        tails.append(piece[tokens:])
    total, far_third = tie((total, far_third))
    last_rows = rows_for(1, three)
    tails = [tail.astype(f32) for tail in tails]
    squares = sum(tail[:ROWS, :SPAN] + tail[:ROWS, SPAN:] for tail in tails)
    top = functools.reduce(jnp.maximum, [tail[ROWS:, :SPAN] for tail in tails])

    def run_of(array, index, run):
        return lax.dynamic_slice_in_dim(array, index * run, run, axis=0)

    def first_sum(index):
        block, so_far = (run_of(far_third, index, run), run_of(total, index, run))
        return so_far + jnp.dot(block, last_rows, preferred_element_type=f32)

    run = tokens // 2
    keeps = rank % 2
    pairs = [(t, t ^ 1) for t in range(ranks)]
    received = lax.ppermute(first_sum(1 - keeps).astype(bf16), "tensor", pairs)
    kept = first_sum(keeps)
    squares = squares + lax.ppermute(squares, "tensor", pairs)
    bit = 2
    while bit < ranks:
        run //= 2
        keeps = (rank // bit) % 2
        pairs = [(t, t ^ bit) for t in range(ranks)]
        sent = run_of(kept, 1 - keeps, run) + run_of(received, 1 - keeps, run).astype(f32)
        kept = run_of(kept, keeps, run) + run_of(received, keeps, run).astype(f32)
        received = lax.ppermute(sent.astype(bf16), "tensor", pairs)
        squares = squares + lax.ppermute(squares, "tensor", pairs)
        bit *= 2
    mean_sq = squares.reshape(count, ranks, own) / (HEADS * HEAD_DIM)
    factors = lax.rsqrt(pick(mean_sq, 1, rank) + epsilon)
    final = (kept + received.astype(f32)).reshape(count, own, -1) * factors[:, :, None]
    final = lax.all_to_all(final.astype(bf16), "seq", split_axis=0, concat_axis=0, tiled=True)
    layer_out = final.transpose(1, 0, 2).reshape(own, count * final.shape[2])
    return (layer_out, jnp.max(top))


def solution(mesh):
    return jax.shard_map(
        by_heads if splits(mesh) else by_tokens,
        mesh=mesh,
        in_specs=(
            P(("seq", "tensor"), None),
            P(),
            P("seq", "tensor"),
            P("seq", "tensor", None, None),
            P("seq", "tensor"),
            P(None, "tensor"),
            P(None, "tensor", None, None),
            P(None, "tensor"),
            P(None, "tensor", None, None),
            P("tensor"),
            P("tensor"),
            P("tensor"),
            P("tensor", None, None),
            P("tensor"),
            P("tensor", "seq"),
        ),
        out_specs=(P(("seq", "tensor"), None), P()),
        check_vma=False,
    )
```

```python
import functools

import jax
import jax.numpy as jnp
from jax import lax
from jax.experimental import pallas as pl
from jax.experimental.pallas import tpu as pltpu
from jax.sharding import PartitionSpec as P

HEADS = 128
HEAD_DIM = 64
STATE = 128
GROUPS = 8
KERNEL = 4
SPAN = 128


epsilon = 1e-05
quant_range = 448.0


def from_behind(value, axis, steps):
    count = lax.axis_size(axis)
    first, last = (max(0, -steps), min(count, count - steps))
    return lax.ppermute(value, axis, [(source, source + steps) for source in range(first, last)])


def carried_in(shard, axis, combine, identity):
    count, here = (lax.axis_size(axis), lax.axis_index(axis))
    everything = jax.tree.map(
        lambda part, kind: lax.all_gather(part.astype(kind), axis),
        shard,
        (jnp.bfloat16, jnp.bfloat16),
    )
    start = jax.tree.map(
        lambda part, zero: jnp.broadcast_to(jnp.asarray(zero, part.dtype), part.shape),
        shard,
        identity,
    )

    def turn(k, before):
        reached = k < here
        new = combine(
            before, jax.tree.map(lambda part, own: part[k].astype(own.dtype), everything, shard)
        )
        return jax.tree.map(lambda a, b: jnp.where(reached, a, b), new, before)

    return lax.fori_loop(0, count, turn, start)


def depthwise(before, projected, conv_taps, length):
    extended = jnp.concatenate([before, projected], axis=0)
    summed = conv_taps[0] * extended[0:length]
    for offset in range(1, KERNEL):
        summed = summed + conv_taps[offset] * extended[offset : offset + length]
    return jax.nn.silu(summed).astype(jnp.bfloat16)


def combine(earlier, later):
    return (earlier[0] * later[0], later[0][:, None, None] * earlier[1] + later[1])


def by_tokens(
    hidden_in,
    prev_amax,
    w_x,
    w_bc,
    w_dt,
    conv_x,
    conv_bc,
    conv_state_x,
    conv_state_bc,
    dt_bias,
    decay_rate,
    skip,
    init_state,
    norm_gain,
    w_out,
):
    margin = KERNEL - 1
    gathered = lax.all_gather(hidden_in, "tensor", axis=0, tiled=True)
    abs_max = lax.pmax(jnp.max(jnp.abs(gathered.astype(jnp.float32))), "seq")
    in_scale = prev_amax / quant_range
    leading = lax.axis_index("seq") == 0
    row_count = gathered.shape[0]
    bc_width = w_bc.shape[1] * w_bc.shape[2] * w_bc.shape[3]
    bc_rows = jnp.reshape(w_bc, (w_bc.shape[0], bc_width))
    scaled = gathered.astype(jnp.float32) * (quant_range / prev_amax)
    quant = jnp.clip(scaled, -quant_range, quant_range).astype(jnp.bfloat16)
    pieces = (
        lax.all_gather(w_x, "seq", axis=0, tiled=True),
        lax.all_gather(bc_rows, "seq", axis=0, tiled=True),
        lax.all_gather(w_dt, "seq", axis=0, tiled=True),
    )
    x_proj, bc_proj, dt_proj = tuple(
        (
            jnp.dot(quant, weight_piece, preferred_element_type=jnp.float32)
            for weight_piece in pieces
        )
    )
    x_whole = (x_proj * in_scale).astype(jnp.bfloat16)
    bc_whole = (bc_proj * in_scale).astype(jnp.bfloat16)
    dt_raw = dt_proj * in_scale
    state_bc = jnp.reshape(conv_state_bc, (margin, bc_width))
    received = from_behind(
        (x_whole[row_count - margin :], bc_whole[row_count - margin :]), "seq", 1
    )
    x_edge = jnp.where(leading, conv_state_x, received[0])
    bc_edge = jnp.where(leading, state_bc, received[1])
    x_act = depthwise(x_edge, x_whole, conv_x, row_count)
    bc_act = depthwise(bc_edge, bc_whole, jnp.reshape(conv_bc, (KERNEL, bc_width)), row_count)
    step_size = jax.nn.softplus(dt_raw + dt_bias)
    heads_here = step_size.shape[1]
    groups_here = w_bc.shape[1]
    per_group = HEADS // GROUPS
    blocks = row_count // SPAN
    x_blocks = x_act.reshape(blocks, SPAN, heads_here, HEAD_DIM)
    bc_blocks = bc_act.reshape(blocks, SPAN, groups_here, 2, STATE)
    in_map = bc_blocks[:, :, :, 0]
    out_map = bc_blocks[:, :, :, 1]
    step_blocks = step_size.reshape(blocks, SPAN, heads_here)
    cum_blocks = jnp.cumsum(-step_blocks * decay_rate, axis=1)
    index_row = jnp.arange(SPAN, dtype=jnp.int32)
    lower_mask = index_row[:, None] >= index_row[None, :]
    intersection = jnp.einsum(
        "ctgn,cugn->cgtu", out_map, in_map, preferred_element_type=jnp.float32
    )
    intersection = jnp.repeat(intersection, per_group, axis=1)
    cum_heads = jnp.transpose(cum_blocks, (0, 2, 1))
    log_gap = cum_heads[:, :, :, None] - cum_heads[:, :, None, :]
    decay = jnp.exp(jnp.where(lower_mask[None, None], log_gap, -1e30))
    step_heads = jnp.transpose(step_blocks, (0, 2, 1))
    weights = (intersection * decay * step_heads[:, :, None, :]).astype(jnp.bfloat16)
    local_part = jnp.einsum(
        "chtu,cuhp->cthp", weights, x_blocks, preferred_element_type=jnp.float32
    )
    last_cum = cum_blocks[:, SPAN - 1, :]
    x_weighted = (
        x_blocks.astype(jnp.float32)
        * (step_blocks * jnp.exp(last_cum[:, None, :] - cum_blocks))[:, :, :, None]
    ).astype(jnp.bfloat16)
    in_heads = jnp.repeat(in_map, per_group, axis=2)
    added = jnp.einsum("cuhp,cuhn->chpn", x_weighted, in_heads, preferred_element_type=jnp.float32)

    def carry_on(carried, element):
        block_decay, block_added = element
        return (block_decay[:, None, None] * carried + block_added, carried)

    empty_state = jnp.zeros((heads_here, HEAD_DIM, STATE), jnp.float32)
    device_state, entering = lax.scan(carry_on, empty_state, (jnp.exp(last_cum), added))
    device_decay = jnp.exp(jnp.sum(last_cum, axis=0))
    seeded = device_state + jnp.where(leading, device_decay[:, None, None] * init_state, 0.0)
    identity = (jnp.ones_like(device_decay), jnp.zeros_like(device_state))
    scanned = carried_in((device_decay, seeded), "seq", combine, identity)
    incoming = jnp.where(leading, init_state, scanned[1])
    prefix = jnp.exp(jnp.cumsum(last_cum, axis=0) - last_cum)
    states_in = entering + prefix[:, :, None, None] * incoming[None]
    out_heads = jnp.repeat(out_map, per_group, axis=2).astype(jnp.float32)
    carried_part = (
        jnp.einsum("cthn,chpn->cthp", out_heads, states_in, precision=lax.Precision.HIGHEST)
        * jnp.exp(cum_blocks)[:, :, :, None]
    )
    ssm_out = local_part + carried_part + skip[None, None, :, None] * x_blocks.astype(jnp.float32)
    ssm_out = ssm_out.reshape(row_count, heads_here * HEAD_DIM)
    squares = lax.psum(jnp.sum(ssm_out * ssm_out, axis=1), "tensor")
    mean_sq = squares / (HEADS * HEAD_DIM)
    normed = (ssm_out * lax.rsqrt(mean_sq + epsilon)[:, None] * norm_gain).astype(jnp.bfloat16)
    partial_out = jnp.dot(
        normed, lax.all_gather(w_out, "seq", axis=1, tiled=True), preferred_element_type=jnp.float32
    )
    layer_out = lax.psum_scatter(
        partial_out.astype(jnp.bfloat16), "tensor", scatter_dimension=0, tiled=True
    )
    return (layer_out, abs_max)


PAIR = 2
LINE = 4
ROWS = 8
CUTS = 2
SMEM = pl.BlockSpec(memory_space=pltpu.SMEM)
VMEM = pl.BlockSpec(memory_space=pltpu.VMEM)
HIGHEST = lax.Precision.HIGHEST


def splits(mesh):
    count, ranks = (mesh.shape["seq"], mesh.shape["tensor"])
    heads_all, groups_here = (HEADS // ranks, GROUPS // ranks)
    if count != PAIR * LINE or groups_here != PAIR or ranks & (ranks - 1):
        return False
    heads_here = heads_all // count
    return 2 * heads_here == ROWS and heads_here * HEAD_DIM == 2 * SPAN


def nt_dot(a, b, **kw):
    return lax.dot_general(
        a, b, (((1,), (1,)), ((), ())), preferred_element_type=jnp.float32, **kw
    )


def project_kernel(ranks, place_ref, factor_ref, *refs):
    hidden = [refs[x * ranks : (x + 1) * ranks] for x in range(PAIR)]
    refs = refs[PAIR * ranks :]
    own_x, x_far, own_bc, own_dt, rest = refs[:5]
    far_refs, near_refs, sent_refs = (
        refs[5 + at : 5 + at + LINE // 2] for at in range(0, 3 * LINE // 2, LINE // 2)
    )
    bc_ref, largest_ref, quant_ref, near_dt, all_dt = refs[5 + 3 * LINE // 2 :]
    side, z = (place_ref[1], place_ref[2])
    factor = factor_ref[0]
    depth = own_x.shape[0]
    largest = None
    for x in range(PAIR):
        for k in range(LINE):
            block = (k ^ z) * PAIR + (side ^ x)
            for j in range(ranks):
                for half in range(PAIR):
                    cut = slice(half * depth, (half + 1) * depth)
                    values = hidden[x][j][k, :, cut].astype(jnp.float32)
                    scaled = jnp.clip(values * factor, -quant_range, quant_range)
                    quant_ref[half, block, j] = scaled.astype(jnp.bfloat16)
                    top = jnp.max(jnp.abs(values).reshape(-1, ROWS, depth), axis=0)
                    largest = top if largest is None else jnp.maximum(largest, top)
    step_rows = own_dt.shape[0]
    other_dt = jnp.concatenate(
        [rest[at : at + step_rows] for at in range(depth, rest.shape[0], step_rows)], axis=1
    )
    width = largest_ref.shape[1]
    top = largest[:, :width]
    for at in range(width, depth, width):
        top = jnp.maximum(top, largest[:, at : at + width])
    largest_ref[...] = top

    channels = near_refs[0].shape[1]
    tokens = bc_ref.shape[0]
    rows = tokens // CUTS
    blocks = quant_ref.shape[1] // CUTS
    extra = rows // channels * ROWS
    upper = lax.broadcasted_iota(jnp.int32, (ROWS, channels), 0) < ROWS // 2

    def steps_of(dt_ref, run):
        dt = dt_ref[run // 2]
        pieces = []
        for at in range(0, rows, channels):
            piece = dt[:, at : at + channels]
            turned = pltpu.roll(piece, ROWS // 2, 0)
            lower_run = jnp.where(upper, piece, turned)
            upper_run = jnp.where(upper, turned, piece)
            pieces.append(split_parts(jnp.where(run % 2 == 0, lower_run, upper_run), upper))
        return jnp.concatenate(pieces, axis=0).astype(jnp.bfloat16)

    def columns(run):
        return pl.ds(pl.multiple_of(run * channels, channels), channels)

    for cut in range(CUTS):
        part = slice(cut * blocks, (cut + 1) * blocks)
        near = quant_ref[side, part].reshape(rows, depth)
        far = quant_ref[1 - side, part].reshape(rows, depth)

        def both(own, other):
            return jnp.dot(near, own, preferred_element_type=jnp.float32) + jnp.dot(
                far, other, preferred_element_type=jnp.float32
            )

        at_rows = slice(cut * rows, (cut + 1) * rows)
        extra_rows = slice(tokens + cut * extra, tokens + (cut + 1) * extra)
        ours = nt_dot(own_dt[...], near)
        near_dt[...] = ours.reshape(near_dt.shape)
        all_dt[...] = (ours + nt_dot(other_dt, far)).reshape(all_dt.shape)
        bc_ref[at_rows] = both(own_bc[...], rest[:depth]).astype(jnp.bfloat16)
        for m in range(LINE // 2):
            owner = z ^ (m + LINE // 2)
            run = side * LINE + owner
            other = x_far[:, columns(owner % (LINE // 2))]
            far_refs[m][at_rows] = both(own_x[:, columns(run)], other).astype(jnp.bfloat16)
            far_refs[m][extra_rows] = steps_of(all_dt, run)
            for out_refs, way in ((near_refs, side), (sent_refs, 1 - side)):
                run = way * LINE + (z ^ m)
                product = jnp.dot(near, own_x[:, columns(run)], preferred_element_type=jnp.float32)
                out_refs[m][at_rows] = product.astype(jnp.bfloat16)
                out_refs[m][extra_rows] = steps_of(near_dt, run)


def split_parts(values, upper):
    top = values.astype(jnp.bfloat16).astype(jnp.float32)
    return jnp.where(upper, top, values - top)


def project(place, factor, hidden, w_x, weights):
    line, own, wide = hidden[0].shape
    ranks = len(hidden) // PAIR
    depth, x_wide = (weights[0].shape[0], 2 * weights[0].shape[1])
    channels, maps_wide = (x_wide // LINE, weights[1].shape[1])
    tokens = line * PAIR * ranks * own
    extra = tokens // channels * ROWS
    dt_shape = (weights[2].shape[0] // ROWS, ROWS, tokens // CUTS)
    payload = jax.ShapeDtypeStruct((tokens + extra, channels), jnp.bfloat16)
    maps = jax.ShapeDtypeStruct((tokens, maps_wide), jnp.bfloat16)
    largest = jax.ShapeDtypeStruct((ROWS, 128), jnp.float32)
    outs = [payload] * (LINE + LINE // 2) + [maps, largest]
    return pl.pallas_call(
        functools.partial(project_kernel, ranks),
        in_specs=[SMEM, SMEM] + [VMEM] * (len(hidden) + 1 + len(weights)),
        out_specs=[VMEM] * len(outs),
        scratch_shapes=[
            pltpu.VMEM((PAIR, line * PAIR, ranks, own, depth), jnp.bfloat16),
            pltpu.VMEM(dt_shape, jnp.float32),
            pltpu.VMEM(dt_shape, jnp.float32),
        ],
        out_shape=outs,
        compiler_params=pltpu.CompilerParams(vmem_limit_bytes=32 * 2**20),
        cost_estimate=pl.CostEstimate(
            flops=2 * tokens * wide * (x_wide + maps_wide),
            bytes_accessed=2 * tokens * (wide + x_wide),
            transcendentals=0,
        ),
        name="project",
    )(place, factor, *hidden, w_x, *weights)


def onward_kernel(*refs):
    share_refs, out_ref = (refs[:-1], refs[-1])
    rows, channels = out_ref.shape
    tokens = rows * channels // (channels + ROWS)
    total = sum(ref[:tokens].astype(jnp.float32) for ref in share_refs)
    out_ref[:tokens] = total.astype(jnp.bfloat16)
    upper = lax.broadcasted_iota(jnp.int32, (ROWS, channels), 0) < ROWS // 2
    extra = sum(ref[tokens:].astype(jnp.float32) for ref in share_refs)
    pieces = []
    for at in range(0, rows - tokens, ROWS):
        piece = extra[at : at + ROWS]
        pieces.append(split_parts(piece + pltpu.roll(piece, ROWS // 2, 0), upper))
    out_ref[tokens:] = jnp.concatenate(pieces, axis=0).astype(jnp.bfloat16)


def onward(*shares):
    own = shares[0]
    return pl.pallas_call(
        onward_kernel,
        in_specs=[VMEM] * len(shares),
        out_specs=VMEM,
        out_shape=jax.ShapeDtypeStruct(own.shape, own.dtype),
        compiler_params=pltpu.CompilerParams(vmem_limit_bytes=8 * 2**20),
        cost_estimate=pl.CostEstimate(
            flops=len(shares) * own.size,
            bytes_accessed=2 * (len(shares) + 1) * own.size,
            transcendentals=0,
        ),
        name="onward",
    )(*shares)


def turned_rank(rank, ranks):
    turned = 0
    while ranks > 1:
        turned, rank, ranks = (2 * turned + rank % 2, rank // 2, ranks // 2)
    return turned


def scan_kernel(place_ref, scale_ref, *refs):
    x_refs, bc_refs = (refs[:-9], refs[-9:-6])
    small_ref, largest_ref, state_ref, out_ref, x_buf, bc_buf = refs[-6:]
    tokens, channels = bc_refs[0].shape
    blocks = tokens // SPAN
    heads = channels // HEAD_DIM
    rank, z = (place_ref[0], place_ref[2])
    ranks = place_ref.shape[0] - 3
    own = SPAN // ranks
    edge = ROWS
    in_scale = scale_ref[0]
    at_end = (z == 0) | (z == LINE - 1)
    x_buf[:edge] = small_ref[:edge]
    bc_buf[:edge] = small_ref[edge : 2 * edge]
    state = state_ref[...].T

    for block in range(blocks):
        for true_rank in range(ranks):
            source = block * SPAN + (true_rank ^ rank) * own
            source = pl.ds(pl.multiple_of(source, own), own)
            at = edge + block * SPAN + true_rank * own
            at = slice(at, at + own)
            total = sum(ref[source].astype(jnp.float32) for ref in x_refs) * in_scale
            x_buf[at] = total.astype(jnp.bfloat16).astype(jnp.float32)
            near, far, done = (ref[source].astype(jnp.float32) for ref in bc_refs)
            total = ((near + far) * in_scale).astype(jnp.bfloat16).astype(jnp.float32)
            bc_buf[at] = jnp.where(at_end, done, total)

    taps = 2 * edge

    def activate(buf, row, block):
        start = edge - (KERNEL - 1) + block * SPAN
        summed = small_ref[row : row + 1] * buf[start : start + SPAN]
        for k in range(1, KERNEL):
            summed = summed + small_ref[row + k : row + k + 1] * buf[start + k : start + k + SPAN]
        return (summed / (1.0 + jnp.exp(-summed))).astype(jnp.bfloat16)

    skip = small_ref[taps + 2 * KERNEL : taps + 2 * KERNEL + 1]
    gain = small_ref[taps + 2 * KERNEL + 1 : taps + 2 * KERNEL + 2]
    bias = small_ref[4 * edge :, :SPAN]
    rate = small_ref[4 * edge :, SPAN:]

    up = lax.broadcasted_iota(jnp.int32, (SPAN, SPAN), 0)
    across = lax.broadcasted_iota(jnp.int32, (SPAN, SPAN), 1)
    together = SPAN // HEAD_DIM
    insides = [
        ((across >= h * HEAD_DIM) & (across < (h + 1) * HEAD_DIM))
        .astype(jnp.float32)
        .astype(jnp.bfloat16)
        for h in range(together)
    ]
    lower = up >= across
    upper = (up <= across).astype(jnp.float32)
    lanes = across[:ROWS]

    dt = sum(ref[tokens:].astype(jnp.float32) for ref in x_refs)
    steps = []
    wide = channels // SPAN
    for block in range(blocks):
        tile = dt[block // wide * ROWS : (block // wide + 1) * ROWS]
        cut = tile[:, block % wide * SPAN : (block % wide + 1) * SPAN]
        cut = (cut + pltpu.roll(cut, ROWS // 2, 0)) * in_scale
        bit = 1
        while bit < ranks:
            shift = bit * own
            flipped = jnp.where(
                (lanes // shift) % 2 == 1,
                pltpu.roll(cut, shift, 1),
                pltpu.roll(cut, SPAN - shift, 1),
            )
            cut = jnp.where((rank & bit) != 0, flipped, cut)
            bit *= 2
        raw = cut + bias
        steps.append(jnp.maximum(raw, 0.0) + jnp.log1p(jnp.exp(-jnp.abs(raw))))
    drops = jnp.concatenate([-step * rate for step in steps], axis=0)
    cums = jnp.dot(drops, upper, precision=HIGHEST, preferred_element_type=jnp.float32)

    sums = jnp.zeros((SPAN, SPAN), jnp.float32)
    for block in range(blocks):
        x_act = activate(x_buf, taps, block)
        bc_act = activate(bc_buf, taps + KERNEL, block)
        in_map, out_map = (bc_act[:, :STATE], bc_act[:, STATE:])
        step, cum = (steps[block], cums[block * ROWS : (block + 1) * ROWS])
        last = cum[:, SPAN - 1 : SPAN]
        turned = jnp.concatenate(
            [
                cum,
                step * jnp.exp(last - cum),
                jnp.exp(cum),
                jnp.zeros((SPAN - 3 * ROWS, SPAN), jnp.float32),
            ],
            axis=0,
        ).T

        def spread(row):
            tiles = []
            for first in range(row, row + heads, together):
                tile = jnp.broadcast_to(turned[:, first : first + 1], across.shape)
                for h in range(1, together):
                    column = turned[:, first + h : first + h + 1]
                    tile = jnp.where(across >= h * HEAD_DIM, column, tile)
                tiles.append(tile)
            return jnp.concatenate(tiles, axis=1)

        inner = jnp.where(lower, nt_dot(out_map, in_map), 0.0)
        x_wide = x_act.astype(jnp.float32)
        local_tiles = []
        for first in range(0, heads, together):
            weights, spaced = ([], [])
            tile = x_act[:, first * HEAD_DIM : (first + together) * HEAD_DIM]
            for h in range(first, first + together):
                gap = jnp.where(lower, turned[:, h : h + 1] - cum[h : h + 1], 0.0)
                weights.append((inner * jnp.exp(gap) * step[h : h + 1]).astype(jnp.bfloat16))
                spaced.append(tile * insides[h - first])
            local_tiles.append(
                jnp.dot(
                    jnp.concatenate(weights, axis=1),
                    jnp.concatenate(spaced, axis=0),
                    preferred_element_type=jnp.float32,
                )
            )
        local_part = jnp.concatenate(local_tiles, axis=1)
        grown = spread(2 * ROWS)
        x_weighted = (x_wide * spread(ROWS)).astype(jnp.bfloat16)
        added = lax.dot_general(
            in_map, x_weighted, (((0,), (0,)), ((), ())), preferred_element_type=jnp.float32
        )
        high = state.astype(jnp.bfloat16)
        rest = (state - high.astype(jnp.float32)).astype(jnp.bfloat16)
        carried = jnp.dot(
            jnp.concatenate([out_map, out_map], axis=1),
            jnp.concatenate([high, rest], axis=0),
            preferred_element_type=jnp.float32,
        )
        ssm_out = local_part + grown * carried + skip * x_wide
        state = grown[SPAN - 1 : SPAN] * state + added
        gained = (ssm_out * gain).astype(jnp.bfloat16)
        for true_rank in range(ranks):
            at = (turned_rank(true_rank, ranks) * blocks + block) * own
            out_ref[at : at + own] = gained[true_rank * own : (true_rank + 1) * own]
        summed = jnp.sum(ssm_out * ssm_out, axis=1, keepdims=True)
        sums = jnp.where(across == block, summed, sums)

    whole = sums.T[:ROWS]
    top = whole.astype(jnp.bfloat16).astype(jnp.float32)
    largest = jnp.broadcast_to(jnp.max(largest_ref[...]), (ROWS, channels))
    extra = jnp.concatenate([jnp.concatenate([top, whole - top], axis=1), largest], axis=0)
    out_ref[tokens:] = extra.astype(jnp.bfloat16)


def scan(place, in_scale, sums, maps, small, largest, state):
    channels = sums[0].shape[1]
    tokens = maps[0].shape[0]

    out = jax.ShapeDtypeStruct((tokens + 2 * ROWS, channels), jnp.bfloat16)
    return pl.pallas_call(
        scan_kernel,
        in_specs=[SMEM, SMEM] + [VMEM] * (len(sums) + len(maps) + 3),
        out_specs=VMEM,
        scratch_shapes=[
            pltpu.VMEM((tokens + ROWS, channels), jnp.float32),
            pltpu.VMEM((tokens + ROWS, 2 * STATE), jnp.float32),
        ],
        out_shape=out,
        compiler_params=pltpu.CompilerParams(vmem_limit_bytes=20 * 2**20),
        cost_estimate=pl.CostEstimate(
            flops=8 * tokens * SPAN * channels,
            bytes_accessed=8 * tokens * channels,
            transcendentals=tokens * (channels + 8 * SPAN),
        ),
        name="scan",
    )(place, in_scale, *sums, *maps, small, largest, state)


def by_heads(
    hidden_in,
    prev_amax,
    w_x,
    w_bc,
    w_dt,
    conv_x,
    conv_bc,
    conv_state_x,
    conv_state_bc,
    dt_bias,
    decay_rate,
    skip,
    init_state,
    norm_gain,
    w_out,
):
    margin = KERNEL - 1
    count, here = (lax.axis_size("seq"), lax.axis_index("seq"))
    ranks, rank = (lax.axis_size("tensor"), lax.axis_index("tensor"))
    z, side = (here // PAIR, here % PAIR)
    place_of = side * LINE + z
    f32, bf16 = (jnp.float32, jnp.bfloat16)
    own, width = hidden_in.shape
    depth = w_x.shape[0]
    channels = w_x.shape[1] // count
    heads_here = w_dt.shape[1] // count
    in_scale = (prev_amax / quant_range).reshape(1)
    factor = (quant_range / prev_amax).reshape(1)
    place = jnp.stack([rank, side, z] + [rank] * ranks).astype(jnp.int32)

    def pick(array, axis, index):
        return lax.dynamic_index_in_dim(array, index, axis, keepdims=False)

    def along(value, pairs):
        moves = [(a * PAIR + x, b * PAIR + x) for a, b in pairs for x in range(PAIR)]
        return lax.ppermute(value, "seq", moves)

    def across(value):
        return lax.ppermute(value, "seq", [(s, s ^ 1) for s in range(count)])

    def of_heads(array):
        return jnp.repeat(array, HEAD_DIM)[None]

    by_channel = jnp.concatenate(
        [conv_state_x.astype(f32), conv_x, of_heads(skip), norm_gain[None]], axis=0
    )
    by_channel = lax.dynamic_slice_in_dim(by_channel, place_of * channels, channels, axis=1)
    by_map = jnp.concatenate([conv_state_bc.astype(f32), conv_bc], axis=0)
    by_map = pick(by_map, 1, side).reshape(margin + KERNEL, 2 * STATE)
    by_head = jnp.stack([dt_bias, decay_rate]).reshape(2, count, heads_here)
    by_head = jnp.tile(pick(by_head, 1, place_of).T, (ROWS // heads_here, 1))
    by_head = jnp.repeat(by_head, SPAN, axis=1)
    blank = jnp.zeros((ROWS - margin, channels), f32)
    small = jnp.concatenate(
        [
            blank,
            by_channel[:margin],
            blank,
            by_map[:margin],
            by_channel[margin : margin + KERNEL],
            by_map[margin:],
            by_channel[margin + KERNEL :],
            jnp.zeros((2 * ROWS - 2 * KERNEL - 2, channels), f32),
            by_head,
        ],
        axis=0,
    )

    start_state = lax.dynamic_slice_in_dim(
        init_state, place_of * heads_here, heads_here, axis=0
    ).reshape(channels, STATE)

    tie = lax.optimization_barrier
    half_run = LINE // 2 * channels
    opposite = (z // (LINE // 2)) ^ 1
    at = ((1 - side) * 2 + opposite) * half_run
    x_sent = lax.dynamic_slice_in_dim(w_x, at, half_run, axis=1)
    dt_rows = w_dt.T
    dt_cut = [dt_rows[:, at : at + 2 * STATE] for at in range(0, depth, 2 * STATE)]
    maps_sent = pick(w_bc, 1, 1 - side).reshape(depth, 2 * STATE)
    rest_other = across(jnp.concatenate([maps_sent, *dt_cut], axis=0))
    bc_own = pick(w_bc, 1, side).reshape(depth, 2 * STATE)

    def line_columns(m):
        return lax.dynamic_slice_in_dim(hidden_in, (z ^ m) * PAIR * depth, PAIR * depth, axis=1)

    arrived = [line_columns(0)]
    for m in range(1, LINE):
        arrived.append(along(line_columns(m), [(s, s ^ m) for s in range(LINE)]))
    stacked = jnp.stack(arrived)
    stacked, x_sent = tie((stacked, x_sent))
    beyond_pair = across(stacked)
    x_far = across(x_sent)
    beyond_pair, small, start_state, bc_own, dt_rows = tie(
        (beyond_pair, small, start_state, bc_own, dt_rows)
    )
    rows = []
    for mine in (stacked, beyond_pair):
        ours = [mine]
        for j in range(1, ranks):
            bit = j & -j
            pairs = [(t, t ^ bit) for t in range(ranks)]
            ours.append(lax.ppermute(ours[j - bit], "tensor", pairs))
        rows.extend(ours)

    start, end = (0, LINE - 1)
    at_end = (z == start) | (z == end)
    next_start, next_end = (1, LINE - 2)
    inward = [(start, next_start), (end, next_end)]
    outward = [(next_start, start), (next_end, end)]
    middle = [(next_start, next_end), (next_end, next_start)]
    over_middle = [(next_start, end), (next_end, start)]
    beside_pairs = [(s, s ^ 1) for s in range(LINE)]
    weights = (x_far, bc_own, dt_rows, rest_other)
    over, far, mine, near, mine_sent, near_sent, maps, largest = project(
        place, factor, rows, w_x, weights
    )

    map_hop = along(maps, inward)
    hop_far = along(far, inward)
    hop_over = along(over, inward)
    near = onward(near, across(near_sent))
    got_mine = across(mine_sent)
    near_out = along(near, outward)
    map_sum = (maps.astype(f32) + map_hop.astype(f32)).astype(bf16)
    map_far = along(map_sum, middle)
    map_done = ((map_sum.astype(f32) + map_far.astype(f32)) * in_scale).astype(bf16)
    sent_end = onward(over, hop_far)
    got_end = along(sent_end, over_middle)
    hop_over, near_out, unused = tie((hop_over, near_out, sent_end))
    sent_next = onward(far, hop_over)
    got_next = along(sent_next, middle)
    near, unused = tie((near, sent_next))
    near_in = along(near, inward)
    got_end, near_in = tie((got_end, near_in))
    near_sum = onward(mine, got_mine, near_out, near_in)
    map_done, unused = tie((map_done, sent_next))
    map_done = along(map_done, outward)
    gained = scan(
        place,
        in_scale,
        [near_sum, got_end, got_next],
        [map_sum, map_far, map_done],
        small,
        largest,
        start_state,
    )

    tokens = gained.shape[0] - 2 * ROWS
    beside = along(gained, beside_pairs)
    facing = along(gained, middle)
    second = jnp.where(at_end, along(facing, outward), facing)
    beyond = along(beside, middle)
    third = jnp.where(at_end, along(beyond, outward), beyond)
    far_own = across(gained)
    far_beside = across(beside)
    second, far_own = tie((second, far_own))
    far_second = across(second)
    third, far_beside = tie((third, far_beside))
    far_third = across(third)
    two, three = (jnp.where(at_end, 2, 3), jnp.where(at_end, 3, 2))

    def rows_for(x, m):
        at = ((side ^ x) * LINE + (z ^ m)) * channels
        return lax.dynamic_slice_in_dim(w_out, at, channels, axis=0)

    total = None
    tails = [far_third[tokens:]]
    for x, m, piece in (
        (0, 0, gained),
        (1, 0, far_own),
        (0, 1, beside),
        (1, 1, far_beside),
        (0, two, second),
        (1, two, far_second),
        (0, three, third),
    ):
        product = jnp.dot(piece, rows_for(x, m), preferred_element_type=f32)
        total = product if total is None else total + product
        tails.append(piece[tokens:])
    total, far_third = tie((total, far_third))
    last_rows = rows_for(1, three)
    tails = [tail.astype(f32) for tail in tails]
    squares = sum(tail[:ROWS, :SPAN] + tail[:ROWS, SPAN:] for tail in tails)
    top = functools.reduce(jnp.maximum, [tail[ROWS:, :SPAN] for tail in tails])

    def run_of(array, index, run):
        return lax.dynamic_slice_in_dim(array, index * run, run, axis=0)

    def first_sum(index):
        block, so_far = (run_of(far_third, index, run), run_of(total, index, run))
        return so_far + jnp.dot(block, last_rows, preferred_element_type=f32)

    run = tokens // 2
    keeps = rank % 2
    pairs = [(t, t ^ 1) for t in range(ranks)]
    received = lax.ppermute(first_sum(1 - keeps).astype(bf16), "tensor", pairs)
    kept = first_sum(keeps)
    squares = squares + lax.ppermute(squares, "tensor", pairs)
    bit = 2
    while bit < ranks:
        run //= 2
        keeps = (rank // bit) % 2
        pairs = [(t, t ^ bit) for t in range(ranks)]
        sent = run_of(kept, 1 - keeps, run) + run_of(received, 1 - keeps, run).astype(f32)
        kept = run_of(kept, keeps, run) + run_of(received, keeps, run).astype(f32)
        received = lax.ppermute(sent.astype(bf16), "tensor", pairs)
        squares = squares + lax.ppermute(squares, "tensor", pairs)
        bit *= 2
    mean_sq = squares.reshape(count, ranks, own) / (HEADS * HEAD_DIM)
    factors = lax.rsqrt(pick(mean_sq, 1, rank) + epsilon)
    final = (kept + received.astype(f32)).reshape(count, own, -1) * factors[:, :, None]
    final = lax.all_to_all(final.astype(bf16), "seq", split_axis=0, concat_axis=0, tiled=True)
    layer_out = final.transpose(1, 0, 2).reshape(own, count * final.shape[2])
    return (layer_out, jnp.max(top))


def solution(mesh):
    return jax.shard_map(
        by_heads if splits(mesh) else by_tokens,
        mesh=mesh,
        in_specs=(
            P(("seq", "tensor"), None),
            P(),
            P("seq", "tensor"),
            P("seq", "tensor", None, None),
            P("seq", "tensor"),
            P(None, "tensor"),
            P(None, "tensor", None, None),
            P(None, "tensor"),
            P(None, "tensor", None, None),
            P("tensor"),
            P("tensor"),
            P("tensor"),
            P("tensor", None, None),
            P("tensor"),
            P("tensor", "seq"),
        ),
        out_specs=(P(("seq", "tensor"), None), P()),
        check_vma=False,
    )
```
